32 devices in a mesh: groups: 2 (over y), seq: 4 (over z), batch: 2 (over x), tp: 2 (over core).
Axes of the slice: x: 2, y: 2, z: 4, core: 2. Of those that a mesh axis runs over, the one named last changes fastest.
Arguments:
- tokens: bfloat16 [4, 1024, 7168], P(('groups', 'batch'), 'seq', 'tp'), parts along dimension 0, may hold values from -24 to 24
- frozen_qkv_matrix: bfloat16 [768, 7168], P('seq', 'tp'), as said below
- adapter_down_weight: bfloat16 [64, 64, 2, 3584], P(None, None, 'tp', ('seq', 'batch')), may hold values from -0.0625 to 0.0625
- adapter_up_weight: bfloat16 [64, 32, 640], P(None, None, ('seq', 'batch')), may hold values from -0.5 to 0.5
- adapter_bank_row: int32 [64], replicated, may hold values from 0 to 63, each once
- document_lengths: int32 [4, 3], P('groups'), parts along dimension 0, may hold values from 1 to 512, 1024 in all within a row
- document_adapter: int32 [4, 3], P('groups'), parts along dimension 0, may hold values from 0 to 63
- output_gradient: bfloat16 [4, 1024, 512], P(('groups', 'batch'), ('seq', 'tp')), parts along dimension 0, may hold values from -6 to 6
Outputs:
- attn_out: bfloat16 [4, 1024, 512], P(('groups', 'batch'), ('seq', 'tp')), parts along dimension 0
- token_grad: bfloat16 [4, 1024, 7168], P(('groups', 'batch'), 'seq', 'tp'), parts along dimension 0
- down_grad: float32 [128, 64, 2, 3584], P('groups', None, 'tp', ('seq', 'batch')), parts along dimension 0
- up_grad: float32 [128, 32, 640], P('groups', None, ('seq', 'batch')), parts along dimension 0
The draws below stay inside these ranges and needn't reach their ends.
There are 2 independent parts, one for each index of `groups`. The reference program is written for one: setup_inputs(seed, part) draws one part's arguments, and reference() takes and returns one part's arrays. A program takes and returns all parts, laid end to end along the dimension named above; an argument that names none is the same for every part. Nothing has to cross between parts.
Inputs may be any that keep to these rules, and one draw needn't show every extreme that they name: Entries of frozen_qkv_matrix are at most 18 / sqrt(7168) in magnitude.
All inputs are finite; a program needn't handle non-finite values.
Results may differ from the reference program's by a relative error of at most 0.0075.
The reference program's roundings to bfloat16 on the way count: a program that leaves them out, or rounds other values in their place, can miss the bound.
Values may be sent and summed in bfloat16 or wider, within the bound.
No kernel may reach another device: no remote copies, remote signals or barrier semaphores. Data moves between devices by JAX's collectives and lax.ppermute only.
A program may use at most 128 MiB of HBM per device.

```python
import math
import jax
import jax.numpy as jnp
import numpy as np
from jax import lax

MODEL_WIDTH = 7168
QHEADS = 4
HEAD_WIDTH = 128
ADAPTER_RANK = 32
ADAPTER_COUNT = 64
SEGS = 3
SAMPLES = 2
LENGTH = 1024
QCOLS = 512
QKV = 768
QUERY_VALUE = 640
JOINT_RANK2 = 64
N_TP = 2


def draw_tokens(key, part):
    key = jax.random.fold_in(key, 11)
    normal_key = jax.random.fold_in(key, 0)
    values = jnp.clip(jax.random.normal(normal_key, (SAMPLES, LENGTH, MODEL_WIDTH), jnp.float32), -6.0, 6.0)
    return values.astype(jnp.bfloat16)


def draw_frozen_qkv_matrix(key, part):
    key = jax.random.fold_in(key, 23)
    noise_key = jax.random.fold_in(key, 1)
    noise = jnp.clip(jax.random.normal(noise_key, (QKV, MODEL_WIDTH), jnp.float32), -6.0, 6.0)
    values = noise
    return (values * MODEL_WIDTH ** (-0.5)).astype(jnp.bfloat16)


def place_ends(drawn, stream_key, low, largest):
    dims = drawn.shape
    index_at = [jax.random.randint(jax.random.fold_in(stream_key, axis), (), 0, dims[axis]) for axis in range(len(dims))]
    drawn = drawn.at[tuple(index_at)].set(low)
    longest = dims.index(max(dims))
    index_at[longest] = (index_at[longest] + 1) % dims[longest]
    return drawn.at[tuple(index_at)].set(largest)


def block_scale(own_key, shape, shards, low, high):
    gain, own = 1.0, jax.random.fold_in(own_key, 6)
    for position, parts in shards:
        heights = jnp.exp(jax.random.uniform(jax.random.fold_in(own, position), (parts,), jnp.float32, low / len(shards), high / len(shards)))
        gain = gain * jnp.repeat(heights, shape[position] // parts).reshape([-1 if axis == position else 1 for axis in range(len(shape))])
    return gain


def rank_table(count, lean):
    portions = [(1 << 20) // math.isqrt(grade ** lean) + 1 for grade in range(1, count + 1)]
    width = 1 + sum(portions) // (1 << 30)
    return np.cumsum(np.array([max(1, weight // width) for weight in portions]))


def ranked_ids(own_key, dims, amount, slope):
    grid = rank_table(amount, slope)
    lot = jax.random.randint(jax.random.fold_in(own_key, 1), dims, 0, int(grid[amount - 1]))
    grade = jnp.searchsorted(jnp.asarray(grid, jnp.int32), lot, side="right")
    return jax.random.permutation(jax.random.fold_in(own_key, 2), amount)[grade].astype(jnp.int32)


def profile(amount, total, most, skew):
    loads = [(1 << 20) // math.isqrt(standing ** skew) + 1 for standing in range(2, amount + 1)]
    spare, counts = total - most - (amount - 1), [1] * (amount - 1)
    while spare > 0:
        candidates = [i for i in range(amount - 1) if counts[i] < most]
        whole, remaining = sum([loads[i] for i in candidates]), spare
        for i in candidates:
            addition = min(most - counts[i], max(1, remaining * loads[i] // whole), spare)
            counts[i] = counts[i] + addition
            spare = spare - addition
    return np.array([most] + counts)


def ragged(stream_key, number_of, total, limit, lean):
    if number_of == 2:
        one = jax.random.randint(stream_key, (), max(1, total - limit), min(limit, total - 1) + 1)
        return jnp.stack([one, total - one])
    sizes = jnp.asarray(profile(number_of, total, limit, lean), jnp.int32)
    twos = (number_of - 1) // 2
    donor, sink = sizes[1:1 + 2 * twos:2], sizes[2:2 + 2 * twos:2]
    room = jnp.minimum(donor - 1, limit - sink)
    moved = jax.random.randint(jax.random.fold_in(stream_key, 1), (twos,), 0, 1 << 20) % (room + 1)
    sizes = sizes.at[1:1 + 2 * twos:2].set(donor - moved).at[2:2 + 2 * twos:2].set(sink + moved)
    return sizes[jax.random.permutation(jax.random.fold_in(stream_key, 2), number_of)]


def gaussian(rng, shape, scale, bound, cuts=(), kind=jnp.bfloat16):
    array = jax.random.normal(rng, shape, jnp.float32) * scale
    if len(cuts) > 0:
        array = block_scale(rng, shape, cuts, -0.22, 0.18) * array
    return jnp.clip(array, min=-bound, max=bound).astype(kind)


def setup_inputs(seed: int = 0, part: int = 0) -> dict:
    streams_of = jax.random.split(jax.random.key(seed), 9)
    part_splits = jax.random.split(jax.random.fold_in(streams_of[8], part), 9)
    return {
        "tokens": draw_tokens(jax.random.fold_in(jax.random.fold_in(streams_of[8], part), 71), part),
        "frozen_qkv_matrix": draw_frozen_qkv_matrix(jax.random.fold_in(streams_of[8], 71), part),
        "adapter_down_weight": gaussian(streams_of[2], (ADAPTER_COUNT, JOINT_RANK2, N_TP, MODEL_WIDTH // N_TP), MODEL_WIDTH ** -0.5, 0.0625, ((2, 2), (3, 8))),
        "adapter_up_weight": gaussian(streams_of[3], (ADAPTER_COUNT, ADAPTER_RANK, QUERY_VALUE), (4 * ADAPTER_RANK) ** -0.5, 0.5, ((2, 8),)),
        "adapter_bank_row": jax.random.permutation(streams_of[4], ADAPTER_COUNT).astype(jnp.int32),
        "document_lengths": jax.vmap(lambda own: ragged(own, SEGS, LENGTH, LENGTH // 2, 1))(jax.random.split(part_splits[5], SAMPLES)).reshape((SAMPLES, SEGS)).astype(jnp.int32),
        "document_adapter": place_ends(ranked_ids(part_splits[6], (SAMPLES, SEGS), ADAPTER_COUNT, 2), jax.random.fold_in(part_splits[6], 3), 0, ADAPTER_COUNT - 1).astype(jnp.int32),
        "output_gradient": gaussian(part_splits[7], (SAMPLES, LENGTH, QCOLS), 1.0, 6.0, ((0, 2), (1, 8))),
    }


adapter_scale = 2.0
rope_base = 5000000.0


def segment_info(lengths, positions):
    segment_ends = jnp.cumsum(lengths).astype(jnp.int32)
    starts = segment_ends - lengths
    crossed = positions[:, None] >= segment_ends[None, :-1]
    segment = jnp.sum(crossed.astype(jnp.int32), axis=1).astype(jnp.int32)
    member = segment[:, None] == jnp.arange(lengths.shape[0], dtype=jnp.int32)[None, :]
    inside = positions - jnp.sum(jnp.where(member, starts[None, :], 0), axis=1).astype(jnp.int32)
    return segment, member, inside


def rope_tables(inside, head_width):
    exponent = jnp.arange(head_width // 2, dtype=jnp.float32) * (2.0 / head_width)
    inverse = jnp.power(jnp.float32(rope_base), -exponent)
    angles = inside.astype(jnp.float32)[:, None] * inverse[None, :]
    return jnp.cos(angles), jnp.sin(angles)


def rotate(values, cosine_table, sine_table):
    half_dim = values.shape[-1] // 2
    front_half = values[..., :half_dim]
    back_half = values[..., half_dim:]
    cosine_wide = cosine_table[:, None, :]
    sine_wide = sine_table[:, None, :]
    return jnp.concatenate([front_half * cosine_wide - back_half * sine_wide, back_half * cosine_wide + front_half * sine_wide], axis=-1)


def unrotate(gradients, cosine_table, sine_table):
    half_dim = gradients.shape[-1] // 2
    front_half = gradients[..., :half_dim]
    back_half = gradients[..., half_dim:]
    cosine_wide = cosine_table[:, None, :]
    sine_wide = sine_table[:, None, :]
    return jnp.concatenate([front_half * cosine_wide + back_half * sine_wide, back_half * cosine_wide - front_half * sine_wide], axis=-1)


def reference(tokens, frozen_qkv_matrix, adapter_down_weight, adapter_up_weight, adapter_bank_row, document_lengths, document_adapter, output_gradient):
    score_scale = HEAD_WIDTH ** -0.5
    query_columns = QHEADS * HEAD_WIDTH
    down_complete = adapter_down_weight.reshape(ADAPTER_COUNT, 2 * ADAPTER_RANK, MODEL_WIDTH)
    matches = document_adapter[..., None] == jnp.arange(ADAPTER_COUNT, dtype=jnp.int32)
    sample_rows = jnp.sum(jnp.where(matches, adapter_bank_row, 0), axis=-1).astype(jnp.int32)
    positions = jnp.arange(LENGTH, dtype=jnp.int32)

    def one_sample(inputs):
        sample_tokens, lengths, bank_row_list, incoming = inputs
        segment, member, inside = segment_info(lengths, positions)
        down_rows = jnp.take(down_complete, bank_row_list, axis=0).astype(jnp.float32)
        up_row_values = jnp.take(adapter_up_weight, bank_row_list, axis=0).astype(jnp.float32)
        base_projection = jnp.dot(sample_tokens, frozen_qkv_matrix.T, preferred_element_type=jnp.float32)
        token_wide = sample_tokens.astype(jnp.float32)
        low_all = jnp.einsum("td,srd->tsr", token_wide, down_rows)
        low_rank = jnp.sum(jnp.where(member[:, :, None], low_all, 0.0), axis=1).astype(jnp.bfloat16)
        low_wide = lax.optimization_barrier(low_rank).astype(jnp.float32)
        query_rank_rows = jnp.where(member[:, :, None], low_wide[:, None, :ADAPTER_RANK], 0.0)
        value_rank_rows = jnp.where(member[:, :, None], low_wide[:, None, ADAPTER_RANK:], 0.0)
        query_delta = jnp.einsum("tsr,src->tc", query_rank_rows, up_row_values)
        value_delta = jnp.einsum("tsr,src->tc", value_rank_rows, up_row_values)
        projected_query = base_projection[:, :query_columns] + adapter_scale * query_delta[:, :query_columns]
        proj_key = base_projection[:, query_columns:query_columns + HEAD_WIDTH]
        projected_value = base_projection[:, query_columns + HEAD_WIDTH:] + adapter_scale * value_delta[:, query_columns:]
        cosine_table, sine_table = rope_tables(inside, HEAD_WIDTH)
        queries = rotate(projected_query.reshape(LENGTH, QHEADS, HEAD_WIDTH), cosine_table, sine_table).astype(jnp.bfloat16)
        key_rows = rotate(proj_key[:, None, :], cosine_table, sine_table)[:, 0].astype(jnp.bfloat16)
        value_rows = projected_value.astype(jnp.bfloat16)
        queries, key_rows, value_rows = lax.optimization_barrier((queries, key_rows, value_rows))
        query_wide = queries.astype(jnp.float32)
        key_wide = key_rows.astype(jnp.float32)
        value_wide = value_rows.astype(jnp.float32)
        scores = jnp.einsum("thd,ud->htu", query_wide, key_wide) * score_scale
        allowed = (positions[None, :] <= positions[:, None]) & (segment[None, :] == segment[:, None])
        scores = jnp.where(allowed[None], scores, -jnp.inf)
        row_max = jnp.max(scores, axis=2, keepdims=True)
        raised = jnp.exp(scores - row_max)
        probabilities = raised / jnp.sum(raised, axis=2, keepdims=True)
        probs_low = lax.optimization_barrier(probabilities.astype(jnp.bfloat16)).astype(jnp.float32)
        attention = jnp.einsum("htu,ud->thd", probs_low, value_wide).astype(jnp.bfloat16)
        attention = lax.optimization_barrier(attention)
        grad_wide = incoming.astype(jnp.float32).reshape(LENGTH, QHEADS, HEAD_WIDTH)
        row_delta = jnp.transpose(jnp.sum(grad_wide * attention.astype(jnp.float32), axis=2))
        prob_grad = jnp.einsum("thd,ud->htu", grad_wide, value_wide)
        score_grad = (probabilities * (prob_grad - row_delta[:, :, None])).astype(jnp.bfloat16)
        score_grad = lax.optimization_barrier(score_grad).astype(jnp.float32)
        query_grad = jnp.einsum("htu,ud->thd", score_grad, key_wide) * score_scale
        key_grad = jnp.einsum("htu,thd->ud", score_grad, query_wide) * score_scale
        value_grad = jnp.einsum("htu,thd->ud", probs_low, grad_wide)
        grad_query = unrotate(query_grad, cosine_table, sine_table).reshape(LENGTH, query_columns).astype(jnp.bfloat16)
        grad_key = unrotate(key_grad[:, None, :], cosine_table, sine_table)[:, 0].astype(jnp.bfloat16)
        grad_rows = jnp.concatenate([grad_query, grad_key, value_grad.astype(jnp.bfloat16)], axis=1)
        grad_rows = lax.optimization_barrier(grad_rows)
        grad_full = grad_rows.astype(jnp.float32)
        qv_grad = jnp.concatenate([grad_full[:, :query_columns], grad_full[:, query_columns + HEAD_WIDTH:]], axis=1)
        is_query = jnp.arange(qv_grad.shape[1]) < query_columns
        query_gradient_part = jnp.where(is_query[None, :], qv_grad, 0.0)
        value_gradient_part = jnp.where(is_query[None, :], 0.0, qv_grad)
        low_query_grad = jnp.einsum("tc,src->tsr", query_gradient_part, up_row_values)
        low_value_grad = jnp.einsum("tc,src->tsr", value_gradient_part, up_row_values)
        rank_gradient = adapter_scale * jnp.concatenate([
            jnp.sum(jnp.where(member[:, :, None], low_query_grad, 0.0), axis=1),
            jnp.sum(jnp.where(member[:, :, None], low_value_grad, 0.0), axis=1)], axis=1)
        rank_gradient = lax.optimization_barrier(rank_gradient.astype(jnp.bfloat16)).astype(jnp.float32)
        up_portion = adapter_scale * (jnp.einsum("ynq,yl->nql", query_rank_rows, query_gradient_part) + jnp.einsum("ynq,yl->nql", value_rank_rows, value_gradient_part))
        low_tokens = jnp.where(member[:, :, None], rank_gradient[:, None, :], 0.0)
        token_part = jnp.dot(grad_rows, frozen_qkv_matrix, preferred_element_type=jnp.float32) + jnp.einsum("tsr,srd->td", low_tokens, down_rows)
        down_part = jnp.einsum("tsr,td->srd", low_tokens, token_wide)
        return attention.reshape(LENGTH, query_columns), token_part.astype(jnp.bfloat16), down_part, up_portion

    attention, token_grad, down_parts, up_parts = lax.map(one_sample, (tokens, document_lengths, sample_rows, output_gradient))
    flat_rows = sample_rows.reshape(-1)
    bank_hot = (flat_rows[:, None] == jnp.arange(ADAPTER_COUNT, dtype=jnp.int32)[None, :]).astype(jnp.float32)
    down_grad = jnp.einsum("na,nx->ax", bank_hot, down_parts.reshape(flat_rows.shape[0], -1), precision=lax.Precision.HIGHEST)
    up_grad = jnp.einsum("na,nx->ax", bank_hot, up_parts.reshape(flat_rows.shape[0], -1), precision=lax.Precision.HIGHEST)
    return attention, token_grad, down_grad.reshape(ADAPTER_COUNT, 2 * ADAPTER_RANK, N_TP, MODEL_WIDTH // N_TP), up_grad.reshape(ADAPTER_COUNT, ADAPTER_RANK, QUERY_VALUE)
```

```python
import jax
import jax.numpy as jnp
from jax import lax
from jax.sharding import PartitionSpec as P

QHEADS = 4
HEAD_WIDTH = 128
ADAPTER_RANK = 32


adapter_scale = 2.0
rope_base = 5000000.0
start_floor = -1e30


def segment_info(lengths, positions):
    segment_ends = jnp.cumsum(lengths)
    starts = segment_ends - lengths
    crossed = positions[:, None] >= segment_ends[None, :-1]
    segment = jnp.sum(crossed.astype(jnp.int32), axis=1)
    member = segment[:, None] == jnp.arange(lengths.shape[0], dtype=jnp.int32)[None, :]
    inside = positions - jnp.sum(jnp.where(member, starts[None, :], 0), axis=1)
    return (segment, member, inside)


def rope_tables(inside, head_width):
    exponent = jnp.arange(head_width // 2, dtype=jnp.float32) * (2.0 / head_width)
    inverse = jnp.power(jnp.float32(rope_base), -exponent)
    angles = inside.astype(jnp.float32)[:, None] * inverse[None, :]
    return (jnp.cos(angles), jnp.sin(angles))


def rotate(values, cosine_table, sine_table):
    half_dim = values.shape[-1] // 2
    front_half = values[..., :half_dim]
    back_half = values[..., half_dim:]
    cosine_wide = cosine_table[:, None, :]
    sine_wide = sine_table[:, None, :]
    return jnp.concatenate(
        [
            front_half * cosine_wide - back_half * sine_wide,
            back_half * cosine_wide + front_half * sine_wide,
        ],
        axis=-1,
    )


def unrotate(gradients, cosine_table, sine_table):
    half_dim = gradients.shape[-1] // 2
    front_half = gradients[..., :half_dim]
    back_half = gradients[..., half_dim:]
    cosine_wide = cosine_table[:, None, :]
    sine_wide = sine_table[:, None, :]
    return jnp.concatenate(
        [
            front_half * cosine_wide + back_half * sine_wide,
            back_half * cosine_wide - front_half * sine_wide,
        ],
        axis=-1,
    )


def lookup_rows(adapter_bank_row, document_adapter):
    matches = document_adapter[..., None] == jnp.arange(adapter_bank_row.shape[0], dtype=jnp.int32)
    return jnp.sum(jnp.where(matches, adapter_bank_row, 0), axis=-1)


def keep_same(carry):
    return carry


def allowed_block(query_pos, query_seg, key_seg, offset, key_block):
    block_pos = offset + jnp.arange(key_block, dtype=jnp.int32)
    block_seg = lax.dynamic_slice_in_dim(key_seg, offset, key_block)
    return (block_pos[None, :] <= query_pos[:, None]) & (block_seg[None, :] == query_seg[:, None])


def block_scores(queries, keys_all, allowed, offset, key_block):
    score_scale = queries.shape[2] ** (-0.5)
    key_rows = lax.dynamic_slice_in_dim(keys_all, offset, key_block)
    scores = (
        jnp.einsum("chd,kd->hck", queries, key_rows, preferred_element_type=jnp.float32)
        * score_scale
    )
    return jnp.where(allowed[None], scores, -jnp.inf)


def attend_rows(queries, query_pos, query_seg, keys_all, values_all, key_seg, key_block):
    row_total_count, head_count, head_width = queries.shape
    block_count = keys_all.shape[0] // key_block

    def gather_stats(block_id, stats):
        offset = block_id * key_block
        allowed = allowed_block(query_pos, query_seg, key_seg, offset, key_block)

        def gather_compute(stats):
            running_max, running_total = stats
            scores = block_scores(queries, keys_all, allowed, offset, key_block)
            new_max = jnp.maximum(running_max, jnp.max(scores, axis=2))
            new_total = running_total * jnp.exp(running_max - new_max) + jnp.sum(
                jnp.exp(scores - new_max[:, :, None]), axis=2
            )
            return (new_max, new_total)

        return lax.cond(jnp.any(allowed), gather_compute, keep_same, stats)

    start_stats = (
        jnp.full((head_count, row_total_count), start_floor, jnp.float32),
        jnp.zeros((head_count, row_total_count), jnp.float32),
    )
    row_max, row_total = lax.fori_loop(0, block_count, gather_stats, start_stats)

    def add_values(block_id, weighted):
        offset = block_id * key_block
        allowed = allowed_block(query_pos, query_seg, key_seg, offset, key_block)

        def add_compute(weighted):
            scores = block_scores(queries, keys_all, allowed, offset, key_block)
            block_low = (jnp.exp(scores - row_max[:, :, None]) / row_total[:, :, None]).astype(
                jnp.bfloat16
            )
            value_rows = lax.dynamic_slice_in_dim(values_all, offset, key_block)
            return weighted + jnp.einsum(
                "hck,kd->chd", block_low, value_rows, preferred_element_type=jnp.float32
            )

        return lax.cond(jnp.any(allowed), add_compute, keep_same, weighted)

    weighted = lax.fori_loop(
        0,
        block_count,
        add_values,
        jnp.zeros((row_total_count, head_count, values_all.shape[1]), jnp.float32),
    )
    return (lax.optimization_barrier(weighted.astype(jnp.bfloat16)), row_max, row_total)


def attend_grad(
    queries,
    output_rows,
    incoming,
    row_max,
    row_total,
    query_pos,
    query_seg,
    keys_all,
    values_all,
    key_seg,
    key_block,
):
    row_total_count, head_count, head_width = queries.shape
    block_count = keys_all.shape[0] // key_block
    score_scale = head_width ** (-0.5)
    row_delta = jnp.transpose(
        jnp.sum(incoming.astype(jnp.float32) * output_rows.astype(jnp.float32), axis=2)
    )

    def backward_step(query_grad, block_id):
        offset = block_id * key_block
        allowed = allowed_block(query_pos, query_seg, key_seg, offset, key_block)

        def backward_compute(query_grad):
            scores = block_scores(queries, keys_all, allowed, offset, key_block)
            prob_block = jnp.exp(scores - row_max[:, :, None]) / row_total[:, :, None]
            low_block = prob_block.astype(jnp.bfloat16)
            key_rows = lax.dynamic_slice_in_dim(keys_all, offset, key_block)
            value_rows = lax.dynamic_slice_in_dim(values_all, offset, key_block)
            prob_grad = jnp.einsum(
                "chd,kd->hck", incoming, value_rows, preferred_element_type=jnp.float32
            )
            score_grad = (prob_block * (prob_grad - row_delta[:, :, None])).astype(jnp.bfloat16)
            query_grad = query_grad + jnp.einsum(
                "hck,kd->chd", score_grad, key_rows, preferred_element_type=jnp.float32
            )
            key_part = (
                jnp.einsum("hck,chd->kd", score_grad, queries, preferred_element_type=jnp.float32)
                * score_scale
            )
            value_part = jnp.einsum(
                "hck,chd->kd", low_block, incoming, preferred_element_type=jnp.float32
            )
            return (query_grad, jnp.concatenate([key_part, value_part], axis=1))

        def skip(query_grad):
            return (query_grad, jnp.zeros((key_block, 2 * head_width), jnp.float32))

        return lax.cond(jnp.any(allowed), backward_compute, skip, query_grad)

    start_grad = jnp.zeros((row_total_count, head_count, head_width), jnp.float32)
    query_grad, block_grads = lax.scan(
        backward_step, start_grad, jnp.arange(block_count, dtype=jnp.int32)
    )
    return (query_grad * score_scale, block_grads.reshape(block_count * key_block, 2 * head_width))


def shards(
    tokens,
    frozen_qkv_matrix,
    adapter_down_weight,
    adapter_up_weight,
    adapter_bank_row,
    document_lengths,
    document_adapter,
    output_gradient,
):
    cycle_size = lax.axis_size(("seq", "tp"))
    cycle_index = lax.axis_index(("seq", "tp"))
    chip_size = lax.axis_size("tp")
    seq_count = lax.axis_size("seq")
    batch_index = lax.axis_index("batch")
    seq_index = lax.axis_index("seq")
    local_tokens = tokens[0]
    tok_count = local_tokens.shape[0]
    row_count = tok_count // chip_size
    half_rows = row_count // 2
    length = cycle_size * row_count
    key_block = min(512, length)
    head_width = HEAD_WIDTH
    query_columns = QHEADS * HEAD_WIDTH
    low_width = ADAPTER_RANK
    adapters = adapter_bank_row.shape[0]
    sample_rows = lookup_rows(adapter_bank_row, document_adapter)
    own_lengths = lax.dynamic_index_in_dim(document_lengths, batch_index, 0, keepdims=False)
    batch_count = lax.axis_size("batch")
    group_count = lax.axis_size("groups")
    segment_count = document_lengths.shape[1]
    plane_index = lax.axis_index(("groups", "batch"))
    plane_count = group_count * batch_count
    flat_rows = sample_rows.reshape(-1)
    frozen_rows = frozen_qkv_matrix.shape[0] // plane_count
    frozen_piece = lax.dynamic_slice_in_dim(
        frozen_qkv_matrix, plane_index * frozen_rows, frozen_rows
    )
    frozen = lax.all_gather(frozen_piece, ("seq", "groups", "batch"), axis=0, tiled=True)
    joint_rank = adapter_down_weight.shape[1]
    outgoing_down = adapter_down_weight[:, :, 0, :][sample_rows]
    outgoing_up = adapter_up_weight[sample_rows]
    got_down = lax.all_to_all(outgoing_down, "batch", split_axis=0, concat_axis=0, tiled=True)
    got_up = lax.all_to_all(outgoing_up, "batch", split_axis=0, concat_axis=0, tiled=True)
    got_down = jnp.transpose(got_down, (1, 2, 0, 3)).reshape(segment_count * joint_rank, -1)
    got_up = jnp.transpose(got_up, (1, 2, 0, 3)).reshape(segment_count * low_width, -1)
    down_all = lax.all_gather(got_down, "seq", axis=0)
    up_all = lax.all_gather(got_up, "seq", axis=0)
    down_width = got_down.shape[1]
    up_rows = jnp.transpose(up_all, (1, 0, 2)).reshape(segment_count, low_width, -1)
    base_part = lax.dot_general(
        local_tokens, frozen, (((1,), (1,)), ((), ())), preferred_element_type=jnp.float32
    )
    token_pos = seq_index * tok_count + jnp.arange(tok_count, dtype=jnp.int32)
    token_seg, token_member, token_inside = segment_info(own_lengths, token_pos)
    low_all = sum(
        lax.dot_general(
            local_tokens[:, owner * down_width : (owner + 1) * down_width],
            down_all[owner],
            (((1,), (1,)), ((), ())),
            preferred_element_type=jnp.float32,
        )
        for owner in range(seq_count)
    ).reshape(tok_count, segment_count, joint_rank)
    low_part = jnp.sum(jnp.where(token_member[:, :, None], low_all, 0.0), axis=1)
    summed_rows = lax.psum_scatter(
        jnp.concatenate([base_part, low_part], axis=1), "tp", scatter_dimension=0, tiled=True
    )
    qkv_width = base_part.shape[1]
    base_row_values = summed_rows[:, :qkv_width]
    low_rows = summed_rows[:, qkv_width:]
    row_pos = cycle_index * row_count + jnp.arange(row_count, dtype=jnp.int32)
    row_seg, row_member, row_inside = segment_info(own_lengths, row_pos)
    low_rank = low_rows.astype(jnp.bfloat16)
    query_rank_rows = jnp.where(row_member[:, :, None], low_rank[:, None, :low_width], 0)
    value_rank_rows = jnp.where(row_member[:, :, None], low_rank[:, None, low_width:], 0)
    query_delta = jnp.einsum(
        "tsr,src->tc", query_rank_rows, up_rows, preferred_element_type=jnp.float32
    )
    value_delta = jnp.einsum(
        "tsr,src->tc", value_rank_rows, up_rows, preferred_element_type=jnp.float32
    )
    projected_query = (
        base_row_values[:, :query_columns] + adapter_scale * query_delta[:, :query_columns]
    )
    proj_key = base_row_values[:, query_columns : query_columns + head_width]
    projected_value = (
        base_row_values[:, query_columns + head_width :]
        + adapter_scale * value_delta[:, query_columns:]
    )
    cosine_table, sine_table = rope_tables(row_inside, head_width)
    queries = rotate(
        projected_query.reshape(row_count, -1, head_width), cosine_table, sine_table
    ).astype(jnp.bfloat16)
    keys_own = rotate(proj_key[:, None, :], cosine_table, sine_table)[:, 0].astype(jnp.bfloat16)
    values_own = projected_value.astype(jnp.bfloat16)
    incoming = output_gradient[0]
    early_pos = cycle_index * row_count + jnp.arange(half_rows, dtype=jnp.int32)
    late_pos = early_pos + half_rows
    current_pos = jnp.concatenate([early_pos, late_pos], axis=0)
    current_seg, current_member, current_inside = segment_info(own_lengths, current_pos)
    pairs_all = lax.all_gather(
        jnp.concatenate([keys_own, values_own], axis=1), ("seq", "tp"), axis=0, tiled=True
    )
    keys_all = pairs_all[:, :head_width]
    values_all = pairs_all[:, head_width:]
    key_seg, key_member, key_inside = segment_info(own_lengths, jnp.arange(length, dtype=jnp.int32))
    incoming_heads = incoming.reshape(row_count, -1, head_width)
    output_rows, row_max, row_total = attend_rows(
        queries, current_pos, current_seg, keys_all, values_all, key_seg, key_block
    )
    query_grad, key_grads = attend_grad(
        queries,
        output_rows,
        incoming_heads,
        row_max,
        row_total,
        current_pos,
        current_seg,
        keys_all,
        values_all,
        key_seg,
        key_block,
    )

    own_key_grads = lax.psum_scatter(key_grads, ("seq", "tp"), scatter_dimension=0, tiled=True)
    current_cos, current_sin = rope_tables(current_inside, head_width)
    grad_query = (
        unrotate(query_grad, current_cos, current_sin).reshape(row_count, -1).astype(jnp.bfloat16)
    )
    grad_key = unrotate(own_key_grads[:, None, :head_width], current_cos, current_sin)[:, 0].astype(
        jnp.bfloat16
    )
    grad_value = own_key_grads[:, head_width:].astype(jnp.bfloat16)
    grad_rows = jnp.concatenate([grad_query, grad_key, grad_value], axis=1)
    attention = output_rows.reshape(row_count, -1)
    both_rows = lax.all_gather(
        jnp.concatenate([grad_rows, low_rank], axis=1), "tp", axis=0, tiled=True
    )
    all_grad = both_rows[:, :qkv_width]
    all_low = both_rows[:, qkv_width:]
    query_gradient_part = all_grad[:, :query_columns]
    value_gradient_part = all_grad[:, query_columns + head_width :]
    token_query_low = jnp.where(token_member[:, :, None], all_low[:, None, :low_width], 0)
    token_value_low = jnp.where(token_member[:, :, None], all_low[:, None, low_width:], 0)
    low_query_grad = jnp.einsum(
        "tc,src->tsr",
        query_gradient_part,
        up_rows[:, :, :query_columns],
        preferred_element_type=jnp.float32,
    )
    low_value_grad = jnp.einsum(
        "tc,src->tsr",
        value_gradient_part,
        up_rows[:, :, query_columns:],
        preferred_element_type=jnp.float32,
    )
    rank_gradient = adapter_scale * jnp.concatenate(
        [
            jnp.sum(jnp.where(token_member[:, :, None], low_query_grad, 0.0), axis=1),
            jnp.sum(jnp.where(token_member[:, :, None], low_value_grad, 0.0), axis=1),
        ],
        axis=1,
    )
    rank_gradient = rank_gradient.astype(jnp.bfloat16)
    up_terms = adapter_scale * jnp.concatenate(
        [
            jnp.einsum(
                "tsr,tc->src",
                token_query_low,
                query_gradient_part,
                preferred_element_type=jnp.float32,
            ),
            jnp.einsum(
                "tsr,tc->src",
                token_value_low,
                value_gradient_part,
                preferred_element_type=jnp.float32,
            ),
        ],
        axis=2,
    )
    low_tokens = jnp.where(token_member[:, :, None], rank_gradient[:, None, :], 0).reshape(
        tok_count, -1
    )
    down_terms = jnp.stack(
        [
            lax.dot_general(
                low_tokens,
                local_tokens[:, owner * down_width : (owner + 1) * down_width],
                (((0,), (0,)), ((), ())),
                preferred_element_type=jnp.float32,
            )
            for owner in range(seq_count)
        ]
    )
    down_sums = lax.psum_scatter(down_terms, "seq", scatter_dimension=0, tiled=False)
    up_split = jnp.transpose(
        up_terms.reshape(segment_count * low_width, seq_count, -1), (1, 0, 2)
    )
    up_sums = lax.psum_scatter(up_split, "seq", scatter_dimension=0, tiled=False)
    token_part = jnp.dot(all_grad, frozen, preferred_element_type=jnp.float32)
    token_part = token_part + jnp.concatenate(
        [
            jnp.dot(low_tokens, down_all[owner], preferred_element_type=jnp.float32)
            for owner in range(seq_count)
        ],
        axis=1,
    )
    token_grad = token_part.astype(jnp.bfloat16)[None]
    down_send = jnp.transpose(
        down_sums.reshape(segment_count, joint_rank, batch_count, -1), (2, 0, 1, 3)
    )
    up_send = jnp.transpose(
        up_sums.reshape(segment_count, low_width, batch_count, -1), (2, 0, 1, 3)
    )
    back_down = lax.all_to_all(down_send, "batch", split_axis=0, concat_axis=0, tiled=True)
    back_up = lax.all_to_all(up_send, "batch", split_axis=0, concat_axis=0, tiled=True)
    bank_hot = (flat_rows[:, None] == jnp.arange(adapters, dtype=jnp.int32)[None, :]).astype(
        jnp.float32
    )
    down_grad = jnp.einsum(
        "na,nx->ax",
        bank_hot,
        back_down.reshape(flat_rows.shape[0], -1),
        precision=lax.Precision.HIGHEST,
    )
    up_grad = jnp.einsum(
        "na,nx->ax",
        bank_hot,
        back_up.reshape(flat_rows.shape[0], -1),
        precision=lax.Precision.HIGHEST,
    )
    down_grad = down_grad.reshape(adapters, joint_rank, 1, -1)
    up_grad = up_grad.reshape(adapters, low_width, -1)
    return (attention[None], token_grad, down_grad, up_grad)


def solution(mesh):
    in_specs = (
        P(("groups", "batch"), "seq", "tp"),
        P("seq", "tp"),
        P(None, None, "tp", ("seq", "batch")),
        P(None, None, ("seq", "batch")),
        P(),
        P("groups", None),
        P("groups", None),
        P(("groups", "batch"), ("seq", "tp"), None),
    )
    out_specs = (
        P(("groups", "batch"), ("seq", "tp"), None),
        P(("groups", "batch"), "seq", "tp"),
        P("groups", None, "tp", ("seq", "batch")),
        P("groups", None, ("seq", "batch")),
    )
    return jax.shard_map(shards, mesh=mesh, in_specs=in_specs, out_specs=out_specs, check_vma=False)
```

```python
import functools

import jax
import jax.numpy as jnp
from jax import lax
from jax.experimental import pallas as pl
from jax.experimental.pallas import tpu as pltpu
from jax.sharding import PartitionSpec as P

QHEADS = 4
HEAD_WIDTH = 128
ADAPTER_RANK = 32
SEGS = 3

adapter_scale = 2.0
rope_base = 5000000.0
masked_score = -1e30
vmem_limit = 48 * 1024 * 1024


def shift(value, axis, steps):
    count = lax.axis_size(axis)
    return lax.ppermute(value, axis, [(at, (at + steps) % count) for at in range(count)])


def push(value, axis, steps):
    count = lax.axis_size(axis)
    pairs = [(at, at + steps) for at in range(count) if 0 <= at + steps < count]
    return lax.ppermute(value, axis, pairs)


def dot_nt(left, right):
    return lax.dot_general(
        left, right, (((1,), (1,)), ((), ())), preferred_element_type=jnp.float32
    )


def dot_nn(left, right):
    return jnp.dot(left, right, preferred_element_type=jnp.float32)


def dot_tn(left, right):
    return lax.dot_general(
        left, right, (((0,), (0,)), ((), ())), preferred_element_type=jnp.float32
    )


def lookup_rows(adapter_bank_row, document_adapter):
    matches = document_adapter[..., None] == jnp.arange(adapter_bank_row.shape[0], dtype=jnp.int32)
    return jnp.sum(jnp.where(matches, adapter_bank_row, 0), axis=-1)


def row_positions(first, count):
    return first + lax.broadcasted_iota(jnp.int32, (count, 1), 0)


def row_segments(marks, positions):
    return (positions >= marks[0]).astype(jnp.int32) + (positions >= marks[1]).astype(jnp.int32)


def cost(flops, bytes_accessed, transcendentals=0):
    return pl.CostEstimate(
        flops=flops, bytes_accessed=bytes_accessed, transcendentals=transcendentals
    )


def in_vmem():
    return pl.BlockSpec(memory_space=pltpu.VMEM)


def in_smem():
    return pl.BlockSpec(memory_space=pltpu.SMEM)


def in_place():
    return pl.BlockSpec(memory_space=pl.ANY)


def fetch_pieces(offsets, pieces, target, semaphore, first):
    copies = []
    for number, piece in enumerate(pieces):
        height, width = piece.shape
        row = pl.multiple_of(offsets[first + number, 0], 16)
        column = pl.multiple_of(offsets[first + number, 1], 128)
        copy = pltpu.make_async_copy(
            piece,
            target.at[pl.ds(row, height), pl.ds(column, width)],
            semaphore.at[first + number],
        )
        copy.start()
        copies.append(copy)
    return copies


def project_kernel(frozen_count, down_count, marks, offsets, tokens, *refs):
    frozen_pieces = refs[:frozen_count]
    down_pieces = refs[frozen_count : frozen_count + down_count]
    part, frozen, down, semaphore = refs[frozen_count + down_count :]
    copies = fetch_pieces(offsets, frozen_pieces, frozen, semaphore, 0)
    copies += fetch_pieces(offsets, down_pieces, down, semaphore, frozen_count)
    for copy in copies:
        copy.wait()
    rows = tokens.shape[0]
    features = frozen.shape[0]
    joint_rank = down.shape[0] // 2
    positions = row_positions(marks[2] * rows, rows)
    second = row_segments(marks, positions) != marks[6]
    values = tokens[...]
    part[:, :features] = dot_nt(values, frozen[...])
    first_low = dot_nt(values, down[:joint_rank])
    second_low = dot_nt(values, down[joint_rank:])
    part[:, features:] = jnp.where(second, second_low, first_low)


def rotated(values, cosines, sines):
    return values * cosines + pltpu.roll(values, values.shape[1] // 2, 1) * sines


def qkv_kernel(marks, mine, theirs, up_blocks, cosines, sines, queries, pairs, low_rank):
    rows = mine.shape[0]
    own_rows = queries.shape[0] // QHEADS
    query_columns = QHEADS * HEAD_WIDTH
    value_start = query_columns + HEAD_WIDTH
    features = value_start + HEAD_WIDTH
    segments = row_segments(marks, row_positions(marks[2] * rows, rows))
    low = (mine[:, features:] + theirs[:, features:]).astype(jnp.bfloat16)
    low_rank[...] = low
    value_delta = jnp.zeros((rows, HEAD_WIDTH), jnp.float32)
    for document in range(SEGS):
        chosen = jnp.where(segments == document, low, jnp.zeros_like(low))
        value_delta += dot_nn(chosen, up_blocks[document, :, query_columns:])
    keys = mine[:, query_columns:value_start] + theirs[:, query_columns:value_start]
    pairs[:, :HEAD_WIDTH] = rotated(keys, cosines[...], sines[...]).astype(jnp.bfloat16)
    values = mine[:, value_start:features] + theirs[:, value_start:features]
    pairs[:, HEAD_WIDTH:] = (values + adapter_scale * value_delta).astype(jnp.bfloat16)
    start = pl.multiple_of(marks[3] * own_rows, own_rows)
    own = pl.ds(start, own_rows)
    own_segments = row_segments(marks, row_positions(marks[2] * rows + start, own_rows))
    own_low = (mine[own, features:] + theirs[own, features:]).astype(jnp.bfloat16)
    query_delta = jnp.zeros((own_rows, query_columns), jnp.float32)
    for document in range(SEGS):
        chosen = jnp.where(own_segments == document, own_low, jnp.zeros_like(own_low))
        query_delta += dot_nn(chosen, up_blocks[document, :, :query_columns])
    projected = mine[own, :query_columns] + theirs[own, :query_columns]
    projected = projected + adapter_scale * query_delta
    for head in range(QHEADS):
        turned = rotated(
            projected[:, head * HEAD_WIDTH : (head + 1) * HEAD_WIDTH], cosines[own], sines[own]
        )
        queries[head * own_rows : (head + 1) * own_rows] = turned.astype(jnp.bfloat16)


def attention_kernel(block_count, marks, queries, incoming, cosines, sines, *refs):
    blocks = refs[:block_count]
    output, query_grad, kept, sent, low_probs = refs[block_count:]
    own_rows, query_columns = incoming.shape
    rows = blocks[0].shape[0]
    score_scale = HEAD_WIDTH ** (-0.5)
    first = marks[2] * rows + marks[3] * own_rows
    positions = row_positions(first, own_rows)
    positions = jnp.concatenate([positions] * QHEADS, axis=0)
    segments = row_segments(marks, positions)
    starts = jnp.where(segments == 0, 0, jnp.where(segments == 1, marks[0], marks[1]))
    scores = []
    for back, block in enumerate(blocks):
        key_positions = (marks[2] - back) * rows + lax.broadcasted_iota(jnp.int32, (1, rows), 1)
        allowed = (key_positions <= positions) & (key_positions >= starts)
        block_scores = dot_nt(queries[...], block[:, :HEAD_WIDTH]) * score_scale
        scores.append(jnp.where(allowed, block_scores, masked_score))
    row_max = functools.reduce(
        jnp.maximum, [jnp.max(part, axis=1, keepdims=True) for part in scores]
    )
    raised = [jnp.exp(part - row_max) for part in scores]
    row_total = sum(jnp.sum(part, axis=1, keepdims=True) for part in raised)
    inverse = 1.0 / row_total
    probs = [part * inverse for part in raised]
    weighted = jnp.zeros((QHEADS * own_rows, HEAD_WIDTH), jnp.float32)
    for back, block in enumerate(blocks):
        low_probs[back] = probs[back].astype(jnp.bfloat16)
        weighted += dot_nn(low_probs[back], block[:, HEAD_WIDTH:])
    attended = weighted.astype(jnp.bfloat16)
    gradients = jnp.concatenate(
        [incoming[:, head * HEAD_WIDTH : (head + 1) * HEAD_WIDTH] for head in range(QHEADS)],
        axis=0,
    )
    row_delta = jnp.sum(
        gradients.astype(jnp.float32) * attended.astype(jnp.float32), axis=1, keepdims=True
    )
    start = pl.multiple_of(marks[3] * own_rows, own_rows)
    other = pl.multiple_of(own_rows - start, own_rows)
    total = jnp.zeros((QHEADS * own_rows, HEAD_WIDTH), jnp.float32)
    for back, block in enumerate(blocks):
        prob_grad = dot_nt(gradients, block[:, HEAD_WIDTH:])
        score_grad = (probs[back] * (prob_grad - row_delta)).astype(jnp.bfloat16)
        total += dot_nn(score_grad, block[:, :HEAD_WIDTH])
        key_part = dot_tn(score_grad, queries[...]) * score_scale
        value_part = dot_tn(low_probs[back], gradients)
        mine = marks[3] == 0
        kept[back, :, :HEAD_WIDTH] = jnp.where(mine, key_part[:own_rows], key_part[own_rows:])
        sent[back, :, :HEAD_WIDTH] = jnp.where(mine, key_part[own_rows:], key_part[:own_rows])
        kept[back, :, HEAD_WIDTH:] = jnp.where(mine, value_part[:own_rows], value_part[own_rows:])
        sent[back, :, HEAD_WIDTH:] = jnp.where(mine, value_part[own_rows:], value_part[:own_rows])
    own = pl.ds(start, own_rows)
    for head in range(QHEADS):
        picked = slice(head * own_rows, (head + 1) * own_rows)
        columns = slice(head * HEAD_WIDTH, (head + 1) * HEAD_WIDTH)
        output[:, columns] = attended[picked]
        query_grad[:, columns] = rotated(
            total[picked] * score_scale, cosines[own], -sines[own]
        ).astype(jnp.bfloat16)


def rank_kernel(
    marks, own_query, other_query, own_pair, other_pair, low_rank, up_blocks,
    gradients, rank_grad, up_terms,
):
    own_rows, query_columns = own_query.shape
    rows = low_rank.shape[0]
    start = pl.multiple_of(marks[3] * own_rows, own_rows)
    other = pl.multiple_of(own_rows - start, own_rows)
    gradients[pl.ds(start, own_rows), :query_columns] = own_query[...]
    gradients[pl.ds(other, own_rows), :query_columns] = other_query[...]
    gradients[pl.ds(start, own_rows), query_columns:] = own_pair[...]
    gradients[pl.ds(other, own_rows), query_columns:] = other_pair[...]
    query_grad = gradients[:, :query_columns]
    value_grad = gradients[:, query_columns + HEAD_WIDTH :]
    low = low_rank[...]
    rank = low.shape[1] // 2
    segments = row_segments(marks, row_positions(marks[2] * rows, rows))
    total = jnp.zeros((rows, low.shape[1]), jnp.float32)
    for document in range(SEGS):
        member = segments == document
        terms = dot_nt(query_grad, up_blocks[document, :, :query_columns])
        terms += dot_nt(value_grad, up_blocks[document, :, query_columns:])
        total = jnp.where(member, terms, total)
        chosen = jnp.where(member, low, jnp.zeros_like(low))
        query_terms = dot_tn(chosen, query_grad)
        value_terms = dot_tn(chosen, value_grad)
        place = slice(document * rank, (document + 1) * rank)
        up_terms[place, :query_columns] = adapter_scale * query_terms[:rank]
        up_terms[place, query_columns:] = adapter_scale * value_terms[rank:]
    rank_grad[...] = (adapter_scale * total).astype(jnp.bfloat16)


def token_kernel(frozen_count, down_count, marks, offsets, gradients, rank_grad, *refs):
    frozen_pieces = refs[:frozen_count]
    down_pieces = refs[frozen_count : frozen_count + down_count]
    token_grad, frozen, down, semaphore = refs[frozen_count + down_count :]
    copies = fetch_pieces(offsets, frozen_pieces, frozen, semaphore, 0)
    copies += fetch_pieces(offsets, down_pieces, down, semaphore, frozen_count)
    for copy in copies:
        copy.wait()
    rows = gradients.shape[0]
    joint_rank = down.shape[0] // 2
    second = row_segments(marks, row_positions(marks[2] * rows, rows)) != marks[6]
    low = rank_grad[...]
    nothing = jnp.zeros_like(low)
    first_low = jnp.where(second, nothing, low)
    second_low = jnp.where(second, low, nothing)
    chunk = 512
    for column in range(0, token_grad.shape[1], chunk):
        columns = slice(column, column + chunk)
        total = dot_nn(gradients[...], frozen[:, columns])
        total += dot_nn(first_low, down[:joint_rank, columns])
        total += dot_nn(second_low, down[joint_rank:, columns])
        token_grad[:, columns] = total.astype(jnp.bfloat16)


def down_kernel(block_count, marks, *refs):
    ranks = refs[:block_count]
    columns = refs[block_count : 2 * block_count]
    terms = refs[2 * block_count]
    rows, joint_rank = ranks[0].shape
    for document in range(SEGS):
        total = jnp.zeros((joint_rank, terms.shape[1]), jnp.float32)
        for behind in range(block_count):
            holder = marks[2] - behind
            holder = jnp.where(holder < 0, holder + block_count, holder)
            segments = row_segments(marks, row_positions(holder * rows, rows))
            low = ranks[behind][...]
            chosen = jnp.where(segments == document, low, jnp.zeros_like(low))
            total += dot_tn(chosen, columns[behind][...])
        terms[document * joint_rank : (document + 1) * joint_rank] = total


def bank_kernel(block_count, bank_rows, *refs):
    down_terms = refs[:block_count]
    up_terms = refs[block_count : 2 * block_count]
    down_out, up_out = refs[2 * block_count + 2 :]
    step = pl.program_id(0)
    joint_rank = down_out.shape[1]
    low_width = up_out.shape[1]
    down_total = jnp.zeros((joint_rank, down_out.shape[3]), jnp.float32)
    up_total = jnp.zeros((low_width, up_out.shape[2]), jnp.float32)
    for block in range(block_count):
        for document in range(SEGS):
            same = bank_rows[block * SEGS + document] == bank_rows[step]
            down_rows = down_terms[block][document * joint_rank : (document + 1) * joint_rank]
            up_rows = up_terms[block][document * low_width : (document + 1) * low_width]
            down_total += jnp.where(same, down_rows, 0.0)
            up_total += jnp.where(same, up_rows, 0.0)
    down_out[0, :, 0, :] = down_total
    up_out[0] = up_total


def shards(
    tokens,
    frozen_qkv_matrix,
    adapter_down_weight,
    adapter_up_weight,
    adapter_bank_row,
    document_lengths,
    document_adapter,
    output_gradient,
):
    seq_count = lax.axis_size("seq")
    batch_count = lax.axis_size("batch")
    group_count = lax.axis_size("groups")
    chip_size = lax.axis_size("tp")
    seq_index = lax.axis_index("seq")
    batch_index = lax.axis_index("batch")
    group_index = lax.axis_index("groups")
    tp_index = lax.axis_index("tp")
    local_tokens = tokens[0]
    rows, width = local_tokens.shape
    own_rows = rows // chip_size
    query_columns = QHEADS * HEAD_WIDTH
    frozen_rows = frozen_qkv_matrix.shape[0]
    features = frozen_rows * seq_count
    low_width = ADAPTER_RANK
    joint_rank = adapter_down_weight.shape[1]
    adapters = adapter_bank_row.shape[0]
    bf16 = jnp.bfloat16
    f32 = jnp.float32

    sample_rows = lookup_rows(adapter_bank_row, document_adapter)
    lengths = lax.dynamic_index_in_dim(document_lengths, batch_index, 0, keepdims=False)
    ends = jnp.cumsum(lengths)
    half_count = seq_count // 2

    def first_document(holder):
        return (holder >= half_count).astype(jnp.int32)

    marks = jnp.stack(
        [
            ends[0],
            ends[1],
            seq_index,
            tp_index,
            batch_index,
            group_index,
            first_document(seq_index),
            jnp.int32(0),
        ]
    ).astype(jnp.int32)

    plane_count = group_count * batch_count
    share = width // plane_count
    pieces, places = [], []
    direct = group_count == 2 and batch_count == 2 and share % 128 == 0 and frozen_rows % 16 == 0
    if direct:
        own_share = lax.dynamic_slice_in_dim(
            frozen_qkv_matrix, (group_index * batch_count + batch_index) * share, share, axis=1
        )
        pieces.append(frozen_qkv_matrix)
        places.append((seq_index * frozen_rows, 0))
        for steps in range(1, seq_count):
            holder = jnp.remainder(seq_index - steps, seq_count)
            here = shift(own_share, "seq", steps)
            if steps % 2 == 1:
                over_batch = shift(here, "batch", 1)
                over_groups = shift(here, "groups", 1)
                over_both = shift(over_batch, "groups", 1)
            else:
                over_groups = shift(here, "groups", 1)
                over_batch = shift(here, "batch", 1)
                over_both = shift(over_groups, "batch", 1)
            for value, group, batch in (
                (here, group_index, batch_index),
                (over_batch, group_index, 1 - batch_index),
                (over_groups, 1 - group_index, batch_index),
                (over_both, 1 - group_index, 1 - batch_index),
            ):
                pieces.append(value)
                places.append((holder * frozen_rows, (group * batch_count + batch) * share))
    else:
        pieces.append(lax.all_gather(frozen_qkv_matrix, "seq", axis=0, tiled=True))
        places.append((0, 0))
    frozen_count = len(pieces)

    down_bank = adapter_down_weight[:, :, 0, :]
    if batch_count == 2:
        own_bank = lax.dynamic_index_in_dim(sample_rows, batch_index, 0, keepdims=False)
        other_bank = lax.dynamic_index_in_dim(sample_rows, 1 - batch_index, 0, keepdims=False)
        own_down, own_up = down_bank[own_bank], adapter_up_weight[own_bank]
        far_down = shift(down_bank[other_bank], "batch", 1)
        far_up = shift(adapter_up_weight[other_bank], "batch", 1)
        ahead = batch_index == 0
        down_block = jnp.concatenate(
            [jnp.where(ahead, own_down, far_down), jnp.where(ahead, far_down, own_down)], axis=2
        )
        up_block = jnp.concatenate(
            [jnp.where(ahead, own_up, far_up), jnp.where(ahead, far_up, own_up)], axis=2
        )
    else:
        got_down = lax.all_to_all(
            down_bank[sample_rows], "batch", split_axis=0, concat_axis=0, tiled=True
        )
        got_up = lax.all_to_all(
            adapter_up_weight[sample_rows], "batch", split_axis=0, concat_axis=0, tiled=True
        )
        down_block = jnp.transpose(got_down, (1, 2, 0, 3)).reshape(SEGS, joint_rank, -1)
        up_block = jnp.transpose(got_up, (1, 2, 0, 3)).reshape(SEGS, low_width, -1)
    down_block = down_block.reshape(SEGS * joint_rank, -1)
    up_block = up_block.reshape(SEGS * low_width, -1)
    down_width = down_block.shape[1]
    down_parts, down_places, up_parts = [], [], []
    for steps in range(seq_count):
        target = jnp.remainder(seq_index + steps, seq_count)
        holder = jnp.remainder(seq_index - steps, seq_count)
        part = lax.dynamic_slice_in_dim(
            down_block, first_document(target) * joint_rank, 2 * joint_rank
        )
        down_parts.append(shift(part, "seq", steps) if steps else part)
        down_places.append((0, holder * down_width))
        up_parts.append(shift(up_block, "seq", steps) if steps else up_block)
    relative = jnp.remainder(seq_index - jnp.arange(seq_count, dtype=jnp.int32), seq_count)
    up_rows = jnp.stack(up_parts)[relative]
    up_rows = jnp.transpose(up_rows, (1, 0, 2)).reshape(SEGS, low_width, -1)
    is_query = jnp.arange(up_rows.shape[2]) < query_columns
    up_blocks = jnp.concatenate(
        [
            jnp.where(is_query[None, None, :], up_rows, 0),
            jnp.where(is_query[None, None, :], 0, up_rows),
        ],
        axis=1,
    )
    if down_width % 128 != 0:
        merged = jnp.stack(down_parts)[relative]
        merged = jnp.transpose(merged, (1, 0, 2)).reshape(2 * joint_rank, -1)
        down_parts, down_places = [merged], [(0, 0)]
    down_count = len(down_parts)
    offsets = jnp.stack(
        [jnp.stack([jnp.int32(0) + row, jnp.int32(0) + column]) for row, column in places + down_places]
    ).astype(jnp.int32)

    positions = seq_index * rows + jnp.arange(rows, dtype=jnp.int32)
    inside = positions - jnp.where(
        positions >= ends[1], ends[1], jnp.where(positions >= ends[0], ends[0], 0)
    )
    exponent = jnp.arange(HEAD_WIDTH // 2, dtype=f32) * (2.0 / HEAD_WIDTH)
    angles = inside.astype(f32)[:, None] * jnp.power(jnp.float32(rope_base), -exponent)[None, :]
    cosines = jnp.tile(jnp.cos(angles), (1, 2))
    sines = jnp.concatenate([-jnp.sin(angles), jnp.sin(angles)], axis=1)

    scratch = [
        pltpu.VMEM((features, width), bf16),
        pltpu.VMEM((2 * joint_rank, width), bf16),
        pltpu.SemaphoreType.DMA((frozen_count + down_count,)),
    ]
    weight_bytes = 2 * width * (features + 2 * joint_rank)
    part = pl.pallas_call(
        functools.partial(project_kernel, frozen_count, down_count),
        out_shape=jax.ShapeDtypeStruct((rows, features + joint_rank), f32),
        in_specs=[in_smem(), in_smem(), in_vmem()] + [in_place()] * (frozen_count + down_count),
        out_specs=in_vmem(),
        scratch_shapes=scratch,
        compiler_params=pltpu.CompilerParams(vmem_limit_bytes=vmem_limit),
        cost_estimate=cost(
            2 * rows * width * (features + 2 * joint_rank), weight_bytes + 2 * rows * width
        ),
        name="project",
    )(marks, offsets, local_tokens, *pieces, *down_parts)

    part, late_tokens = lax.optimization_barrier((part, local_tokens))
    column_parts = []
    for steps in range(seq_count):
        target = jnp.remainder(seq_index + steps, seq_count)
        part_columns = lax.dynamic_slice_in_dim(
            late_tokens, target * down_width, down_width, axis=1
        )
        column_parts.append(shift(part_columns, "seq", steps) if steps else part_columns)

    other_part = shift(part, "tp", 1)
    queries, pairs, low_rank = pl.pallas_call(
        qkv_kernel,
        out_shape=(
            jax.ShapeDtypeStruct((QHEADS * own_rows, HEAD_WIDTH), bf16),
            jax.ShapeDtypeStruct((rows, 2 * HEAD_WIDTH), bf16),
            jax.ShapeDtypeStruct((rows, joint_rank), bf16),
        ),
        in_specs=[in_smem()] + [in_vmem()] * 5,
        out_specs=(in_vmem(),) * 3,
        compiler_params=pltpu.CompilerParams(vmem_limit_bytes=vmem_limit),
        cost_estimate=cost(2 * rows * 3 * 64 * 640, 8 * rows * features),
        name="qkv",
    )(marks, part, other_part, up_blocks, cosines, sines)

    blocks = [pairs] + [push(pairs, "seq", back) for back in range(1, half_count + 1)]
    block_count = len(blocks)
    incoming = output_gradient[0]
    attention, query_grad, kept, sent = pl.pallas_call(
        functools.partial(attention_kernel, block_count),
        out_shape=(
            jax.ShapeDtypeStruct((own_rows, query_columns), bf16),
            jax.ShapeDtypeStruct((own_rows, query_columns), bf16),
            jax.ShapeDtypeStruct((block_count, own_rows, 2 * HEAD_WIDTH), f32),
            jax.ShapeDtypeStruct((block_count, own_rows, 2 * HEAD_WIDTH), f32),
        ),
        in_specs=[in_smem()] + [in_vmem()] * (4 + block_count),
        out_specs=(in_vmem(),) * 4,
        scratch_shapes=[pltpu.VMEM((block_count, QHEADS * own_rows, rows), bf16)],
        compiler_params=pltpu.CompilerParams(vmem_limit_bytes=vmem_limit),
        cost_estimate=cost(
            10 * block_count * QHEADS * own_rows * rows * HEAD_WIDTH,
            4 * rows * features,
            block_count * QHEADS * own_rows * rows,
        ),
        name="attention",
    )(marks, queries, incoming, cosines, sines, *blocks)

    other_query = shift(query_grad, "tp", 1)
    pair_sums = kept + shift(sent, "tp", 1)
    own_sum = pair_sums[0]
    for back in range(1, block_count):
        own_sum = own_sum + push(pair_sums[back], "seq", -back)
    own_place = tp_index * own_rows
    own_cosines = lax.dynamic_slice_in_dim(cosines, own_place, own_rows)
    own_sines = lax.dynamic_slice_in_dim(sines, own_place, own_rows)
    key_grad = own_sum[:, :HEAD_WIDTH]
    key_grad = key_grad * own_cosines - jnp.roll(key_grad, HEAD_WIDTH // 2, axis=1) * own_sines
    pair_grad = jnp.concatenate([key_grad, own_sum[:, HEAD_WIDTH:]], axis=1).astype(bf16)
    other_pair = shift(pair_grad, "tp", 1)

    gradients, rank_grad, up_terms = pl.pallas_call(
        rank_kernel,
        out_shape=(
            jax.ShapeDtypeStruct((rows, features), bf16),
            jax.ShapeDtypeStruct((rows, joint_rank), bf16),
            jax.ShapeDtypeStruct((SEGS * low_width, features - HEAD_WIDTH), f32),
        ),
        in_specs=[in_smem()] + [in_vmem()] * 6,
        out_specs=(in_vmem(),) * 3,
        compiler_params=pltpu.CompilerParams(vmem_limit_bytes=vmem_limit),
        cost_estimate=cost(4 * rows * 3 * 64 * 640, 4 * rows * features),
        name="rank_gradients",
    )(marks, query_grad, other_query, pair_grad, other_pair, low_rank, up_blocks)

    rank_parts = [rank_grad] + [shift(rank_grad, "seq", steps) for steps in range(1, seq_count)]
    up_split = jnp.transpose(
        up_terms.reshape(SEGS * low_width, seq_count, -1), (1, 0, 2)
    )
    up_sum = lax.dynamic_index_in_dim(up_split, seq_index, 0, keepdims=False)
    for steps in range(1, seq_count):
        target = jnp.remainder(seq_index + steps, seq_count)
        up_sum = up_sum + shift(
            lax.dynamic_index_in_dim(up_split, target, 0, keepdims=False), "seq", steps
        )

    token_grad = pl.pallas_call(
        functools.partial(token_kernel, frozen_count, down_count),
        out_shape=jax.ShapeDtypeStruct((rows, width), bf16),
        in_specs=[in_smem(), in_smem(), in_vmem(), in_vmem()]
        + [in_place()] * (frozen_count + down_count),
        out_specs=in_vmem(),
        scratch_shapes=scratch,
        compiler_params=pltpu.CompilerParams(vmem_limit_bytes=vmem_limit),
        cost_estimate=cost(
            2 * rows * width * (features + 2 * joint_rank), weight_bytes + 2 * rows * width
        ),
        name="token_gradient",
    )(marks, offsets, gradients, rank_grad, *pieces, *down_parts)

    down_terms = pl.pallas_call(
        functools.partial(down_kernel, seq_count),
        out_shape=jax.ShapeDtypeStruct((SEGS * joint_rank, down_width), f32),
        in_specs=[in_smem()] + [in_vmem()] * (2 * seq_count),
        out_specs=in_vmem(),
        compiler_params=pltpu.CompilerParams(vmem_limit_bytes=vmem_limit),
        cost_estimate=cost(
            2 * seq_count * rows * SEGS * joint_rank * down_width, 2 * seq_count * rows * down_width
        ),
        name="down_terms",
    )(marks, *rank_parts, *column_parts)

    held_down = down_width // batch_count
    held_up = up_sum.shape[1] // batch_count
    if batch_count == 2:
        ahead = batch_index == 0
        own_terms = jnp.where(ahead, down_terms[:, :held_down], down_terms[:, held_down:])
        far_terms = jnp.where(ahead, down_terms[:, held_down:], down_terms[:, :held_down])
        own_ups = jnp.where(ahead, up_sum[:, :held_up], up_sum[:, held_up:])
        far_ups = jnp.where(ahead, up_sum[:, held_up:], up_sum[:, :held_up])
        bank_downs = [own_terms, shift(far_terms, "batch", 1)]
        bank_ups = [own_ups, shift(far_ups, "batch", 1)]
        bank_rows = jnp.concatenate([own_bank, other_bank])
    else:
        down_send = jnp.transpose(
            down_terms.reshape(SEGS * joint_rank, batch_count, held_down), (1, 0, 2)
        )
        up_send = jnp.transpose(
            up_sum.reshape(SEGS * low_width, batch_count, held_up), (1, 0, 2)
        )
        back_down = lax.all_to_all(down_send, "batch", split_axis=0, concat_axis=0, tiled=True)
        back_up = lax.all_to_all(up_send, "batch", split_axis=0, concat_axis=0, tiled=True)
        bank_downs = [back_down[batch] for batch in range(batch_count)]
        bank_ups = [back_up[batch] for batch in range(batch_count)]
        bank_rows = sample_rows.reshape(-1)
    down_zeros = jnp.zeros((adapters, joint_rank, 1, held_down), f32)
    up_zeros = jnp.zeros((adapters, low_width, held_up), f32)

    def whole(array):
        return pl.BlockSpec(array.shape, lambda step, bank: (0,) * array.ndim)

    down_grad, up_grad = pl.pallas_call(
        functools.partial(bank_kernel, batch_count),
        out_shape=(
            jax.ShapeDtypeStruct(down_zeros.shape, f32),
            jax.ShapeDtypeStruct(up_zeros.shape, f32),
        ),
        grid_spec=pltpu.PrefetchScalarGridSpec(
            num_scalar_prefetch=1,
            grid=(batch_count * SEGS,),
            in_specs=[whole(array) for array in bank_downs + bank_ups] + [in_place()] * 2,
            out_specs=(
                pl.BlockSpec(
                    (1, joint_rank, 1, held_down), lambda step, bank: (bank[step], 0, 0, 0)
                ),
                pl.BlockSpec((1, low_width, held_up), lambda step, bank: (bank[step], 0, 0)),
            ),
        ),
        input_output_aliases={1 + 2 * batch_count: 0, 2 + 2 * batch_count: 1},
        compiler_params=pltpu.CompilerParams(vmem_limit_bytes=vmem_limit),
        name="bank_rows",
    )(bank_rows, *bank_downs, *bank_ups, down_zeros, up_zeros)
    return (attention[None], token_grad[None], down_grad, up_grad)


def solution(mesh):
    in_specs = (
        P(("groups", "batch"), "seq", "tp"),
        P("seq", "tp"),
        P(None, None, "tp", ("seq", "batch")),
        P(None, None, ("seq", "batch")),
        P(),
        P("groups", None),
        P("groups", None),
        P(("groups", "batch"), ("seq", "tp"), None),
    )
    out_specs = (
        P(("groups", "batch"), ("seq", "tp"), None),
        P(("groups", "batch"), "seq", "tp"),
        P("groups", None, "tp", ("seq", "batch")),
        P("groups", None, ("seq", "batch")),
    )
    return jax.shard_map(shards, mesh=mesh, in_specs=in_specs, out_specs=out_specs, check_vma=False)
```

```python
import functools

import jax
import jax.numpy as jnp
from jax import lax
from jax.experimental import pallas as pl
from jax.experimental.pallas import tpu as pltpu
from jax.sharding import PartitionSpec as P

QHEADS = 4
HEAD_WIDTH = 128
ADAPTER_RANK = 32
SEGS = 3

adapter_scale = 2.0
rope_base = 5000000.0
masked_score = -1e30
mebibyte = 1024 * 1024


def shift(value, axis, steps):
    count = lax.axis_size(axis)
    return lax.ppermute(value, axis, [(at, (at + steps) % count) for at in range(count)])


def push(value, axis, steps):
    count = lax.axis_size(axis)
    pairs = [(at, at + steps) for at in range(count) if 0 <= at + steps < count]
    return lax.ppermute(value, axis, pairs)


def dot_nt(left, right):
    return lax.dot_general(
        left, right, (((1,), (1,)), ((), ())), preferred_element_type=jnp.float32
    )


def dot_nn(left, right):
    return jnp.dot(left, right, preferred_element_type=jnp.float32)


def dot_tn(left, right):
    return lax.dot_general(
        left, right, (((0,), (0,)), ((), ())), preferred_element_type=jnp.float32
    )


def lookup_rows(adapter_bank_row, document_adapter):
    matches = document_adapter[..., None] == jnp.arange(adapter_bank_row.shape[0], dtype=jnp.int32)
    return jnp.sum(jnp.where(matches, adapter_bank_row, 0), axis=-1)


def row_positions(first, count):
    return first + lax.broadcasted_iota(jnp.int32, (count, 1), 0)


def ring_index(index, count):
    return lax.rem(index + count, count)


def kernel_marks(lengths):
    batch = lax.axis_index("batch")
    first_end = lengths[batch, 0]
    return first_end, first_end + lengths[batch, 1]


def row_segments(ends, positions):
    return (positions >= ends[0]).astype(jnp.int32) + (positions >= ends[1]).astype(jnp.int32)


def cost(flops, bytes_accessed, transcendentals=0):
    return pl.CostEstimate(
        flops=flops, bytes_accessed=bytes_accessed, transcendentals=transcendentals
    )


def in_vmem():
    return pl.BlockSpec(memory_space=pltpu.VMEM)


def in_smem():
    return pl.BlockSpec(memory_space=pltpu.SMEM)


def in_place():
    return pl.BlockSpec(memory_space=pl.ANY)


def fetch_pieces(places, pieces, target, semaphore, first):
    copies = []
    for number, (place, piece) in enumerate(zip(places, pieces)):
        height, width = piece.shape
        row, column = place()
        copy = pltpu.make_async_copy(
            piece,
            target.at[
                pl.ds(pl.multiple_of(row, 16), height), pl.ds(pl.multiple_of(column, 128), width)
            ],
            semaphore.at[first + number],
        )
        copy.start()
        copies.append(copy)
    return copies


def frozen_place(seq_count, rows, share, behind, batch_step, group_step):
    def place():
        holder = ring_index(lax.axis_index("seq") - behind, seq_count)
        if share is None:
            return holder * rows, 0
        batch = lax.rem(lax.axis_index("batch") + batch_step, 2)
        group = lax.rem(lax.axis_index("groups") + group_step, 2)
        return holder * rows, (group * 2 + batch) * share

    return place


def down_place(seq_count, width, behind):
    def place():
        return 0, ring_index(lax.axis_index("seq") - behind, seq_count) * width

    return place


def whole_place():
    return 0, 0


def second_document(ends, rows, seq_count):
    seq_index = lax.axis_index("seq")
    first = (seq_index >= seq_count // 2).astype(jnp.int32)
    return row_segments(ends, row_positions(seq_index * rows, rows)) != first


def project_kernel(frozen_places, down_places, unused, seq_count, lengths, tokens, *refs):
    frozen_count, down_count = len(frozen_places), len(down_places)
    frozen_pieces = refs[:frozen_count]
    down_pieces = refs[frozen_count : frozen_count + down_count]
    refs = refs[frozen_count + down_count + unused :]
    part, columns, (frozen, down, semaphore) = refs[0], refs[1:-3], refs[-3:]
    copies = fetch_pieces(frozen_places, frozen_pieces, frozen, semaphore, 0)
    copies += fetch_pieces(down_places, down_pieces, down, semaphore, frozen_count)
    rows, width = tokens.shape
    for steps, block in enumerate(columns):
        target = ring_index(lax.axis_index("seq") + steps - seq_count, seq_count)
        held = block.shape[1]
        block[...] = tokens[:, pl.ds(pl.multiple_of(target * held, 128), held)]
    for copy in copies:
        copy.wait()
    features = frozen.shape[0]
    joint_rank = down.shape[0] // 2
    second = second_document(kernel_marks(lengths), rows, seq_count)
    values = tokens[...]
    part[:, :features] = dot_nt(values, frozen[...])
    first_low = dot_nt(values, down[:joint_rank])
    second_low = dot_nt(values, down[joint_rank:])
    part[:, features : features + joint_rank] = jnp.where(second, second_low, first_low)


def rotated(values, cosines, sines):
    return values * cosines + pltpu.roll(values, values.shape[1] // 2, 1) * sines


def qkv_kernel(lengths, mine, theirs, up_blocks, cosines, sines, queries, pairs, low_rank):
    rows = mine.shape[0]
    own_rows = queries.shape[0] // QHEADS
    query_columns = QHEADS * HEAD_WIDTH
    value_start = query_columns + HEAD_WIDTH
    features = value_start + HEAD_WIDTH
    low_columns = slice(features, features + low_rank.shape[1])
    ends = kernel_marks(lengths)
    first_row = lax.axis_index("seq") * rows
    segments = row_segments(ends, row_positions(first_row, rows))
    low = (mine[:, low_columns] + theirs[:, low_columns]).astype(jnp.bfloat16)
    low_rank[...] = low
    value_delta = jnp.zeros((rows, HEAD_WIDTH), jnp.float32)
    for document in range(SEGS):
        chosen = jnp.where(segments == document, low, jnp.zeros_like(low))
        value_delta += dot_nn(chosen, up_blocks[document, :, query_columns:])
    keys = mine[:, query_columns:value_start] + theirs[:, query_columns:value_start]
    pairs[:, :HEAD_WIDTH] = rotated(keys, cosines[...], sines[...]).astype(jnp.bfloat16)
    values = mine[:, value_start:features] + theirs[:, value_start:features]
    pairs[:, HEAD_WIDTH:] = (values + adapter_scale * value_delta).astype(jnp.bfloat16)
    start = pl.multiple_of(lax.axis_index("tp") * own_rows, own_rows)
    own = pl.ds(start, own_rows)
    own_segments = row_segments(ends, row_positions(first_row + start, own_rows))
    own_low = (mine[own, low_columns] + theirs[own, low_columns]).astype(jnp.bfloat16)
    query_delta = jnp.zeros((own_rows, query_columns), jnp.float32)
    for document in range(SEGS):
        chosen = jnp.where(own_segments == document, own_low, jnp.zeros_like(own_low))
        query_delta += dot_nn(chosen, up_blocks[document, :, :query_columns])
    projected = mine[own, :query_columns] + theirs[own, :query_columns]
    projected = projected + adapter_scale * query_delta
    for head in range(QHEADS):
        turned = rotated(
            projected[:, head * HEAD_WIDTH : (head + 1) * HEAD_WIDTH], cosines[own], sines[own]
        )
        queries[head * own_rows : (head + 1) * own_rows] = turned.astype(jnp.bfloat16)


def attention_kernel(block_count, lengths, queries, incoming, cosines, sines, *refs):
    blocks = refs[:block_count]
    output, query_grad, kept, sent, low_probs = refs[block_count:]
    own_rows, query_columns = incoming.shape
    rows = blocks[0].shape[0]
    score_scale = HEAD_WIDTH ** (-0.5)
    ends = kernel_marks(lengths)
    seq_index, tp_index = lax.axis_index("seq"), lax.axis_index("tp")
    positions = row_positions(seq_index * rows + tp_index * own_rows, own_rows)
    positions = jnp.concatenate([positions] * QHEADS, axis=0)
    segments = row_segments(ends, positions)
    starts = jnp.where(segments == 0, 0, jnp.where(segments == 1, ends[0], ends[1]))
    scores = []
    for back, block in enumerate(blocks):
        key_positions = (seq_index - back) * rows + lax.broadcasted_iota(jnp.int32, (1, rows), 1)
        allowed = (key_positions <= positions) & (key_positions >= starts)
        block_scores = dot_nt(queries[...], block[:, :HEAD_WIDTH]) * score_scale
        scores.append(jnp.where(allowed, block_scores, masked_score))
    row_max = functools.reduce(
        jnp.maximum, [jnp.max(part, axis=1, keepdims=True) for part in scores]
    )
    raised = [jnp.exp(part - row_max) for part in scores]
    row_total = sum(jnp.sum(part, axis=1, keepdims=True) for part in raised)
    inverse = 1.0 / row_total
    probs = [part * inverse for part in raised]
    weighted = jnp.zeros((QHEADS * own_rows, HEAD_WIDTH), jnp.float32)
    for back, block in enumerate(blocks):
        low_probs[back] = probs[back].astype(jnp.bfloat16)
        weighted += dot_nn(low_probs[back], block[:, HEAD_WIDTH:])
    attended = weighted.astype(jnp.bfloat16)
    gradients = jnp.concatenate(
        [incoming[:, head * HEAD_WIDTH : (head + 1) * HEAD_WIDTH] for head in range(QHEADS)],
        axis=0,
    )
    row_delta = jnp.sum(
        gradients.astype(jnp.float32) * attended.astype(jnp.float32), axis=1, keepdims=True
    )
    start = pl.multiple_of(tp_index * own_rows, own_rows)
    total = jnp.zeros((QHEADS * own_rows, HEAD_WIDTH), jnp.float32)
    for back, block in enumerate(blocks):
        prob_grad = dot_nt(gradients, block[:, HEAD_WIDTH:])
        score_grad = (probs[back] * (prob_grad - row_delta)).astype(jnp.bfloat16)
        total += dot_nn(score_grad, block[:, :HEAD_WIDTH])
        key_part = dot_tn(score_grad, queries[...]) * score_scale
        value_part = dot_tn(low_probs[back], gradients)
        mine = tp_index == 0
        kept[back, :, :HEAD_WIDTH] = jnp.where(mine, key_part[:own_rows], key_part[own_rows:])
        sent[back, :, :HEAD_WIDTH] = jnp.where(mine, key_part[own_rows:], key_part[:own_rows])
        kept[back, :, HEAD_WIDTH:] = jnp.where(mine, value_part[:own_rows], value_part[own_rows:])
        sent[back, :, HEAD_WIDTH:] = jnp.where(mine, value_part[own_rows:], value_part[:own_rows])
    own = pl.ds(start, own_rows)
    for head in range(QHEADS):
        picked = slice(head * own_rows, (head + 1) * own_rows)
        columns = slice(head * HEAD_WIDTH, (head + 1) * HEAD_WIDTH)
        output[:, columns] = attended[picked]
        query_grad[:, columns] = rotated(
            total[picked] * score_scale, cosines[own], -sines[own]
        ).astype(jnp.bfloat16)


def rank_kernel(
    unused, seq_count, lengths, own_query, other_query, own_pair, other_pair, low_rank, up_blocks, *refs
):
    refs = refs[unused:]
    gradients, rank_grad = refs[:2]
    split_terms, (terms, blocks) = refs[2:-2], refs[-2:]
    own_rows, query_columns = own_query.shape
    rows = low_rank.shape[0]
    seq_index = lax.axis_index("seq")
    start = pl.multiple_of(lax.axis_index("tp") * own_rows, own_rows)
    other = pl.multiple_of(own_rows - start, own_rows)
    gradients[pl.ds(start, own_rows), :query_columns] = own_query[...]
    gradients[pl.ds(other, own_rows), :query_columns] = other_query[...]
    gradients[pl.ds(start, own_rows), query_columns:] = own_pair[...]
    gradients[pl.ds(other, own_rows), query_columns:] = other_pair[...]
    query_grad = gradients[:, :query_columns]
    value_grad = gradients[:, query_columns + HEAD_WIDTH :]
    low = low_rank[...]
    rank = low.shape[1] // 2
    segments = row_segments(kernel_marks(lengths), row_positions(seq_index * rows, rows))
    total = jnp.zeros((rows, low.shape[1]), jnp.float32)
    for document in range(SEGS):
        member = segments == document
        parts = dot_nt(query_grad, up_blocks[document, :, :query_columns])
        parts += dot_nt(value_grad, up_blocks[document, :, query_columns:])
        total = jnp.where(member, parts, total)
        chosen = jnp.where(member, low, jnp.zeros_like(low))
        query_terms = dot_tn(chosen, query_grad)
        value_terms = dot_tn(chosen, value_grad)
        place = slice(document * rank, (document + 1) * rank)
        terms[place, :query_columns] = adapter_scale * query_terms[:rank]
        terms[place, query_columns:] = adapter_scale * value_terms[rank:]
    rank_grad[...] = (adapter_scale * total).astype(jnp.bfloat16)
    held = blocks.shape[2]
    for holder in range(seq_count):
        blocks[holder] = terms[:, holder * held : (holder + 1) * held]
    for steps, block in enumerate(split_terms):
        block[...] = blocks[ring_index(seq_index + steps - seq_count, seq_count)]


def token_kernel(frozen_places, down_places, seq_count, lengths, gradients, rank_grad, *refs):
    frozen_count, down_count = len(frozen_places), len(down_places)
    frozen_pieces = refs[:frozen_count]
    down_pieces = refs[frozen_count : frozen_count + down_count]
    token_grad, frozen, down, semaphore = refs[frozen_count + down_count :]
    copies = fetch_pieces(frozen_places, frozen_pieces, frozen, semaphore, 0)
    copies += fetch_pieces(down_places, down_pieces, down, semaphore, frozen_count)
    for copy in copies:
        copy.wait()
    rows = gradients.shape[0]
    joint_rank = down.shape[0] // 2
    second = second_document(kernel_marks(lengths), rows, seq_count)
    low = rank_grad[...]
    nothing = jnp.zeros_like(low)
    first_low = jnp.where(second, nothing, low)
    second_low = jnp.where(second, low, nothing)
    chunk = 512
    for column in range(0, token_grad.shape[1], chunk):
        columns = slice(column, column + chunk)
        total = dot_nn(gradients[...], frozen[:, columns])
        total += dot_nn(first_low, down[:joint_rank, columns])
        total += dot_nn(second_low, down[joint_rank:, columns])
        token_grad[:, columns] = total.astype(jnp.bfloat16)


def split_halves(terms, own, far):
    held = own.shape[1]
    left, right = terms[:, :held], terms[:, held:]
    ahead = lax.axis_index("batch") == 0
    own[...] = jnp.where(ahead, left, right)
    far[...] = jnp.where(ahead, right, left)


def down_kernel(block_count, lengths, *refs):
    ranks = refs[:block_count]
    columns = refs[block_count : 2 * block_count]
    up_parts = refs[2 * block_count : 3 * block_count]
    outputs = refs[3 * block_count :]
    rows, joint_rank = ranks[0].shape
    ends = kernel_marks(lengths)
    all_terms = []
    for document in range(SEGS):
        total = jnp.zeros((joint_rank, columns[0].shape[1]), jnp.float32)
        for behind in range(block_count):
            holder = ring_index(lax.axis_index("seq") - behind, block_count)
            segments = row_segments(ends, row_positions(holder * rows, rows))
            low = ranks[behind][...]
            chosen = jnp.where(segments == document, low, jnp.zeros_like(low))
            total += dot_tn(chosen, columns[behind][...])
        all_terms.append(total)
    down_terms = jnp.concatenate(all_terms, axis=0)
    up_terms = sum(part[...] for part in up_parts)
    if len(outputs) == 2:
        outputs[0][...] = down_terms
        outputs[1][...] = up_terms
    else:
        split_halves(down_terms, *outputs[:2])
        split_halves(up_terms, *outputs[2:])


def bank_kernel(block_count, bank_rows, *refs):
    down_terms = refs[:block_count]
    up_terms = refs[block_count : 2 * block_count]
    down_out, up_out = refs[2 * block_count + 2 :]
    step = pl.program_id(0)
    joint_rank = down_out.shape[1]
    low_width = up_out.shape[1]
    down_total = jnp.zeros((joint_rank, down_out.shape[3]), jnp.float32)
    up_total = jnp.zeros((low_width, up_out.shape[2]), jnp.float32)
    for block in range(block_count):
        for document in range(SEGS):
            same = bank_rows[block * SEGS + document] == bank_rows[step]
            down_rows = down_terms[block][document * joint_rank : (document + 1) * joint_rank]
            up_rows = up_terms[block][document * low_width : (document + 1) * low_width]
            down_total += jnp.where(same, down_rows, 0.0)
            up_total += jnp.where(same, up_rows, 0.0)
    down_out[0, :, 0, :] = down_total
    up_out[0] = up_total


def shards(
    tokens,
    frozen_qkv_matrix,
    adapter_down_weight,
    adapter_up_weight,
    adapter_bank_row,
    document_lengths,
    document_adapter,
    output_gradient,
):
    seq_count = lax.axis_size("seq")
    batch_count = lax.axis_size("batch")
    group_count = lax.axis_size("groups")
    chip_size = lax.axis_size("tp")
    seq_index = lax.axis_index("seq")
    batch_index = lax.axis_index("batch")
    group_index = lax.axis_index("groups")
    tp_index = lax.axis_index("tp")
    local_tokens = tokens[0]
    rows, width = local_tokens.shape
    own_rows = rows // chip_size
    query_columns = QHEADS * HEAD_WIDTH
    frozen_rows = frozen_qkv_matrix.shape[0]
    features = frozen_rows * seq_count
    low_width = ADAPTER_RANK
    joint_rank = adapter_down_weight.shape[1]
    adapters = adapter_bank_row.shape[0]
    bf16 = jnp.bfloat16
    f32 = jnp.float32

    sample_rows = lookup_rows(adapter_bank_row, document_adapter)
    lengths = lax.dynamic_index_in_dim(document_lengths, batch_index, 0, keepdims=False)
    ends = jnp.cumsum(lengths)
    half_count = seq_count // 2

    def first_document(holder):
        return (holder >= half_count).astype(jnp.int32)

    plane_count = group_count * batch_count
    share = width // plane_count
    pieces, places = [], []
    direct = group_count == 2 and batch_count == 2 and share % 128 == 0 and frozen_rows % 16 == 0
    if direct:
        own_share = lax.dynamic_slice_in_dim(
            frozen_qkv_matrix, (group_index * batch_count + batch_index) * share, share, axis=1
        )
        pieces.append(frozen_qkv_matrix)
        places.append(frozen_place(seq_count, frozen_rows, None, 0, 0, 0))
        before = shift(own_share, "seq", 1)
        after = shift(own_share, "seq", seq_count - 1)
        arrivals = [(1, before), (seq_count - 1, after)]
        for steps in range(2, seq_count - 1):
            before = shift(before, "seq", 1)
            arrivals.append((steps, before))
        for steps, here in arrivals:
            if steps < seq_count - 1:
                over_batch = shift(here, "batch", 1)
                over_groups = shift(here, "groups", 1)
                over_both = shift(over_batch, "groups", 1)
            else:
                over_groups = shift(here, "groups", 1)
                over_batch = shift(here, "batch", 1)
                over_both = shift(over_groups, "batch", 1)
            for value, batch_step, group_step in (
                (here, 0, 0),
                (over_batch, 1, 0),
                (over_groups, 0, 1),
                (over_both, 1, 1),
            ):
                pieces.append(value)
                places.append(
                    frozen_place(seq_count, frozen_rows, share, steps, batch_step, group_step)
                )
    else:
        pieces.append(lax.all_gather(frozen_qkv_matrix, "seq", axis=0, tiled=True))
        places.append(whole_place)

    down_bank = adapter_down_weight[:, :, 0, :]
    if batch_count == 2:
        own_bank = lax.dynamic_index_in_dim(sample_rows, batch_index, 0, keepdims=False)
        other_bank = lax.dynamic_index_in_dim(sample_rows, 1 - batch_index, 0, keepdims=False)
        own_down, own_up = down_bank[own_bank], adapter_up_weight[own_bank]
        far_down = shift(down_bank[other_bank], "batch", 1)
        far_up = shift(adapter_up_weight[other_bank], "batch", 1)
        ahead = batch_index == 0
        down_block = jnp.concatenate(
            [jnp.where(ahead, own_down, far_down), jnp.where(ahead, far_down, own_down)], axis=2
        )
        up_block = jnp.concatenate(
            [jnp.where(ahead, own_up, far_up), jnp.where(ahead, far_up, own_up)], axis=2
        )
    else:
        got_down = lax.all_to_all(
            down_bank[sample_rows], "batch", split_axis=0, concat_axis=0, tiled=True
        )
        got_up = lax.all_to_all(
            adapter_up_weight[sample_rows], "batch", split_axis=0, concat_axis=0, tiled=True
        )
        down_block = jnp.transpose(got_down, (1, 2, 0, 3)).reshape(SEGS, joint_rank, -1)
        up_block = jnp.transpose(got_up, (1, 2, 0, 3)).reshape(SEGS, low_width, -1)
    down_block = down_block.reshape(SEGS * joint_rank, -1)
    up_block = up_block.reshape(SEGS * low_width, -1)
    down_width = down_block.shape[1]
    down_parts, down_places, up_parts = [], [], []
    for steps in range(seq_count):
        target = jnp.remainder(seq_index + steps, seq_count)
        part = lax.dynamic_slice_in_dim(
            down_block, first_document(target) * joint_rank, 2 * joint_rank
        )
        down_parts.append(shift(part, "seq", steps) if steps else part)
        down_places.append(down_place(seq_count, down_width, steps))
        up_parts.append(shift(up_block, "seq", steps) if steps else up_block)
    relative = jnp.remainder(seq_index - jnp.arange(seq_count, dtype=jnp.int32), seq_count)
    up_rows = jnp.stack(up_parts)[relative]
    up_rows = jnp.transpose(up_rows, (1, 0, 2)).reshape(SEGS, low_width, -1)
    is_query = jnp.arange(up_rows.shape[2]) < query_columns
    up_blocks = jnp.concatenate(
        [
            jnp.where(is_query[None, None, :], up_rows, 0),
            jnp.where(is_query[None, None, :], 0, up_rows),
        ],
        axis=1,
    )
    if down_width % 128 != 0:
        merged = jnp.stack(down_parts)[relative]
        merged = jnp.transpose(merged, (1, 0, 2)).reshape(2 * joint_rank, -1)
        down_parts, down_places = [merged], [whole_place]

    positions = seq_index * rows + jnp.arange(rows, dtype=jnp.int32)
    inside = positions - jnp.where(
        positions >= ends[1], ends[1], jnp.where(positions >= ends[0], ends[0], 0)
    )
    exponent = jnp.arange(HEAD_WIDTH // 2, dtype=f32) * (2.0 / HEAD_WIDTH)
    angles = inside.astype(f32)[:, None] * jnp.power(jnp.float32(rope_base), -exponent)[None, :]
    cosines = jnp.tile(jnp.cos(angles), (1, 2))
    sines = jnp.concatenate([-jnp.sin(angles), jnp.sin(angles)], axis=1)

    scratch = [
        pltpu.VMEM((features, width), bf16),
        pltpu.VMEM((2 * joint_rank, width), bf16),
        pltpu.SemaphoreType.DMA((len(pieces) + len(down_parts),)),
    ]
    weight_bytes = 2 * width * (features + 2 * joint_rank)
    held_down = down_width // batch_count
    held_up = up_blocks.shape[2] // (seq_count * batch_count)
    down_zeros = jnp.zeros((adapters, joint_rank, 1, held_down), f32)
    up_zeros = jnp.zeros((adapters, low_width, held_up), f32)
    early = [down_zeros, up_zeros, cosines, sines, up_blocks]
    part_width = features + 128
    column_count = seq_count if down_width % 128 == 0 else 0
    part, *column_blocks = pl.pallas_call(
        functools.partial(project_kernel, places, down_places, len(early), seq_count),
        out_shape=[jax.ShapeDtypeStruct((rows, part_width), f32)]
        + [jax.ShapeDtypeStruct((rows, down_width), bf16)] * column_count,
        in_specs=[in_smem(), in_vmem()]
        + [in_place()] * (len(pieces) + len(down_parts) + len(early)),
        out_specs=[in_vmem()] * (1 + column_count),
        scratch_shapes=scratch,
        compiler_params=pltpu.CompilerParams(vmem_limit_bytes=20 * mebibyte),
        cost_estimate=cost(
            2 * rows * width * (features + 2 * joint_rank), weight_bytes + 2 * rows * width
        ),
        name="project",
    )(document_lengths, local_tokens, *pieces, *down_parts, *early)

    if column_count == 0:
        column_blocks = [
            lax.dynamic_slice_in_dim(
                local_tokens,
                jnp.remainder(seq_index + steps, seq_count) * down_width,
                down_width,
                axis=1,
            )
            for steps in range(seq_count)
        ]
    column_parts = [
        shift(block, "seq", steps) if steps else block
        for steps, block in enumerate(column_blocks)
    ]

    other_part = shift(part, "tp", 1)
    queries, pairs, low_rank = pl.pallas_call(
        qkv_kernel,
        out_shape=(
            jax.ShapeDtypeStruct((QHEADS * own_rows, HEAD_WIDTH), bf16),
            jax.ShapeDtypeStruct((rows, 2 * HEAD_WIDTH), bf16),
            jax.ShapeDtypeStruct((rows, joint_rank), bf16),
        ),
        in_specs=[in_smem()] + [in_vmem()] * 5,
        out_specs=(in_vmem(),) * 3,
        compiler_params=pltpu.CompilerParams(vmem_limit_bytes=8 * mebibyte),
        cost_estimate=cost(2 * rows * 3 * 64 * 640, 8 * rows * features),
        name="qkv",
    )(document_lengths, part, other_part, up_blocks, cosines, sines)

    blocks = [pairs] + [push(pairs, "seq", back) for back in range(1, half_count + 1)]
    block_count = len(blocks)
    incoming = output_gradient[0]
    attention, query_grad, kept, sent = pl.pallas_call(
        functools.partial(attention_kernel, block_count),
        out_shape=(
            jax.ShapeDtypeStruct((own_rows, query_columns), bf16),
            jax.ShapeDtypeStruct((own_rows, query_columns), bf16),
            jax.ShapeDtypeStruct((block_count, own_rows, 2 * HEAD_WIDTH), f32),
            jax.ShapeDtypeStruct((block_count, own_rows, 2 * HEAD_WIDTH), f32),
        ),
        in_specs=[in_smem()] + [in_vmem()] * (4 + block_count),
        out_specs=(in_vmem(),) * 4,
        scratch_shapes=[pltpu.VMEM((block_count, QHEADS * own_rows, rows), bf16)],
        compiler_params=pltpu.CompilerParams(vmem_limit_bytes=(4 + 4 * block_count) * mebibyte),
        cost_estimate=cost(
            10 * block_count * QHEADS * own_rows * rows * HEAD_WIDTH,
            4 * rows * features,
            block_count * QHEADS * own_rows * rows,
        ),
        name="attention",
    )(document_lengths, queries, incoming, cosines, sines, *blocks)

    other_query = shift(query_grad, "tp", 1)
    pair_sums = kept + shift(sent, "tp", 1)
    own_sum = pair_sums[0]
    for back in range(1, block_count):
        own_sum = own_sum + push(pair_sums[back], "seq", -back)
    own_place = tp_index * own_rows
    own_cosines = lax.dynamic_slice_in_dim(cosines, own_place, own_rows)
    own_sines = lax.dynamic_slice_in_dim(sines, own_place, own_rows)
    key_grad = own_sum[:, :HEAD_WIDTH]
    key_grad = key_grad * own_cosines - jnp.roll(key_grad, HEAD_WIDTH // 2, axis=1) * own_sines
    pair_grad = jnp.concatenate([key_grad, own_sum[:, HEAD_WIDTH:]], axis=1).astype(bf16)
    other_pair = shift(pair_grad, "tp", 1)

    gradients, rank_grad, *up_split = pl.pallas_call(
        functools.partial(rank_kernel, seq_count - 1, seq_count),
        out_shape=[
            jax.ShapeDtypeStruct((rows, features), bf16),
            jax.ShapeDtypeStruct((rows, joint_rank), bf16),
        ]
        + [jax.ShapeDtypeStruct((SEGS * low_width, held_up * batch_count), f32)] * seq_count,
        in_specs=[in_smem()] + [in_vmem()] * 6 + [in_place()] * (seq_count - 1),
        out_specs=[in_vmem()] * (2 + seq_count),
        scratch_shapes=[
            pltpu.VMEM((SEGS * low_width, features - HEAD_WIDTH), f32),
            pltpu.VMEM((seq_count, SEGS * low_width, held_up * batch_count), f32),
        ],
        compiler_params=pltpu.CompilerParams(vmem_limit_bytes=8 * mebibyte),
        cost_estimate=cost(4 * rows * 3 * 64 * 640, 4 * rows * features),
        name="rank_gradients",
    )(
        document_lengths, query_grad, other_query, pair_grad, other_pair, low_rank, up_blocks,
        *column_parts[1:],
    )

    rank_parts = [rank_grad] + [shift(rank_grad, "seq", steps) for steps in range(1, seq_count)]
    up_sums = [
        shift(block, "seq", steps) if steps else block for steps, block in enumerate(up_split)
    ]

    token_grad = pl.pallas_call(
        functools.partial(token_kernel, places, down_places, seq_count),
        out_shape=jax.ShapeDtypeStruct((rows, width), bf16),
        in_specs=[in_smem(), in_vmem(), in_vmem()]
        + [in_place()] * (len(pieces) + len(down_parts)),
        out_specs=in_vmem(),
        scratch_shapes=scratch,
        compiler_params=pltpu.CompilerParams(vmem_limit_bytes=20 * mebibyte),
        cost_estimate=cost(
            2 * rows * width * (features + 2 * joint_rank), weight_bytes + 2 * rows * width
        ),
        name="token_gradient",
    )(document_lengths, gradients, rank_grad, *pieces, *down_parts)

    if batch_count == 2:
        term_shapes = [(SEGS * joint_rank, held_down)] * 2 + [(SEGS * low_width, held_up)] * 2
    else:
        term_shapes = [(SEGS * joint_rank, down_width), (SEGS * low_width, held_up * batch_count)]
    terms = pl.pallas_call(
        functools.partial(down_kernel, seq_count),
        out_shape=[jax.ShapeDtypeStruct(shape, f32) for shape in term_shapes],
        in_specs=[in_smem()] + [in_vmem()] * (3 * seq_count),
        out_specs=[in_vmem()] * len(term_shapes),
        compiler_params=pltpu.CompilerParams(vmem_limit_bytes=8 * mebibyte),
        cost_estimate=cost(
            2 * seq_count * rows * SEGS * joint_rank * down_width, 2 * seq_count * rows * down_width
        ),
        name="down_terms",
    )(document_lengths, *rank_parts, *column_parts, *up_sums)

    if batch_count == 2:
        bank_downs = [terms[0], shift(terms[1], "batch", 1)]
        bank_ups = [terms[2], shift(terms[3], "batch", 1)]
        bank_rows = jnp.concatenate([own_bank, other_bank])
    else:
        down_send = jnp.transpose(
            terms[0].reshape(SEGS * joint_rank, batch_count, held_down), (1, 0, 2)
        )
        up_send = jnp.transpose(
            terms[1].reshape(SEGS * low_width, batch_count, held_up), (1, 0, 2)
        )
        back_down = lax.all_to_all(down_send, "batch", split_axis=0, concat_axis=0, tiled=True)
        back_up = lax.all_to_all(up_send, "batch", split_axis=0, concat_axis=0, tiled=True)
        bank_downs = [back_down[batch] for batch in range(batch_count)]
        bank_ups = [back_up[batch] for batch in range(batch_count)]
        bank_rows = sample_rows.reshape(-1)

    def whole(array):
        return pl.BlockSpec(array.shape, lambda step, bank: (0,) * array.ndim)

    down_grad, up_grad = pl.pallas_call(
        functools.partial(bank_kernel, batch_count),
        out_shape=(
            jax.ShapeDtypeStruct(down_zeros.shape, f32),
            jax.ShapeDtypeStruct(up_zeros.shape, f32),
        ),
        grid_spec=pltpu.PrefetchScalarGridSpec(
            num_scalar_prefetch=1,
            grid=(batch_count * SEGS,),
            in_specs=[whole(array) for array in bank_downs + bank_ups] + [in_place()] * 2,
            out_specs=(
                pl.BlockSpec(
                    (1, joint_rank, 1, held_down), lambda step, bank: (bank[step], 0, 0, 0)
                ),
                pl.BlockSpec((1, low_width, held_up), lambda step, bank: (bank[step], 0, 0)),
            ),
        ),
        input_output_aliases={1 + 2 * batch_count: 0, 2 + 2 * batch_count: 1},
        compiler_params=pltpu.CompilerParams(vmem_limit_bytes=16 * mebibyte),
        name="bank_rows",
    )(bank_rows, *bank_downs, *bank_ups, down_zeros, up_zeros)
    return (attention[None], token_grad[None], down_grad, up_grad)


def solution(mesh):
    in_specs = (
        P(("groups", "batch"), "seq", "tp"),
        P("seq", "tp"),
        P(None, None, "tp", ("seq", "batch")),
        P(None, None, ("seq", "batch")),
        P(),
        P("groups", None),
        P("groups", None),
        P(("groups", "batch"), ("seq", "tp"), None),
    )
    out_specs = (
        P(("groups", "batch"), ("seq", "tp"), None),
        P(("groups", "batch"), "seq", "tp"),
        P("groups", None, "tp", ("seq", "batch")),
        P("groups", None, ("seq", "batch")),
    )
    return jax.shard_map(shards, mesh=mesh, in_specs=in_specs, out_specs=out_specs, check_vma=False)
```

```python
import functools

import jax
import jax.numpy as jnp
from jax import lax
from jax.experimental import pallas as pl
from jax.experimental.pallas import tpu as pltpu
from jax.sharding import PartitionSpec as P

QHEADS = 4
HEAD_WIDTH = 128
ADAPTER_RANK = 32
SEGS = 3

adapter_scale = 2.0
rope_base = 5000000.0
masked_score = -1e30
mebibyte = 1024 * 1024


def shift(value, axis, steps):
    count = lax.axis_size(axis)
    return lax.ppermute(value, axis, [(at, (at + steps) % count) for at in range(count)])


def push(value, axis, steps):
    count = lax.axis_size(axis)
    pairs = [(at, at + steps) for at in range(count) if 0 <= at + steps < count]
    return lax.ppermute(value, axis, pairs)


def dot_nt(left, right):
    return lax.dot_general(
        left, right, (((1,), (1,)), ((), ())), preferred_element_type=jnp.float32
    )


def dot_nn(left, right):
    return jnp.dot(left, right, preferred_element_type=jnp.float32)


def dot_tn(left, right):
    return lax.dot_general(
        left, right, (((0,), (0,)), ((), ())), preferred_element_type=jnp.float32
    )


def lookup_rows(adapter_bank_row, document_adapter):
    matches = document_adapter[..., None] == jnp.arange(adapter_bank_row.shape[0], dtype=jnp.int32)
    return jnp.sum(jnp.where(matches, adapter_bank_row, 0), axis=-1)


def row_positions(first, count):
    return first + lax.broadcasted_iota(jnp.int32, (count, 1), 0)


def ring_index(index, count):
    return lax.rem(index + count, count)


def kernel_marks(lengths):
    batch = lax.axis_index("batch")
    first_end = lengths[batch, 0]
    return first_end, first_end + lengths[batch, 1]


def row_segments(ends, positions):
    return (positions >= ends[0]).astype(jnp.int32) + (positions >= ends[1]).astype(jnp.int32)


def cost(flops, bytes_accessed, transcendentals=0):
    return pl.CostEstimate(
        flops=flops, bytes_accessed=bytes_accessed, transcendentals=transcendentals
    )


def in_vmem():
    return pl.BlockSpec(memory_space=pltpu.VMEM)


def in_smem():
    return pl.BlockSpec(memory_space=pltpu.SMEM)


def in_place():
    return pl.BlockSpec(memory_space=pl.ANY)


def fetch(piece, target, place, semaphore):
    height, width = piece.shape
    row, column = place()
    copy = pltpu.make_async_copy(
        piece,
        target.at[
            pl.ds(pl.multiple_of(row, 16), height), pl.ds(pl.multiple_of(column, 128), width)
        ],
        semaphore,
    )
    copy.start()
    return copy


def frozen_place(seq_count, rows, share, behind, batch_step, group_step):
    def place():
        holder = ring_index(lax.axis_index("seq") - behind, seq_count)
        if share is None:
            return holder * rows, 0
        batch = lax.rem(lax.axis_index("batch") + batch_step, 2)
        group = lax.rem(lax.axis_index("groups") + group_step, 2)
        return holder * rows, (group * 2 + batch) * share

    return place


def down_place(seq_count, width, behind):
    def place():
        return 0, ring_index(lax.axis_index("seq") - behind, seq_count) * width

    return place


def whole_place():
    return 0, 0


def second_document(ends, rows, seq_count):
    seq_index = lax.axis_index("seq")
    first = (seq_index >= seq_count // 2).astype(jnp.int32)
    return row_segments(ends, row_positions(seq_index * rows, rows)) != first


def select_kernel(bank_row, adapters, down_bank, up_bank, *refs):
    outputs, semaphore = refs[:4], refs[4]
    batch = lax.axis_index("batch")
    copies = []
    for which, sample in enumerate((batch, 1 - batch)):
        for document in range(SEGS):
            row = bank_row[adapters[sample, document]]
            for source, target in ((down_bank, outputs[which]), (up_bank, outputs[2 + which])):
                copy = pltpu.make_async_copy(
                    source.at[row], target.at[document], semaphore.at[len(copies)]
                )
                copy.start()
                copies.append(copy)
    for copy in copies:
        copy.wait()


def pack_kernel(unused, seq_count, own_down, far_down, own_up, far_up, tokens, *refs):
    refs = refs[unused:]
    payloads, columns = refs[:seq_count], refs[seq_count : 2 * seq_count]
    down, up = refs[2 * seq_count :]
    ahead = lax.axis_index("batch") == 0
    joint_rank, held = own_down.shape[1:]
    low_width, held_up = own_up.shape[1:]
    for document in range(SEGS):
        rows = slice(document * joint_rank, (document + 1) * joint_rank)
        down[rows, :held] = jnp.where(ahead, own_down[document], far_down[document])
        down[rows, held:] = jnp.where(ahead, far_down[document], own_down[document])
        up[document, :, :held_up] = jnp.where(ahead, own_up[document], far_up[document])
        up[document, :, held_up:] = jnp.where(ahead, far_up[document], own_up[document])
    half, slot = low_width // 2, down.shape[1] // 4
    for steps in range(seq_count):
        target = ring_index(lax.axis_index("seq") + steps - seq_count, seq_count)
        first = (target >= seq_count // 2).astype(jnp.int32)
        start = pl.multiple_of(first * joint_rank, joint_rank)
        payload = payloads[steps]
        payload[: 2 * joint_rank] = down[pl.ds(start, 2 * joint_rank)]
        for index in range(2):
            block = up[first + index]
            for part in range(2):
                column = (2 * index + part) * slot
                payload[2 * joint_rank :, column : column + 2 * held_up] = block[
                    part * half : (part + 1) * half
                ]
        width = columns[steps].shape[1]
        columns[steps][...] = tokens[:, pl.ds(pl.multiple_of(target * width, 128), width)]


def assemble_up(seq_count, arrived, up_blocks):
    low_width = up_blocks.shape[1] // 2
    query_columns = QHEADS * HEAD_WIDTH
    seq_index = lax.axis_index("seq")
    first = (seq_index >= seq_count // 2).astype(jnp.int32)
    held = up_blocks.shape[2] // seq_count
    half, slot = low_width // 2, arrived.shape[2] // 4
    up_blocks[...] = jnp.zeros_like(up_blocks)
    for holder in range(seq_count):
        block = arrived[ring_index(seq_index - holder, seq_count)]
        start, stop = holder * held, (holder + 1) * held
        middle = min(max(query_columns, start), stop)
        for index in range(2):
            for part in range(2):
                offset = (2 * index + part) * slot
                if middle > start:
                    up_blocks[first + index, part * half : (part + 1) * half, start:middle] = block[
                        :, offset : offset + middle - start
                    ]
                if stop > middle:
                    low = low_width + part * half
                    up_blocks[first + index, low : low + half, middle:stop] = block[
                        :, offset + middle - start : offset + held
                    ]


def project_kernel(frozen_places, down_places, unused, seq_count, lengths, tokens, *refs):
    frozen_count, down_count = len(frozen_places), len(down_places)
    frozen_pieces = refs[:frozen_count]
    down_pieces = refs[frozen_count : frozen_count + down_count]
    refs = refs[frozen_count + down_count + unused :]
    packed = down_count > 1
    part, frozen, down = refs[:3]
    semaphore = refs[-1]
    copies = []
    for piece, place in zip(frozen_pieces, frozen_places):
        copies.append(fetch(piece, frozen, place, semaphore.at[len(copies)]))
    joint_rank = down.shape[0] // 2
    for number, (piece, place) in enumerate(zip(down_pieces, down_places)):
        rows = piece.at[pl.ds(0, 2 * joint_rank)] if packed else piece
        copies.append(fetch(rows, down, place, semaphore.at[len(copies)]))
        if packed:
            extra = piece.shape[0] - 2 * joint_rank
            copy = pltpu.make_async_copy(
                piece.at[pl.ds(2 * joint_rank, extra)],
                refs[4].at[number],
                semaphore.at[len(copies)],
            )
            copy.start()
            copies.append(copy)
    for copy in copies:
        copy.wait()
    rows = tokens.shape[0]
    features = frozen.shape[0]
    second = second_document(kernel_marks(lengths), rows, seq_count)
    values = tokens[...]
    part[:, :features] = dot_nt(values, frozen[...])
    first_low = dot_nt(values, down[:joint_rank])
    second_low = dot_nt(values, down[joint_rank:])
    part[:, features : features + joint_rank] = jnp.where(second, second_low, first_low)
    if packed:
        assemble_up(seq_count, refs[4], refs[3])


def rotated(values, cosines, sines):
    return values * cosines + pltpu.roll(values, values.shape[1] // 2, 1) * sines


def qkv_kernel(lengths, mine, theirs, up_blocks, cosines, sines, queries, pairs, low_rank):
    rows = mine.shape[0]
    own_rows = queries.shape[0] // QHEADS
    query_columns = QHEADS * HEAD_WIDTH
    value_start = query_columns + HEAD_WIDTH
    features = value_start + HEAD_WIDTH
    low_columns = slice(features, features + low_rank.shape[1])
    ends = kernel_marks(lengths)
    first_row = lax.axis_index("seq") * rows
    segments = row_segments(ends, row_positions(first_row, rows))
    low = (mine[:, low_columns] + theirs[:, low_columns]).astype(jnp.bfloat16)
    low_rank[...] = low
    value_delta = jnp.zeros((rows, HEAD_WIDTH), jnp.float32)
    for document in range(SEGS):
        chosen = jnp.where(segments == document, low, jnp.zeros_like(low))
        value_delta += dot_nn(chosen, up_blocks[document, :, query_columns:])
    keys = mine[:, query_columns:value_start] + theirs[:, query_columns:value_start]
    pairs[:, :HEAD_WIDTH] = rotated(keys, cosines[...], sines[...]).astype(jnp.bfloat16)
    values = mine[:, value_start:features] + theirs[:, value_start:features]
    pairs[:, HEAD_WIDTH:] = (values + adapter_scale * value_delta).astype(jnp.bfloat16)
    start = pl.multiple_of(lax.axis_index("tp") * own_rows, own_rows)
    own = pl.ds(start, own_rows)
    own_segments = row_segments(ends, row_positions(first_row + start, own_rows))
    own_low = (mine[own, low_columns] + theirs[own, low_columns]).astype(jnp.bfloat16)
    query_delta = jnp.zeros((own_rows, query_columns), jnp.float32)
    for document in range(SEGS):
        chosen = jnp.where(own_segments == document, own_low, jnp.zeros_like(own_low))
        query_delta += dot_nn(chosen, up_blocks[document, :, :query_columns])
    projected = mine[own, :query_columns] + theirs[own, :query_columns]
    projected = projected + adapter_scale * query_delta
    for head in range(QHEADS):
        turned = rotated(
            projected[:, head * HEAD_WIDTH : (head + 1) * HEAD_WIDTH], cosines[own], sines[own]
        )
        queries[head * own_rows : (head + 1) * own_rows] = turned.astype(jnp.bfloat16)


def attention_kernel(block_count, unused, lengths, queries, incoming, cosines, sines, *refs):
    blocks = refs[:block_count]
    output, query_grad, kept, sent, low_probs = refs[block_count + unused :]
    own_rows, query_columns = incoming.shape
    rows = blocks[0].shape[0]
    score_scale = HEAD_WIDTH ** (-0.5)
    ends = kernel_marks(lengths)
    seq_index, tp_index = lax.axis_index("seq"), lax.axis_index("tp")
    positions = row_positions(seq_index * rows + tp_index * own_rows, own_rows)
    positions = jnp.concatenate([positions] * QHEADS, axis=0)
    segments = row_segments(ends, positions)
    starts = jnp.where(segments == 0, 0, jnp.where(segments == 1, ends[0], ends[1]))
    scores = []
    for back, block in enumerate(blocks):
        key_positions = (seq_index - back) * rows + lax.broadcasted_iota(jnp.int32, (1, rows), 1)
        allowed = (key_positions <= positions) & (key_positions >= starts)
        block_scores = dot_nt(queries[...], block[:, :HEAD_WIDTH]) * score_scale
        scores.append(jnp.where(allowed, block_scores, masked_score))
    row_max = functools.reduce(
        jnp.maximum, [jnp.max(part, axis=1, keepdims=True) for part in scores]
    )
    raised = [jnp.exp(part - row_max) for part in scores]
    row_total = sum(jnp.sum(part, axis=1, keepdims=True) for part in raised)
    inverse = 1.0 / row_total
    probs = [part * inverse for part in raised]
    weighted = jnp.zeros((QHEADS * own_rows, HEAD_WIDTH), jnp.float32)
    for back, block in enumerate(blocks):
        low_probs[back] = probs[back].astype(jnp.bfloat16)
        weighted += dot_nn(low_probs[back], block[:, HEAD_WIDTH:])
    attended = weighted.astype(jnp.bfloat16)
    gradients = jnp.concatenate(
        [incoming[:, head * HEAD_WIDTH : (head + 1) * HEAD_WIDTH] for head in range(QHEADS)],
        axis=0,
    )
    row_delta = jnp.sum(
        gradients.astype(jnp.float32) * attended.astype(jnp.float32), axis=1, keepdims=True
    )
    start = pl.multiple_of(tp_index * own_rows, own_rows)
    total = jnp.zeros((QHEADS * own_rows, HEAD_WIDTH), jnp.float32)
    for back, block in enumerate(blocks):
        prob_grad = dot_nt(gradients, block[:, HEAD_WIDTH:])
        score_grad = (probs[back] * (prob_grad - row_delta)).astype(jnp.bfloat16)
        total += dot_nn(score_grad, block[:, :HEAD_WIDTH])
        key_part = dot_tn(score_grad, queries[...]) * score_scale
        value_part = dot_tn(low_probs[back], gradients)
        mine = tp_index == 0
        kept[back, :, :HEAD_WIDTH] = jnp.where(mine, key_part[:own_rows], key_part[own_rows:])
        sent[back, :, :HEAD_WIDTH] = jnp.where(mine, key_part[own_rows:], key_part[:own_rows])
        kept[back, :, HEAD_WIDTH:] = jnp.where(mine, value_part[:own_rows], value_part[own_rows:])
        sent[back, :, HEAD_WIDTH:] = jnp.where(mine, value_part[own_rows:], value_part[:own_rows])
    own = pl.ds(start, own_rows)
    for head in range(QHEADS):
        picked = slice(head * own_rows, (head + 1) * own_rows)
        columns = slice(head * HEAD_WIDTH, (head + 1) * HEAD_WIDTH)
        output[:, columns] = attended[picked]
        query_grad[:, columns] = rotated(
            total[picked] * score_scale, cosines[own], -sines[own]
        ).astype(jnp.bfloat16)


def rank_kernel(
    unused, seq_count, lengths, own_query, other_query, own_pair, other_pair, low_rank, up_blocks, *refs
):
    refs = refs[unused:]
    gradients, rank_grad = refs[:2]
    split_terms, (terms, blocks) = refs[2:-2], refs[-2:]
    own_rows, query_columns = own_query.shape
    rows = low_rank.shape[0]
    seq_index = lax.axis_index("seq")
    start = pl.multiple_of(lax.axis_index("tp") * own_rows, own_rows)
    other = pl.multiple_of(own_rows - start, own_rows)
    gradients[pl.ds(start, own_rows), :query_columns] = own_query[...]
    gradients[pl.ds(other, own_rows), :query_columns] = other_query[...]
    gradients[pl.ds(start, own_rows), query_columns:] = own_pair[...]
    gradients[pl.ds(other, own_rows), query_columns:] = other_pair[...]
    query_grad = gradients[:, :query_columns]
    value_grad = gradients[:, query_columns + HEAD_WIDTH :]
    low = low_rank[...]
    rank = low.shape[1] // 2
    segments = row_segments(kernel_marks(lengths), row_positions(seq_index * rows, rows))
    total = jnp.zeros((rows, low.shape[1]), jnp.float32)
    for document in range(SEGS):
        member = segments == document
        parts = dot_nt(query_grad, up_blocks[document, :, :query_columns])
        parts += dot_nt(value_grad, up_blocks[document, :, query_columns:])
        total = jnp.where(member, parts, total)
        chosen = jnp.where(member, low, jnp.zeros_like(low))
        query_terms = dot_tn(chosen, query_grad)
        value_terms = dot_tn(chosen, value_grad)
        place = slice(document * rank, (document + 1) * rank)
        terms[place, :query_columns] = adapter_scale * query_terms[:rank]
        terms[place, query_columns:] = adapter_scale * value_terms[rank:]
    rank_grad[...] = (adapter_scale * total).astype(jnp.bfloat16)
    held = blocks.shape[2]
    for holder in range(seq_count):
        blocks[holder] = terms[:, holder * held : (holder + 1) * held]
    for steps, block in enumerate(split_terms):
        block[...] = blocks[ring_index(seq_index + steps - seq_count, seq_count)]


def token_kernel(seq_count, lengths, gradients, rank_grad, frozen, down, token_grad):
    rows = gradients.shape[0]
    joint_rank = down.shape[0] // 2
    second = second_document(kernel_marks(lengths), rows, seq_count)
    low = rank_grad[...]
    nothing = jnp.zeros_like(low)
    first_low = jnp.where(second, nothing, low)
    second_low = jnp.where(second, low, nothing)
    chunk = 512
    for column in range(0, token_grad.shape[1], chunk):
        columns = slice(column, column + chunk)
        total = dot_nn(gradients[...], frozen[:, columns])
        total += dot_nn(first_low, down[:joint_rank, columns])
        total += dot_nn(second_low, down[joint_rank:, columns])
        token_grad[:, columns] = total.astype(jnp.bfloat16)


def split_halves(terms, own, far):
    held = own.shape[1]
    left, right = terms[:, :held], terms[:, held:]
    ahead = lax.axis_index("batch") == 0
    own[...] = jnp.where(ahead, left, right)
    far[...] = jnp.where(ahead, right, left)


def down_kernel(block_count, lengths, *refs):
    ranks = refs[:block_count]
    columns = refs[block_count : 2 * block_count]
    up_parts = refs[2 * block_count : 3 * block_count]
    outputs = refs[3 * block_count :]
    rows, joint_rank = ranks[0].shape
    ends = kernel_marks(lengths)
    all_terms = []
    for document in range(SEGS):
        total = jnp.zeros((joint_rank, columns[0].shape[1]), jnp.float32)
        for behind in range(block_count):
            holder = ring_index(lax.axis_index("seq") - behind, block_count)
            segments = row_segments(ends, row_positions(holder * rows, rows))
            low = ranks[behind][...]
            chosen = jnp.where(segments == document, low, jnp.zeros_like(low))
            total += dot_tn(chosen, columns[behind][...])
        all_terms.append(total)
    down_terms = jnp.concatenate(all_terms, axis=0)
    up_terms = sum(part[...] for part in up_parts)
    if len(outputs) == 2:
        outputs[0][...] = down_terms
        outputs[1][...] = up_terms
    else:
        split_halves(down_terms, *outputs[:2])
        split_halves(up_terms, *outputs[2:])


def bank_kernel(block_count, bank_rows, *refs):
    down_terms = refs[:block_count]
    up_terms = refs[block_count : 2 * block_count]
    down_out, up_out = refs[2 * block_count + 2 :]
    step = pl.program_id(0)
    row = bank_rows[step]
    joint_rank = down_out.shape[1]
    low_width = up_out.shape[1]
    down_total = jnp.zeros((joint_rank, down_out.shape[3]), jnp.float32)
    up_total = jnp.zeros((low_width, up_out.shape[2]), jnp.float32)
    for block in range(block_count):
        for document in range(SEGS):
            same = bank_rows[block * SEGS + document] == row
            down_rows = down_terms[block][document * joint_rank : (document + 1) * joint_rank]
            up_rows = up_terms[block][document * low_width : (document + 1) * low_width]
            down_total += jnp.where(same, down_rows, 0.0)
            up_total += jnp.where(same, up_rows, 0.0)
    down_out[0, :, 0, :] = down_total
    up_out[0] = up_total


def shards(
    tokens,
    frozen_qkv_matrix,
    adapter_down_weight,
    adapter_up_weight,
    adapter_bank_row,
    document_lengths,
    document_adapter,
    output_gradient,
):
    seq_count = lax.axis_size("seq")
    batch_count = lax.axis_size("batch")
    group_count = lax.axis_size("groups")
    chip_size = lax.axis_size("tp")
    seq_index = lax.axis_index("seq")
    batch_index = lax.axis_index("batch")
    group_index = lax.axis_index("groups")
    tp_index = lax.axis_index("tp")
    local_tokens = tokens[0]
    rows, width = local_tokens.shape
    own_rows = rows // chip_size
    query_columns = QHEADS * HEAD_WIDTH
    frozen_rows = frozen_qkv_matrix.shape[0]
    features = frozen_rows * seq_count
    low_width = ADAPTER_RANK
    joint_rank = adapter_down_weight.shape[1]
    adapters = adapter_bank_row.shape[0]
    bf16 = jnp.bfloat16
    f32 = jnp.float32

    lengths = lax.dynamic_index_in_dim(document_lengths, batch_index, 0, keepdims=False)
    first_end = lengths[0]
    second_end = first_end + lengths[1]
    half_count = seq_count // 2

    plane_count = group_count * batch_count
    share = width // plane_count
    pieces, places = [], []
    held_down = adapter_down_weight.shape[3]
    held_up = adapter_up_weight.shape[2]
    down_width = held_down * batch_count
    direct = (
        group_count == 2
        and batch_count == 2
        and share % 128 == 0
        and down_width % 128 == 0
        and frozen_rows % 16 == 0
        and 4 * 2 * held_up <= down_width
    )
    if direct:
        own_share = lax.dynamic_slice_in_dim(
            frozen_qkv_matrix, (group_index * batch_count + batch_index) * share, share, axis=1
        )
        pieces.append(frozen_qkv_matrix)
        places.append(frozen_place(seq_count, frozen_rows, None, 0, 0, 0))
        before = shift(own_share, "seq", 1)
        after = shift(own_share, "seq", seq_count - 1)
        arrivals = [(1, before), (seq_count - 1, after)]
        for steps in range(2, seq_count - 1):
            before = shift(before, "seq", 1)
            arrivals.append((steps, before))
        for steps, here in arrivals:
            if steps < seq_count - 1:
                over_batch = shift(here, "batch", 1)
                over_groups = shift(here, "groups", 1)
                over_both = shift(over_batch, "groups", 1)
            else:
                over_groups = shift(here, "groups", 1)
                over_batch = shift(here, "batch", 1)
                over_both = shift(over_groups, "batch", 1)
            for value, batch_step, group_step in (
                (here, 0, 0),
                (over_batch, 1, 0),
                (over_groups, 0, 1),
                (over_both, 1, 1),
            ):
                pieces.append(value)
                places.append(
                    frozen_place(seq_count, frozen_rows, share, steps, batch_step, group_step)
                )
    else:
        pieces.append(lax.all_gather(frozen_qkv_matrix, "seq", axis=0, tiled=True))
        places.append(whole_place)

    down_bank = adapter_down_weight[:, :, 0, :]
    column_blocks, up_blocks = None, None
    if direct:
        row_shapes = [(SEGS, joint_rank, held_down)] * 2 + [(SEGS, low_width, held_up)] * 2
        own_down, far_down, own_up, far_up = pl.pallas_call(
            select_kernel,
            out_shape=[jax.ShapeDtypeStruct(shape, bf16) for shape in row_shapes],
            in_specs=[in_smem()] * 2 + [in_place()] * 2,
            out_specs=[in_place()] * 4,
            scratch_shapes=[pltpu.SemaphoreType.DMA((4 * SEGS,))],
            cost_estimate=cost(0, 4 * SEGS * joint_rank * held_down * 2),
            name="select",
        )(adapter_bank_row, document_adapter, down_bank, adapter_up_weight)
        far_down = shift(far_down, "batch", 1)
        far_up = shift(far_up, "batch", 1)
        payload_rows = 2 * joint_rank + low_width // 2
        packed = pl.pallas_call(
            functools.partial(pack_kernel, 1, seq_count),
            out_shape=[jax.ShapeDtypeStruct((payload_rows, down_width), bf16)] * seq_count
            + [jax.ShapeDtypeStruct((rows, down_width), bf16)] * seq_count,
            in_specs=[in_vmem()] * 5 + [in_place()],
            out_specs=[in_vmem()] * (2 * seq_count),
            scratch_shapes=[
                pltpu.VMEM((SEGS * joint_rank, down_width), bf16),
                pltpu.VMEM((SEGS, low_width, 2 * held_up), bf16),
            ],
            compiler_params=pltpu.CompilerParams(vmem_limit_bytes=8 * mebibyte),
            cost_estimate=cost(0, 4 * rows * width),
            name="pack",
        )(own_down, far_down, own_up, far_up, local_tokens, before)
        column_blocks = packed[seq_count:]
        down_parts = [
            shift(part, "seq", steps) if steps else part
            for steps, part in enumerate(packed[:seq_count])
        ]
        down_places = [down_place(seq_count, down_width, steps) for steps in range(seq_count)]
    else:
        sample_rows = lookup_rows(adapter_bank_row, document_adapter)
        got_down = lax.all_to_all(
            down_bank[sample_rows], "batch", split_axis=0, concat_axis=0, tiled=True
        )
        got_up = lax.all_to_all(
            adapter_up_weight[sample_rows], "batch", split_axis=0, concat_axis=0, tiled=True
        )
        down_block = jnp.transpose(got_down, (1, 2, 0, 3)).reshape(SEGS * joint_rank, -1)
        up_block = jnp.transpose(got_up, (1, 2, 0, 3)).reshape(SEGS * low_width, -1)
        all_down = lax.all_gather(down_block, "seq", axis=0)
        all_up = lax.all_gather(up_block, "seq", axis=0)
        first = (seq_index >= half_count).astype(jnp.int32)
        merged = jnp.transpose(all_down, (1, 0, 2)).reshape(SEGS * joint_rank, -1)
        down_parts = [lax.dynamic_slice_in_dim(merged, first * joint_rank, 2 * joint_rank)]
        down_places = [whole_place]
        up_rows = jnp.transpose(all_up, (1, 0, 2)).reshape(SEGS, low_width, -1)
        is_query = jnp.arange(up_rows.shape[2]) < query_columns
        up_blocks = jnp.concatenate(
            [
                jnp.where(is_query[None, None, :], up_rows, 0),
                jnp.where(is_query[None, None, :], 0, up_rows),
            ],
            axis=1,
        )
        column_blocks = [
            lax.dynamic_slice_in_dim(
                local_tokens,
                jnp.remainder(seq_index + steps, seq_count) * down_width,
                down_width,
                axis=1,
            )
            for steps in range(seq_count)
        ]

    positions = seq_index * rows + jnp.arange(rows, dtype=jnp.int32)
    inside = positions - jnp.where(
        positions >= second_end, second_end, jnp.where(positions >= first_end, first_end, 0)
    )
    exponent = jnp.arange(HEAD_WIDTH // 2, dtype=f32) * (2.0 / HEAD_WIDTH)
    inverse = jnp.power(jnp.float32(rope_base), -exponent)
    angles = inside.astype(f32)[:, None] * jnp.concatenate([inverse, inverse])[None, :]
    signs = jnp.where(jnp.arange(HEAD_WIDTH) < HEAD_WIDTH // 2, -1.0, 1.0).astype(f32)
    cosines = jnp.cos(angles)
    sines = jnp.sin(angles) * signs[None, :]

    sample_rows = lookup_rows(adapter_bank_row, document_adapter)
    down_zeros = jnp.zeros((adapters, joint_rank, 1, held_down), f32)
    up_zeros = jnp.zeros((adapters, low_width, held_up), f32)
    early = [down_zeros, up_zeros, cosines, sines]
    up_shape = jax.ShapeDtypeStruct((SEGS, joint_rank, query_columns + HEAD_WIDTH), bf16)
    arrived = [pltpu.VMEM((seq_count, low_width // 2, down_width), bf16)] if direct else []
    weight_bytes = 2 * width * (features + 2 * joint_rank)
    part, frozen, down, *built = pl.pallas_call(
        functools.partial(project_kernel, places, down_places, len(early), seq_count),
        out_shape=[
            jax.ShapeDtypeStruct((rows, features + 128), f32),
            jax.ShapeDtypeStruct((features, width), bf16),
            jax.ShapeDtypeStruct((2 * joint_rank, width), bf16),
        ]
        + ([up_shape] if direct else []),
        in_specs=[in_smem(), in_vmem()]
        + [in_place()] * (len(pieces) + len(down_parts) + len(early)),
        out_specs=[in_vmem()] * (4 if direct else 3),
        scratch_shapes=arrived
        + [pltpu.SemaphoreType.DMA((len(pieces) + 2 * len(down_parts),))],
        compiler_params=pltpu.CompilerParams(vmem_limit_bytes=12 * mebibyte),
        cost_estimate=cost(
            2 * rows * width * (features + 2 * joint_rank), weight_bytes + 2 * rows * width
        ),
        name="project",
    )(document_lengths, local_tokens, *pieces, *down_parts, *early)
    if direct:
        up_blocks = built[0]

    column_parts = [
        shift(block, "seq", steps) if steps else block
        for steps, block in enumerate(column_blocks)
    ]

    other_part = shift(part, "tp", 1)
    queries, pairs, low_rank = pl.pallas_call(
        qkv_kernel,
        out_shape=(
            jax.ShapeDtypeStruct((QHEADS * own_rows, HEAD_WIDTH), bf16),
            jax.ShapeDtypeStruct((rows, 2 * HEAD_WIDTH), bf16),
            jax.ShapeDtypeStruct((rows, joint_rank), bf16),
        ),
        in_specs=[in_smem()] + [in_vmem()] * 5,
        out_specs=(in_vmem(),) * 3,
        compiler_params=pltpu.CompilerParams(vmem_limit_bytes=8 * mebibyte),
        cost_estimate=cost(2 * rows * 3 * 64 * 640, 8 * rows * features),
        name="qkv",
    )(document_lengths, part, other_part, up_blocks, cosines, sines)

    blocks = [pairs] + [push(pairs, "seq", back) for back in range(1, half_count + 1)]
    block_count = len(blocks)
    incoming = output_gradient[0]
    early_columns = [column_parts[1], column_parts[-1]]
    attention, query_grad, kept, sent = pl.pallas_call(
        functools.partial(attention_kernel, block_count, len(early_columns)),
        out_shape=(
            jax.ShapeDtypeStruct((own_rows, query_columns), bf16),
            jax.ShapeDtypeStruct((own_rows, query_columns), bf16),
            jax.ShapeDtypeStruct((block_count, own_rows, 2 * HEAD_WIDTH), f32),
            jax.ShapeDtypeStruct((block_count, own_rows, 2 * HEAD_WIDTH), f32),
        ),
        in_specs=[in_smem()]
        + [in_vmem()] * (4 + block_count)
        + [in_place()] * len(early_columns),
        out_specs=(in_vmem(),) * 4,
        scratch_shapes=[pltpu.VMEM((block_count, QHEADS * own_rows, rows), bf16)],
        compiler_params=pltpu.CompilerParams(vmem_limit_bytes=(4 + 4 * block_count) * mebibyte),
        cost_estimate=cost(
            10 * block_count * QHEADS * own_rows * rows * HEAD_WIDTH,
            4 * rows * features,
            block_count * QHEADS * own_rows * rows,
        ),
        name="attention",
    )(document_lengths, queries, incoming, cosines, sines, *blocks, *early_columns)

    other_query = shift(query_grad, "tp", 1)
    pair_sums = kept + shift(sent, "tp", 1)
    own_sum = pair_sums[0]
    for back in range(1, block_count):
        own_sum = own_sum + push(pair_sums[back], "seq", -back)
    own_place = tp_index * own_rows
    own_cosines = lax.dynamic_slice_in_dim(cosines, own_place, own_rows)
    own_sines = lax.dynamic_slice_in_dim(sines, own_place, own_rows)
    key_grad = own_sum[:, :HEAD_WIDTH]
    key_grad = key_grad * own_cosines - jnp.roll(key_grad, HEAD_WIDTH // 2, axis=1) * own_sines
    pair_grad = jnp.concatenate([key_grad, own_sum[:, HEAD_WIDTH:]], axis=1).astype(bf16)
    other_pair = shift(pair_grad, "tp", 1)

    gradients, rank_grad, *up_split = pl.pallas_call(
        functools.partial(rank_kernel, 0, seq_count),
        out_shape=[
            jax.ShapeDtypeStruct((rows, features), bf16),
            jax.ShapeDtypeStruct((rows, joint_rank), bf16),
        ]
        + [jax.ShapeDtypeStruct((SEGS * low_width, held_up * batch_count), f32)] * seq_count,
        in_specs=[in_smem()] + [in_vmem()] * 6,
        out_specs=[in_vmem()] * (2 + seq_count),
        scratch_shapes=[
            pltpu.VMEM((SEGS * low_width, features - HEAD_WIDTH), f32),
            pltpu.VMEM((seq_count, SEGS * low_width, held_up * batch_count), f32),
        ],
        compiler_params=pltpu.CompilerParams(vmem_limit_bytes=8 * mebibyte),
        cost_estimate=cost(4 * rows * 3 * 64 * 640, 4 * rows * features),
        name="rank_gradients",
    )(
        document_lengths, query_grad, other_query, pair_grad, other_pair, low_rank, up_blocks
    )

    rank_parts = [rank_grad] + [shift(rank_grad, "seq", steps) for steps in range(1, seq_count)]
    up_sums = [
        shift(block, "seq", steps) if steps else block for steps, block in enumerate(up_split)
    ]

    token_grad = pl.pallas_call(
        functools.partial(token_kernel, seq_count),
        out_shape=jax.ShapeDtypeStruct((rows, width), bf16),
        in_specs=[in_smem()] + [in_vmem()] * 4,
        out_specs=in_vmem(),
        compiler_params=pltpu.CompilerParams(vmem_limit_bytes=8 * mebibyte),
        cost_estimate=cost(
            2 * rows * width * (features + 2 * joint_rank), weight_bytes + 2 * rows * width
        ),
        name="token_gradient",
    )(document_lengths, gradients, rank_grad, frozen, down)

    if batch_count == 2:
        term_shapes = [(SEGS * joint_rank, held_down)] * 2 + [(SEGS * low_width, held_up)] * 2
    else:
        term_shapes = [(SEGS * joint_rank, down_width), (SEGS * low_width, held_up * batch_count)]
    terms = pl.pallas_call(
        functools.partial(down_kernel, seq_count),
        out_shape=[jax.ShapeDtypeStruct(shape, f32) for shape in term_shapes],
        in_specs=[in_smem()] + [in_vmem()] * (3 * seq_count),
        out_specs=[in_vmem()] * len(term_shapes),
        compiler_params=pltpu.CompilerParams(vmem_limit_bytes=8 * mebibyte),
        cost_estimate=cost(
            2 * seq_count * rows * SEGS * joint_rank * down_width, 2 * seq_count * rows * down_width
        ),
        name="down_terms",
    )(document_lengths, *rank_parts, *column_parts, *up_sums)

    if batch_count == 2:
        bank_downs = [terms[0], shift(terms[1], "batch", 1)]
        bank_ups = [terms[2], shift(terms[3], "batch", 1)]
        sample_rows = jnp.where(batch_index == 0, sample_rows, sample_rows[::-1])
    else:
        down_send = jnp.transpose(
            terms[0].reshape(SEGS * joint_rank, batch_count, held_down), (1, 0, 2)
        )
        up_send = jnp.transpose(
            terms[1].reshape(SEGS * low_width, batch_count, held_up), (1, 0, 2)
        )
        back_down = lax.all_to_all(down_send, "batch", split_axis=0, concat_axis=0, tiled=True)
        back_up = lax.all_to_all(up_send, "batch", split_axis=0, concat_axis=0, tiled=True)
        bank_downs = [back_down[batch] for batch in range(batch_count)]
        bank_ups = [back_up[batch] for batch in range(batch_count)]

    bank_rows = sample_rows.reshape(-1)

    def whole(array):
        return pl.BlockSpec(array.shape, lambda step, bank: (0,) * array.ndim)

    down_grad, up_grad = pl.pallas_call(
        functools.partial(bank_kernel, batch_count),
        out_shape=(
            jax.ShapeDtypeStruct(down_zeros.shape, f32),
            jax.ShapeDtypeStruct(up_zeros.shape, f32),
        ),
        grid_spec=pltpu.PrefetchScalarGridSpec(
            num_scalar_prefetch=1,
            grid=(batch_count * SEGS,),
            in_specs=[whole(array) for array in bank_downs + bank_ups] + [in_place()] * 2,
            out_specs=(
                pl.BlockSpec(
                    (1, joint_rank, 1, held_down),
                    lambda step, bank: (bank[step], 0, 0, 0),
                ),
                pl.BlockSpec(
                    (1, low_width, held_up),
                    lambda step, bank: (bank[step], 0, 0),
                ),
            ),
        ),
        input_output_aliases={1 + 2 * batch_count: 0, 2 + 2 * batch_count: 1},
        compiler_params=pltpu.CompilerParams(vmem_limit_bytes=16 * mebibyte),
        name="bank_rows",
    )(
        bank_rows,
        *bank_downs,
        *bank_ups,
        down_zeros,
        up_zeros,
    )
    return (attention[None], token_grad[None], down_grad, up_grad)


def solution(mesh):
    in_specs = (
        P(("groups", "batch"), "seq", "tp"),
        P("seq", "tp"),
        P(None, None, "tp", ("seq", "batch")),
        P(None, None, ("seq", "batch")),
        P(),
        P("groups", None),
        P("groups", None),
        P(("groups", "batch"), ("seq", "tp"), None),
    )
    out_specs = (
        P(("groups", "batch"), ("seq", "tp"), None),
        P(("groups", "batch"), "seq", "tp"),
        P("groups", None, "tp", ("seq", "batch")),
        P("groups", None, ("seq", "batch")),
    )
    return jax.shard_map(shards, mesh=mesh, in_specs=in_specs, out_specs=out_specs, check_vma=False)
```

```python
import functools

import jax
import jax.numpy as jnp
from jax import lax
from jax.experimental import pallas as pl
from jax.experimental.pallas import tpu as pltpu
from jax.sharding import PartitionSpec as P

QHEADS = 4
HEAD_WIDTH = 128
ADAPTER_RANK = 32
SEGS = 3

adapter_scale = 2.0
rope_base = 5000000.0
masked_score = -1e30
mebibyte = 1024 * 1024


def shift(value, axis, steps):
    count = lax.axis_size(axis)
    return lax.ppermute(value, axis, [(at, (at + steps) % count) for at in range(count)])


def push(value, axis, steps):
    count = lax.axis_size(axis)
    pairs = [(at, at + steps) for at in range(count) if 0 <= at + steps < count]
    return lax.ppermute(value, axis, pairs)


def dot_nt(left, right):
    return lax.dot_general(
        left, right, (((1,), (1,)), ((), ())), preferred_element_type=jnp.float32
    )


def dot_nn(left, right):
    return jnp.dot(left, right, preferred_element_type=jnp.float32)


def dot_tn(left, right):
    return lax.dot_general(
        left, right, (((0,), (0,)), ((), ())), preferred_element_type=jnp.float32
    )


def lookup_rows(adapter_bank_row, document_adapter):
    matches = document_adapter[..., None] == jnp.arange(adapter_bank_row.shape[0], dtype=jnp.int32)
    return jnp.sum(jnp.where(matches, adapter_bank_row, 0), axis=-1)


def row_positions(first, count):
    return first + lax.broadcasted_iota(jnp.int32, (count, 1), 0)


def ring_index(index, count):
    return lax.rem(index + count, count)


def kernel_marks(lengths):
    batch = lax.axis_index("batch")
    first_end = lengths[batch, 0]
    return first_end, first_end + lengths[batch, 1]


def row_segments(ends, positions):
    return (positions >= ends[0]).astype(jnp.int32) + (positions >= ends[1]).astype(jnp.int32)


def cost(flops, bytes_accessed, transcendentals=0):
    return pl.CostEstimate(
        flops=flops, bytes_accessed=bytes_accessed, transcendentals=transcendentals
    )


def in_vmem():
    return pl.BlockSpec(memory_space=pltpu.VMEM)


def in_smem():
    return pl.BlockSpec(memory_space=pltpu.SMEM)


def by_block(shape):
    return pl.BlockSpec(shape, lambda: (0,) * len(shape))


def in_place():
    return pl.BlockSpec(memory_space=pl.ANY)


def fetch(piece, target, place, semaphore):
    height, width = piece.shape
    row, column = place()
    copy = pltpu.make_async_copy(
        piece,
        target.at[
            pl.ds(pl.multiple_of(row, 16), height), pl.ds(pl.multiple_of(column, 128), width)
        ],
        semaphore,
    )
    copy.start()
    return copy


def frozen_place(seq_count, rows, share, behind, batch_step, group_step):
    def place():
        holder = ring_index(lax.axis_index("seq") - behind, seq_count)
        if share is None:
            return holder * rows, 0
        batch = lax.rem(lax.axis_index("batch") + batch_step, 2)
        group = lax.rem(lax.axis_index("groups") + group_step, 2)
        return holder * rows, (group * 2 + batch) * share

    return place


def down_place(seq_count, features, width, behind):
    def place():
        return features, ring_index(lax.axis_index("seq") - behind, seq_count) * width

    return place


def whole_place(row):
    def place():
        return row, 0

    return place


def select_kernel(bank_row, adapters, frozen, down_bank, up_bank, *refs):
    share, outputs, rows, semaphore = refs[0], refs[1:5], refs[5], refs[6]
    batch = lax.axis_index("batch")
    width = share.shape[1]
    place = (lax.axis_index("groups") * 2 + batch) * width
    copies = [
        pltpu.make_async_copy(
            frozen.at[:, pl.ds(pl.multiple_of(place, 128), width)], share, semaphore.at[0]
        )
    ]
    copies[0].start()
    for which, sample in enumerate((batch, 1 - batch)):
        for document in range(SEGS):
            row = bank_row[adapters[sample, document]]
            rows[which * SEGS + document] = row
            for source, target in ((down_bank, outputs[which]), (up_bank, outputs[2 + which])):
                copy = pltpu.make_async_copy(
                    source.at[row], target.at[document], semaphore.at[len(copies)]
                )
                copy.start()
                copies.append(copy)
    for copy in copies:
        copy.wait()


def pack_kernel(unused, seq_count, own_down, far_down, own_up, far_up, tokens, *refs):
    refs = refs[unused:]
    payloads, columns = refs[:seq_count], refs[seq_count : 2 * seq_count]
    down, up = refs[2 * seq_count :]
    ahead = lax.axis_index("batch") == 0
    joint_rank, held = own_down.shape[1:]
    low_width, held_up = own_up.shape[1:]
    for document in range(SEGS):
        rows = slice(document * joint_rank, (document + 1) * joint_rank)
        down[rows, :held] = jnp.where(ahead, own_down[document], far_down[document])
        down[rows, held:] = jnp.where(ahead, far_down[document], own_down[document])
        up[document, :, :held_up] = jnp.where(ahead, own_up[document], far_up[document])
        up[document, :, held_up:] = jnp.where(ahead, far_up[document], own_up[document])
    half, slot = low_width // 2, down.shape[1] // 4
    for steps in range(seq_count):
        target = ring_index(lax.axis_index("seq") + steps - seq_count, seq_count)
        first = (target >= seq_count // 2).astype(jnp.int32)
        start = pl.multiple_of(first * joint_rank, joint_rank)
        payload = payloads[steps]
        payload[: 2 * joint_rank] = down[pl.ds(start, 2 * joint_rank)]
        for index in range(2):
            block = up[first + index]
            for part in range(2):
                column = (2 * index + part) * slot
                payload[2 * joint_rank :, column : column + 2 * held_up] = block[
                    part * half : (part + 1) * half
                ]
        width = columns[steps].shape[1]
        columns[steps][...] = tokens[:, pl.ds(pl.multiple_of(target * width, 128), width)]


def assemble_up(seq_count, arrived, up_blocks):
    low_width = up_blocks.shape[1] // 2
    query_columns = QHEADS * HEAD_WIDTH
    seq_index = lax.axis_index("seq")
    first = (seq_index >= seq_count // 2).astype(jnp.int32)
    held = up_blocks.shape[2] // seq_count
    half, slot = low_width // 2, arrived.shape[2] // 4
    up_blocks[...] = jnp.zeros_like(up_blocks)
    for holder in range(seq_count):
        block = arrived[ring_index(seq_index - holder, seq_count)]
        start, stop = holder * held, (holder + 1) * held
        middle = min(max(query_columns, start), stop)
        for index in range(2):
            for part in range(2):
                offset = (2 * index + part) * slot
                if middle > start:
                    up_blocks[first + index, part * half : (part + 1) * half, start:middle] = block[
                        :, offset : offset + middle - start
                    ]
                if stop > middle:
                    low = low_width + part * half
                    up_blocks[first + index, low : low + half, middle:stop] = block[
                        :, offset + middle - start : offset + held
                    ]


def project_kernel(frozen_places, down_places, unused, seq_count, tokens, *refs):
    frozen_count, down_count = len(frozen_places), len(down_places)
    frozen_pieces = refs[:frozen_count]
    down_pieces = refs[frozen_count : frozen_count + down_count]
    refs = refs[frozen_count + down_count + unused :]
    packed = down_count > 1
    part, matrix = refs[:2]
    weights, semaphore = refs[-2:]
    features = part.shape[1] - 2 * ADAPTER_RANK * 2
    copies = []
    for piece, place in zip(frozen_pieces, frozen_places):
        copies.append(fetch(piece, weights, place, semaphore.at[len(copies)]))
    joint_rank = 2 * ADAPTER_RANK
    for number, (piece, place) in enumerate(zip(down_pieces, down_places)):
        rows = piece.at[pl.ds(0, 2 * joint_rank)] if packed else piece
        copies.append(fetch(rows, weights, place, semaphore.at[len(copies)]))
        if packed:
            extra = piece.shape[0] - 2 * joint_rank
            copy = pltpu.make_async_copy(
                piece.at[pl.ds(2 * joint_rank, extra)],
                refs[3].at[number],
                semaphore.at[len(copies)],
            )
            copy.start()
            copies.append(copy)
    for copy in copies:
        copy.wait()
    keep = pltpu.make_async_copy(weights, matrix, semaphore.at[len(copies)])
    keep.start()
    part[...] = dot_nt(tokens[...], weights[...])
    if packed:
        assemble_up(seq_count, refs[3], refs[2])
    keep.wait()


def rotated(values, cosines, sines):
    return values * cosines + pltpu.roll(values, values.shape[1] // 2, 1) * sines


def qkv_kernel(seq_count, lengths, mine, theirs, up_blocks, cosines, sines, queries, pairs, low_rank):
    rows = mine.shape[0]
    own_rows = queries.shape[0] // QHEADS
    query_columns = QHEADS * HEAD_WIDTH
    value_start = query_columns + HEAD_WIDTH
    features = value_start + HEAD_WIDTH
    joint_rank = low_rank.shape[1]
    middle = features + joint_rank
    ends = kernel_marks(lengths)

    def low_rows(picked, second):
        first_low = mine[picked, features:middle] + theirs[picked, features:middle]
        second_low = mine[picked, middle:] + theirs[picked, middle:]
        return jnp.where(second, second_low, first_low).astype(jnp.bfloat16)

    first = (lax.axis_index("seq") >= seq_count // 2).astype(jnp.int32)
    first_row = lax.axis_index("seq") * rows
    segments = row_segments(ends, row_positions(first_row, rows))
    low = low_rows(slice(None), segments != first)
    low_rank[...] = low
    value_delta = jnp.zeros((rows, HEAD_WIDTH), jnp.float32)
    for document in range(SEGS):
        chosen = jnp.where(segments == document, low, jnp.zeros_like(low))
        value_delta += dot_nn(chosen, up_blocks[document, :, query_columns:])
    keys = mine[:, query_columns:value_start] + theirs[:, query_columns:value_start]
    pairs[:, :HEAD_WIDTH] = rotated(keys, cosines[...], sines[...]).astype(jnp.bfloat16)
    values = mine[:, value_start:features] + theirs[:, value_start:features]
    pairs[:, HEAD_WIDTH:] = (values + adapter_scale * value_delta).astype(jnp.bfloat16)
    start = pl.multiple_of(lax.axis_index("tp") * own_rows, own_rows)
    own = pl.ds(start, own_rows)
    own_segments = row_segments(ends, row_positions(first_row + start, own_rows))
    own_low = low_rows(own, own_segments != first)
    query_delta = jnp.zeros((own_rows, query_columns), jnp.float32)
    for document in range(SEGS):
        chosen = jnp.where(own_segments == document, own_low, jnp.zeros_like(own_low))
        query_delta += dot_nn(chosen, up_blocks[document, :, :query_columns])
    projected = mine[own, :query_columns] + theirs[own, :query_columns]
    projected = projected + adapter_scale * query_delta
    for head in range(QHEADS):
        turned = rotated(
            projected[:, head * HEAD_WIDTH : (head + 1) * HEAD_WIDTH], cosines[own], sines[own]
        )
        queries[head * own_rows : (head + 1) * own_rows] = turned.astype(jnp.bfloat16)


def attention_kernel(block_count, unused, lengths, queries, incoming, cosines, sines, *refs):
    blocks = refs[:block_count]
    output, query_grad, kept, sent, down_zeros, up_zeros = refs[block_count + unused : -4]
    low_probs, down_blank, up_blank, semaphore = refs[-4:]
    down_blank[...] = jnp.zeros_like(down_blank)
    up_blank[...] = jnp.zeros_like(up_blank)
    copies = []
    for blank, zeros in ((down_blank, down_zeros), (up_blank, up_zeros)):
        step = blank.shape[0]
        for start in range(0, zeros.shape[0], step):
            copy = pltpu.make_async_copy(
                blank, zeros.at[pl.ds(start, step)], semaphore.at[len(copies)]
            )
            copy.start()
            copies.append(copy)
    own_rows, query_columns = incoming.shape
    rows = blocks[0].shape[0]
    score_scale = HEAD_WIDTH ** (-0.5)
    ends = kernel_marks(lengths)
    seq_index, tp_index = lax.axis_index("seq"), lax.axis_index("tp")
    positions = row_positions(seq_index * rows + tp_index * own_rows, own_rows)
    positions = jnp.concatenate([positions] * QHEADS, axis=0)
    segments = row_segments(ends, positions)
    starts = jnp.where(segments == 0, 0, jnp.where(segments == 1, ends[0], ends[1]))
    scores = []
    for back, block in enumerate(blocks):
        key_positions = (seq_index - back) * rows + lax.broadcasted_iota(jnp.int32, (1, rows), 1)
        allowed = (key_positions <= positions) & (key_positions >= starts)
        block_scores = dot_nt(queries[...], block[:, :HEAD_WIDTH]) * score_scale
        scores.append(jnp.where(allowed, block_scores, masked_score))
    row_max = functools.reduce(
        jnp.maximum, [jnp.max(part, axis=1, keepdims=True) for part in scores]
    )
    raised = [jnp.exp(part - row_max) for part in scores]
    row_total = sum(jnp.sum(part, axis=1, keepdims=True) for part in raised)
    inverse = 1.0 / row_total
    probs = [part * inverse for part in raised]
    weighted = jnp.zeros((QHEADS * own_rows, HEAD_WIDTH), jnp.float32)
    for back, block in enumerate(blocks):
        low_probs[back] = probs[back].astype(jnp.bfloat16)
        weighted += dot_nn(low_probs[back], block[:, HEAD_WIDTH:])
    attended = weighted.astype(jnp.bfloat16)
    gradients = jnp.concatenate(
        [incoming[:, head * HEAD_WIDTH : (head + 1) * HEAD_WIDTH] for head in range(QHEADS)],
        axis=0,
    )
    row_delta = jnp.sum(
        gradients.astype(jnp.float32) * attended.astype(jnp.float32), axis=1, keepdims=True
    )
    start = pl.multiple_of(tp_index * own_rows, own_rows)
    total = jnp.zeros((QHEADS * own_rows, HEAD_WIDTH), jnp.float32)
    for back, block in enumerate(blocks):
        prob_grad = dot_nt(gradients, block[:, HEAD_WIDTH:])
        score_grad = (probs[back] * (prob_grad - row_delta)).astype(jnp.bfloat16)
        total += dot_nn(score_grad, block[:, :HEAD_WIDTH])
        key_part = dot_tn(score_grad, queries[...]) * score_scale
        value_part = dot_tn(low_probs[back], gradients)
        mine = tp_index == 0
        kept[back, :, :HEAD_WIDTH] = jnp.where(mine, key_part[:own_rows], key_part[own_rows:])
        sent[back, :, :HEAD_WIDTH] = jnp.where(mine, key_part[own_rows:], key_part[:own_rows])
        kept[back, :, HEAD_WIDTH:] = jnp.where(mine, value_part[:own_rows], value_part[own_rows:])
        sent[back, :, HEAD_WIDTH:] = jnp.where(mine, value_part[own_rows:], value_part[:own_rows])
    own = pl.ds(start, own_rows)
    for head in range(QHEADS):
        picked = slice(head * own_rows, (head + 1) * own_rows)
        columns = slice(head * HEAD_WIDTH, (head + 1) * HEAD_WIDTH)
        output[:, columns] = attended[picked]
        query_grad[:, columns] = rotated(
            total[picked] * score_scale, cosines[own], -sines[own]
        ).astype(jnp.bfloat16)
    for copy in copies:
        copy.wait()


def sum_kernel(kept, arrived, *sums):
    for back, total in enumerate(sums):
        total[...] = kept[back] + arrived[back]


def pair_kernel(terms, cosines, sines, *refs):
    parts, pair = refs[:terms], refs[-2]
    own_rows = pair.shape[0]
    total = sum(part[...] for part in parts)
    own = pl.ds(pl.multiple_of(lax.axis_index("tp") * own_rows, own_rows), own_rows)
    keys = rotated(total[:, :HEAD_WIDTH], cosines[own], -sines[own])
    pair[:, :HEAD_WIDTH] = keys.astype(jnp.bfloat16)
    pair[:, HEAD_WIDTH:] = total[:, HEAD_WIDTH:].astype(jnp.bfloat16)


def rank_kernel(
    seq_count, lengths, own_query, other_query, own_pair, other_pair, low_rank, up_blocks, *refs
):
    gradients, rank_grad = refs[:2]
    split_terms, (terms, blocks) = refs[2:-2], refs[-2:]
    own_rows, query_columns = own_query.shape
    rows = low_rank.shape[0]
    seq_index = lax.axis_index("seq")
    start = pl.multiple_of(lax.axis_index("tp") * own_rows, own_rows)
    other = pl.multiple_of(own_rows - start, own_rows)
    gradients[pl.ds(start, own_rows), :query_columns] = own_query[...]
    gradients[pl.ds(other, own_rows), :query_columns] = other_query[...]
    value_start = query_columns + HEAD_WIDTH
    features = value_start + HEAD_WIDTH
    gradients[pl.ds(start, own_rows), query_columns:features] = own_pair[...]
    gradients[pl.ds(other, own_rows), query_columns:features] = other_pair[...]
    query_grad = gradients[:, :query_columns]
    value_grad = gradients[:, value_start:features]
    low = low_rank[...]
    rank = low.shape[1] // 2
    segments = row_segments(kernel_marks(lengths), row_positions(seq_index * rows, rows))
    total = jnp.zeros((rows, low.shape[1]), jnp.float32)
    for document in range(SEGS):
        member = segments == document
        parts = dot_nt(query_grad, up_blocks[document, :, :query_columns])
        parts += dot_nt(value_grad, up_blocks[document, :, query_columns:])
        total = jnp.where(member, parts, total)
        chosen = jnp.where(member, low, jnp.zeros_like(low))
        query_terms = dot_tn(chosen, query_grad)
        value_terms = dot_tn(chosen, value_grad)
        place = slice(document * rank, (document + 1) * rank)
        terms[place, :query_columns] = adapter_scale * query_terms[:rank]
        terms[place, query_columns:] = adapter_scale * value_terms[rank:]
    turned = (adapter_scale * total).astype(jnp.bfloat16)
    rank_grad[...] = turned
    second = segments != (seq_index >= seq_count // 2).astype(jnp.int32)
    nothing = jnp.zeros_like(turned)
    middle = features + low.shape[1]
    gradients[:, features:middle] = jnp.where(second, nothing, turned)
    gradients[:, middle:] = jnp.where(second, turned, nothing)
    held = blocks.shape[2]
    for holder in range(seq_count):
        blocks[holder] = terms[:, holder * held : (holder + 1) * held]
    for steps, block in enumerate(split_terms):
        block[...] = blocks[ring_index(seq_index + steps - seq_count, seq_count)]


def token_kernel(gradients, matrix, token_grad):
    token_grad[...] = dot_nn(gradients[...], matrix[...]).astype(jnp.bfloat16)


def split_halves(terms, own, far):
    held = own.shape[1]
    left, right = terms[:, :held], terms[:, held:]
    ahead = lax.axis_index("batch") == 0
    own[...] = jnp.where(ahead, left, right)
    far[...] = jnp.where(ahead, right, left)


def down_kernel(block_count, lengths, *refs):
    ranks = refs[:block_count]
    columns = refs[block_count : 2 * block_count]
    up_parts = refs[2 * block_count : 3 * block_count]
    outputs = refs[3 * block_count :]
    rows, joint_rank = ranks[0].shape
    ends = kernel_marks(lengths)
    all_terms = []
    for document in range(SEGS):
        total = jnp.zeros((joint_rank, columns[0].shape[1]), jnp.float32)
        for behind in range(block_count):
            holder = ring_index(lax.axis_index("seq") - behind, block_count)
            segments = row_segments(ends, row_positions(holder * rows, rows))
            low = ranks[behind][...]
            chosen = jnp.where(segments == document, low, jnp.zeros_like(low))
            total += dot_tn(chosen, columns[behind][...])
        all_terms.append(total)
    down_terms = jnp.concatenate(all_terms, axis=0)
    up_terms = sum(part[...] for part in up_parts)
    if len(outputs) == 2:
        outputs[0][...] = down_terms
        outputs[1][...] = up_terms
    else:
        split_halves(down_terms, *outputs[:2])
        split_halves(up_terms, *outputs[2:])


def bank_kernel(block_count, bank_rows, *refs):
    down_terms = refs[:block_count]
    up_terms = refs[block_count : 2 * block_count]
    down_out, up_out = refs[2 * block_count + 2 :]
    step = pl.program_id(0)
    row = bank_rows[step]
    joint_rank = down_out.shape[1]
    low_width = up_out.shape[1]
    down_total = jnp.zeros((joint_rank, down_out.shape[3]), jnp.float32)
    up_total = jnp.zeros((low_width, up_out.shape[2]), jnp.float32)
    for block in range(block_count):
        for document in range(SEGS):
            same = bank_rows[block * SEGS + document] == row
            down_rows = down_terms[block][document * joint_rank : (document + 1) * joint_rank]
            up_rows = up_terms[block][document * low_width : (document + 1) * low_width]
            down_total += jnp.where(same, down_rows, 0.0)
            up_total += jnp.where(same, up_rows, 0.0)
    down_out[0, :, 0, :] = down_total
    up_out[0] = up_total


def shards(
    tokens,
    frozen_qkv_matrix,
    adapter_down_weight,
    adapter_up_weight,
    adapter_bank_row,
    document_lengths,
    document_adapter,
    output_gradient,
):
    seq_count = lax.axis_size("seq")
    batch_count = lax.axis_size("batch")
    group_count = lax.axis_size("groups")
    chip_size = lax.axis_size("tp")
    seq_index = lax.axis_index("seq")
    batch_index = lax.axis_index("batch")
    group_index = lax.axis_index("groups")
    tp_index = lax.axis_index("tp")
    local_tokens = tokens[0]
    rows, width = local_tokens.shape
    own_rows = rows // chip_size
    query_columns = QHEADS * HEAD_WIDTH
    frozen_rows = frozen_qkv_matrix.shape[0]
    features = frozen_rows * seq_count
    low_width = ADAPTER_RANK
    joint_rank = adapter_down_weight.shape[1]
    adapters = adapter_bank_row.shape[0]
    bf16 = jnp.bfloat16
    f32 = jnp.float32

    lengths = lax.dynamic_index_in_dim(document_lengths, batch_index, 0, keepdims=False)
    first_end = lengths[0]
    second_end = first_end + lengths[1]
    half_count = seq_count // 2

    down_bank = adapter_down_weight[:, :, 0, :]
    plane_count = group_count * batch_count
    share = width // plane_count
    pieces, places = [], []
    held_down = adapter_down_weight.shape[3]
    held_up = adapter_up_weight.shape[2]
    down_width = held_down * batch_count
    direct = (
        group_count == 2
        and batch_count == 2
        and share % 128 == 0
        and down_width % 128 == 0
        and frozen_rows % 16 == 0
        and 4 * 2 * held_up <= down_width
    )
    if direct:
        row_shapes = [(frozen_rows, share)]
        row_shapes += [(SEGS, joint_rank, held_down)] * 2 + [(SEGS, low_width, held_up)] * 2
        own_share, own_down, far_down, own_up, far_up, bank_rows = pl.pallas_call(
            select_kernel,
            out_shape=[jax.ShapeDtypeStruct(shape, bf16) for shape in row_shapes]
            + [jax.ShapeDtypeStruct((2 * SEGS,), jnp.int32)],
            in_specs=[in_smem()] * 2 + [in_place()] * 3,
            out_specs=[in_place()] * 5 + [in_smem()],
            scratch_shapes=[pltpu.SemaphoreType.DMA((1 + 4 * SEGS,))],
            cost_estimate=cost(0, 4 * SEGS * joint_rank * held_down * 2),
            name="select",
        )(adapter_bank_row, document_adapter, frozen_qkv_matrix, down_bank, adapter_up_weight)
        pieces.append(frozen_qkv_matrix)
        places.append(frozen_place(seq_count, frozen_rows, None, 0, 0, 0))
        before = shift(own_share, "seq", 1)
        after = shift(own_share, "seq", seq_count - 1)
        arrivals = [(1, before), (seq_count - 1, after)]
        for steps in range(2, seq_count - 1):
            before = shift(before, "seq", 1)
            arrivals.append((steps, before))
        for steps, here in arrivals:
            if steps < seq_count - 1:
                over_batch = shift(here, "batch", 1)
                over_groups = shift(here, "groups", 1)
                over_both = shift(over_batch, "groups", 1)
            else:
                over_groups = shift(here, "groups", 1)
                over_batch = shift(here, "batch", 1)
                over_both = shift(over_groups, "batch", 1)
            for value, batch_step, group_step in (
                (here, 0, 0),
                (over_batch, 1, 0),
                (over_groups, 0, 1),
                (over_both, 1, 1),
            ):
                pieces.append(value)
                places.append(
                    frozen_place(seq_count, frozen_rows, share, steps, batch_step, group_step)
                )
    else:
        pieces.append(lax.all_gather(frozen_qkv_matrix, "seq", axis=0, tiled=True))
        places.append(whole_place(0))

    column_blocks, up_blocks = None, None
    if direct:
        far_down = shift(far_down, "batch", 1)
        far_up = shift(far_up, "batch", 1)
        payload_rows = 2 * joint_rank + low_width // 2
        packed = pl.pallas_call(
            functools.partial(pack_kernel, 1, seq_count),
            out_shape=[jax.ShapeDtypeStruct((payload_rows, down_width), bf16)] * seq_count
            + [jax.ShapeDtypeStruct((rows, down_width), bf16)] * seq_count,
            in_specs=[in_vmem()] * 5 + [in_place()],
            out_specs=[by_block((payload_rows, down_width))] * seq_count
            + [by_block((rows, down_width))] * seq_count,
            scratch_shapes=[
                pltpu.VMEM((SEGS * joint_rank, down_width), bf16),
                pltpu.VMEM((SEGS, low_width, 2 * held_up), bf16),
            ],
            compiler_params=pltpu.CompilerParams(vmem_limit_bytes=16 * mebibyte),
            cost_estimate=cost(0, 4 * rows * width),
            name="pack",
        )(own_down, far_down, own_up, far_up, local_tokens, before)
        column_blocks = packed[seq_count:]
        down_parts = [
            shift(part, "seq", steps) if steps else part
            for steps, part in enumerate(packed[:seq_count])
        ]
        down_places = [down_place(seq_count, features, down_width, steps) for steps in range(seq_count)]
    else:
        sample_rows = lookup_rows(adapter_bank_row, document_adapter)
        got_down = lax.all_to_all(
            down_bank[sample_rows], "batch", split_axis=0, concat_axis=0, tiled=True
        )
        got_up = lax.all_to_all(
            adapter_up_weight[sample_rows], "batch", split_axis=0, concat_axis=0, tiled=True
        )
        down_block = jnp.transpose(got_down, (1, 2, 0, 3)).reshape(SEGS * joint_rank, -1)
        up_block = jnp.transpose(got_up, (1, 2, 0, 3)).reshape(SEGS * low_width, -1)
        all_down = lax.all_gather(down_block, "seq", axis=0)
        all_up = lax.all_gather(up_block, "seq", axis=0)
        first = (seq_index >= half_count).astype(jnp.int32)
        merged = jnp.transpose(all_down, (1, 0, 2)).reshape(SEGS * joint_rank, -1)
        down_parts = [lax.dynamic_slice_in_dim(merged, first * joint_rank, 2 * joint_rank)]
        down_places = [whole_place(features)]
        up_rows = jnp.transpose(all_up, (1, 0, 2)).reshape(SEGS, low_width, -1)
        is_query = jnp.arange(up_rows.shape[2]) < query_columns
        up_blocks = jnp.concatenate(
            [
                jnp.where(is_query[None, None, :], up_rows, 0),
                jnp.where(is_query[None, None, :], 0, up_rows),
            ],
            axis=1,
        )
        column_blocks = [
            lax.dynamic_slice_in_dim(
                local_tokens,
                jnp.remainder(seq_index + steps, seq_count) * down_width,
                down_width,
                axis=1,
            )
            for steps in range(seq_count)
        ]

    positions = seq_index * rows + jnp.arange(rows, dtype=jnp.int32)
    inside = positions - jnp.where(
        positions >= second_end, second_end, jnp.where(positions >= first_end, first_end, 0)
    )
    exponent = jnp.arange(HEAD_WIDTH // 2, dtype=f32) * (2.0 / HEAD_WIDTH)
    inverse = jnp.power(jnp.float32(rope_base), -exponent)
    angles = inside.astype(f32)[:, None] * jnp.concatenate([inverse, inverse])[None, :]
    signs = jnp.where(jnp.arange(HEAD_WIDTH) < HEAD_WIDTH // 2, -1.0, 1.0).astype(f32)
    cosines = jnp.cos(angles)
    sines = jnp.sin(angles) * signs[None, :]

    column_parts = [
        shift(block, "seq", steps) if steps else block
        for steps, block in enumerate(column_blocks)
    ]
    early = [cosines, sines] + ([column_parts[2]] if seq_count > 3 else [])
    up_shape = (SEGS, joint_rank, query_columns + HEAD_WIDTH)
    matrix_rows = features + 2 * joint_rank
    arrived = [pltpu.VMEM((seq_count, low_width // 2, down_width), bf16)] if direct else []
    part, matrix, *built = pl.pallas_call(
        functools.partial(project_kernel, places, down_places, len(early), seq_count),
        out_shape=[
            jax.ShapeDtypeStruct((rows, matrix_rows), f32),
            jax.ShapeDtypeStruct((matrix_rows, width), bf16),
        ]
        + ([jax.ShapeDtypeStruct(up_shape, bf16)] if direct else []),
        in_specs=[in_vmem()] + [in_place()] * (len(pieces) + len(down_parts) + len(early)),
        out_specs=[in_vmem(), in_place()] + ([by_block(up_shape)] if direct else []),
        scratch_shapes=arrived
        + [
            pltpu.VMEM((matrix_rows, width), bf16),
            pltpu.SemaphoreType.DMA((len(pieces) + 2 * len(down_parts) + 1,)),
        ],
        compiler_params=pltpu.CompilerParams(vmem_limit_bytes=20 * mebibyte),
        cost_estimate=cost(2 * rows * width * matrix_rows, 2 * width * (matrix_rows + rows)),
        name="project",
    )(local_tokens, *pieces, *down_parts, *early)
    if direct:
        up_blocks = built[0]

    other_part = shift(part, "tp", 1)
    queries, pairs, low_rank = pl.pallas_call(
        functools.partial(qkv_kernel, seq_count),
        out_shape=(
            jax.ShapeDtypeStruct((QHEADS * own_rows, HEAD_WIDTH), bf16),
            jax.ShapeDtypeStruct((rows, 2 * HEAD_WIDTH), bf16),
            jax.ShapeDtypeStruct((rows, joint_rank), bf16),
        ),
        in_specs=[in_smem()] + [in_vmem()] * 5,
        out_specs=(in_vmem(),) * 3,
        compiler_params=pltpu.CompilerParams(vmem_limit_bytes=8 * mebibyte),
        cost_estimate=cost(2 * rows * 3 * 64 * 640, 8 * rows * features),
        name="qkv",
    )(document_lengths, part, other_part, up_blocks, cosines, sines)

    blocks = [pairs] + [push(pairs, "seq", back) for back in range(1, half_count + 1)]
    block_count = len(blocks)
    incoming = output_gradient[0]
    early_columns = [column_parts[1]]
    blank_rows = 4
    bank_shapes = [(adapters, joint_rank, 1, held_down), (adapters, low_width, held_up)]
    attention, query_grad, kept, sent, down_zeros, up_zeros = pl.pallas_call(
        functools.partial(attention_kernel, block_count, len(early_columns)),
        out_shape=(
            jax.ShapeDtypeStruct((own_rows, query_columns), bf16),
            jax.ShapeDtypeStruct((own_rows, query_columns), bf16),
            jax.ShapeDtypeStruct((block_count, own_rows, 2 * HEAD_WIDTH), f32),
            jax.ShapeDtypeStruct((block_count, own_rows, 2 * HEAD_WIDTH), f32),
        )
        + tuple(jax.ShapeDtypeStruct(shape, f32) for shape in bank_shapes),
        in_specs=[in_smem()]
        + [in_vmem()] * (4 + block_count)
        + [in_place()] * len(early_columns),
        out_specs=(in_vmem(),) * 4 + (in_place(),) * 2,
        scratch_shapes=[
            pltpu.VMEM((block_count, QHEADS * own_rows, rows), bf16),
            pltpu.VMEM((blank_rows,) + bank_shapes[0][1:], f32),
            pltpu.VMEM((blank_rows,) + bank_shapes[1][1:], f32),
            pltpu.SemaphoreType.DMA((2 * adapters // blank_rows,)),
        ],
        compiler_params=pltpu.CompilerParams(vmem_limit_bytes=(8 + 4 * block_count) * mebibyte),
        cost_estimate=cost(
            10 * block_count * QHEADS * own_rows * rows * HEAD_WIDTH,
            4 * rows * features,
            block_count * QHEADS * own_rows * rows,
        ),
        name="attention",
    )(document_lengths, queries, incoming, cosines, sines, *blocks, *early_columns)

    other_query = shift(query_grad, "tp", 1)
    pair_sums = pl.pallas_call(
        sum_kernel,
        out_shape=[jax.ShapeDtypeStruct((own_rows, 2 * HEAD_WIDTH), f32)] * block_count,
        in_specs=[in_vmem()] * 2,
        out_specs=[in_vmem()] * block_count,
        compiler_params=pltpu.CompilerParams(vmem_limit_bytes=8 * mebibyte),
        cost_estimate=cost(0, 12 * block_count * own_rows * 2 * HEAD_WIDTH),
        name="pair_sums",
    )(kept, shift(sent, "tp", 1))
    pair_terms = [pair_sums[0]]
    pair_terms += [push(pair_sums[back], "seq", -back) for back in range(1, block_count)]
    pair_grad, late_block = pl.pallas_call(
        functools.partial(pair_kernel, block_count),
        out_shape=[
            jax.ShapeDtypeStruct((own_rows, 2 * HEAD_WIDTH), bf16),
            jax.ShapeDtypeStruct((rows, down_width), bf16),
        ],
        in_specs=[in_vmem()] * (2 + block_count) + [in_place()],
        out_specs=[in_vmem(), in_place()],
        input_output_aliases={2 + block_count: 1},
        compiler_params=pltpu.CompilerParams(vmem_limit_bytes=8 * mebibyte),
        cost_estimate=cost(0, 12 * block_count * own_rows * 2 * HEAD_WIDTH),
        name="pair_gradients",
    )(cosines, sines, *pair_terms, column_blocks[-1])
    column_parts[-1] = shift(late_block, "seq", seq_count - 1)
    other_pair = shift(pair_grad, "tp", 1)

    gradients, rank_grad, *up_split = pl.pallas_call(
        functools.partial(rank_kernel, seq_count),
        out_shape=[
            jax.ShapeDtypeStruct((rows, matrix_rows), bf16),
            jax.ShapeDtypeStruct((rows, joint_rank), bf16),
        ]
        + [jax.ShapeDtypeStruct((SEGS * low_width, held_up * batch_count), f32)] * seq_count,
        in_specs=[in_smem()] + [in_vmem()] * 6,
        out_specs=[by_block((rows, matrix_rows)), in_vmem()]
        + [by_block((SEGS * low_width, held_up * batch_count))] * seq_count,
        scratch_shapes=[
            pltpu.VMEM((SEGS * low_width, features - HEAD_WIDTH), f32),
            pltpu.VMEM((seq_count, SEGS * low_width, held_up * batch_count), f32),
        ],
        compiler_params=pltpu.CompilerParams(vmem_limit_bytes=8 * mebibyte),
        cost_estimate=cost(4 * rows * 3 * 64 * 640, 4 * rows * features),
        name="rank_gradients",
    )(
        document_lengths, query_grad, other_query, pair_grad, other_pair, low_rank, up_blocks
    )

    rank_parts = [rank_grad] + [shift(rank_grad, "seq", steps) for steps in range(1, seq_count)]
    up_sums = [
        shift(block, "seq", steps) if steps else block for steps, block in enumerate(up_split)
    ]

    chunk = 512
    token_grad = pl.pallas_call(
        token_kernel,
        grid=(width // chunk,),
        out_shape=jax.ShapeDtypeStruct((rows, width), bf16),
        in_specs=[
            pl.BlockSpec((rows, matrix_rows), lambda step: (0, 0)),
            pl.BlockSpec((matrix_rows, chunk), lambda step: (0, step)),
        ],
        out_specs=pl.BlockSpec((rows, chunk), lambda step: (0, step)),
        compiler_params=pltpu.CompilerParams(vmem_limit_bytes=12 * mebibyte),
        cost_estimate=cost(2 * rows * width * matrix_rows, 2 * width * (matrix_rows + rows)),
        name="token_gradient",
    )(gradients, matrix)

    if direct:
        term_shapes = [(SEGS * joint_rank, held_down)] * 2 + [(SEGS * low_width, held_up)] * 2
    else:
        term_shapes = [(SEGS * joint_rank, down_width), (SEGS * low_width, held_up * batch_count)]
    terms = pl.pallas_call(
        functools.partial(down_kernel, seq_count),
        out_shape=[jax.ShapeDtypeStruct(shape, f32) for shape in term_shapes],
        in_specs=[in_smem()] + [in_vmem()] * (3 * seq_count),
        out_specs=[in_vmem()] * len(term_shapes),
        compiler_params=pltpu.CompilerParams(vmem_limit_bytes=8 * mebibyte),
        cost_estimate=cost(
            2 * seq_count * rows * SEGS * joint_rank * down_width, 2 * seq_count * rows * down_width
        ),
        name="down_terms",
    )(document_lengths, *rank_parts, *column_parts, *up_sums)

    if direct:
        bank_downs = [terms[0], shift(terms[1], "batch", 1)]
        bank_ups = [terms[2], shift(terms[3], "batch", 1)]
    else:
        down_send = jnp.transpose(
            terms[0].reshape(SEGS * joint_rank, batch_count, held_down), (1, 0, 2)
        )
        up_send = jnp.transpose(
            terms[1].reshape(SEGS * low_width, batch_count, held_up), (1, 0, 2)
        )
        back_down = lax.all_to_all(down_send, "batch", split_axis=0, concat_axis=0, tiled=True)
        back_up = lax.all_to_all(up_send, "batch", split_axis=0, concat_axis=0, tiled=True)
        bank_downs = [back_down[batch] for batch in range(batch_count)]
        bank_ups = [back_up[batch] for batch in range(batch_count)]

    if not direct:
        bank_rows = sample_rows.reshape(-1)

    def whole(array):
        return pl.BlockSpec(array.shape, lambda step, bank: (0,) * array.ndim)

    down_grad, up_grad = pl.pallas_call(
        functools.partial(bank_kernel, batch_count),
        out_shape=(
            jax.ShapeDtypeStruct(down_zeros.shape, f32),
            jax.ShapeDtypeStruct(up_zeros.shape, f32),
        ),
        grid_spec=pltpu.PrefetchScalarGridSpec(
            num_scalar_prefetch=1,
            grid=(batch_count * SEGS,),
            in_specs=[whole(array) for array in bank_downs + bank_ups] + [in_place()] * 2,
            out_specs=(
                pl.BlockSpec(
                    (1, joint_rank, 1, held_down),
                    lambda step, bank: (bank[step], 0, 0, 0),
                ),
                pl.BlockSpec(
                    (1, low_width, held_up),
                    lambda step, bank: (bank[step], 0, 0),
                ),
            ),
        ),
        input_output_aliases={1 + 2 * batch_count: 0, 2 + 2 * batch_count: 1},
        compiler_params=pltpu.CompilerParams(vmem_limit_bytes=16 * mebibyte),
        name="bank_rows",
    )(
        bank_rows,
        *bank_downs,
        *bank_ups,
        down_zeros,
        up_zeros,
    )
    return (attention[None], token_grad[None], down_grad, up_grad)


def solution(mesh):
    in_specs = (
        P(("groups", "batch"), "seq", "tp"),
        P("seq", "tp"),
        P(None, None, "tp", ("seq", "batch")),
        P(None, None, ("seq", "batch")),
        P(),
        P("groups", None),
        P("groups", None),
        P(("groups", "batch"), ("seq", "tp"), None),
    )
    out_specs = (
        P(("groups", "batch"), ("seq", "tp"), None),
        P(("groups", "batch"), "seq", "tp"),
        P("groups", None, "tp", ("seq", "batch")),
        P("groups", None, ("seq", "batch")),
    )
    return jax.shard_map(shards, mesh=mesh, in_specs=in_specs, out_specs=out_specs, check_vma=False)
```

```python
import functools

import jax
import jax.numpy as jnp
from jax import lax
from jax.experimental import pallas as pl
from jax.experimental.pallas import tpu as pltpu
from jax.sharding import PartitionSpec as P

QHEADS = 4
HEAD_WIDTH = 128
ADAPTER_RANK = 32
SEGS = 3

adapter_scale = 2.0
rope_base = 5000000.0
masked_score = -1e30
mebibyte = 1024 * 1024


def shift(value, axis, steps):
    count = lax.axis_size(axis)
    return lax.ppermute(value, axis, [(at, (at + steps) % count) for at in range(count)])


def push(value, axis, steps):
    count = lax.axis_size(axis)
    pairs = [(at, at + steps) for at in range(count) if 0 <= at + steps < count]
    return lax.ppermute(value, axis, pairs)


def dot_nt(left, right):
    return lax.dot_general(
        left, right, (((1,), (1,)), ((), ())), preferred_element_type=jnp.float32
    )


def dot_nn(left, right):
    return jnp.dot(left, right, preferred_element_type=jnp.float32)


def dot_tn(left, right):
    return lax.dot_general(
        left, right, (((0,), (0,)), ((), ())), preferred_element_type=jnp.float32
    )


def lookup_rows(adapter_bank_row, document_adapter):
    matches = document_adapter[..., None] == jnp.arange(adapter_bank_row.shape[0], dtype=jnp.int32)
    return jnp.sum(jnp.where(matches, adapter_bank_row, 0), axis=-1)


def row_positions(first, count):
    return first + lax.broadcasted_iota(jnp.int32, (count, 1), 0)


def ring_index(index, count):
    return lax.rem(index + count, count)


def kernel_marks(lengths):
    batch = lax.axis_index("batch")
    first_end = lengths[batch, 0]
    return first_end, first_end + lengths[batch, 1]


def row_segments(ends, positions):
    return (positions >= ends[0]).astype(jnp.int32) + (positions >= ends[1]).astype(jnp.int32)


def cost(flops, bytes_accessed, transcendentals=0):
    return pl.CostEstimate(
        flops=flops, bytes_accessed=bytes_accessed, transcendentals=transcendentals
    )


def in_vmem():
    return pl.BlockSpec(memory_space=pltpu.VMEM)


def in_smem():
    return pl.BlockSpec(memory_space=pltpu.SMEM)


def by_block(shape):
    return pl.BlockSpec(shape, lambda: (0,) * len(shape))


def in_place():
    return pl.BlockSpec(memory_space=pl.ANY)


def fetch(piece, target, place, semaphore):
    height, width = piece.shape
    row, column = place()
    copy = pltpu.make_async_copy(
        piece,
        target.at[
            pl.ds(pl.multiple_of(row, 16), height), pl.ds(pl.multiple_of(column, 128), width)
        ],
        semaphore,
    )
    copy.start()
    return copy


def frozen_place(seq_count, rows, share, behind, batch_step, group_step):
    def place():
        holder = ring_index(lax.axis_index("seq") - behind, seq_count)
        if share is None:
            return holder * rows, 0
        batch = lax.rem(lax.axis_index("batch") + batch_step, 2)
        group = lax.rem(lax.axis_index("groups") + group_step, 2)
        return holder * rows, (group * 2 + batch) * share

    return place


def down_place(seq_count, features, width, behind):
    def place():
        return features, ring_index(lax.axis_index("seq") - behind, seq_count) * width

    return place


def whole_place(row):
    def place():
        return row, 0

    return place


def pack_kernel(unused, seq_count, own_down, far_down, own_up, far_up, tokens, *refs):
    refs = refs[unused:]
    payloads, columns = refs[:seq_count], refs[seq_count : 2 * seq_count]
    down, up = refs[2 * seq_count :]
    ahead = lax.axis_index("batch") == 0
    joint_rank, held = own_down.shape[1:]
    low_width, held_up = own_up.shape[1:]
    for document in range(SEGS):
        rows = slice(document * joint_rank, (document + 1) * joint_rank)
        down[rows, :held] = jnp.where(ahead, own_down[document], far_down[document])
        down[rows, held:] = jnp.where(ahead, far_down[document], own_down[document])
        up[document, :, :held_up] = jnp.where(ahead, own_up[document], far_up[document])
        up[document, :, held_up:] = jnp.where(ahead, far_up[document], own_up[document])
    half, slot = low_width // 2, down.shape[1] // 4
    for steps in range(seq_count):
        target = ring_index(lax.axis_index("seq") + steps - seq_count, seq_count)
        first = (target >= seq_count // 2).astype(jnp.int32)
        start = pl.multiple_of(first * joint_rank, joint_rank)
        payload = payloads[steps]
        payload[: 2 * joint_rank] = down[pl.ds(start, 2 * joint_rank)]
        for index in range(2):
            block = up[first + index]
            for part in range(2):
                column = (2 * index + part) * slot
                payload[2 * joint_rank :, column : column + 2 * held_up] = block[
                    part * half : (part + 1) * half
                ]
        width = columns[steps].shape[1]
        columns[steps][...] = tokens[:, pl.ds(pl.multiple_of(target * width, 128), width)]


def assemble_up(seq_count, arrived, up_blocks):
    low_width = up_blocks.shape[1] // 2
    query_columns = QHEADS * HEAD_WIDTH
    seq_index = lax.axis_index("seq")
    first = (seq_index >= seq_count // 2).astype(jnp.int32)
    held = up_blocks.shape[2] // seq_count
    half, slot = low_width // 2, arrived.shape[2] // 4
    up_blocks[...] = jnp.zeros_like(up_blocks)
    for holder in range(seq_count):
        block = arrived[ring_index(seq_index - holder, seq_count)]
        start, stop = holder * held, (holder + 1) * held
        middle = min(max(query_columns, start), stop)
        for index in range(2):
            for part in range(2):
                offset = (2 * index + part) * slot
                if middle > start:
                    up_blocks[first + index, part * half : (part + 1) * half, start:middle] = block[
                        :, offset : offset + middle - start
                    ]
                if stop > middle:
                    low = low_width + part * half
                    up_blocks[first + index, low : low + half, middle:stop] = block[
                        :, offset + middle - start : offset + held
                    ]


def project_kernel(frozen_places, down_places, unused, seq_count, tokens, *refs):
    frozen_count, down_count = len(frozen_places), len(down_places)
    frozen_pieces = refs[:frozen_count]
    down_pieces = refs[frozen_count : frozen_count + down_count]
    refs = refs[frozen_count + down_count + unused :]
    packed = down_count > 1
    part, matrix = refs[:2]
    weights, semaphore = refs[-2:]
    features = part.shape[1] - 2 * ADAPTER_RANK * 2
    copies = []
    for piece, place in zip(frozen_pieces, frozen_places):
        copies.append(fetch(piece, weights, place, semaphore.at[len(copies)]))
    joint_rank = 2 * ADAPTER_RANK
    for number, (piece, place) in enumerate(zip(down_pieces, down_places)):
        rows = piece.at[pl.ds(0, 2 * joint_rank)] if packed else piece
        copies.append(fetch(rows, weights, place, semaphore.at[len(copies)]))
        if packed:
            extra = piece.shape[0] - 2 * joint_rank
            copy = pltpu.make_async_copy(
                piece.at[pl.ds(2 * joint_rank, extra)],
                refs[3].at[number],
                semaphore.at[len(copies)],
            )
            copy.start()
            copies.append(copy)
    for copy in copies:
        copy.wait()
    keep = pltpu.make_async_copy(weights, matrix, semaphore.at[len(copies)])
    keep.start()
    part[...] = dot_nt(tokens[...], weights[...])
    if packed:
        assemble_up(seq_count, refs[3], refs[2])
    keep.wait()


def rotated(values, cosines, sines):
    return values * cosines + pltpu.roll(values, values.shape[1] // 2, 1) * sines


def qkv_kernel(seq_count, lengths, mine, theirs, up_blocks, cosines, sines, queries, pairs, low_rank):
    rows = mine.shape[0]
    own_rows = queries.shape[0] // QHEADS
    query_columns = QHEADS * HEAD_WIDTH
    value_start = query_columns + HEAD_WIDTH
    features = value_start + HEAD_WIDTH
    joint_rank = low_rank.shape[1]
    middle = features + joint_rank
    ends = kernel_marks(lengths)

    def low_rows(picked, second):
        first_low = mine[picked, features:middle] + theirs[picked, features:middle]
        second_low = mine[picked, middle:] + theirs[picked, middle:]
        return jnp.where(second, second_low, first_low).astype(jnp.bfloat16)

    first = (lax.axis_index("seq") >= seq_count // 2).astype(jnp.int32)
    first_row = lax.axis_index("seq") * rows
    segments = row_segments(ends, row_positions(first_row, rows))
    low = low_rows(slice(None), segments != first)
    low_rank[...] = low
    value_delta = jnp.zeros((rows, HEAD_WIDTH), jnp.float32)
    for document in range(SEGS):
        chosen = jnp.where(segments == document, low, jnp.zeros_like(low))
        value_delta += dot_nn(chosen, up_blocks[document, :, query_columns:])
    keys = mine[:, query_columns:value_start] + theirs[:, query_columns:value_start]
    pairs[:, :HEAD_WIDTH] = rotated(keys, cosines[...], sines[...]).astype(jnp.bfloat16)
    values = mine[:, value_start:features] + theirs[:, value_start:features]
    pairs[:, HEAD_WIDTH:] = (values + adapter_scale * value_delta).astype(jnp.bfloat16)
    start = pl.multiple_of(lax.axis_index("tp") * own_rows, own_rows)
    own = pl.ds(start, own_rows)
    own_segments = row_segments(ends, row_positions(first_row + start, own_rows))
    own_low = low_rows(own, own_segments != first)
    query_delta = jnp.zeros((own_rows, query_columns), jnp.float32)
    for document in range(SEGS):
        chosen = jnp.where(own_segments == document, own_low, jnp.zeros_like(own_low))
        query_delta += dot_nn(chosen, up_blocks[document, :, :query_columns])
    projected = mine[own, :query_columns] + theirs[own, :query_columns]
    projected = projected + adapter_scale * query_delta
    for head in range(QHEADS):
        turned = rotated(
            projected[:, head * HEAD_WIDTH : (head + 1) * HEAD_WIDTH], cosines[own], sines[own]
        )
        queries[head * own_rows : (head + 1) * own_rows] = turned.astype(jnp.bfloat16)


def attention_kernel(block_count, unused, lengths, queries, incoming, cosines, sines, *refs):
    blocks = refs[:block_count]
    output, query_grad, kept, sent, low_probs = refs[block_count + unused :]
    own_rows, query_columns = incoming.shape
    rows = blocks[0].shape[0]
    score_scale = HEAD_WIDTH ** (-0.5)
    ends = kernel_marks(lengths)
    seq_index, tp_index = lax.axis_index("seq"), lax.axis_index("tp")
    positions = row_positions(seq_index * rows + tp_index * own_rows, own_rows)
    positions = jnp.concatenate([positions] * QHEADS, axis=0)
    segments = row_segments(ends, positions)
    starts = jnp.where(segments == 0, 0, jnp.where(segments == 1, ends[0], ends[1]))
    scores = []
    for back, block in enumerate(blocks):
        key_positions = (seq_index - back) * rows + lax.broadcasted_iota(jnp.int32, (1, rows), 1)
        allowed = (key_positions <= positions) & (key_positions >= starts)
        block_scores = dot_nt(queries[...], block[:, :HEAD_WIDTH]) * score_scale
        scores.append(jnp.where(allowed, block_scores, masked_score))
    row_max = functools.reduce(
        jnp.maximum, [jnp.max(part, axis=1, keepdims=True) for part in scores]
    )
    raised = [jnp.exp(part - row_max) for part in scores]
    row_total = sum(jnp.sum(part, axis=1, keepdims=True) for part in raised)
    inverse = 1.0 / row_total
    probs = [part * inverse for part in raised]
    weighted = jnp.zeros((QHEADS * own_rows, HEAD_WIDTH), jnp.float32)
    for back, block in enumerate(blocks):
        low_probs[back] = probs[back].astype(jnp.bfloat16)
        weighted += dot_nn(low_probs[back], block[:, HEAD_WIDTH:])
    attended = weighted.astype(jnp.bfloat16)
    gradients = jnp.concatenate(
        [incoming[:, head * HEAD_WIDTH : (head + 1) * HEAD_WIDTH] for head in range(QHEADS)],
        axis=0,
    )
    row_delta = jnp.sum(
        gradients.astype(jnp.float32) * attended.astype(jnp.float32), axis=1, keepdims=True
    )
    start = pl.multiple_of(tp_index * own_rows, own_rows)
    total = jnp.zeros((QHEADS * own_rows, HEAD_WIDTH), jnp.float32)
    for back, block in enumerate(blocks):
        prob_grad = dot_nt(gradients, block[:, HEAD_WIDTH:])
        score_grad = (probs[back] * (prob_grad - row_delta)).astype(jnp.bfloat16)
        total += dot_nn(score_grad, block[:, :HEAD_WIDTH])
        key_part = dot_tn(score_grad, queries[...]) * score_scale
        value_part = dot_tn(low_probs[back], gradients)
        mine = tp_index == 0
        kept[back, :, :HEAD_WIDTH] = jnp.where(mine, key_part[:own_rows], key_part[own_rows:])
        sent[back, :, :HEAD_WIDTH] = jnp.where(mine, key_part[own_rows:], key_part[:own_rows])
        kept[back, :, HEAD_WIDTH:] = jnp.where(mine, value_part[:own_rows], value_part[own_rows:])
        sent[back, :, HEAD_WIDTH:] = jnp.where(mine, value_part[own_rows:], value_part[:own_rows])
    own = pl.ds(start, own_rows)
    for head in range(QHEADS):
        picked = slice(head * own_rows, (head + 1) * own_rows)
        columns = slice(head * HEAD_WIDTH, (head + 1) * HEAD_WIDTH)
        output[:, columns] = attended[picked]
        query_grad[:, columns] = rotated(
            total[picked] * score_scale, cosines[own], -sines[own]
        ).astype(jnp.bfloat16)


def sum_kernel(kept, arrived, *sums):
    for back, total in enumerate(sums):
        total[...] = kept[back] + arrived[back]


def pair_kernel(terms, cosines, sines, *refs):
    parts, pair = refs[:terms], refs[-2]
    own_rows = pair.shape[0]
    total = sum(part[...] for part in parts)
    own = pl.ds(pl.multiple_of(lax.axis_index("tp") * own_rows, own_rows), own_rows)
    keys = rotated(total[:, :HEAD_WIDTH], cosines[own], -sines[own])
    pair[:, :HEAD_WIDTH] = keys.astype(jnp.bfloat16)
    pair[:, HEAD_WIDTH:] = total[:, HEAD_WIDTH:].astype(jnp.bfloat16)


def rank_kernel(
    seq_count, lengths, own_query, other_query, own_pair, other_pair, low_rank, up_blocks, *refs
):
    gradients, rank_grad = refs[:2]
    split_terms, (terms, blocks) = refs[2:-2], refs[-2:]
    own_rows, query_columns = own_query.shape
    rows = low_rank.shape[0]
    seq_index = lax.axis_index("seq")
    start = pl.multiple_of(lax.axis_index("tp") * own_rows, own_rows)
    other = pl.multiple_of(own_rows - start, own_rows)
    gradients[pl.ds(start, own_rows), :query_columns] = own_query[...]
    gradients[pl.ds(other, own_rows), :query_columns] = other_query[...]
    value_start = query_columns + HEAD_WIDTH
    features = value_start + HEAD_WIDTH
    gradients[pl.ds(start, own_rows), query_columns:features] = own_pair[...]
    gradients[pl.ds(other, own_rows), query_columns:features] = other_pair[...]
    query_grad = gradients[:, :query_columns]
    value_grad = gradients[:, value_start:features]
    low = low_rank[...]
    rank = low.shape[1] // 2
    segments = row_segments(kernel_marks(lengths), row_positions(seq_index * rows, rows))
    total = jnp.zeros((rows, low.shape[1]), jnp.float32)
    for document in range(SEGS):
        member = segments == document
        parts = dot_nt(query_grad, up_blocks[document, :, :query_columns])
        parts += dot_nt(value_grad, up_blocks[document, :, query_columns:])
        total = jnp.where(member, parts, total)
        chosen = jnp.where(member, low, jnp.zeros_like(low))
        query_terms = dot_tn(chosen, query_grad)
        value_terms = dot_tn(chosen, value_grad)
        place = slice(document * rank, (document + 1) * rank)
        terms[place, :query_columns] = adapter_scale * query_terms[:rank]
        terms[place, query_columns:] = adapter_scale * value_terms[rank:]
    turned = (adapter_scale * total).astype(jnp.bfloat16)
    rank_grad[...] = turned
    second = segments != (seq_index >= seq_count // 2).astype(jnp.int32)
    nothing = jnp.zeros_like(turned)
    middle = features + low.shape[1]
    gradients[:, features:middle] = jnp.where(second, nothing, turned)
    gradients[:, middle:] = jnp.where(second, turned, nothing)
    held = blocks.shape[2]
    for holder in range(seq_count):
        blocks[holder] = terms[:, holder * held : (holder + 1) * held]
    for steps, block in enumerate(split_terms):
        mine = blocks[ring_index(seq_index + steps - seq_count, seq_count)]
        if block.shape == mine.shape:
            block[...] = mine
            continue
        tail = held - 128
        count = 128 // tail
        height = mine.shape[0] // count
        first_low = mine.shape[0] + height
        block[: mine.shape[0]] = mine[:, :128]
        for part in range(count):
            block[mine.shape[0] : first_low, part * tail : (part + 1) * tail] = mine[
                part * height : (part + 1) * height, 128:
            ]
        block[first_low:, : low.shape[1]] = turned[: rows // 2].astype(jnp.float32)
        block[first_low:, low.shape[1] :] = turned[rows // 2 :].astype(jnp.float32)


def token_kernel(gradients, matrix, token_grad):
    token_grad[...] = dot_nn(gradients[...], matrix[...]).astype(jnp.bfloat16)


def down_kernel(block_count, lengths, *refs):
    columns = refs[:block_count]
    up_parts = refs[block_count : 2 * block_count]
    packed = up_parts[0].shape != up_parts[1].shape
    rank_count = 1 if packed else block_count
    ranks = refs[2 * block_count : 2 * block_count + rank_count]
    outputs = refs[2 * block_count + rank_count :]
    rows, joint_rank = ranks[0].shape
    ends = kernel_marks(lengths)
    up_rows, up_width = up_parts[0].shape
    lows, ups = [ranks[0][...]], [up_parts[0][...]]
    for behind in range(1, block_count):
        if not packed:
            lows.append(ranks[behind][...])
            ups.append(up_parts[behind][...])
            continue
        part = up_parts[behind]
        count = 128 // (up_width - 128)
        first_low = up_rows + up_rows // count
        halves = [part[first_low:, :joint_rank], part[first_low:, joint_rank:]]
        lows.append(jnp.concatenate(halves, axis=0).astype(jnp.bfloat16))
    all_terms = []
    for document in range(SEGS):
        total = jnp.zeros((joint_rank, columns[0].shape[1]), jnp.float32)
        for behind in range(block_count):
            holder = ring_index(lax.axis_index("seq") - behind, block_count)
            segments = row_segments(ends, row_positions(holder * rows, rows))
            chosen = jnp.where(segments == document, lows[behind], jnp.zeros_like(lows[behind]))
            total += dot_tn(chosen, columns[behind][...])
        all_terms.append(total)
    down_terms = jnp.concatenate(all_terms, axis=0)
    if not packed:
        outputs[0][...] = down_terms
        outputs[1][...] = sum(ups)
        return
    own_down, far, own_up, up_terms = outputs
    tail = up_width - 128
    height = up_rows // (128 // tail)
    up_terms[...] = ups[0]
    for part in up_parts[1:]:
        up_terms[:, :128] += part[:up_rows]
        for piece in range(128 // tail):
            up_terms[piece * height : (piece + 1) * height, 128:] += part[
                up_rows : up_rows + height, piece * tail : (piece + 1) * tail
            ]
    held, held_up = own_down.shape[1], own_up.shape[1]
    ahead = lax.axis_index("batch") == 0
    own_down[...] = jnp.where(ahead, down_terms[:, :held], down_terms[:, held:])
    far[:, :held] = jnp.where(ahead, down_terms[:, held:], down_terms[:, :held])
    left, right = up_terms[:, :held_up], up_terms[:, held_up:]
    own_up[...] = jnp.where(ahead, left, right)
    far_up = jnp.where(ahead, right, left)
    spare = far.shape[1] - held
    far[:up_rows, held:] = far_up[:, :spare]
    far[up_rows:, held : held + held_up - spare] = far_up[:, spare:]


def packed_bank_kernel(bank_rows, own_down, far, own_up, down_zeros, up_zeros, down_out, up_out):
    step = pl.program_id(0)
    joint_rank, held = down_out.shape[1], down_out.shape[3]
    low_width, held_up = up_out.shape[1:]
    up_rows = own_up.shape[0]
    spare = far.shape[1] - held
    down_total = jnp.zeros((joint_rank, held), jnp.float32)
    head = jnp.zeros((low_width, spare), jnp.float32)
    rest = jnp.zeros((low_width, held_up - spare), jnp.float32)
    for document in range(SEGS):
        rows = slice(document * joint_rank, (document + 1) * joint_rank)
        lows = slice(document * low_width, (document + 1) * low_width)
        same = bank_rows[document] == bank_rows[step]
        down_total += jnp.where(same, own_down[rows], 0.0)
        head += jnp.where(same, own_up[lows, :spare], 0.0)
        rest += jnp.where(same, own_up[lows, spare:], 0.0)
        same = bank_rows[SEGS + document] == bank_rows[step]
        down_total += jnp.where(same, far[rows, :held], 0.0)
        head += jnp.where(same, far[lows, held:], 0.0)
        lows = slice(up_rows + document * low_width, up_rows + (document + 1) * low_width)
        rest += jnp.where(same, far[lows, held : held + held_up - spare], 0.0)
    down_out[0, :, 0, :] = down_total
    up_out[0, :, :spare] = head
    up_out[0, :, spare:] = rest


def bank_kernel(block_count, bank_rows, *refs):
    down_terms = refs[:block_count]
    up_terms = refs[block_count : 2 * block_count]
    down_out, up_out = refs[2 * block_count + 2 :]
    step = pl.program_id(0)
    row = bank_rows[step]
    joint_rank = down_out.shape[1]
    low_width = up_out.shape[1]
    down_total = jnp.zeros((joint_rank, down_out.shape[3]), jnp.float32)
    up_total = jnp.zeros((low_width, up_out.shape[2]), jnp.float32)
    for block in range(block_count):
        for document in range(SEGS):
            same = bank_rows[block * SEGS + document] == row
            down_rows = down_terms[block][document * joint_rank : (document + 1) * joint_rank]
            up_rows = up_terms[block][document * low_width : (document + 1) * low_width]
            down_total += jnp.where(same, down_rows, 0.0)
            up_total += jnp.where(same, up_rows, 0.0)
    down_out[0, :, 0, :] = down_total
    up_out[0] = up_total


def shards(
    tokens,
    frozen_qkv_matrix,
    adapter_down_weight,
    adapter_up_weight,
    adapter_bank_row,
    document_lengths,
    document_adapter,
    output_gradient,
):
    seq_count = lax.axis_size("seq")
    batch_count = lax.axis_size("batch")
    group_count = lax.axis_size("groups")
    chip_size = lax.axis_size("tp")
    seq_index = lax.axis_index("seq")
    batch_index = lax.axis_index("batch")
    group_index = lax.axis_index("groups")
    tp_index = lax.axis_index("tp")
    local_tokens = tokens[0]
    rows, width = local_tokens.shape
    own_rows = rows // chip_size
    query_columns = QHEADS * HEAD_WIDTH
    frozen_rows = frozen_qkv_matrix.shape[0]
    features = frozen_rows * seq_count
    low_width = ADAPTER_RANK
    joint_rank = adapter_down_weight.shape[1]
    adapters = adapter_bank_row.shape[0]
    bf16 = jnp.bfloat16
    f32 = jnp.float32

    lengths = lax.dynamic_index_in_dim(document_lengths, batch_index, 0, keepdims=False)
    first_end = lengths[0]
    second_end = first_end + lengths[1]
    half_count = seq_count // 2
    held_down = adapter_down_weight.shape[3]
    held_up = adapter_up_weight.shape[2]
    down_width = held_down * batch_count
    up_width = held_up * batch_count

    positions = seq_index * rows + jnp.arange(rows, dtype=jnp.int32)
    inside = positions - jnp.where(
        positions >= second_end, second_end, jnp.where(positions >= first_end, first_end, 0)
    )
    exponent = jnp.arange(HEAD_WIDTH // 2, dtype=f32) * (2.0 / HEAD_WIDTH)
    inverse = jnp.power(jnp.float32(rope_base), -exponent)
    angles = inside.astype(f32)[:, None] * jnp.concatenate([inverse, inverse])[None, :]
    signs = jnp.where(jnp.arange(HEAD_WIDTH) < HEAD_WIDTH // 2, -1.0, 1.0).astype(f32)
    cosines = jnp.cos(angles)
    sines = jnp.sin(angles) * signs[None, :]

    sample_rows = lookup_rows(adapter_bank_row, document_adapter)
    bank_rows = sample_rows.reshape(-1)
    if batch_count == 2:
        own_bank = jnp.where(batch_index == 0, sample_rows[0], sample_rows[1])
        far_bank = jnp.where(batch_index == 0, sample_rows[1], sample_rows[0])
        bank_rows = jnp.concatenate([own_bank, far_bank])
    down_bank = adapter_down_weight[:, :, 0, :]
    down_zeros = jnp.zeros((adapters, joint_rank, 1, held_down), f32)
    up_zeros = jnp.zeros((adapters, low_width, held_up), f32)

    plane_count = group_count * batch_count
    share = width // plane_count
    pieces, places = [], []
    padded_down = (held_down + 127) // 128 * 128
    direct = (
        group_count == 2
        and batch_count == 2
        and share % 128 == 0
        and down_width % 128 == 0
        and frozen_rows % 16 == 0
        and 4 * up_width <= down_width
        and up_width > 128
        and 128 % (up_width - 128) == 0
        and 0 < held_up + held_down - padded_down <= padded_down - held_down
    )
    if direct:
        own_share = lax.dynamic_slice_in_dim(
            frozen_qkv_matrix, (group_index * batch_count + batch_index) * share, share, axis=1
        )
        pieces.append(frozen_qkv_matrix)
        places.append(frozen_place(seq_count, frozen_rows, None, 0, 0, 0))
        before = shift(own_share, "seq", 1)
        after = shift(own_share, "seq", seq_count - 1)
        arrivals = [(1, before), (seq_count - 1, after)]
        for steps in range(2, seq_count - 1):
            before = shift(before, "seq", 1)
            arrivals.append((steps, before))
        for steps, here in arrivals:
            over_batch = shift(here, "batch", 1)
            over_groups = shift(here, "groups", 1)
            over_both = lax.ppermute(
                here, ("groups", "batch"), [(at, plane_count - 1 - at) for at in range(plane_count)]
            )
            for value, batch_step, group_step in (
                (here, 0, 0),
                (over_batch, 1, 0),
                (over_groups, 0, 1),
                (over_both, 1, 1),
            ):
                pieces.append(value)
                places.append(
                    frozen_place(seq_count, frozen_rows, share, steps, batch_step, group_step)
                )
    else:
        pieces.append(lax.all_gather(frozen_qkv_matrix, "seq", axis=0, tiled=True))
        places.append(whole_place(0))

    column_blocks, up_blocks = None, None
    if direct:
        far_down = shift(down_bank[far_bank], "batch", 1)
        far_up = shift(adapter_up_weight[far_bank], "batch", 1)
        own_down, own_up = down_bank[own_bank], adapter_up_weight[own_bank]
        early = [before, down_zeros, up_zeros, cosines, sines, bank_rows]
        payload_rows = 2 * joint_rank + low_width // 2
        packed = pl.pallas_call(
            functools.partial(pack_kernel, len(early), seq_count),
            out_shape=[jax.ShapeDtypeStruct((payload_rows, down_width), bf16)] * seq_count
            + [jax.ShapeDtypeStruct((rows, down_width), bf16)] * seq_count,
            in_specs=[in_vmem()] * 5 + [in_place()] * len(early),
            out_specs=[by_block((payload_rows, down_width))] * seq_count
            + [by_block((rows, down_width))] * seq_count,
            scratch_shapes=[
                pltpu.VMEM((SEGS * joint_rank, down_width), bf16),
                pltpu.VMEM((SEGS, low_width, 2 * held_up), bf16),
            ],
            compiler_params=pltpu.CompilerParams(vmem_limit_bytes=16 * mebibyte),
            cost_estimate=cost(0, 4 * rows * width),
            name="pack",
        )(own_down, far_down, own_up, far_up, local_tokens, *early)
        column_blocks = packed[seq_count:]
        down_parts = [
            shift(part, "seq", steps) if steps else part
            for steps, part in enumerate(packed[:seq_count])
        ]
        down_places = [down_place(seq_count, features, down_width, steps) for steps in range(seq_count)]
    else:
        bank_rows = sample_rows.reshape(-1)
        got_down = lax.all_to_all(
            down_bank[sample_rows], "batch", split_axis=0, concat_axis=0, tiled=True
        )
        got_up = lax.all_to_all(
            adapter_up_weight[sample_rows], "batch", split_axis=0, concat_axis=0, tiled=True
        )
        down_block = jnp.transpose(got_down, (1, 2, 0, 3)).reshape(SEGS * joint_rank, -1)
        up_block = jnp.transpose(got_up, (1, 2, 0, 3)).reshape(SEGS * low_width, -1)
        all_down = lax.all_gather(down_block, "seq", axis=0)
        all_up = lax.all_gather(up_block, "seq", axis=0)
        first = (seq_index >= half_count).astype(jnp.int32)
        merged = jnp.transpose(all_down, (1, 0, 2)).reshape(SEGS * joint_rank, -1)
        down_parts = [lax.dynamic_slice_in_dim(merged, first * joint_rank, 2 * joint_rank)]
        down_places = [whole_place(features)]
        up_rows = jnp.transpose(all_up, (1, 0, 2)).reshape(SEGS, low_width, -1)
        is_query = jnp.arange(up_rows.shape[2]) < query_columns
        up_blocks = jnp.concatenate(
            [
                jnp.where(is_query[None, None, :], up_rows, 0),
                jnp.where(is_query[None, None, :], 0, up_rows),
            ],
            axis=1,
        )
        column_blocks = [
            lax.dynamic_slice_in_dim(
                local_tokens,
                jnp.remainder(seq_index + steps, seq_count) * down_width,
                down_width,
                axis=1,
            )
            for steps in range(seq_count)
        ]

    column_parts = [
        shift(block, "seq", steps) if steps else block
        for steps, block in enumerate(column_blocks)
    ]
    early = [column_parts[2]] if direct and seq_count > 3 else []
    up_shape = (SEGS, joint_rank, query_columns + HEAD_WIDTH)
    matrix_rows = features + 2 * joint_rank
    arrived = [pltpu.VMEM((seq_count, low_width // 2, down_width), bf16)] if direct else []
    part, matrix, *built = pl.pallas_call(
        functools.partial(project_kernel, places, down_places, len(early), seq_count),
        out_shape=[
            jax.ShapeDtypeStruct((rows, matrix_rows), f32),
            jax.ShapeDtypeStruct((matrix_rows, width), bf16),
        ]
        + ([jax.ShapeDtypeStruct(up_shape, bf16)] if direct else []),
        in_specs=[in_vmem()] + [in_place()] * (len(pieces) + len(down_parts) + len(early)),
        out_specs=[in_vmem(), in_place()] + ([by_block(up_shape)] if direct else []),
        scratch_shapes=arrived
        + [
            pltpu.VMEM((matrix_rows, width), bf16),
            pltpu.SemaphoreType.DMA((len(pieces) + 2 * len(down_parts) + 1,)),
        ],
        compiler_params=pltpu.CompilerParams(vmem_limit_bytes=20 * mebibyte),
        cost_estimate=cost(2 * rows * width * matrix_rows, 2 * width * (matrix_rows + rows)),
        name="project",
    )(local_tokens, *pieces, *down_parts, *early)
    if direct:
        up_blocks = built[0]

    other_part = shift(part, "tp", 1)
    queries, pairs, low_rank = pl.pallas_call(
        functools.partial(qkv_kernel, seq_count),
        out_shape=(
            jax.ShapeDtypeStruct((QHEADS * own_rows, HEAD_WIDTH), bf16),
            jax.ShapeDtypeStruct((rows, 2 * HEAD_WIDTH), bf16),
            jax.ShapeDtypeStruct((rows, joint_rank), bf16),
        ),
        in_specs=[in_smem()] + [in_vmem()] * 5,
        out_specs=(in_vmem(),) * 3,
        compiler_params=pltpu.CompilerParams(vmem_limit_bytes=8 * mebibyte),
        cost_estimate=cost(2 * rows * 3 * 64 * 640, 8 * rows * features),
        name="qkv",
    )(document_lengths, part, other_part, up_blocks, cosines, sines)

    blocks = [pairs] + [push(pairs, "seq", back) for back in range(1, half_count + 1)]
    block_count = len(blocks)
    incoming = output_gradient[0]
    early_columns = [column_parts[1]]
    attention, query_grad, kept, sent = pl.pallas_call(
        functools.partial(attention_kernel, block_count, len(early_columns)),
        out_shape=(
            jax.ShapeDtypeStruct((own_rows, query_columns), bf16),
            jax.ShapeDtypeStruct((own_rows, query_columns), bf16),
            jax.ShapeDtypeStruct((block_count, own_rows, 2 * HEAD_WIDTH), f32),
            jax.ShapeDtypeStruct((block_count, own_rows, 2 * HEAD_WIDTH), f32),
        ),
        in_specs=[in_smem()]
        + [in_vmem()] * (4 + block_count)
        + [in_place()] * len(early_columns),
        out_specs=(in_vmem(),) * 4,
        scratch_shapes=[pltpu.VMEM((block_count, QHEADS * own_rows, rows), bf16)],
        compiler_params=pltpu.CompilerParams(vmem_limit_bytes=(8 + 4 * block_count) * mebibyte),
        cost_estimate=cost(
            10 * block_count * QHEADS * own_rows * rows * HEAD_WIDTH,
            4 * rows * features,
            block_count * QHEADS * own_rows * rows,
        ),
        name="attention",
    )(document_lengths, queries, incoming, cosines, sines, *blocks, *early_columns)

    other_query = shift(query_grad, "tp", 1)
    pair_sums = pl.pallas_call(
        sum_kernel,
        out_shape=[jax.ShapeDtypeStruct((own_rows, 2 * HEAD_WIDTH), f32)] * block_count,
        in_specs=[in_vmem()] * 2,
        out_specs=[in_vmem()] * block_count,
        compiler_params=pltpu.CompilerParams(vmem_limit_bytes=8 * mebibyte),
        cost_estimate=cost(0, 12 * block_count * own_rows * 2 * HEAD_WIDTH),
        name="pair_sums",
    )(kept, shift(sent, "tp", 1))
    pair_terms = [pair_sums[0]]
    pair_terms += [push(pair_sums[back], "seq", -back) for back in range(1, block_count)]
    pair_grad, late_block = pl.pallas_call(
        functools.partial(pair_kernel, block_count),
        out_shape=[
            jax.ShapeDtypeStruct((own_rows, 2 * HEAD_WIDTH), bf16),
            jax.ShapeDtypeStruct((rows, down_width), bf16),
        ],
        in_specs=[in_vmem()] * (2 + block_count) + [in_place()],
        out_specs=[in_vmem(), in_place()],
        input_output_aliases={2 + block_count: 1},
        compiler_params=pltpu.CompilerParams(vmem_limit_bytes=8 * mebibyte),
        cost_estimate=cost(0, 12 * block_count * own_rows * 2 * HEAD_WIDTH),
        name="pair_gradients",
    )(cosines, sines, *pair_terms, column_blocks[-1])
    column_parts[-1] = shift(late_block, "seq", seq_count - 1)
    other_pair = shift(pair_grad, "tp", 1)

    split_shapes = [(SEGS * low_width, up_width)] * seq_count
    if direct:
        sent_rows = SEGS * low_width * up_width // 128 + rows // 2
        split_shapes[1:] = [(sent_rows, 128)] * (seq_count - 1)
    gradients, rank_grad, *up_split = pl.pallas_call(
        functools.partial(rank_kernel, seq_count),
        out_shape=[
            jax.ShapeDtypeStruct((rows, matrix_rows), bf16),
            jax.ShapeDtypeStruct((rows, joint_rank), bf16),
        ]
        + [jax.ShapeDtypeStruct(shape, f32) for shape in split_shapes],
        in_specs=[in_smem()] + [in_vmem()] * 6,
        out_specs=[by_block((rows, matrix_rows)), in_vmem()]
        + [by_block(shape) for shape in split_shapes],
        scratch_shapes=[
            pltpu.VMEM((SEGS * low_width, features - HEAD_WIDTH), f32),
            pltpu.VMEM((seq_count, SEGS * low_width, held_up * batch_count), f32),
        ],
        compiler_params=pltpu.CompilerParams(vmem_limit_bytes=8 * mebibyte),
        cost_estimate=cost(4 * rows * 3 * 64 * 640, 4 * rows * features),
        name="rank_gradients",
    )(
        document_lengths, query_grad, other_query, pair_grad, other_pair, low_rank, up_blocks
    )

    rank_parts = [rank_grad]
    if not direct:
        rank_parts += [shift(rank_grad, "seq", steps) for steps in range(1, seq_count)]
    up_sums = [
        shift(block, "seq", steps) if steps else block for steps, block in enumerate(up_split)
    ]

    chunk = 512
    token_grad = pl.pallas_call(
        token_kernel,
        grid=(width // chunk,),
        out_shape=jax.ShapeDtypeStruct((rows, width), bf16),
        in_specs=[
            pl.BlockSpec((rows, matrix_rows), lambda step: (0, 0)),
            pl.BlockSpec((matrix_rows, chunk), lambda step: (0, step)),
        ],
        out_specs=pl.BlockSpec((rows, chunk), lambda step: (0, step)),
        compiler_params=pltpu.CompilerParams(vmem_limit_bytes=12 * mebibyte),
        cost_estimate=cost(2 * rows * width * matrix_rows, 2 * width * (matrix_rows + rows)),
        name="token_gradient",
    )(gradients, matrix)

    if direct:
        term_shapes = [(SEGS * joint_rank, held_down), (SEGS * joint_rank, padded_down)]
        term_shapes += [(SEGS * low_width, held_up)]
    else:
        term_shapes = [(SEGS * joint_rank, down_width), (SEGS * low_width, up_width)]
    terms = pl.pallas_call(
        functools.partial(down_kernel, seq_count),
        out_shape=[jax.ShapeDtypeStruct(shape, f32) for shape in term_shapes],
        in_specs=[in_smem()] + [in_vmem()] * (2 * seq_count + len(rank_parts)),
        out_specs=[in_vmem()] * len(term_shapes),
        scratch_shapes=[pltpu.VMEM((SEGS * low_width, up_width), f32)] if direct else [],
        compiler_params=pltpu.CompilerParams(vmem_limit_bytes=8 * mebibyte),
        cost_estimate=cost(
            2 * seq_count * rows * SEGS * joint_rank * down_width, 2 * seq_count * rows * down_width
        ),
        name="down_terms",
    )(document_lengths, *column_parts, *up_sums, *rank_parts)

    if direct:
        bank_terms = [terms[0], shift(terms[1], "batch", 1), terms[2]]
    else:
        down_send = jnp.transpose(
            terms[0].reshape(SEGS * joint_rank, batch_count, held_down), (1, 0, 2)
        )
        up_send = jnp.transpose(
            terms[1].reshape(SEGS * low_width, batch_count, held_up), (1, 0, 2)
        )
        back_down = lax.all_to_all(down_send, "batch", split_axis=0, concat_axis=0, tiled=True)
        back_up = lax.all_to_all(up_send, "batch", split_axis=0, concat_axis=0, tiled=True)
        bank_downs = [back_down[batch] for batch in range(batch_count)]
        bank_ups = [back_up[batch] for batch in range(batch_count)]
        bank_terms = bank_downs + bank_ups


    def whole(array):
        return pl.BlockSpec(array.shape, lambda step, bank: (0,) * array.ndim)

    term_count = len(bank_terms)
    down_grad, up_grad = pl.pallas_call(
        packed_bank_kernel if direct else functools.partial(bank_kernel, batch_count),
        out_shape=(
            jax.ShapeDtypeStruct(down_zeros.shape, f32),
            jax.ShapeDtypeStruct(up_zeros.shape, f32),
        ),
        grid_spec=pltpu.PrefetchScalarGridSpec(
            num_scalar_prefetch=1,
            grid=(batch_count * SEGS,),
            in_specs=[whole(array) for array in bank_terms] + [in_place()] * 2,
            out_specs=(
                pl.BlockSpec(
                    (1, joint_rank, 1, held_down),
                    lambda step, bank: (bank[step], 0, 0, 0),
                ),
                pl.BlockSpec(
                    (1, low_width, held_up),
                    lambda step, bank: (bank[step], 0, 0),
                ),
            ),
        ),
        input_output_aliases={1 + term_count: 0, 2 + term_count: 1},
        compiler_params=pltpu.CompilerParams(vmem_limit_bytes=16 * mebibyte),
        name="bank_rows",
    )(
        bank_rows,
        *bank_terms,
        down_zeros,
        up_zeros,
    )
    return (attention[None], token_grad[None], down_grad, up_grad)


def solution(mesh):
    in_specs = (
        P(("groups", "batch"), "seq", "tp"),
        P("seq", "tp"),
        P(None, None, "tp", ("seq", "batch")),
        P(None, None, ("seq", "batch")),
        P(),
        P("groups", None),
        P("groups", None),
        P(("groups", "batch"), ("seq", "tp"), None),
    )
    out_specs = (
        P(("groups", "batch"), ("seq", "tp"), None),
        P(("groups", "batch"), "seq", "tp"),
        P("groups", None, "tp", ("seq", "batch")),
        P("groups", None, ("seq", "batch")),
    )
    return jax.shard_map(shards, mesh=mesh, in_specs=in_specs, out_specs=out_specs, check_vma=False)
```

```python
import functools

import jax
import jax.numpy as jnp
from jax import lax
from jax.experimental import pallas as pl
from jax.experimental.pallas import tpu as pltpu
from jax.sharding import PartitionSpec as P

QHEADS = 4
HEAD_WIDTH = 128
ADAPTER_RANK = 32
SEGS = 3

adapter_scale = 2.0
rope_base = 5000000.0
masked_score = -1e30
mebibyte = 1024 * 1024


def shift(value, axis, steps):
    count = lax.axis_size(axis)
    return lax.ppermute(value, axis, [(at, (at + steps) % count) for at in range(count)])


def push(value, axis, steps):
    count = lax.axis_size(axis)
    pairs = [(at, at + steps) for at in range(count) if 0 <= at + steps < count]
    return lax.ppermute(value, axis, pairs)


def dot_nt(left, right):
    return lax.dot_general(
        left, right, (((1,), (1,)), ((), ())), preferred_element_type=jnp.float32
    )


def dot_nn(left, right):
    return jnp.dot(left, right, preferred_element_type=jnp.float32)


def dot_tn(left, right):
    return lax.dot_general(
        left, right, (((0,), (0,)), ((), ())), preferred_element_type=jnp.float32
    )


def lookup_rows(adapter_bank_row, document_adapter):
    matches = document_adapter[..., None] == jnp.arange(adapter_bank_row.shape[0], dtype=jnp.int32)
    return jnp.sum(jnp.where(matches, adapter_bank_row, 0), axis=-1)


def row_positions(first, count):
    return first + lax.broadcasted_iota(jnp.int32, (count, 1), 0)


def ring_index(index, count):
    return lax.rem(index + count, count)


def kernel_marks(lengths):
    batch = lax.axis_index("batch")
    first_end = lengths[batch, 0]
    return first_end, first_end + lengths[batch, 1]


def row_segments(ends, positions):
    return (positions >= ends[0]).astype(jnp.int32) + (positions >= ends[1]).astype(jnp.int32)


def cost(flops, bytes_accessed, transcendentals=0):
    return pl.CostEstimate(
        flops=flops, bytes_accessed=bytes_accessed, transcendentals=transcendentals
    )


def in_vmem():
    return pl.BlockSpec(memory_space=pltpu.VMEM)


def in_smem():
    return pl.BlockSpec(memory_space=pltpu.SMEM)


def by_block(shape):
    return pl.BlockSpec(shape, lambda: (0,) * len(shape))


def in_place():
    return pl.BlockSpec(memory_space=pl.ANY)


def fetch(piece, target, place, semaphore):
    height, width = piece.shape
    row, column = place()
    copy = pltpu.make_async_copy(
        piece,
        target.at[
            pl.ds(pl.multiple_of(row, 16), height), pl.ds(pl.multiple_of(column, 128), width)
        ],
        semaphore,
    )
    copy.start()
    return copy


def frozen_place(seq_count, rows, share, behind, batch_step, group_step):
    def place():
        holder = ring_index(lax.axis_index("seq") - behind, seq_count)
        if share is None:
            return holder * rows, 0
        batch = lax.rem(lax.axis_index("batch") + batch_step, 2)
        group = lax.rem(lax.axis_index("groups") + group_step, 2)
        return holder * rows, (group * 2 + batch) * share

    return place


def down_place(seq_count, features, width, behind):
    def place():
        return features, ring_index(lax.axis_index("seq") - behind, seq_count) * width

    return place


def whole_place(row):
    def place():
        return row, 0

    return place


def pack_kernel(own_down, far_down, own_up, far_up, before, after, *refs):
    plane, forward, payloads, (down, up) = refs[0], refs[1], refs[2:-2], refs[-2:]
    ahead = lax.axis_index("batch") == 0
    joint_rank, held = own_down.shape[1:]
    low_width, held_up = own_up.shape[1:]
    frozen_rows = before.shape[0]
    plane[:frozen_rows] = before[...]
    plane[frozen_rows:] = after[...]
    forward[:frozen_rows] = before[...]
    for document in range(SEGS):
        rows = slice(document * joint_rank, (document + 1) * joint_rank)
        down[rows, :held] = jnp.where(ahead, own_down[document], far_down[document])
        down[rows, held:] = jnp.where(ahead, far_down[document], own_down[document])
        up[document, :, :held_up] = jnp.where(ahead, own_up[document], far_up[document])
        up[document, :, held_up:] = jnp.where(ahead, far_up[document], own_up[document])
    half, slot = low_width // 2, down.shape[1] // 4
    targets = [(0, payloads[0], 0), (1, forward, frozen_rows)]
    targets += [(steps + 2, payload, 0) for steps, payload in enumerate(payloads[1:])]
    seq_count = len(targets)
    for steps, payload, base in targets:
        target = ring_index(lax.axis_index("seq") + steps - seq_count, seq_count)
        first = (target >= seq_count // 2).astype(jnp.int32)
        start = pl.multiple_of(first * joint_rank, joint_rank)
        payload[base : base + 2 * joint_rank] = down[pl.ds(start, 2 * joint_rank)]
        base = base + 2 * joint_rank
        for index in range(2):
            block = up[first + index]
            for part in range(2):
                column = (2 * index + part) * slot
                payload[base : base + half, column : column + 2 * held_up] = block[
                    part * half : (part + 1) * half
                ]


def cut_kernel(unused, seq_count, tokens, *refs):
    for steps, block in enumerate(refs[unused:]):
        target = ring_index(lax.axis_index("seq") + steps - seq_count, seq_count)
        width = block.shape[1]
        block[...] = tokens[:, pl.ds(pl.multiple_of(target * width, 128), width)]


def assemble_up(seq_count, arrived, up_blocks):
    low_width = up_blocks.shape[1] // 2
    query_columns = QHEADS * HEAD_WIDTH
    seq_index = lax.axis_index("seq")
    first = (seq_index >= seq_count // 2).astype(jnp.int32)
    held = up_blocks.shape[2] // seq_count
    half, slot = low_width // 2, arrived.shape[2] // 4
    up_blocks[...] = jnp.zeros_like(up_blocks)
    for holder in range(seq_count):
        block = arrived[ring_index(seq_index - holder, seq_count)]
        start, stop = holder * held, (holder + 1) * held
        middle = min(max(query_columns, start), stop)
        for index in range(2):
            for part in range(2):
                offset = (2 * index + part) * slot
                if middle > start:
                    up_blocks[first + index, part * half : (part + 1) * half, start:middle] = block[
                        :, offset : offset + middle - start
                    ]
                if stop > middle:
                    low = low_width + part * half
                    up_blocks[first + index, low : low + half, middle:stop] = block[
                        :, offset + middle - start : offset + held
                    ]


def project_kernel(array_count, entries, up_entries, unused, seq_count, tokens, *refs):
    arrays = refs[:array_count]
    refs = refs[array_count + unused :]
    part, matrix = refs[:2]
    weights, semaphore = refs[-2:]
    copies = []
    for number, start, height, place in entries:
        piece = arrays[number].at[pl.ds(start, height)]
        copies.append(fetch(piece, weights, place, semaphore.at[len(copies)]))
    for number, start, slot in up_entries:
        copy = pltpu.make_async_copy(
            arrays[number].at[pl.ds(start, refs[3].shape[1])],
            refs[3].at[slot],
            semaphore.at[len(copies)],
        )
        copy.start()
        copies.append(copy)
    for copy in copies:
        copy.wait()
    keep = pltpu.make_async_copy(weights, matrix, semaphore.at[len(copies)])
    keep.start()
    part[...] = dot_nt(tokens[...], weights[...])
    if up_entries:
        assemble_up(seq_count, refs[3], refs[2])
    keep.wait()


def rotated(values, cosines, sines):
    return values * cosines + pltpu.roll(values, values.shape[1] // 2, 1) * sines


def qkv_kernel(seq_count, unused, lengths, mine, theirs, up_blocks, cosines, sines, *refs):
    queries, pairs, low_rank = refs[unused:]
    rows = mine.shape[0]
    own_rows = queries.shape[0] // QHEADS
    query_columns = QHEADS * HEAD_WIDTH
    value_start = query_columns + HEAD_WIDTH
    features = value_start + HEAD_WIDTH
    joint_rank = low_rank.shape[1]
    middle = features + joint_rank
    ends = kernel_marks(lengths)

    def low_rows(picked, second):
        first_low = mine[picked, features:middle] + theirs[picked, features:middle]
        second_low = mine[picked, middle:] + theirs[picked, middle:]
        return jnp.where(second, second_low, first_low).astype(jnp.bfloat16)

    first = (lax.axis_index("seq") >= seq_count // 2).astype(jnp.int32)
    first_row = lax.axis_index("seq") * rows
    segments = row_segments(ends, row_positions(first_row, rows))
    low = low_rows(slice(None), segments != first)
    low_rank[...] = low
    value_delta = jnp.zeros((rows, HEAD_WIDTH), jnp.float32)
    for document in range(SEGS):
        chosen = jnp.where(segments == document, low, jnp.zeros_like(low))
        value_delta += dot_nn(chosen, up_blocks[document, :, query_columns:])
    keys = mine[:, query_columns:value_start] + theirs[:, query_columns:value_start]
    pairs[:, :HEAD_WIDTH] = rotated(keys, cosines[...], sines[...]).astype(jnp.bfloat16)
    values = mine[:, value_start:features] + theirs[:, value_start:features]
    pairs[:, HEAD_WIDTH:] = (values + adapter_scale * value_delta).astype(jnp.bfloat16)
    start = pl.multiple_of(lax.axis_index("tp") * own_rows, own_rows)
    own = pl.ds(start, own_rows)
    own_segments = row_segments(ends, row_positions(first_row + start, own_rows))
    own_low = low_rows(own, own_segments != first)
    query_delta = jnp.zeros((own_rows, query_columns), jnp.float32)
    for document in range(SEGS):
        chosen = jnp.where(own_segments == document, own_low, jnp.zeros_like(own_low))
        query_delta += dot_nn(chosen, up_blocks[document, :, :query_columns])
    projected = mine[own, :query_columns] + theirs[own, :query_columns]
    projected = projected + adapter_scale * query_delta
    for head in range(QHEADS):
        turned = rotated(
            projected[:, head * HEAD_WIDTH : (head + 1) * HEAD_WIDTH], cosines[own], sines[own]
        )
        queries[head * own_rows : (head + 1) * own_rows] = turned.astype(jnp.bfloat16)


def attention_kernel(block_count, unused, lengths, queries, incoming, cosines, sines, *refs):
    blocks = refs[:block_count]
    output, query_grad, kept, sent, low_probs = refs[block_count + unused :]
    own_rows, query_columns = incoming.shape
    rows = blocks[0].shape[0]
    score_scale = HEAD_WIDTH ** (-0.5)
    ends = kernel_marks(lengths)
    seq_index, tp_index = lax.axis_index("seq"), lax.axis_index("tp")
    positions = row_positions(seq_index * rows + tp_index * own_rows, own_rows)
    positions = jnp.concatenate([positions] * QHEADS, axis=0)
    segments = row_segments(ends, positions)
    starts = jnp.where(segments == 0, 0, jnp.where(segments == 1, ends[0], ends[1]))
    scores = []
    for back, block in enumerate(blocks):
        key_positions = (seq_index - back) * rows + lax.broadcasted_iota(jnp.int32, (1, rows), 1)
        allowed = (key_positions <= positions) & (key_positions >= starts)
        block_scores = dot_nt(queries[...], block[:, :HEAD_WIDTH]) * score_scale
        scores.append(jnp.where(allowed, block_scores, masked_score))
    row_max = functools.reduce(
        jnp.maximum, [jnp.max(part, axis=1, keepdims=True) for part in scores]
    )
    raised = [jnp.exp(part - row_max) for part in scores]
    row_total = sum(jnp.sum(part, axis=1, keepdims=True) for part in raised)
    inverse = 1.0 / row_total
    probs = [part * inverse for part in raised]
    weighted = jnp.zeros((QHEADS * own_rows, HEAD_WIDTH), jnp.float32)
    for back, block in enumerate(blocks):
        low_probs[back] = probs[back].astype(jnp.bfloat16)
        weighted += dot_nn(low_probs[back], block[:, HEAD_WIDTH:])
    attended = weighted.astype(jnp.bfloat16)
    gradients = jnp.concatenate(
        [incoming[:, head * HEAD_WIDTH : (head + 1) * HEAD_WIDTH] for head in range(QHEADS)],
        axis=0,
    )
    row_delta = jnp.sum(
        gradients.astype(jnp.float32) * attended.astype(jnp.float32), axis=1, keepdims=True
    )
    start = pl.multiple_of(tp_index * own_rows, own_rows)
    total = jnp.zeros((QHEADS * own_rows, HEAD_WIDTH), jnp.float32)
    for back, block in enumerate(blocks):
        prob_grad = dot_nt(gradients, block[:, HEAD_WIDTH:])
        score_grad = (probs[back] * (prob_grad - row_delta)).astype(jnp.bfloat16)
        total += dot_nn(score_grad, block[:, :HEAD_WIDTH])
        key_part = dot_tn(score_grad, queries[...]) * score_scale
        value_part = dot_tn(low_probs[back], gradients)
        mine = tp_index == 0
        kept[back, :, :HEAD_WIDTH] = jnp.where(mine, key_part[:own_rows], key_part[own_rows:])
        sent[back, :, :HEAD_WIDTH] = jnp.where(mine, key_part[own_rows:], key_part[:own_rows])
        kept[back, :, HEAD_WIDTH:] = jnp.where(mine, value_part[:own_rows], value_part[own_rows:])
        sent[back, :, HEAD_WIDTH:] = jnp.where(mine, value_part[own_rows:], value_part[:own_rows])
    own = pl.ds(start, own_rows)
    for head in range(QHEADS):
        picked = slice(head * own_rows, (head + 1) * own_rows)
        columns = slice(head * HEAD_WIDTH, (head + 1) * HEAD_WIDTH)
        output[:, columns] = attended[picked]
        query_grad[:, columns] = rotated(
            total[picked] * score_scale, cosines[own], -sines[own]
        ).astype(jnp.bfloat16)


def sum_kernel(kept, arrived, *sums):
    for back, total in enumerate(sums):
        total[...] = kept[back] + arrived[back]


def pair_kernel(terms, cosines, sines, *refs):
    parts, pair = refs[:terms], refs[-2]
    own_rows = pair.shape[0]
    total = sum(part[...] for part in parts)
    own = pl.ds(pl.multiple_of(lax.axis_index("tp") * own_rows, own_rows), own_rows)
    keys = rotated(total[:, :HEAD_WIDTH], cosines[own], -sines[own])
    pair[:, :HEAD_WIDTH] = keys.astype(jnp.bfloat16)
    pair[:, HEAD_WIDTH:] = total[:, HEAD_WIDTH:].astype(jnp.bfloat16)


def rank_kernel(
    seq_count, lengths, own_query, other_query, own_pair, other_pair, low_rank, up_blocks, *refs
):
    gradients, rank_grad = refs[:2]
    split_terms, (terms, blocks) = refs[2:-2], refs[-2:]
    own_rows, query_columns = own_query.shape
    rows = low_rank.shape[0]
    seq_index = lax.axis_index("seq")
    start = pl.multiple_of(lax.axis_index("tp") * own_rows, own_rows)
    other = pl.multiple_of(own_rows - start, own_rows)
    gradients[pl.ds(start, own_rows), :query_columns] = own_query[...]
    gradients[pl.ds(other, own_rows), :query_columns] = other_query[...]
    value_start = query_columns + HEAD_WIDTH
    features = value_start + HEAD_WIDTH
    gradients[pl.ds(start, own_rows), query_columns:features] = own_pair[...]
    gradients[pl.ds(other, own_rows), query_columns:features] = other_pair[...]
    query_grad = gradients[:, :query_columns]
    value_grad = gradients[:, value_start:features]
    low = low_rank[...]
    rank = low.shape[1] // 2
    segments = row_segments(kernel_marks(lengths), row_positions(seq_index * rows, rows))
    total = jnp.zeros((rows, low.shape[1]), jnp.float32)
    for document in range(SEGS):
        member = segments == document
        parts = dot_nt(query_grad, up_blocks[document, :, :query_columns])
        parts += dot_nt(value_grad, up_blocks[document, :, query_columns:])
        total = jnp.where(member, parts, total)
        chosen = jnp.where(member, low, jnp.zeros_like(low))
        query_terms = dot_tn(chosen, query_grad)
        value_terms = dot_tn(chosen, value_grad)
        place = slice(document * rank, (document + 1) * rank)
        terms[place, :query_columns] = adapter_scale * query_terms[:rank]
        terms[place, query_columns:] = adapter_scale * value_terms[rank:]
    turned = (adapter_scale * total).astype(jnp.bfloat16)
    rank_grad[...] = turned
    second = segments != (seq_index >= seq_count // 2).astype(jnp.int32)
    nothing = jnp.zeros_like(turned)
    middle = features + low.shape[1]
    gradients[:, features:middle] = jnp.where(second, nothing, turned)
    gradients[:, middle:] = jnp.where(second, turned, nothing)
    held = blocks.shape[2]
    for holder in range(seq_count):
        blocks[holder] = terms[:, holder * held : (holder + 1) * held]
    for steps, block in enumerate(split_terms):
        mine = blocks[ring_index(seq_index + steps - seq_count, seq_count)]
        if block.shape == mine.shape:
            block[...] = mine
            continue
        tail = held - 128
        count = 128 // tail
        height = mine.shape[0] // count
        first_low = mine.shape[0] + height
        block[: mine.shape[0]] = mine[:, :128]
        for part in range(count):
            block[mine.shape[0] : first_low, part * tail : (part + 1) * tail] = mine[
                part * height : (part + 1) * height, 128:
            ]
        block[first_low:, : low.shape[1]] = turned[: rows // 2].astype(jnp.float32)
        block[first_low:, low.shape[1] :] = turned[rows // 2 :].astype(jnp.float32)


def token_kernel(gradients, matrix, token_grad):
    token_grad[...] = dot_nn(gradients[...], matrix[...]).astype(jnp.bfloat16)


def down_kernel(block_count, lengths, *refs):
    columns = refs[:block_count]
    up_parts = refs[block_count : 2 * block_count]
    packed = up_parts[0].shape != up_parts[1].shape
    rank_count = 1 if packed else block_count
    ranks = refs[2 * block_count : 2 * block_count + rank_count]
    outputs = refs[2 * block_count + rank_count :]
    rows, joint_rank = ranks[0].shape
    ends = kernel_marks(lengths)
    up_rows, up_width = up_parts[0].shape
    lows, ups = [ranks[0][...]], [up_parts[0][...]]
    for behind in range(1, block_count):
        if not packed:
            lows.append(ranks[behind][...])
            ups.append(up_parts[behind][...])
            continue
        part = up_parts[behind]
        count = 128 // (up_width - 128)
        first_low = up_rows + up_rows // count
        halves = [part[first_low:, :joint_rank], part[first_low:, joint_rank:]]
        lows.append(jnp.concatenate(halves, axis=0).astype(jnp.bfloat16))
    all_terms = []
    for document in range(SEGS):
        total = jnp.zeros((joint_rank, columns[0].shape[1]), jnp.float32)
        for behind in range(block_count):
            holder = ring_index(lax.axis_index("seq") - behind, block_count)
            segments = row_segments(ends, row_positions(holder * rows, rows))
            chosen = jnp.where(segments == document, lows[behind], jnp.zeros_like(lows[behind]))
            total += dot_tn(chosen, columns[behind][...])
        all_terms.append(total)
    down_terms = jnp.concatenate(all_terms, axis=0)
    if not packed:
        outputs[0][...] = down_terms
        outputs[1][...] = sum(ups)
        return
    own_down, far, own_up, up_terms = outputs
    tail = up_width - 128
    height = up_rows // (128 // tail)
    up_terms[...] = ups[0]
    for part in up_parts[1:]:
        up_terms[:, :128] += part[:up_rows]
        for piece in range(128 // tail):
            up_terms[piece * height : (piece + 1) * height, 128:] += part[
                up_rows : up_rows + height, piece * tail : (piece + 1) * tail
            ]
    held, held_up = own_down.shape[1], own_up.shape[1]
    ahead = lax.axis_index("batch") == 0
    own_down[...] = jnp.where(ahead, down_terms[:, :held], down_terms[:, held:])
    far[:, :held] = jnp.where(ahead, down_terms[:, held:], down_terms[:, :held])
    left, right = up_terms[:, :held_up], up_terms[:, held_up:]
    own_up[...] = jnp.where(ahead, left, right)
    far_up = jnp.where(ahead, right, left)
    spare = far.shape[1] - held
    far[:up_rows, held:] = far_up[:, :spare]
    far[up_rows:, held : held + held_up - spare] = far_up[:, spare:]


def packed_bank_kernel(bank_rows, own_down, far, own_up, down_zeros, up_zeros, down_out, up_out):
    step = pl.program_id(0)
    joint_rank, held = down_out.shape[1], down_out.shape[3]
    low_width, held_up = up_out.shape[1:]
    up_rows = own_up.shape[0]
    spare = far.shape[1] - held
    down_total = jnp.zeros((joint_rank, held), jnp.float32)
    head = jnp.zeros((low_width, spare), jnp.float32)
    rest = jnp.zeros((low_width, held_up - spare), jnp.float32)
    for document in range(SEGS):
        rows = slice(document * joint_rank, (document + 1) * joint_rank)
        lows = slice(document * low_width, (document + 1) * low_width)
        same = bank_rows[document] == bank_rows[step]
        down_total += jnp.where(same, own_down[rows], 0.0)
        head += jnp.where(same, own_up[lows, :spare], 0.0)
        rest += jnp.where(same, own_up[lows, spare:], 0.0)
        same = bank_rows[SEGS + document] == bank_rows[step]
        down_total += jnp.where(same, far[rows, :held], 0.0)
        head += jnp.where(same, far[lows, held:], 0.0)
        lows = slice(up_rows + document * low_width, up_rows + (document + 1) * low_width)
        rest += jnp.where(same, far[lows, held : held + held_up - spare], 0.0)
    down_out[0, :, 0, :] = down_total
    up_out[0, :, :spare] = head
    up_out[0, :, spare:] = rest


def bank_kernel(block_count, bank_rows, *refs):
    down_terms = refs[:block_count]
    up_terms = refs[block_count : 2 * block_count]
    down_out, up_out = refs[2 * block_count + 2 :]
    step = pl.program_id(0)
    row = bank_rows[step]
    joint_rank = down_out.shape[1]
    low_width = up_out.shape[1]
    down_total = jnp.zeros((joint_rank, down_out.shape[3]), jnp.float32)
    up_total = jnp.zeros((low_width, up_out.shape[2]), jnp.float32)
    for block in range(block_count):
        for document in range(SEGS):
            same = bank_rows[block * SEGS + document] == row
            down_rows = down_terms[block][document * joint_rank : (document + 1) * joint_rank]
            up_rows = up_terms[block][document * low_width : (document + 1) * low_width]
            down_total += jnp.where(same, down_rows, 0.0)
            up_total += jnp.where(same, up_rows, 0.0)
    down_out[0, :, 0, :] = down_total
    up_out[0] = up_total


def shards(
    tokens,
    frozen_qkv_matrix,
    adapter_down_weight,
    adapter_up_weight,
    adapter_bank_row,
    document_lengths,
    document_adapter,
    output_gradient,
):
    seq_count = lax.axis_size("seq")
    batch_count = lax.axis_size("batch")
    group_count = lax.axis_size("groups")
    chip_size = lax.axis_size("tp")
    seq_index = lax.axis_index("seq")
    batch_index = lax.axis_index("batch")
    group_index = lax.axis_index("groups")
    tp_index = lax.axis_index("tp")
    local_tokens = tokens[0]
    rows, width = local_tokens.shape
    own_rows = rows // chip_size
    query_columns = QHEADS * HEAD_WIDTH
    frozen_rows = frozen_qkv_matrix.shape[0]
    features = frozen_rows * seq_count
    low_width = ADAPTER_RANK
    joint_rank = adapter_down_weight.shape[1]
    adapters = adapter_bank_row.shape[0]
    bf16 = jnp.bfloat16
    f32 = jnp.float32

    lengths = lax.dynamic_index_in_dim(document_lengths, batch_index, 0, keepdims=False)
    first_end = lengths[0]
    second_end = first_end + lengths[1]
    half_count = seq_count // 2
    held_down = adapter_down_weight.shape[3]
    held_up = adapter_up_weight.shape[2]
    down_width = held_down * batch_count
    up_width = held_up * batch_count

    positions = seq_index * rows + jnp.arange(rows, dtype=jnp.int32)
    inside = positions - jnp.where(
        positions >= second_end, second_end, jnp.where(positions >= first_end, first_end, 0)
    )
    exponent = jnp.arange(HEAD_WIDTH // 2, dtype=f32) * (2.0 / HEAD_WIDTH)
    inverse = jnp.power(jnp.float32(rope_base), -exponent)
    angles = inside.astype(f32)[:, None] * jnp.concatenate([inverse, inverse])[None, :]
    signs = jnp.where(jnp.arange(HEAD_WIDTH) < HEAD_WIDTH // 2, -1.0, 1.0).astype(f32)
    cosines = jnp.cos(angles)
    sines = jnp.sin(angles) * signs[None, :]

    sample_rows = lookup_rows(adapter_bank_row, document_adapter)
    bank_rows = sample_rows.reshape(-1)
    if batch_count == 2:
        own_bank = jnp.where(batch_index == 0, sample_rows[0], sample_rows[1])
        far_bank = jnp.where(batch_index == 0, sample_rows[1], sample_rows[0])
        bank_rows = jnp.concatenate([own_bank, far_bank])
    down_bank = adapter_down_weight[:, :, 0, :]
    down_zeros = jnp.zeros((adapters, joint_rank, 1, held_down), f32)
    up_zeros = jnp.zeros((adapters, low_width, held_up), f32)

    plane_count = group_count * batch_count
    share = width // plane_count
    padded_down = (held_down + 127) // 128 * 128
    direct = (
        group_count == 2
        and seq_count == 4
        and share == down_width
        and batch_count == 2
        and share % 128 == 0
        and down_width % 128 == 0
        and frozen_rows % 16 == 0
        and 4 * up_width <= down_width
        and up_width > 128
        and 128 % (up_width - 128) == 0
        and 0 < held_up + held_down - padded_down <= padded_down - held_down
    )
    up_entries = []
    if direct:
        own_share = lax.dynamic_slice_in_dim(
            frozen_qkv_matrix, (group_index * batch_count + batch_index) * share, share, axis=1
        )
        before = shift(own_share, "seq", 1)
        after = shift(own_share, "seq", 3)
        far_down = shift(down_bank[far_bank], "batch", 1)
        far_up = shift(adapter_up_weight[far_bank], "batch", 1)
        own_down, own_up = down_bank[own_bank], adapter_up_weight[own_bank]
        payload_rows = 2 * joint_rank + low_width // 2
        pack_shapes = [(2 * frozen_rows, share), (frozen_rows + payload_rows, share)]
        pack_shapes += [(payload_rows, share)] * 3
        plane, forward, payload, *payloads = pl.pallas_call(
            pack_kernel,
            out_shape=[jax.ShapeDtypeStruct(shape, bf16) for shape in pack_shapes],
            in_specs=[in_vmem()] * 6,
            out_specs=[by_block(shape) for shape in pack_shapes],
            scratch_shapes=[
                pltpu.VMEM((SEGS * joint_rank, down_width), bf16),
                pltpu.VMEM((SEGS, low_width, 2 * held_up), bf16),
            ],
            compiler_params=pltpu.CompilerParams(vmem_limit_bytes=16 * mebibyte),
            cost_estimate=cost(0, 8 * frozen_rows * share),
            name="pack",
        )(own_down, far_down, own_up, far_up, before, after)

        def over_plane(value):
            over_both = [(at, plane_count - 1 - at) for at in range(plane_count)]
            return [
                shift(value, "batch", 1),
                shift(value, "groups", 1),
                lax.ppermute(value, ("groups", "batch"), over_both),
            ]

        plane_parts = over_plane(plane)
        forward = shift(forward, "seq", 1)
        middle = forward[:frozen_rows]
        middle_parts = over_plane(middle)
        payloads = [shift(part, "seq", steps + 2) for steps, part in enumerate(payloads)]
        arrays = [frozen_qkv_matrix, before, after, forward, payload] + payloads
        arrays += plane_parts + middle_parts

        def frozen_at(behind, batch_step, group_step):
            return frozen_place(seq_count, frozen_rows, share, behind, batch_step, group_step)

        def down_at(behind):
            return down_place(seq_count, features, down_width, behind)

        entries = [
            (0, 0, frozen_rows, frozen_place(seq_count, frozen_rows, None, 0, 0, 0)),
            (1, 0, frozen_rows, frozen_at(1, 0, 0)),
            (2, 0, frozen_rows, frozen_at(3, 0, 0)),
            (3, 0, frozen_rows, frozen_at(2, 0, 0)),
            (4, 0, 2 * joint_rank, down_at(0)),
            (3, frozen_rows, 2 * joint_rank, down_at(1)),
            (5, 0, 2 * joint_rank, down_at(2)),
            (6, 0, 2 * joint_rank, down_at(3)),
        ]
        up_entries = [(4, 2 * joint_rank, 0), (3, frozen_rows + 2 * joint_rank, 1)]
        up_entries += [(5, 2 * joint_rank, 2), (6, 2 * joint_rank, 3)]
        for number, (batch_step, group_step) in enumerate(((1, 0), (0, 1), (1, 1))):
            entries += [
                (7 + number, 0, frozen_rows, frozen_at(1, batch_step, group_step)),
                (7 + number, frozen_rows, frozen_rows, frozen_at(3, batch_step, group_step)),
                (10 + number, 0, frozen_rows, frozen_at(2, batch_step, group_step)),
            ]
        early = [forward, down_zeros, up_zeros, cosines, sines, bank_rows]
        column_blocks = pl.pallas_call(
            functools.partial(cut_kernel, len(early), seq_count),
            out_shape=[jax.ShapeDtypeStruct((rows, down_width), bf16)] * seq_count,
            in_specs=[in_vmem()] + [in_place()] * len(early),
            out_specs=[by_block((rows, down_width))] * seq_count,
            compiler_params=pltpu.CompilerParams(vmem_limit_bytes=16 * mebibyte),
            cost_estimate=cost(0, 4 * rows * width),
            name="cut",
        )(local_tokens, *early)
    else:
        bank_rows = sample_rows.reshape(-1)
        got_down = lax.all_to_all(
            down_bank[sample_rows], "batch", split_axis=0, concat_axis=0, tiled=True
        )
        got_up = lax.all_to_all(
            adapter_up_weight[sample_rows], "batch", split_axis=0, concat_axis=0, tiled=True
        )
        down_block = jnp.transpose(got_down, (1, 2, 0, 3)).reshape(SEGS * joint_rank, -1)
        up_block = jnp.transpose(got_up, (1, 2, 0, 3)).reshape(SEGS * low_width, -1)
        all_down = lax.all_gather(down_block, "seq", axis=0)
        all_up = lax.all_gather(up_block, "seq", axis=0)
        first = (seq_index >= half_count).astype(jnp.int32)
        merged = jnp.transpose(all_down, (1, 0, 2)).reshape(SEGS * joint_rank, -1)
        arrays = [
            lax.all_gather(frozen_qkv_matrix, "seq", axis=0, tiled=True),
            lax.dynamic_slice_in_dim(merged, first * joint_rank, 2 * joint_rank),
        ]
        entries = [
            (0, 0, features, whole_place(0)),
            (1, 0, 2 * joint_rank, whole_place(features)),
        ]
        up_rows = jnp.transpose(all_up, (1, 0, 2)).reshape(SEGS, low_width, -1)
        is_query = jnp.arange(up_rows.shape[2]) < query_columns
        up_blocks = jnp.concatenate(
            [
                jnp.where(is_query[None, None, :], up_rows, 0),
                jnp.where(is_query[None, None, :], 0, up_rows),
            ],
            axis=1,
        )
        column_blocks = [
            lax.dynamic_slice_in_dim(
                local_tokens,
                jnp.remainder(seq_index + steps, seq_count) * down_width,
                down_width,
                axis=1,
            )
            for steps in range(seq_count)
        ]

    column_parts = [
        shift(block, "seq", steps) if steps else block
        for steps, block in enumerate(column_blocks)
    ]
    early = [column_parts[2]] if direct and seq_count > 3 else []
    up_shape = (SEGS, joint_rank, query_columns + HEAD_WIDTH)
    matrix_rows = features + 2 * joint_rank
    arrived = [pltpu.VMEM((seq_count, low_width // 2, down_width), bf16)] if direct else []
    part, matrix, *built = pl.pallas_call(
        functools.partial(
            project_kernel, len(arrays), entries, up_entries, len(early), seq_count
        ),
        out_shape=[
            jax.ShapeDtypeStruct((rows, matrix_rows), f32),
            jax.ShapeDtypeStruct((matrix_rows, width), bf16),
        ]
        + ([jax.ShapeDtypeStruct(up_shape, bf16)] if direct else []),
        in_specs=[in_vmem()] + [in_place()] * (len(arrays) + len(early)),
        out_specs=[in_vmem(), in_place()] + ([by_block(up_shape)] if direct else []),
        scratch_shapes=arrived
        + [
            pltpu.VMEM((matrix_rows, width), bf16),
            pltpu.SemaphoreType.DMA((len(entries) + len(up_entries) + 1,)),
        ],
        compiler_params=pltpu.CompilerParams(vmem_limit_bytes=20 * mebibyte),
        cost_estimate=cost(2 * rows * width * matrix_rows, 2 * width * (matrix_rows + rows)),
        name="project",
    )(local_tokens, *arrays, *early)
    if direct:
        up_blocks = built[0]

    other_part = shift(part, "tp", 1)
    queries, pairs, low_rank = pl.pallas_call(
        functools.partial(qkv_kernel, seq_count, 1),
        out_shape=(
            jax.ShapeDtypeStruct((QHEADS * own_rows, HEAD_WIDTH), bf16),
            jax.ShapeDtypeStruct((rows, 2 * HEAD_WIDTH), bf16),
            jax.ShapeDtypeStruct((rows, joint_rank), bf16),
        ),
        in_specs=[in_smem()] + [in_vmem()] * 5 + [in_place()],
        out_specs=(in_vmem(),) * 3,
        compiler_params=pltpu.CompilerParams(vmem_limit_bytes=8 * mebibyte),
        cost_estimate=cost(2 * rows * 3 * 64 * 640, 8 * rows * features),
        name="qkv",
    )(document_lengths, part, other_part, up_blocks, cosines, sines, column_parts[1])

    blocks = [pairs] + [push(pairs, "seq", back) for back in range(1, half_count + 1)]
    block_count = len(blocks)
    incoming = output_gradient[0]
    early_columns = []
    attention, query_grad, kept, sent = pl.pallas_call(
        functools.partial(attention_kernel, block_count, len(early_columns)),
        out_shape=(
            jax.ShapeDtypeStruct((own_rows, query_columns), bf16),
            jax.ShapeDtypeStruct((own_rows, query_columns), bf16),
            jax.ShapeDtypeStruct((block_count, own_rows, 2 * HEAD_WIDTH), f32),
            jax.ShapeDtypeStruct((block_count, own_rows, 2 * HEAD_WIDTH), f32),
        ),
        in_specs=[in_smem()]
        + [in_vmem()] * (4 + block_count)
        + [in_place()] * len(early_columns),
        out_specs=(in_vmem(),) * 4,
        scratch_shapes=[pltpu.VMEM((block_count, QHEADS * own_rows, rows), bf16)],
        compiler_params=pltpu.CompilerParams(vmem_limit_bytes=(8 + 4 * block_count) * mebibyte),
        cost_estimate=cost(
            10 * block_count * QHEADS * own_rows * rows * HEAD_WIDTH,
            4 * rows * features,
            block_count * QHEADS * own_rows * rows,
        ),
        name="attention",
    )(document_lengths, queries, incoming, cosines, sines, *blocks, *early_columns)

    other_query = shift(query_grad, "tp", 1)
    pair_sums = pl.pallas_call(
        sum_kernel,
        out_shape=[jax.ShapeDtypeStruct((own_rows, 2 * HEAD_WIDTH), f32)] * block_count,
        in_specs=[in_vmem()] * 2,
        out_specs=[in_vmem()] * block_count,
        compiler_params=pltpu.CompilerParams(vmem_limit_bytes=8 * mebibyte),
        cost_estimate=cost(0, 12 * block_count * own_rows * 2 * HEAD_WIDTH),
        name="pair_sums",
    )(kept, shift(sent, "tp", 1))
    pair_terms = [pair_sums[0]]
    pair_terms += [push(pair_sums[back], "seq", -back) for back in range(1, block_count)]
    pair_grad, late_block = pl.pallas_call(
        functools.partial(pair_kernel, block_count),
        out_shape=[
            jax.ShapeDtypeStruct((own_rows, 2 * HEAD_WIDTH), bf16),
            jax.ShapeDtypeStruct((rows, down_width), bf16),
        ],
        in_specs=[in_vmem()] * (2 + block_count) + [in_place()],
        out_specs=[in_vmem(), in_place()],
        input_output_aliases={2 + block_count: 1},
        compiler_params=pltpu.CompilerParams(vmem_limit_bytes=8 * mebibyte),
        cost_estimate=cost(0, 12 * block_count * own_rows * 2 * HEAD_WIDTH),
        name="pair_gradients",
    )(cosines, sines, *pair_terms, column_blocks[-1])
    column_parts[-1] = shift(late_block, "seq", seq_count - 1)
    other_pair = shift(pair_grad, "tp", 1)

    split_shapes = [(SEGS * low_width, up_width)] * seq_count
    if direct:
        sent_rows = SEGS * low_width * up_width // 128 + rows // 2
        split_shapes[1:] = [(sent_rows, 128)] * (seq_count - 1)
    gradients, rank_grad, *up_split = pl.pallas_call(
        functools.partial(rank_kernel, seq_count),
        out_shape=[
            jax.ShapeDtypeStruct((rows, matrix_rows), bf16),
            jax.ShapeDtypeStruct((rows, joint_rank), bf16),
        ]
        + [jax.ShapeDtypeStruct(shape, f32) for shape in split_shapes],
        in_specs=[in_smem()] + [in_vmem()] * 6,
        out_specs=[by_block((rows, matrix_rows)), in_vmem()]
        + [by_block(shape) for shape in split_shapes],
        scratch_shapes=[
            pltpu.VMEM((SEGS * low_width, features - HEAD_WIDTH), f32),
            pltpu.VMEM((seq_count, SEGS * low_width, held_up * batch_count), f32),
        ],
        compiler_params=pltpu.CompilerParams(vmem_limit_bytes=8 * mebibyte),
        cost_estimate=cost(4 * rows * 3 * 64 * 640, 4 * rows * features),
        name="rank_gradients",
    )(
        document_lengths, query_grad, other_query, pair_grad, other_pair, low_rank, up_blocks
    )

    rank_parts = [rank_grad]
    if not direct:
        rank_parts += [shift(rank_grad, "seq", steps) for steps in range(1, seq_count)]
    up_sums = [
        shift(block, "seq", steps) if steps else block for steps, block in enumerate(up_split)
    ]

    chunk = 512
    token_grad = pl.pallas_call(
        token_kernel,
        grid=(width // chunk,),
        out_shape=jax.ShapeDtypeStruct((rows, width), bf16),
        in_specs=[
            pl.BlockSpec((rows, matrix_rows), lambda step: (0, 0)),
            pl.BlockSpec((matrix_rows, chunk), lambda step: (0, step)),
        ],
        out_specs=pl.BlockSpec((rows, chunk), lambda step: (0, step)),
        compiler_params=pltpu.CompilerParams(vmem_limit_bytes=12 * mebibyte),
        cost_estimate=cost(2 * rows * width * matrix_rows, 2 * width * (matrix_rows + rows)),
        name="token_gradient",
    )(gradients, matrix)

    if direct:
        term_shapes = [(SEGS * joint_rank, held_down), (SEGS * joint_rank, padded_down)]
        term_shapes += [(SEGS * low_width, held_up)]
    else:
        term_shapes = [(SEGS * joint_rank, down_width), (SEGS * low_width, up_width)]
    terms = pl.pallas_call(
        functools.partial(down_kernel, seq_count),
        out_shape=[jax.ShapeDtypeStruct(shape, f32) for shape in term_shapes],
        in_specs=[in_smem()] + [in_vmem()] * (2 * seq_count + len(rank_parts)),
        out_specs=[in_vmem()] * len(term_shapes),
        scratch_shapes=[pltpu.VMEM((SEGS * low_width, up_width), f32)] if direct else [],
        compiler_params=pltpu.CompilerParams(vmem_limit_bytes=8 * mebibyte),
        cost_estimate=cost(
            2 * seq_count * rows * SEGS * joint_rank * down_width, 2 * seq_count * rows * down_width
        ),
        name="down_terms",
    )(document_lengths, *column_parts, *up_sums, *rank_parts)

    if direct:
        bank_terms = [terms[0], shift(terms[1], "batch", 1), terms[2]]
    else:
        down_send = jnp.transpose(
            terms[0].reshape(SEGS * joint_rank, batch_count, held_down), (1, 0, 2)
        )
        up_send = jnp.transpose(
            terms[1].reshape(SEGS * low_width, batch_count, held_up), (1, 0, 2)
        )
        back_down = lax.all_to_all(down_send, "batch", split_axis=0, concat_axis=0, tiled=True)
        back_up = lax.all_to_all(up_send, "batch", split_axis=0, concat_axis=0, tiled=True)
        bank_downs = [back_down[batch] for batch in range(batch_count)]
        bank_ups = [back_up[batch] for batch in range(batch_count)]
        bank_terms = bank_downs + bank_ups


    def whole(array):
        return pl.BlockSpec(array.shape, lambda step, bank: (0,) * array.ndim)

    term_count = len(bank_terms)
    down_grad, up_grad = pl.pallas_call(
        packed_bank_kernel if direct else functools.partial(bank_kernel, batch_count),
        out_shape=(
            jax.ShapeDtypeStruct(down_zeros.shape, f32),
            jax.ShapeDtypeStruct(up_zeros.shape, f32),
        ),
        grid_spec=pltpu.PrefetchScalarGridSpec(
            num_scalar_prefetch=1,
            grid=(batch_count * SEGS,),
            in_specs=[whole(array) for array in bank_terms] + [in_place()] * 2,
            out_specs=(
                pl.BlockSpec(
                    (1, joint_rank, 1, held_down),
                    lambda step, bank: (bank[step], 0, 0, 0),
                ),
                pl.BlockSpec(
                    (1, low_width, held_up),
                    lambda step, bank: (bank[step], 0, 0),
                ),
            ),
        ),
        input_output_aliases={1 + term_count: 0, 2 + term_count: 1},
        compiler_params=pltpu.CompilerParams(vmem_limit_bytes=16 * mebibyte),
        name="bank_rows",
    )(
        bank_rows,
        *bank_terms,
        down_zeros,
        up_zeros,
    )
    return (attention[None], token_grad[None], down_grad, up_grad)


def solution(mesh):
    in_specs = (
        P(("groups", "batch"), "seq", "tp"),
        P("seq", "tp"),
        P(None, None, "tp", ("seq", "batch")),
        P(None, None, ("seq", "batch")),
        P(),
        P("groups", None),
        P("groups", None),
        P(("groups", "batch"), ("seq", "tp"), None),
    )
    out_specs = (
        P(("groups", "batch"), ("seq", "tp"), None),
        P(("groups", "batch"), "seq", "tp"),
        P("groups", None, "tp", ("seq", "batch")),
        P("groups", None, ("seq", "batch")),
    )
    return jax.shard_map(shards, mesh=mesh, in_specs=in_specs, out_specs=out_specs, check_vma=False)
```

```python
import functools

import jax
import jax.numpy as jnp
from jax import lax
from jax.experimental import pallas as pl
from jax.experimental.pallas import tpu as pltpu
from jax.sharding import PartitionSpec as P

QHEADS = 4
HEAD_WIDTH = 128
ADAPTER_RANK = 32
SEGS = 3

adapter_scale = 2.0
rope_base = 5000000.0
masked_score = -1e30
mebibyte = 1024 * 1024


def shift(value, axis, steps):
    count = lax.axis_size(axis)
    return lax.ppermute(value, axis, [(at, (at + steps) % count) for at in range(count)])


def push(value, axis, steps):
    count = lax.axis_size(axis)
    pairs = [(at, at + steps) for at in range(count) if 0 <= at + steps < count]
    return lax.ppermute(value, axis, pairs)


def dot_nt(left, right):
    return lax.dot_general(
        left, right, (((1,), (1,)), ((), ())), preferred_element_type=jnp.float32
    )


def dot_nn(left, right):
    return jnp.dot(left, right, preferred_element_type=jnp.float32)


def dot_tn(left, right):
    return lax.dot_general(
        left, right, (((0,), (0,)), ((), ())), preferred_element_type=jnp.float32
    )


def lookup_rows(adapter_bank_row, document_adapter):
    matches = document_adapter[..., None] == jnp.arange(adapter_bank_row.shape[0], dtype=jnp.int32)
    return jnp.sum(jnp.where(matches, adapter_bank_row, 0), axis=-1)


def row_positions(first, count):
    return first + lax.broadcasted_iota(jnp.int32, (count, 1), 0)


def ring_index(index, count):
    return lax.rem(index + count, count)


def kernel_marks(lengths):
    batch = lax.axis_index("batch")
    first_end = lengths[batch, 0]
    return first_end, first_end + lengths[batch, 1]


def row_segments(ends, positions):
    return (positions >= ends[0]).astype(jnp.int32) + (positions >= ends[1]).astype(jnp.int32)


def cost(flops, bytes_accessed, transcendentals=0):
    return pl.CostEstimate(
        flops=flops, bytes_accessed=bytes_accessed, transcendentals=transcendentals
    )


def in_vmem():
    return pl.BlockSpec(memory_space=pltpu.VMEM)


def in_smem():
    return pl.BlockSpec(memory_space=pltpu.SMEM)


def by_block(shape):
    return pl.BlockSpec(shape, lambda: (0,) * len(shape))


def in_place():
    return pl.BlockSpec(memory_space=pl.ANY)


def fetch(piece, target, place, semaphore):
    height, width = piece.shape
    row, column = place()
    copy = pltpu.make_async_copy(
        piece,
        target.at[
            pl.ds(pl.multiple_of(row, 16), height), pl.ds(pl.multiple_of(column, 128), width)
        ],
        semaphore,
    )
    copy.start()
    return copy


def frozen_place(seq_count, rows, share, behind, batch_step, group_step):
    def place():
        holder = ring_index(lax.axis_index("seq") - behind, seq_count)
        if share is None:
            return holder * rows, 0
        batch = lax.rem(lax.axis_index("batch") + batch_step, 2)
        group = lax.rem(lax.axis_index("groups") + group_step, 2)
        return holder * rows, (group * 2 + batch) * share

    return place


def down_place(seq_count, features, width, behind):
    def place():
        return features, ring_index(lax.axis_index("seq") - behind, seq_count) * width

    return place


def whole_place(row):
    def place():
        return row, 0

    return place


def join_kernel(before, after, plane):
    rows = before.shape[0]
    plane[:rows] = before[...]
    plane[rows:] = after[...]


def pass_kernel(*refs):
    del refs


def block_kernel(own_down, far_down, down):
    ahead = lax.axis_index("batch") == 0
    joint_rank, held = own_down.shape[1:]
    for document in range(SEGS):
        rows = slice(document * joint_rank, (document + 1) * joint_rank)
        down[rows, :held] = jnp.where(ahead, own_down[document], far_down[document])
        down[rows, held:] = jnp.where(ahead, far_down[document], own_down[document])


def target_of(steps, seq_count):
    target = ring_index(lax.axis_index("seq") + steps - seq_count, seq_count)
    return target, (target >= seq_count // 2).astype(jnp.int32)


def pack_kernel(unused, down, *refs):
    payloads = refs[unused:]
    joint_rank = down.shape[0] // SEGS
    for steps, payload in enumerate(payloads):
        target, first = target_of(steps, len(payloads))
        start = pl.multiple_of(first * joint_rank, joint_rank)
        payload[...] = down[pl.ds(start, 2 * joint_rank)]


def cut_kernel(unused, tokens, own_up, far_up, *refs):
    blocks, up = refs[unused:-1], refs[-1]
    ahead = lax.axis_index("batch") == 0
    low_width, held_up = own_up.shape[1:]
    for document in range(SEGS):
        up[document, :, :held_up] = jnp.where(ahead, own_up[document], far_up[document])
        up[document, :, held_up:] = jnp.where(ahead, far_up[document], own_up[document])
    rows = tokens.shape[0]
    half = low_width // 2
    for steps, block in enumerate(blocks):
        target, first = target_of(steps, len(blocks))
        width = block.shape[1]
        block[:rows] = tokens[:, pl.ds(pl.multiple_of(target * width, 128), width)]
        slot = width // 4
        for index in range(2):
            rows_up = up[first + index]
            for part in range(2):
                column = (2 * index + part) * slot
                block[rows:, column : column + 2 * held_up] = rows_up[
                    part * half : (part + 1) * half
                ]


def low_kernel(seq_count, lengths, down, *refs):
    columns, (own, *sends) = refs[:seq_count], refs[seq_count:]
    joint_rank = down.shape[0] // SEGS
    rows = own.shape[0]
    ends = kernel_marks(lengths)
    for behind in range(seq_count):
        holder = ring_index(lax.axis_index("seq") - behind, seq_count)
        first = (holder >= seq_count // 2).astype(jnp.int32)
        second = row_segments(ends, row_positions(holder * rows, rows)) != first
        start = pl.multiple_of(first * joint_rank, joint_rank)
        values = columns[behind][:rows]
        first_low = dot_nt(values, down[pl.ds(start, joint_rank)])
        start = pl.multiple_of(start + joint_rank, joint_rank)
        second_low = dot_nt(values, down[pl.ds(start, joint_rank)])
        low = jnp.where(second, second_low, first_low)
        if behind == 0:
            own[...] = low
        else:
            sends[behind - 1][:, :joint_rank] = low[: rows // 2]
            sends[behind - 1][:, joint_rank:] = low[rows // 2 :]


def assemble_up(seq_count, arrived, up_blocks):
    low_width = up_blocks.shape[1] // 2
    query_columns = QHEADS * HEAD_WIDTH
    seq_index = lax.axis_index("seq")
    first = (seq_index >= seq_count // 2).astype(jnp.int32)
    held = up_blocks.shape[2] // seq_count
    half, slot = low_width // 2, arrived.shape[2] // 4
    up_blocks[...] = jnp.zeros_like(up_blocks)
    for holder in range(seq_count):
        block = arrived[ring_index(seq_index - holder, seq_count)]
        start, stop = holder * held, (holder + 1) * held
        middle = min(max(query_columns, start), stop)
        for index in range(2):
            for part in range(2):
                offset = (2 * index + part) * slot
                if middle > start:
                    up_blocks[first + index, part * half : (part + 1) * half, start:middle] = block[
                        :, offset : offset + middle - start
                    ]
                if stop > middle:
                    low = low_width + part * half
                    up_blocks[first + index, low : low + half, middle:stop] = block[
                        :, offset + middle - start : offset + held
                    ]


def project_kernel(array_count, entries, up_entries, low_count, seq_count, tokens, *refs):
    arrays, lows = refs[:array_count], refs[array_count : array_count + low_count]
    refs = refs[array_count + low_count :]
    part, matrix = refs[:2]
    frozen, semaphore = refs[-2:]
    copies = []
    for number, start, height, place in entries:
        piece = arrays[number].at[pl.ds(start, height)]
        copies.append(fetch(piece, frozen, place, semaphore.at[len(copies)]))
    for number, start, slot in up_entries:
        copy = pltpu.make_async_copy(
            arrays[number].at[pl.ds(start, refs[3].shape[1])],
            refs[3].at[slot],
            semaphore.at[len(copies)],
        )
        copy.start()
        copies.append(copy)
    for copy in copies:
        copy.wait()
    keep = pltpu.make_async_copy(frozen, matrix, semaphore.at[len(copies)])
    keep.start()
    features, rows = frozen.shape[0], tokens.shape[0]
    part[:, :features] = dot_nt(tokens[...], frozen[...])
    joint_rank = 2 * ADAPTER_RANK
    middle = features + joint_rank
    total = lows[0][...]
    if low_count > 1:
        upper = sum(low[:, :joint_rank] for low in lows[1:])
        lower = sum(low[:, joint_rank:] for low in lows[1:])
        total = total + jnp.concatenate([upper, lower], axis=0)
    part[:, features:middle] = total
    part[:, middle:] = jnp.zeros_like(total)
    if up_entries:
        assemble_up(seq_count, refs[3], refs[2])
    keep.wait()


def rotated(values, cosines, sines):
    return values * cosines + pltpu.roll(values, values.shape[1] // 2, 1) * sines


def qkv_kernel(unused, lengths, mine, theirs, up_blocks, cosines, sines, *refs):
    queries, pairs, low_rank = refs[unused:]
    rows = mine.shape[0]
    own_rows = queries.shape[0] // QHEADS
    query_columns = QHEADS * HEAD_WIDTH
    value_start = query_columns + HEAD_WIDTH
    features = value_start + HEAD_WIDTH
    middle = features + low_rank.shape[1]
    ends = kernel_marks(lengths)
    first_row = lax.axis_index("seq") * rows
    segments = row_segments(ends, row_positions(first_row, rows))
    low = (mine[:, features:middle] + theirs[:, features:middle]).astype(jnp.bfloat16)
    low_rank[...] = low
    value_delta = jnp.zeros((rows, HEAD_WIDTH), jnp.float32)
    for document in range(SEGS):
        chosen = jnp.where(segments == document, low, jnp.zeros_like(low))
        value_delta += dot_nn(chosen, up_blocks[document, :, query_columns:])
    keys = mine[:, query_columns:value_start] + theirs[:, query_columns:value_start]
    pairs[:, :HEAD_WIDTH] = rotated(keys, cosines[...], sines[...]).astype(jnp.bfloat16)
    values = mine[:, value_start:features] + theirs[:, value_start:features]
    pairs[:, HEAD_WIDTH:] = (values + adapter_scale * value_delta).astype(jnp.bfloat16)
    start = pl.multiple_of(lax.axis_index("tp") * own_rows, own_rows)
    own = pl.ds(start, own_rows)
    own_segments = row_segments(ends, row_positions(first_row + start, own_rows))
    own_low = (mine[own, features:middle] + theirs[own, features:middle]).astype(jnp.bfloat16)
    query_delta = jnp.zeros((own_rows, query_columns), jnp.float32)
    for document in range(SEGS):
        chosen = jnp.where(own_segments == document, own_low, jnp.zeros_like(own_low))
        query_delta += dot_nn(chosen, up_blocks[document, :, :query_columns])
    projected = mine[own, :query_columns] + theirs[own, :query_columns]
    projected = projected + adapter_scale * query_delta
    for head in range(QHEADS):
        turned = rotated(
            projected[:, head * HEAD_WIDTH : (head + 1) * HEAD_WIDTH], cosines[own], sines[own]
        )
        queries[head * own_rows : (head + 1) * own_rows] = turned.astype(jnp.bfloat16)


def attention_kernel(block_count, unused, lengths, queries, incoming, cosines, sines, *refs):
    blocks = refs[:block_count]
    output, query_grad, kept, sent, low_probs = refs[block_count + unused :]
    own_rows, query_columns = incoming.shape
    rows = blocks[0].shape[0]
    score_scale = HEAD_WIDTH ** (-0.5)
    ends = kernel_marks(lengths)
    seq_index, tp_index = lax.axis_index("seq"), lax.axis_index("tp")
    positions = row_positions(seq_index * rows + tp_index * own_rows, own_rows)
    positions = jnp.concatenate([positions] * QHEADS, axis=0)
    segments = row_segments(ends, positions)
    starts = jnp.where(segments == 0, 0, jnp.where(segments == 1, ends[0], ends[1]))
    scores = []
    for back, block in enumerate(blocks):
        key_positions = (seq_index - back) * rows + lax.broadcasted_iota(jnp.int32, (1, rows), 1)
        allowed = (key_positions <= positions) & (key_positions >= starts)
        block_scores = dot_nt(queries[...], block[:, :HEAD_WIDTH]) * score_scale
        scores.append(jnp.where(allowed, block_scores, masked_score))
    row_max = functools.reduce(
        jnp.maximum, [jnp.max(part, axis=1, keepdims=True) for part in scores]
    )
    raised = [jnp.exp(part - row_max) for part in scores]
    row_total = sum(jnp.sum(part, axis=1, keepdims=True) for part in raised)
    inverse = 1.0 / row_total
    probs = [part * inverse for part in raised]
    weighted = jnp.zeros((QHEADS * own_rows, HEAD_WIDTH), jnp.float32)
    for back, block in enumerate(blocks):
        low_probs[back] = probs[back].astype(jnp.bfloat16)
        weighted += dot_nn(low_probs[back], block[:, HEAD_WIDTH:])
    attended = weighted.astype(jnp.bfloat16)
    gradients = jnp.concatenate(
        [incoming[:, head * HEAD_WIDTH : (head + 1) * HEAD_WIDTH] for head in range(QHEADS)],
        axis=0,
    )
    row_delta = jnp.sum(
        gradients.astype(jnp.float32) * attended.astype(jnp.float32), axis=1, keepdims=True
    )
    start = pl.multiple_of(tp_index * own_rows, own_rows)
    total = jnp.zeros((QHEADS * own_rows, HEAD_WIDTH), jnp.float32)
    for back, block in enumerate(blocks):
        prob_grad = dot_nt(gradients, block[:, HEAD_WIDTH:])
        score_grad = (probs[back] * (prob_grad - row_delta)).astype(jnp.bfloat16)
        total += dot_nn(score_grad, block[:, :HEAD_WIDTH])
        key_part = dot_tn(score_grad, queries[...]) * score_scale
        value_part = dot_tn(low_probs[back], gradients)
        mine = tp_index == 0
        kept[back, :, :HEAD_WIDTH] = jnp.where(mine, key_part[:own_rows], key_part[own_rows:])
        sent[back, :, :HEAD_WIDTH] = jnp.where(mine, key_part[own_rows:], key_part[:own_rows])
        kept[back, :, HEAD_WIDTH:] = jnp.where(mine, value_part[:own_rows], value_part[own_rows:])
        sent[back, :, HEAD_WIDTH:] = jnp.where(mine, value_part[own_rows:], value_part[:own_rows])
    own = pl.ds(start, own_rows)
    for head in range(QHEADS):
        picked = slice(head * own_rows, (head + 1) * own_rows)
        columns = slice(head * HEAD_WIDTH, (head + 1) * HEAD_WIDTH)
        output[:, columns] = attended[picked]
        query_grad[:, columns] = rotated(
            total[picked] * score_scale, cosines[own], -sines[own]
        ).astype(jnp.bfloat16)


def sum_kernel(kept, arrived, *sums):
    for back, total in enumerate(sums):
        total[...] = kept[back] + arrived[back]


def pair_kernel(terms, cosines, sines, *refs):
    parts, pair = refs[:terms], refs[-1]
    own_rows = pair.shape[0]
    total = sum(part[...] for part in parts)
    own = pl.ds(pl.multiple_of(lax.axis_index("tp") * own_rows, own_rows), own_rows)
    keys = rotated(total[:, :HEAD_WIDTH], cosines[own], -sines[own])
    pair[:, :HEAD_WIDTH] = keys.astype(jnp.bfloat16)
    pair[:, HEAD_WIDTH:] = total[:, HEAD_WIDTH:].astype(jnp.bfloat16)


def rank_kernel(
    seq_count, lengths, own_query, other_query, own_pair, other_pair, low_rank, up_blocks, *refs
):
    gradients, rank_grad, packed_grad = refs[:3]
    split_terms, (terms, blocks) = refs[3:-2], refs[-2:]
    own_rows, query_columns = own_query.shape
    rows = low_rank.shape[0]
    seq_index = lax.axis_index("seq")
    start = pl.multiple_of(lax.axis_index("tp") * own_rows, own_rows)
    other = pl.multiple_of(own_rows - start, own_rows)
    gradients[pl.ds(start, own_rows), :query_columns] = own_query[...]
    gradients[pl.ds(other, own_rows), :query_columns] = other_query[...]
    value_start = query_columns + HEAD_WIDTH
    features = value_start + HEAD_WIDTH
    gradients[pl.ds(start, own_rows), query_columns:features] = own_pair[...]
    gradients[pl.ds(other, own_rows), query_columns:features] = other_pair[...]
    query_grad = gradients[:, :query_columns]
    value_grad = gradients[:, value_start:features]
    low = low_rank[...]
    rank = low.shape[1] // 2
    segments = row_segments(kernel_marks(lengths), row_positions(seq_index * rows, rows))
    total = jnp.zeros((rows, low.shape[1]), jnp.float32)
    for document in range(SEGS):
        member = segments == document
        parts = dot_nt(query_grad, up_blocks[document, :, :query_columns])
        parts += dot_nt(value_grad, up_blocks[document, :, query_columns:])
        total = jnp.where(member, parts, total)
        chosen = jnp.where(member, low, jnp.zeros_like(low))
        query_terms = dot_tn(chosen, query_grad)
        value_terms = dot_tn(chosen, value_grad)
        place = slice(document * rank, (document + 1) * rank)
        terms[place, :query_columns] = adapter_scale * query_terms[:rank]
        terms[place, query_columns:] = adapter_scale * value_terms[rank:]
    turned = (adapter_scale * total).astype(jnp.bfloat16)
    rank_grad[...] = turned
    packed_grad[:, : low.shape[1]] = turned[: rows // 2]
    packed_grad[:, low.shape[1] :] = turned[rows // 2 :]
    second = segments != (seq_index >= seq_count // 2).astype(jnp.int32)
    nothing = jnp.zeros_like(turned)
    middle = features + low.shape[1]
    gradients[:, features:middle] = jnp.where(second, nothing, turned)
    gradients[:, middle:] = jnp.where(second, turned, nothing)
    held = blocks.shape[2]
    for holder in range(seq_count):
        blocks[holder] = terms[:, holder * held : (holder + 1) * held]
    for steps, block in enumerate(split_terms):
        mine = blocks[ring_index(seq_index + steps - seq_count, seq_count)]
        if block.shape == mine.shape:
            block[...] = mine
            continue
        tail = held - 128
        count = 128 // tail
        height = mine.shape[0] // count
        block[: mine.shape[0]] = mine[:, :128]
        for part in range(count):
            block[mine.shape[0] :, part * tail : (part + 1) * tail] = mine[
                part * height : (part + 1) * height, 128:
            ]


def token_kernel(places, gradients, matrix, *refs):
    weights, (token_grad, down, semaphore) = refs[:-3], refs[-3:]
    step = pl.program_id(0)
    width = token_grad.shape[1]

    @pl.when(step == 0)
    def load():
        copies = [
            fetch(piece, down, place, semaphore.at[number])
            for number, (piece, place) in enumerate(zip(weights, places))
        ]
        for copy in copies:
            copy.wait()

    features = matrix.shape[0]
    total = dot_nn(gradients[:, :features], matrix[...])
    columns = pl.ds(pl.multiple_of(step * width, 128), width)
    total += dot_nn(gradients[:, features:], down[:, columns])
    token_grad[...] = total.astype(jnp.bfloat16)


def down_kernel(block_count, lengths, *refs):
    columns, ranks = refs[:block_count], refs[block_count : 2 * block_count]
    outputs = refs[2 * block_count :]
    rows, joint_rank = ranks[0].shape
    ends = kernel_marks(lengths)
    lows = [ranks[0][...]]
    for part in ranks[1:]:
        lows.append(jnp.concatenate([part[:, :joint_rank], part[:, joint_rank:]], axis=0))
    all_terms = []
    for document in range(SEGS):
        total = jnp.zeros((joint_rank, columns[0].shape[1]), jnp.float32)
        for behind in range(block_count):
            holder = ring_index(lax.axis_index("seq") - behind, block_count)
            segments = row_segments(ends, row_positions(holder * rows, rows))
            chosen = jnp.where(segments == document, lows[behind], jnp.zeros_like(lows[behind]))
            total += dot_tn(chosen, columns[behind][:rows])
        all_terms.append(total)
    down_terms = jnp.concatenate(all_terms, axis=0)
    if len(outputs) == 1:
        outputs[0][...] = down_terms
        return
    own_down, far_down = outputs
    held = own_down.shape[1]
    ahead = lax.axis_index("batch") == 0
    own_down[...] = jnp.where(ahead, down_terms[:, :held], down_terms[:, held:])
    far_down[...] = jnp.where(ahead, down_terms[:, held:], down_terms[:, :held])


def up_kernel(block_count, *refs):
    up_parts, outputs = refs[:block_count], refs[block_count:]
    if len(outputs) == 1:
        outputs[0][...] = sum(part[...] for part in up_parts)
        return
    own_up, far_up, up_terms = outputs
    up_rows, up_width = up_terms.shape
    tail = up_width - 128
    height = up_rows // (128 // tail)
    up_terms[...] = up_parts[0][...]
    for part in up_parts[1:]:
        up_terms[:, :128] += part[:up_rows]
        for piece in range(128 // tail):
            up_terms[piece * height : (piece + 1) * height, 128:] += part[
                up_rows:, piece * tail : (piece + 1) * tail
            ]
    held_up = own_up.shape[1]
    ahead = lax.axis_index("batch") == 0
    left, right = up_terms[:, :held_up], up_terms[:, held_up:]
    own_up[...] = jnp.where(ahead, left, right)
    far_up[...] = jnp.where(ahead, right, left)


def packed_bank_kernel(
    bank_rows, own_down, far_down, own_up, far_up, down_zeros, up_zeros, down_out, up_out
):
    step = pl.program_id(0)
    joint_rank, low_width = down_out.shape[1], up_out.shape[1]
    down_total = jnp.zeros((joint_rank, down_out.shape[3]), jnp.float32)
    up_total = jnp.zeros((low_width, up_out.shape[2]), jnp.float32)
    for block, (down, up) in enumerate(((own_down, own_up), (far_down, far_up))):
        for document in range(SEGS):
            same = bank_rows[block * SEGS + document] == bank_rows[step]
            rows = slice(document * joint_rank, (document + 1) * joint_rank)
            lows = slice(document * low_width, (document + 1) * low_width)
            down_total += jnp.where(same, down[rows], 0.0)
            up_total += jnp.where(same, up[lows], 0.0)
    down_out[0, :, 0, :] = down_total
    up_out[0] = up_total


def bank_kernel(block_count, bank_rows, *refs):
    down_terms = refs[:block_count]
    up_terms = refs[block_count : 2 * block_count]
    down_out, up_out = refs[2 * block_count + 2 :]
    step = pl.program_id(0)
    row = bank_rows[step]
    joint_rank = down_out.shape[1]
    low_width = up_out.shape[1]
    down_total = jnp.zeros((joint_rank, down_out.shape[3]), jnp.float32)
    up_total = jnp.zeros((low_width, up_out.shape[2]), jnp.float32)
    for block in range(block_count):
        for document in range(SEGS):
            same = bank_rows[block * SEGS + document] == row
            down_rows = down_terms[block][document * joint_rank : (document + 1) * joint_rank]
            up_rows = up_terms[block][document * low_width : (document + 1) * low_width]
            down_total += jnp.where(same, down_rows, 0.0)
            up_total += jnp.where(same, up_rows, 0.0)
    down_out[0, :, 0, :] = down_total
    up_out[0] = up_total


def shards(
    tokens,
    frozen_qkv_matrix,
    adapter_down_weight,
    adapter_up_weight,
    adapter_bank_row,
    document_lengths,
    document_adapter,
    output_gradient,
):
    seq_count = lax.axis_size("seq")
    batch_count = lax.axis_size("batch")
    group_count = lax.axis_size("groups")
    chip_size = lax.axis_size("tp")
    seq_index = lax.axis_index("seq")
    batch_index = lax.axis_index("batch")
    group_index = lax.axis_index("groups")
    tp_index = lax.axis_index("tp")
    local_tokens = tokens[0]
    rows, width = local_tokens.shape
    own_rows = rows // chip_size
    query_columns = QHEADS * HEAD_WIDTH
    frozen_rows = frozen_qkv_matrix.shape[0]
    features = frozen_rows * seq_count
    low_width = ADAPTER_RANK
    joint_rank = adapter_down_weight.shape[1]
    adapters = adapter_bank_row.shape[0]
    bf16 = jnp.bfloat16
    f32 = jnp.float32

    lengths = lax.dynamic_index_in_dim(document_lengths, batch_index, 0, keepdims=False)
    first_end = lengths[0]
    second_end = first_end + lengths[1]
    half_count = seq_count // 2
    held_down = adapter_down_weight.shape[3]
    held_up = adapter_up_weight.shape[2]
    down_width = held_down * batch_count
    up_width = held_up * batch_count

    positions = seq_index * rows + jnp.arange(rows, dtype=jnp.int32)
    inside = positions - jnp.where(
        positions >= second_end, second_end, jnp.where(positions >= first_end, first_end, 0)
    )
    exponent = jnp.arange(HEAD_WIDTH // 2, dtype=f32) * (2.0 / HEAD_WIDTH)
    inverse = jnp.power(jnp.float32(rope_base), -exponent)
    angles = inside.astype(f32)[:, None] * jnp.concatenate([inverse, inverse])[None, :]
    signs = jnp.where(jnp.arange(HEAD_WIDTH) < HEAD_WIDTH // 2, -1.0, 1.0).astype(f32)
    cosines = jnp.cos(angles)
    sines = jnp.sin(angles) * signs[None, :]

    sample_rows = lookup_rows(adapter_bank_row, document_adapter)
    bank_rows = sample_rows.reshape(-1)
    if batch_count == 2:
        own_bank = jnp.where(batch_index == 0, sample_rows[0], sample_rows[1])
        far_bank = jnp.where(batch_index == 0, sample_rows[1], sample_rows[0])
        bank_rows = jnp.concatenate([own_bank, far_bank])
    down_bank = adapter_down_weight[:, :, 0, :]
    down_zeros = jnp.zeros((adapters, joint_rank, 1, held_down), f32)
    up_zeros = jnp.zeros((adapters, low_width, held_up), f32)

    plane_count = group_count * batch_count
    share = width // plane_count
    padded_down = (held_down + 127) // 128 * 128
    direct = (
        group_count == 2
        and seq_count == 4
        and share == down_width
        and batch_count == 2
        and share % 128 == 0
        and down_width % 128 == 0
        and frozen_rows % 16 == 0
        and 4 * up_width <= down_width
        and up_width > 128
        and 128 % (up_width - 128) == 0
        and 0 < held_up + held_down - padded_down <= padded_down - held_down
    )
    up_entries = []
    if direct:
        own_share = lax.dynamic_slice_in_dim(
            frozen_qkv_matrix, (group_index * batch_count + batch_index) * share, share, axis=1
        )
        before = shift(own_share, "seq", 1)
        after = shift(own_share, "seq", 3)
        far_down = shift(down_bank[far_bank], "batch", 1)
        far_up = shift(adapter_up_weight[far_bank], "batch", 1)
        own_down, own_up = down_bank[own_bank], adapter_up_weight[own_bank]
        down_block = pl.pallas_call(
            block_kernel,
            out_shape=jax.ShapeDtypeStruct((SEGS * joint_rank, down_width), bf16),
            in_specs=[in_vmem()] * 2,
            out_specs=in_vmem(),
            compiler_params=pltpu.CompilerParams(vmem_limit_bytes=8 * mebibyte),
            cost_estimate=cost(0, 4 * SEGS * joint_rank * down_width),
            name="down_block",
        )(own_down, far_down)
        plane = pl.pallas_call(
            join_kernel,
            out_shape=jax.ShapeDtypeStruct((2 * frozen_rows, share), bf16),
            in_specs=[in_vmem()] * 2,
            out_specs=in_vmem(),
            compiler_params=pltpu.CompilerParams(vmem_limit_bytes=8 * mebibyte),
            cost_estimate=cost(0, 8 * frozen_rows * share),
            name="join",
        )(before, after)

        def over_plane(value):
            over_both = [(at, plane_count - 1 - at) for at in range(plane_count)]
            return [
                shift(value, "batch", 1),
                shift(value, "groups", 1),
                lax.ppermute(value, ("groups", "batch"), over_both),
            ]

        plane_parts = over_plane(plane)
        middle = pl.pallas_call(
            pass_kernel,
            out_shape=jax.ShapeDtypeStruct((frozen_rows, share), bf16),
            in_specs=[in_place()] * 3,
            out_specs=in_place(),
            input_output_aliases={0: 0},
            name="pass_middle",
        )(shift(before, "seq", 1), down_zeros, up_zeros)
        middle_parts = over_plane(middle)

        early = [before, cosines, sines, bank_rows]
        block_rows = rows + low_width // 2
        column_blocks = pl.pallas_call(
            functools.partial(cut_kernel, len(early)),
            out_shape=[jax.ShapeDtypeStruct((block_rows, down_width), bf16)] * seq_count,
            in_specs=[in_vmem()] * 3 + [in_place()] * len(early),
            out_specs=[by_block((block_rows, down_width))] * seq_count,
            scratch_shapes=[pltpu.VMEM((SEGS, low_width, 2 * held_up), bf16)],
            compiler_params=pltpu.CompilerParams(vmem_limit_bytes=16 * mebibyte),
            cost_estimate=cost(0, 4 * rows * width),
            name="cut",
        )(local_tokens, own_up, far_up, *early)
        column_parts = [
            shift(block, "seq", steps) if steps else block
            for steps, block in enumerate(column_blocks)
        ]
        low_shapes = [(rows, joint_rank)] + [(rows // 2, 2 * joint_rank)] * (seq_count - 1)
        lows = pl.pallas_call(
            functools.partial(low_kernel, seq_count),
            out_shape=[jax.ShapeDtypeStruct(shape, f32) for shape in low_shapes],
            in_specs=[in_smem()] + [in_vmem()] * (1 + seq_count),
            out_specs=[in_vmem()] * seq_count,
            compiler_params=pltpu.CompilerParams(vmem_limit_bytes=8 * mebibyte),
            cost_estimate=cost(
                4 * seq_count * rows * joint_rank * down_width, 2 * seq_count * rows * down_width
            ),
            name="low",
        )(document_lengths, down_block, *column_parts)
        lows = [lows[0]] + [
            shift(low, "seq", seq_count - 1 - steps) for steps, low in enumerate(lows[1:])
        ]
        arrays = [frozen_qkv_matrix, before, after, middle] + plane_parts + middle_parts
        arrays += column_parts

        def frozen_at(behind, batch_step, group_step):
            return frozen_place(seq_count, frozen_rows, share, behind, batch_step, group_step)

        entries = [
            (0, 0, frozen_rows, frozen_place(seq_count, frozen_rows, None, 0, 0, 0)),
            (1, 0, frozen_rows, frozen_at(1, 0, 0)),
            (2, 0, frozen_rows, frozen_at(3, 0, 0)),
            (3, 0, frozen_rows, frozen_at(2, 0, 0)),
        ]
        for number, (batch_step, group_step) in enumerate(((1, 0), (0, 1), (1, 1))):
            entries += [
                (4 + number, 0, frozen_rows, frozen_at(1, batch_step, group_step)),
                (4 + number, frozen_rows, frozen_rows, frozen_at(3, batch_step, group_step)),
                (7 + number, 0, frozen_rows, frozen_at(2, batch_step, group_step)),
            ]
        up_entries = [(10 + behind, rows, behind) for behind in range(seq_count)]
    else:
        bank_rows = sample_rows.reshape(-1)
        got_down = lax.all_to_all(
            down_bank[sample_rows], "batch", split_axis=0, concat_axis=0, tiled=True
        )
        got_up = lax.all_to_all(
            adapter_up_weight[sample_rows], "batch", split_axis=0, concat_axis=0, tiled=True
        )
        down_block = jnp.transpose(got_down, (1, 2, 0, 3)).reshape(SEGS * joint_rank, -1)
        up_block = jnp.transpose(got_up, (1, 2, 0, 3)).reshape(SEGS * low_width, -1)
        all_down = lax.all_gather(down_block, "seq", axis=0)
        all_up = lax.all_gather(up_block, "seq", axis=0)
        first = (seq_index >= half_count).astype(jnp.int32)
        merged = jnp.transpose(all_down, (1, 0, 2)).reshape(SEGS * joint_rank, -1)
        pair_rows = lax.dynamic_slice_in_dim(merged, first * joint_rank, 2 * joint_rank)
        arrays = [lax.all_gather(frozen_qkv_matrix, "seq", axis=0, tiled=True)]
        entries = [(0, 0, features, whole_place(0))]
        both_lows = lax.dot_general(
            local_tokens, pair_rows, (((1,), (1,)), ((), ())), preferred_element_type=f32
        )
        segments = (positions >= first_end).astype(jnp.int32) + (positions >= second_end)
        lows = [
            jnp.where(
                (segments == first)[:, None], both_lows[:, :joint_rank], both_lows[:, joint_rank:]
            )
        ]
        weight_parts, weight_places = [pair_rows], [whole_place(0)]
        up_rows = jnp.transpose(all_up, (1, 0, 2)).reshape(SEGS, low_width, -1)
        is_query = jnp.arange(up_rows.shape[2]) < query_columns
        up_blocks = jnp.concatenate(
            [
                jnp.where(is_query[None, None, :], up_rows, 0),
                jnp.where(is_query[None, None, :], 0, up_rows),
            ],
            axis=1,
        )
        column_blocks = [
            lax.dynamic_slice_in_dim(
                local_tokens,
                jnp.remainder(seq_index + steps, seq_count) * down_width,
                down_width,
                axis=1,
            )
            for steps in range(seq_count)
        ]

    if not direct:
        column_parts = [
            shift(block, "seq", steps) if steps else block
            for steps, block in enumerate(column_blocks)
        ]
    up_shape = (SEGS, joint_rank, query_columns + HEAD_WIDTH)
    part_width = features + 2 * joint_rank
    arrived = [pltpu.VMEM((seq_count, low_width // 2, down_width), bf16)] if direct else []
    part, matrix, *built = pl.pallas_call(
        functools.partial(
            project_kernel, len(arrays), entries, up_entries, len(lows), seq_count
        ),
        out_shape=[
            jax.ShapeDtypeStruct((rows, part_width), f32),
            jax.ShapeDtypeStruct((features, width), bf16),
        ]
        + ([jax.ShapeDtypeStruct(up_shape, bf16)] if direct else []),
        in_specs=[in_vmem()] + [in_place()] * len(arrays) + [in_vmem()] * len(lows),
        out_specs=[in_vmem(), in_place()] + ([by_block(up_shape)] if direct else []),
        scratch_shapes=arrived
        + [
            pltpu.VMEM((features, width), bf16),
            pltpu.SemaphoreType.DMA((len(entries) + len(up_entries) + 1,)),
        ],
        compiler_params=pltpu.CompilerParams(vmem_limit_bytes=20 * mebibyte),
        cost_estimate=cost(2 * rows * width * features, 2 * width * (features + rows)),
        name="project",
    )(local_tokens, *arrays, *lows)
    if direct:
        up_blocks = built[0]
        payloads = pl.pallas_call(
            functools.partial(pack_kernel, 1),
            out_shape=[jax.ShapeDtypeStruct((2 * joint_rank, down_width), bf16)] * seq_count,
            in_specs=[in_vmem()] + [in_place()],
            out_specs=[by_block((2 * joint_rank, down_width))] * seq_count,
            compiler_params=pltpu.CompilerParams(vmem_limit_bytes=8 * mebibyte),
            cost_estimate=cost(0, 16 * joint_rank * down_width),
            name="pack",
        )(down_block, part)
        weight_parts = [
            shift(part, "seq", steps) if steps else part for steps, part in enumerate(payloads)
        ]
        weight_places = [down_place(seq_count, 0, down_width, steps) for steps in range(seq_count)]

    other_part = shift(part, "tp", 1)
    queries, pairs, low_rank = pl.pallas_call(
        functools.partial(qkv_kernel, 0),
        out_shape=(
            jax.ShapeDtypeStruct((QHEADS * own_rows, HEAD_WIDTH), bf16),
            jax.ShapeDtypeStruct((rows, 2 * HEAD_WIDTH), bf16),
            jax.ShapeDtypeStruct((rows, joint_rank), bf16),
        ),
        in_specs=[in_smem()] + [in_vmem()] * 5,
        out_specs=(in_vmem(),) * 3,
        compiler_params=pltpu.CompilerParams(vmem_limit_bytes=8 * mebibyte),
        cost_estimate=cost(2 * rows * 3 * 64 * 640, 8 * rows * features),
        name="qkv",
    )(document_lengths, part, other_part, up_blocks, cosines, sines)

    blocks = [pairs] + [push(pairs, "seq", back) for back in range(1, half_count + 1)]
    block_count = len(blocks)
    incoming = output_gradient[0]
    early_columns = [weight_parts[1], weight_parts[-1]] if direct else []
    attention, query_grad, kept, sent = pl.pallas_call(
        functools.partial(attention_kernel, block_count, len(early_columns)),
        out_shape=(
            jax.ShapeDtypeStruct((own_rows, query_columns), bf16),
            jax.ShapeDtypeStruct((own_rows, query_columns), bf16),
            jax.ShapeDtypeStruct((block_count, own_rows, 2 * HEAD_WIDTH), f32),
            jax.ShapeDtypeStruct((block_count, own_rows, 2 * HEAD_WIDTH), f32),
        ),
        in_specs=[in_smem()]
        + [in_vmem()] * (4 + block_count)
        + [in_place()] * len(early_columns),
        out_specs=(in_vmem(),) * 4,
        scratch_shapes=[pltpu.VMEM((block_count, QHEADS * own_rows, rows), bf16)],
        compiler_params=pltpu.CompilerParams(vmem_limit_bytes=(8 + 4 * block_count) * mebibyte),
        cost_estimate=cost(
            10 * block_count * QHEADS * own_rows * rows * HEAD_WIDTH,
            4 * rows * features,
            block_count * QHEADS * own_rows * rows,
        ),
        name="attention",
    )(document_lengths, queries, incoming, cosines, sines, *blocks, *early_columns)

    other_query = shift(query_grad, "tp", 1)
    pair_sums = pl.pallas_call(
        sum_kernel,
        out_shape=[jax.ShapeDtypeStruct((own_rows, 2 * HEAD_WIDTH), f32)] * block_count,
        in_specs=[in_vmem()] * 2,
        out_specs=[in_vmem()] * block_count,
        compiler_params=pltpu.CompilerParams(vmem_limit_bytes=8 * mebibyte),
        cost_estimate=cost(0, 12 * block_count * own_rows * 2 * HEAD_WIDTH),
        name="pair_sums",
    )(kept, shift(sent, "tp", 1))
    pair_terms = [pair_sums[0]]
    pair_terms += [push(pair_sums[back], "seq", -back) for back in range(1, block_count)]
    pair_grad = pl.pallas_call(
        functools.partial(pair_kernel, block_count),
        out_shape=jax.ShapeDtypeStruct((own_rows, 2 * HEAD_WIDTH), bf16),
        in_specs=[in_vmem()] * (2 + block_count),
        out_specs=in_vmem(),
        compiler_params=pltpu.CompilerParams(vmem_limit_bytes=8 * mebibyte),
        cost_estimate=cost(0, 12 * block_count * own_rows * 2 * HEAD_WIDTH),
        name="pair_gradients",
    )(cosines, sines, *pair_terms)
    other_pair = shift(pair_grad, "tp", 1)

    split_shapes = [(SEGS * low_width, up_width)] * seq_count
    if direct:
        sent_rows = SEGS * low_width * up_width // 128
        split_shapes[1:] = [(sent_rows, 128)] * (seq_count - 1)
    gradients, rank_grad, packed_grad, *up_split = pl.pallas_call(
        functools.partial(rank_kernel, seq_count),
        out_shape=[
            jax.ShapeDtypeStruct((rows, part_width), bf16),
            jax.ShapeDtypeStruct((rows, joint_rank), bf16),
            jax.ShapeDtypeStruct((rows // 2, 2 * joint_rank), bf16),
        ]
        + [jax.ShapeDtypeStruct(shape, f32) for shape in split_shapes],
        in_specs=[in_smem()] + [in_vmem()] * 6,
        out_specs=[by_block((rows, part_width)), in_vmem(), in_vmem()]
        + [by_block(shape) for shape in split_shapes],
        scratch_shapes=[
            pltpu.VMEM((SEGS * low_width, features - HEAD_WIDTH), f32),
            pltpu.VMEM((seq_count, SEGS * low_width, held_up * batch_count), f32),
        ],
        compiler_params=pltpu.CompilerParams(vmem_limit_bytes=8 * mebibyte),
        cost_estimate=cost(4 * rows * 3 * 64 * 640, 4 * rows * features),
        name="rank_gradients",
    )(
        document_lengths, query_grad, other_query, pair_grad, other_pair, low_rank, up_blocks
    )

    rank_parts = [rank_grad]
    rank_parts += [shift(packed_grad, "seq", steps) for steps in range(1, seq_count)]
    up_sums = [
        shift(block, "seq", steps) if steps else block for steps, block in enumerate(up_split)
    ]

    chunk = 512
    token_grad = pl.pallas_call(
        functools.partial(token_kernel, weight_places),
        grid=(width // chunk,),
        out_shape=jax.ShapeDtypeStruct((rows, width), bf16),
        in_specs=[
            pl.BlockSpec((rows, part_width), lambda step: (0, 0)),
            pl.BlockSpec((features, chunk), lambda step: (0, step)),
        ]
        + [in_place()] * len(weight_parts),
        out_specs=pl.BlockSpec((rows, chunk), lambda step: (0, step)),
        scratch_shapes=[
            pltpu.VMEM((2 * joint_rank, width), bf16),
            pltpu.SemaphoreType.DMA((len(weight_parts),)),
        ],
        compiler_params=pltpu.CompilerParams(vmem_limit_bytes=12 * mebibyte),
        cost_estimate=cost(2 * rows * width * part_width, 2 * width * (part_width + rows)),
        name="token_gradient",
    )(gradients, matrix, *weight_parts)

    term_shapes = [(SEGS * joint_rank, held_down)] * 2
    up_shapes = [(SEGS * low_width, held_up)] * 2
    if not direct:
        term_shapes = [(SEGS * joint_rank, down_width)]
        up_shapes = [(SEGS * low_width, up_width)]
    terms = pl.pallas_call(
        functools.partial(down_kernel, seq_count),
        out_shape=[jax.ShapeDtypeStruct(shape, f32) for shape in term_shapes],
        in_specs=[in_smem()] + [in_vmem()] * (2 * seq_count),
        out_specs=[in_vmem()] * len(term_shapes),
        compiler_params=pltpu.CompilerParams(vmem_limit_bytes=8 * mebibyte),
        cost_estimate=cost(
            2 * seq_count * rows * SEGS * joint_rank * down_width, 2 * seq_count * rows * down_width
        ),
        name="down_terms",
    )(document_lengths, *column_parts, *rank_parts)
    ups = pl.pallas_call(
        functools.partial(up_kernel, seq_count),
        out_shape=[jax.ShapeDtypeStruct(shape, f32) for shape in up_shapes],
        in_specs=[in_vmem()] * seq_count,
        out_specs=[in_vmem()] * len(up_shapes),
        scratch_shapes=[pltpu.VMEM((SEGS * low_width, up_width), f32)] if direct else [],
        compiler_params=pltpu.CompilerParams(vmem_limit_bytes=8 * mebibyte),
        name="up_terms",
    )(*up_sums)

    if direct:
        bank_terms = [terms[0], shift(terms[1], "batch", 1), ups[0], shift(ups[1], "batch", 1)]
    else:
        down_send = jnp.transpose(
            terms[0].reshape(SEGS * joint_rank, batch_count, held_down), (1, 0, 2)
        )
        up_send = jnp.transpose(
            ups[0].reshape(SEGS * low_width, batch_count, held_up), (1, 0, 2)
        )
        back_down = lax.all_to_all(down_send, "batch", split_axis=0, concat_axis=0, tiled=True)
        back_up = lax.all_to_all(up_send, "batch", split_axis=0, concat_axis=0, tiled=True)
        bank_downs = [back_down[batch] for batch in range(batch_count)]
        bank_ups = [back_up[batch] for batch in range(batch_count)]
        bank_terms = bank_downs + bank_ups


    def whole(array):
        return pl.BlockSpec(array.shape, lambda step, bank: (0,) * array.ndim)

    term_count = len(bank_terms)
    down_grad, up_grad = pl.pallas_call(
        packed_bank_kernel if direct else functools.partial(bank_kernel, batch_count),
        out_shape=(
            jax.ShapeDtypeStruct(down_zeros.shape, f32),
            jax.ShapeDtypeStruct(up_zeros.shape, f32),
        ),
        grid_spec=pltpu.PrefetchScalarGridSpec(
            num_scalar_prefetch=1,
            grid=(batch_count * SEGS,),
            in_specs=[whole(array) for array in bank_terms] + [in_place()] * 2,
            out_specs=(
                pl.BlockSpec(
                    (1, joint_rank, 1, held_down),
                    lambda step, bank: (bank[step], 0, 0, 0),
                ),
                pl.BlockSpec(
                    (1, low_width, held_up),
                    lambda step, bank: (bank[step], 0, 0),
                ),
            ),
        ),
        input_output_aliases={1 + term_count: 0, 2 + term_count: 1},
        compiler_params=pltpu.CompilerParams(vmem_limit_bytes=16 * mebibyte),
        name="bank_rows",
    )(
        bank_rows,
        *bank_terms,
        down_zeros,
        up_zeros,
    )
    return (attention[None], token_grad[None], down_grad, up_grad)


def solution(mesh):
    in_specs = (
        P(("groups", "batch"), "seq", "tp"),
        P("seq", "tp"),
        P(None, None, "tp", ("seq", "batch")),
        P(None, None, ("seq", "batch")),
        P(),
        P("groups", None),
        P("groups", None),
        P(("groups", "batch"), ("seq", "tp"), None),
    )
    out_specs = (
        P(("groups", "batch"), ("seq", "tp"), None),
        P(("groups", "batch"), "seq", "tp"),
        P("groups", None, "tp", ("seq", "batch")),
        P("groups", None, ("seq", "batch")),
    )
    return jax.shard_map(shards, mesh=mesh, in_specs=in_specs, out_specs=out_specs, check_vma=False)
```

```python
import functools

import jax
import jax.numpy as jnp
from jax import lax
from jax.experimental import pallas as pl
from jax.experimental.pallas import tpu as pltpu
from jax.sharding import PartitionSpec as P

QHEADS = 4
HEAD_WIDTH = 128
ADAPTER_RANK = 32
SEGS = 3

adapter_scale = 2.0
rope_base = 5000000.0
masked_score = -1e30
mebibyte = 1024 * 1024


def shift(value, axis, steps):
    count = lax.axis_size(axis)
    return lax.ppermute(value, axis, [(at, (at + steps) % count) for at in range(count)])


def push(value, axis, steps):
    count = lax.axis_size(axis)
    pairs = [(at, at + steps) for at in range(count) if 0 <= at + steps < count]
    return lax.ppermute(value, axis, pairs)


def dot_nt(left, right):
    return lax.dot_general(
        left, right, (((1,), (1,)), ((), ())), preferred_element_type=jnp.float32
    )


def dot_nn(left, right):
    return jnp.dot(left, right, preferred_element_type=jnp.float32)


def dot_tn(left, right):
    return lax.dot_general(
        left, right, (((0,), (0,)), ((), ())), preferred_element_type=jnp.float32
    )


def lookup_rows(adapter_bank_row, document_adapter):
    matches = document_adapter[..., None] == jnp.arange(adapter_bank_row.shape[0], dtype=jnp.int32)
    return jnp.sum(jnp.where(matches, adapter_bank_row, 0), axis=-1)


def row_positions(first, count):
    return first + lax.broadcasted_iota(jnp.int32, (count, 1), 0)


def ring_index(index, count):
    return lax.rem(index + count, count)


def kernel_marks(lengths):
    batch = lax.axis_index("batch")
    first_end = lengths[batch, 0]
    return first_end, first_end + lengths[batch, 1]


def row_segments(ends, positions):
    return (positions >= ends[0]).astype(jnp.int32) + (positions >= ends[1]).astype(jnp.int32)


def cost(flops, bytes_accessed, transcendentals=0):
    return pl.CostEstimate(
        flops=flops, bytes_accessed=bytes_accessed, transcendentals=transcendentals
    )


def in_vmem():
    return pl.BlockSpec(memory_space=pltpu.VMEM)


def in_smem():
    return pl.BlockSpec(memory_space=pltpu.SMEM)


def by_block(shape):
    return pl.BlockSpec(shape, lambda: (0,) * len(shape))


def in_place():
    return pl.BlockSpec(memory_space=pl.ANY)


def fetch(piece, target, place, semaphore):
    height, width = piece.shape
    row, column = place()
    copy = pltpu.make_async_copy(
        piece,
        target.at[
            pl.ds(pl.multiple_of(row, 16), height), pl.ds(pl.multiple_of(column, 128), width)
        ],
        semaphore,
    )
    copy.start()
    return copy


def frozen_place(seq_count, rows, share, behind, batch_step, group_step):
    def place():
        holder = ring_index(lax.axis_index("seq") - behind, seq_count)
        if share is None:
            return holder * rows, 0
        batch = lax.rem(lax.axis_index("batch") + batch_step, 2)
        group = lax.rem(lax.axis_index("groups") + group_step, 2)
        return holder * rows, (group * 2 + batch) * share

    return place


def down_place(seq_count, features, width, behind):
    def place():
        return features, ring_index(lax.axis_index("seq") - behind, seq_count) * width

    return place


def whole_place(row):
    def place():
        return row, 0

    return place


def join_kernel(before, after, *refs):
    plane = refs[-1]
    rows = before.shape[0]
    plane[:rows] = before[...]
    plane[rows:] = after[...]


def block_kernel(own_down, far_down, down):
    ahead = lax.axis_index("batch") == 0
    joint_rank, held = own_down.shape[1:]
    for document in range(SEGS):
        rows = slice(document * joint_rank, (document + 1) * joint_rank)
        down[rows, :held] = jnp.where(ahead, own_down[document], far_down[document])
        down[rows, held:] = jnp.where(ahead, far_down[document], own_down[document])


def target_of(steps, seq_count):
    target = ring_index(lax.axis_index("seq") + steps - seq_count, seq_count)
    return target, (target >= seq_count // 2).astype(jnp.int32)


def pack_kernel(unused, down, *refs):
    payloads = refs[unused:]
    joint_rank = down.shape[0] // SEGS
    for steps, payload in enumerate(payloads):
        target, first = target_of(steps, len(payloads))
        start = pl.multiple_of(first * joint_rank, joint_rank)
        payload[...] = down[pl.ds(start, 2 * joint_rank)]


def cut_kernel(unused, steps_of, seq_count, tokens, own_up, far_up, *refs):
    blocks, up = refs[unused:-1], refs[-1]
    ahead = lax.axis_index("batch") == 0
    low_width, held_up = own_up.shape[1:]
    for document in range(SEGS):
        up[document, :, :held_up] = jnp.where(ahead, own_up[document], far_up[document])
        up[document, :, held_up:] = jnp.where(ahead, far_up[document], own_up[document])
    rows = tokens.shape[0]
    half = low_width // 2
    for steps, block in zip(steps_of, blocks):
        target, first = target_of(steps, seq_count)
        width = block.shape[1]
        block[:rows] = tokens[:, pl.ds(pl.multiple_of(target * width, 128), width)]
        slot = width // 4
        for index in range(2):
            rows_up = up[first + index]
            for part in range(2):
                column = (2 * index + part) * slot
                block[rows:, column : column + 2 * held_up] = rows_up[
                    part * half : (part + 1) * half
                ]


def low_kernel(seq_count, lengths, down, *refs):
    columns, (own, *sends) = refs[:seq_count], refs[seq_count:]
    joint_rank = down.shape[0] // SEGS
    rows = own.shape[0]
    ends = kernel_marks(lengths)
    for behind in range(seq_count):
        holder = ring_index(lax.axis_index("seq") - behind, seq_count)
        first = (holder >= seq_count // 2).astype(jnp.int32)
        second = row_segments(ends, row_positions(holder * rows, rows)) != first
        start = pl.multiple_of(first * joint_rank, joint_rank)
        values = columns[behind][:rows]
        first_low = dot_nt(values, down[pl.ds(start, joint_rank)])
        start = pl.multiple_of(start + joint_rank, joint_rank)
        second_low = dot_nt(values, down[pl.ds(start, joint_rank)])
        low = jnp.where(second, second_low, first_low)
        if behind == 0:
            own[...] = low
        else:
            sends[behind - 1][:, :joint_rank] = low[: rows // 2]
            sends[behind - 1][:, joint_rank:] = low[rows // 2 :]


def assemble_up(seq_count, arrived, up_blocks):
    low_width = up_blocks.shape[1] // 2
    query_columns = QHEADS * HEAD_WIDTH
    seq_index = lax.axis_index("seq")
    first = (seq_index >= seq_count // 2).astype(jnp.int32)
    held = up_blocks.shape[2] // seq_count
    half, slot = low_width // 2, arrived.shape[2] // 4
    up_blocks[...] = jnp.zeros_like(up_blocks)
    for holder in range(seq_count):
        block = arrived[ring_index(seq_index - holder, seq_count)]
        start, stop = holder * held, (holder + 1) * held
        middle = min(max(query_columns, start), stop)
        for index in range(2):
            for part in range(2):
                offset = (2 * index + part) * slot
                if middle > start:
                    up_blocks[first + index, part * half : (part + 1) * half, start:middle] = block[
                        :, offset : offset + middle - start
                    ]
                if stop > middle:
                    low = low_width + part * half
                    up_blocks[first + index, low : low + half, middle:stop] = block[
                        :, offset + middle - start : offset + held
                    ]


def project_kernel(array_count, entries, up_entries, low_count, seq_count, tokens, *refs):
    arrays, lows = refs[:array_count], refs[array_count : array_count + low_count]
    refs = refs[array_count + low_count :]
    part, matrix = refs[:2]
    frozen, semaphore = refs[-2:]
    copies = []
    for number, start, height, place in entries:
        piece = arrays[number].at[pl.ds(start, height)]
        copies.append(fetch(piece, frozen, place, semaphore.at[len(copies)]))
    for number, start, slot in up_entries:
        copy = pltpu.make_async_copy(
            arrays[number].at[pl.ds(start, refs[3].shape[1])],
            refs[3].at[slot],
            semaphore.at[len(copies)],
        )
        copy.start()
        copies.append(copy)
    for copy in copies:
        copy.wait()
    keep = pltpu.make_async_copy(frozen, matrix, semaphore.at[len(copies)])
    keep.start()
    features, rows = frozen.shape[0], tokens.shape[0]
    part[:, :features] = dot_nt(tokens[...], frozen[...])
    joint_rank = 2 * ADAPTER_RANK
    middle = features + joint_rank
    total = lows[0][...]
    if low_count > 1:
        upper = sum(low[:, :joint_rank] for low in lows[1:])
        lower = sum(low[:, joint_rank:] for low in lows[1:])
        total = total + jnp.concatenate([upper, lower], axis=0)
    part[:, features:middle] = total
    part[:, middle:] = jnp.zeros_like(total)
    if up_entries:
        assemble_up(seq_count, refs[3], refs[2])
    keep.wait()


def rotated(values, cosines, sines):
    return values * cosines + pltpu.roll(values, values.shape[1] // 2, 1) * sines


def qkv_kernel(unused, lengths, mine, theirs, up_blocks, cosines, sines, *refs):
    queries, pairs, low_rank = refs[unused:]
    rows = mine.shape[0]
    own_rows = queries.shape[0] // QHEADS
    query_columns = QHEADS * HEAD_WIDTH
    value_start = query_columns + HEAD_WIDTH
    features = value_start + HEAD_WIDTH
    middle = features + low_rank.shape[1]
    ends = kernel_marks(lengths)
    first_row = lax.axis_index("seq") * rows
    segments = row_segments(ends, row_positions(first_row, rows))
    low = (mine[:, features:middle] + theirs[:, features:middle]).astype(jnp.bfloat16)
    low_rank[...] = low
    value_delta = jnp.zeros((rows, HEAD_WIDTH), jnp.float32)
    for document in range(SEGS):
        chosen = jnp.where(segments == document, low, jnp.zeros_like(low))
        value_delta += dot_nn(chosen, up_blocks[document, :, query_columns:])
    keys = mine[:, query_columns:value_start] + theirs[:, query_columns:value_start]
    pairs[:, :HEAD_WIDTH] = rotated(keys, cosines[...], sines[...]).astype(jnp.bfloat16)
    values = mine[:, value_start:features] + theirs[:, value_start:features]
    pairs[:, HEAD_WIDTH:] = (values + adapter_scale * value_delta).astype(jnp.bfloat16)
    start = pl.multiple_of(lax.axis_index("tp") * own_rows, own_rows)
    own = pl.ds(start, own_rows)
    own_segments = row_segments(ends, row_positions(first_row + start, own_rows))
    own_low = (mine[own, features:middle] + theirs[own, features:middle]).astype(jnp.bfloat16)
    query_delta = jnp.zeros((own_rows, query_columns), jnp.float32)
    for document in range(SEGS):
        chosen = jnp.where(own_segments == document, own_low, jnp.zeros_like(own_low))
        query_delta += dot_nn(chosen, up_blocks[document, :, :query_columns])
    projected = mine[own, :query_columns] + theirs[own, :query_columns]
    projected = projected + adapter_scale * query_delta
    for head in range(QHEADS):
        turned = rotated(
            projected[:, head * HEAD_WIDTH : (head + 1) * HEAD_WIDTH], cosines[own], sines[own]
        )
        queries[head * own_rows : (head + 1) * own_rows] = turned.astype(jnp.bfloat16)


def attention_kernel(block_count, unused, lengths, queries, incoming, cosines, sines, *refs):
    blocks = refs[:block_count]
    output, query_grad, kept, sent, low_probs = refs[block_count + unused :]
    own_rows, query_columns = incoming.shape
    rows = blocks[0].shape[0]
    score_scale = HEAD_WIDTH ** (-0.5)
    ends = kernel_marks(lengths)
    seq_index, tp_index = lax.axis_index("seq"), lax.axis_index("tp")
    positions = row_positions(seq_index * rows + tp_index * own_rows, own_rows)
    positions = jnp.concatenate([positions] * QHEADS, axis=0)
    segments = row_segments(ends, positions)
    starts = jnp.where(segments == 0, 0, jnp.where(segments == 1, ends[0], ends[1]))
    scores = []
    for back, block in enumerate(blocks):
        key_positions = (seq_index - back) * rows + lax.broadcasted_iota(jnp.int32, (1, rows), 1)
        allowed = (key_positions <= positions) & (key_positions >= starts)
        block_scores = dot_nt(queries[...], block[:, :HEAD_WIDTH]) * score_scale
        scores.append(jnp.where(allowed, block_scores, masked_score))
    row_max = functools.reduce(
        jnp.maximum, [jnp.max(part, axis=1, keepdims=True) for part in scores]
    )
    raised = [jnp.exp(part - row_max) for part in scores]
    row_total = sum(jnp.sum(part, axis=1, keepdims=True) for part in raised)
    inverse = 1.0 / row_total
    probs = [part * inverse for part in raised]
    weighted = jnp.zeros((QHEADS * own_rows, HEAD_WIDTH), jnp.float32)
    for back, block in enumerate(blocks):
        low_probs[back] = probs[back].astype(jnp.bfloat16)
        weighted += dot_nn(low_probs[back], block[:, HEAD_WIDTH:])
    attended = weighted.astype(jnp.bfloat16)
    gradients = jnp.concatenate(
        [incoming[:, head * HEAD_WIDTH : (head + 1) * HEAD_WIDTH] for head in range(QHEADS)],
        axis=0,
    )
    row_delta = jnp.sum(
        gradients.astype(jnp.float32) * attended.astype(jnp.float32), axis=1, keepdims=True
    )
    start = pl.multiple_of(tp_index * own_rows, own_rows)
    total = jnp.zeros((QHEADS * own_rows, HEAD_WIDTH), jnp.float32)
    for back, block in enumerate(blocks):
        prob_grad = dot_nt(gradients, block[:, HEAD_WIDTH:])
        score_grad = (probs[back] * (prob_grad - row_delta)).astype(jnp.bfloat16)
        total += dot_nn(score_grad, block[:, :HEAD_WIDTH])
        key_part = dot_tn(score_grad, queries[...]) * score_scale
        value_part = dot_tn(low_probs[back], gradients)
        mine = tp_index == 0
        kept[back, :, :HEAD_WIDTH] = jnp.where(mine, key_part[:own_rows], key_part[own_rows:])
        sent[back, :, :HEAD_WIDTH] = jnp.where(mine, key_part[own_rows:], key_part[:own_rows])
        kept[back, :, HEAD_WIDTH:] = jnp.where(mine, value_part[:own_rows], value_part[own_rows:])
        sent[back, :, HEAD_WIDTH:] = jnp.where(mine, value_part[own_rows:], value_part[:own_rows])
    own = pl.ds(start, own_rows)
    for head in range(QHEADS):
        picked = slice(head * own_rows, (head + 1) * own_rows)
        columns = slice(head * HEAD_WIDTH, (head + 1) * HEAD_WIDTH)
        output[:, columns] = attended[picked]
        query_grad[:, columns] = rotated(
            total[picked] * score_scale, cosines[own], -sines[own]
        ).astype(jnp.bfloat16)


def sum_kernel(kept, arrived, *sums):
    for back, total in enumerate(sums):
        total[...] = kept[back] + arrived[back]


def pair_kernel(terms, cosines, sines, *refs):
    parts, pair = refs[:terms], refs[-1]
    own_rows = pair.shape[0]
    total = sum(part[...] for part in parts)
    own = pl.ds(pl.multiple_of(lax.axis_index("tp") * own_rows, own_rows), own_rows)
    keys = rotated(total[:, :HEAD_WIDTH], cosines[own], -sines[own])
    pair[:, :HEAD_WIDTH] = keys.astype(jnp.bfloat16)
    pair[:, HEAD_WIDTH:] = total[:, HEAD_WIDTH:].astype(jnp.bfloat16)


def rank_kernel(
    seq_count, lengths, own_query, other_query, own_pair, other_pair, low_rank, up_blocks, *refs
):
    gradients, rank_grad, packed_grad = refs[:3]
    split_terms, (terms, blocks) = refs[3:-2], refs[-2:]
    own_rows, query_columns = own_query.shape
    rows = low_rank.shape[0]
    seq_index = lax.axis_index("seq")
    start = pl.multiple_of(lax.axis_index("tp") * own_rows, own_rows)
    other = pl.multiple_of(own_rows - start, own_rows)
    gradients[pl.ds(start, own_rows), :query_columns] = own_query[...]
    gradients[pl.ds(other, own_rows), :query_columns] = other_query[...]
    value_start = query_columns + HEAD_WIDTH
    features = value_start + HEAD_WIDTH
    gradients[pl.ds(start, own_rows), query_columns:features] = own_pair[...]
    gradients[pl.ds(other, own_rows), query_columns:features] = other_pair[...]
    query_grad = gradients[:, :query_columns]
    value_grad = gradients[:, value_start:features]
    low = low_rank[...]
    rank = low.shape[1] // 2
    segments = row_segments(kernel_marks(lengths), row_positions(seq_index * rows, rows))
    total = jnp.zeros((rows, low.shape[1]), jnp.float32)
    for document in range(SEGS):
        member = segments == document
        parts = dot_nt(query_grad, up_blocks[document, :, :query_columns])
        parts += dot_nt(value_grad, up_blocks[document, :, query_columns:])
        total = jnp.where(member, parts, total)
        chosen = jnp.where(member, low, jnp.zeros_like(low))
        query_terms = dot_tn(chosen, query_grad)
        value_terms = dot_tn(chosen, value_grad)
        place = slice(document * rank, (document + 1) * rank)
        terms[place, :query_columns] = adapter_scale * query_terms[:rank]
        terms[place, query_columns:] = adapter_scale * value_terms[rank:]
    turned = (adapter_scale * total).astype(jnp.bfloat16)
    rank_grad[...] = turned
    packed_grad[:, : low.shape[1]] = turned[: rows // 2]
    packed_grad[:, low.shape[1] :] = turned[rows // 2 :]
    second = segments != (seq_index >= seq_count // 2).astype(jnp.int32)
    nothing = jnp.zeros_like(turned)
    middle = features + low.shape[1]
    gradients[:, features:middle] = jnp.where(second, nothing, turned)
    gradients[:, middle:] = jnp.where(second, turned, nothing)
    held = blocks.shape[2]
    for holder in range(seq_count):
        blocks[holder] = terms[:, holder * held : (holder + 1) * held]
    for steps, block in enumerate(split_terms):
        mine = blocks[ring_index(seq_index + steps - seq_count, seq_count)]
        if block.shape == mine.shape:
            block[...] = mine
            continue
        tail = held - 128
        count = 128 // tail
        height = mine.shape[0] // count
        block[: mine.shape[0]] = mine[:, :128]
        for part in range(count):
            block[mine.shape[0] :, part * tail : (part + 1) * tail] = mine[
                part * height : (part + 1) * height, 128:
            ]


def token_kernel(places, gradients, matrix, *refs):
    weights, (token_grad, down, semaphore) = refs[:-3], refs[-3:]
    step = pl.program_id(0)
    width = token_grad.shape[1]

    @pl.when(step == 0)
    def load():
        copies = [
            fetch(piece, down, place, semaphore.at[number])
            for number, (piece, place) in enumerate(zip(weights, places))
        ]
        for copy in copies:
            copy.wait()

    features = matrix.shape[0]
    total = dot_nn(gradients[:, :features], matrix[...])
    columns = pl.ds(pl.multiple_of(step * width, 128), width)
    total += dot_nn(gradients[:, features:], down[:, columns])
    token_grad[...] = total.astype(jnp.bfloat16)


def down_kernel(block_count, lengths, *refs):
    columns, ranks = refs[:block_count], refs[block_count : 2 * block_count]
    outputs = refs[2 * block_count + 1 :]
    rows, joint_rank = ranks[0].shape
    ends = kernel_marks(lengths)
    lows = [ranks[0][...]]
    for part in ranks[1:]:
        lows.append(jnp.concatenate([part[:, :joint_rank], part[:, joint_rank:]], axis=0))
    all_terms = []
    for document in range(SEGS):
        total = jnp.zeros((joint_rank, columns[0].shape[1]), jnp.float32)
        for behind in range(block_count):
            holder = ring_index(lax.axis_index("seq") - behind, block_count)
            segments = row_segments(ends, row_positions(holder * rows, rows))
            chosen = jnp.where(segments == document, lows[behind], jnp.zeros_like(lows[behind]))
            total += dot_tn(chosen, columns[behind][:rows])
        all_terms.append(total)
    down_terms = jnp.concatenate(all_terms, axis=0)
    if len(outputs) == 1:
        outputs[0][...] = down_terms
        return
    own_down, far_down = outputs
    held = own_down.shape[1]
    ahead = lax.axis_index("batch") == 0
    own_down[...] = jnp.where(ahead, down_terms[:, :held], down_terms[:, held:])
    far_down[...] = jnp.where(ahead, down_terms[:, held:], down_terms[:, :held])


def up_kernel(block_count, *refs):
    up_parts, outputs = refs[:block_count], refs[block_count:]
    if len(outputs) == 1:
        outputs[0][...] = sum(part[...] for part in up_parts)
        return
    own_up, far_up, up_terms = outputs
    up_rows, up_width = up_terms.shape
    tail = up_width - 128
    height = up_rows // (128 // tail)
    up_terms[...] = up_parts[0][...]
    for part in up_parts[1:]:
        up_terms[:, :128] += part[:up_rows]
        for piece in range(128 // tail):
            up_terms[piece * height : (piece + 1) * height, 128:] += part[
                up_rows:, piece * tail : (piece + 1) * tail
            ]
    held_up = own_up.shape[1]
    ahead = lax.axis_index("batch") == 0
    left, right = up_terms[:, :held_up], up_terms[:, held_up:]
    own_up[...] = jnp.where(ahead, left, right)
    far_up[...] = jnp.where(ahead, right, left)


def packed_bank_kernel(
    bank_rows, own_down, far_down, own_up, far_up, down_zeros, up_zeros, down_out, up_out
):
    step = pl.program_id(0)
    joint_rank, low_width = down_out.shape[1], up_out.shape[1]
    down_total = jnp.zeros((joint_rank, down_out.shape[3]), jnp.float32)
    up_total = jnp.zeros((low_width, up_out.shape[2]), jnp.float32)
    for block, (down, up) in enumerate(((own_down, own_up), (far_down, far_up))):
        for document in range(SEGS):
            same = bank_rows[block * SEGS + document] == bank_rows[step]
            rows = slice(document * joint_rank, (document + 1) * joint_rank)
            lows = slice(document * low_width, (document + 1) * low_width)
            down_total += jnp.where(same, down[rows], 0.0)
            up_total += jnp.where(same, up[lows], 0.0)
    down_out[0, :, 0, :] = down_total
    up_out[0] = up_total


def bank_kernel(block_count, bank_rows, *refs):
    down_terms = refs[:block_count]
    up_terms = refs[block_count : 2 * block_count]
    down_out, up_out = refs[2 * block_count + 2 :]
    step = pl.program_id(0)
    row = bank_rows[step]
    joint_rank = down_out.shape[1]
    low_width = up_out.shape[1]
    down_total = jnp.zeros((joint_rank, down_out.shape[3]), jnp.float32)
    up_total = jnp.zeros((low_width, up_out.shape[2]), jnp.float32)
    for block in range(block_count):
        for document in range(SEGS):
            same = bank_rows[block * SEGS + document] == row
            down_rows = down_terms[block][document * joint_rank : (document + 1) * joint_rank]
            up_rows = up_terms[block][document * low_width : (document + 1) * low_width]
            down_total += jnp.where(same, down_rows, 0.0)
            up_total += jnp.where(same, up_rows, 0.0)
    down_out[0, :, 0, :] = down_total
    up_out[0] = up_total


def shards(
    tokens,
    frozen_qkv_matrix,
    adapter_down_weight,
    adapter_up_weight,
    adapter_bank_row,
    document_lengths,
    document_adapter,
    output_gradient,
):
    seq_count = lax.axis_size("seq")
    batch_count = lax.axis_size("batch")
    group_count = lax.axis_size("groups")
    chip_size = lax.axis_size("tp")
    seq_index = lax.axis_index("seq")
    batch_index = lax.axis_index("batch")
    group_index = lax.axis_index("groups")
    tp_index = lax.axis_index("tp")
    local_tokens = tokens[0]
    rows, width = local_tokens.shape
    own_rows = rows // chip_size
    query_columns = QHEADS * HEAD_WIDTH
    frozen_rows = frozen_qkv_matrix.shape[0]
    features = frozen_rows * seq_count
    low_width = ADAPTER_RANK
    joint_rank = adapter_down_weight.shape[1]
    adapters = adapter_bank_row.shape[0]
    bf16 = jnp.bfloat16
    f32 = jnp.float32

    lengths = lax.dynamic_index_in_dim(document_lengths, batch_index, 0, keepdims=False)
    first_end = lengths[0]
    second_end = first_end + lengths[1]
    half_count = seq_count // 2
    held_down = adapter_down_weight.shape[3]
    held_up = adapter_up_weight.shape[2]
    down_width = held_down * batch_count
    up_width = held_up * batch_count

    positions = seq_index * rows + jnp.arange(rows, dtype=jnp.int32)
    inside = positions - jnp.where(
        positions >= second_end, second_end, jnp.where(positions >= first_end, first_end, 0)
    )
    exponent = jnp.arange(HEAD_WIDTH // 2, dtype=f32) * (2.0 / HEAD_WIDTH)
    inverse = jnp.power(jnp.float32(rope_base), -exponent)
    angles = inside.astype(f32)[:, None] * jnp.concatenate([inverse, inverse])[None, :]
    signs = jnp.where(jnp.arange(HEAD_WIDTH) < HEAD_WIDTH // 2, -1.0, 1.0).astype(f32)
    cosines = jnp.cos(angles)
    sines = jnp.sin(angles) * signs[None, :]

    sample_rows = lookup_rows(adapter_bank_row, document_adapter)
    bank_rows = sample_rows.reshape(-1)
    if batch_count == 2:
        own_bank = jnp.where(batch_index == 0, sample_rows[0], sample_rows[1])
        far_bank = jnp.where(batch_index == 0, sample_rows[1], sample_rows[0])
        bank_rows = jnp.concatenate([own_bank, far_bank])
    down_bank = adapter_down_weight[:, :, 0, :]
    down_zeros = jnp.zeros((adapters, joint_rank, 1, held_down), f32)
    up_zeros = jnp.zeros((adapters, low_width, held_up), f32)

    plane_count = group_count * batch_count
    share = width // plane_count
    padded_down = (held_down + 127) // 128 * 128
    direct = (
        group_count == 2
        and seq_count == 4
        and share == down_width
        and batch_count == 2
        and share % 128 == 0
        and down_width % 128 == 0
        and frozen_rows % 16 == 0
        and 4 * up_width <= down_width
        and up_width > 128
        and 128 % (up_width - 128) == 0
        and 0 < held_up + held_down - padded_down <= padded_down - held_down
    )
    up_entries = []
    if direct:
        own_share = lax.dynamic_slice_in_dim(
            frozen_qkv_matrix, (group_index * batch_count + batch_index) * share, share, axis=1
        )
        before = shift(own_share, "seq", 1)
        after = shift(own_share, "seq", 3)
        far_down = shift(down_bank[far_bank], "batch", 1)
        far_up = shift(adapter_up_weight[far_bank], "batch", 1)
        own_down, own_up = down_bank[own_bank], adapter_up_weight[own_bank]
        down_block = pl.pallas_call(
            block_kernel,
            out_shape=jax.ShapeDtypeStruct((SEGS * joint_rank, down_width), bf16),
            in_specs=[in_vmem()] * 2,
            out_specs=in_vmem(),
            compiler_params=pltpu.CompilerParams(vmem_limit_bytes=8 * mebibyte),
            cost_estimate=cost(0, 4 * SEGS * joint_rank * down_width),
            name="down_block",
        )(own_down, far_down)
        plane = pl.pallas_call(
            join_kernel,
            out_shape=jax.ShapeDtypeStruct((2 * frozen_rows, share), bf16),
            in_specs=[in_vmem()] * 2,
            out_specs=in_vmem(),
            compiler_params=pltpu.CompilerParams(vmem_limit_bytes=8 * mebibyte),
            cost_estimate=cost(0, 8 * frozen_rows * share),
            name="join",
        )(before, after)

        def over_plane(value):
            over_both = [(at, plane_count - 1 - at) for at in range(plane_count)]
            return [
                shift(value, "batch", 1),
                shift(value, "groups", 1),
                lax.ppermute(value, ("groups", "batch"), over_both),
            ]

        plane_parts = over_plane(plane)
        middle = shift(before, "seq", 1)
        middle_parts = over_plane(middle)

        block_rows = rows + low_width // 2

        def cut_columns(steps_of, early):
            blocks = pl.pallas_call(
                functools.partial(cut_kernel, len(early), steps_of, seq_count),
                out_shape=[jax.ShapeDtypeStruct((block_rows, down_width), bf16)] * len(steps_of),
                in_specs=[in_vmem()] * 3 + [in_place()] * len(early),
                out_specs=[by_block((block_rows, down_width))] * len(steps_of),
                scratch_shapes=[pltpu.VMEM((SEGS, low_width, 2 * held_up), bf16)],
                compiler_params=pltpu.CompilerParams(vmem_limit_bytes=16 * mebibyte),
                cost_estimate=cost(0, len(steps_of) * rows * width),
                name="cut",
            )(local_tokens, own_up, far_up, *early)
            return [
                shift(block, "seq", steps) if steps else block
                for steps, block in zip(steps_of, blocks)
            ]

        near_before, near_after = cut_columns((1, 3), [plane, down_block])
        own_columns, far_columns = cut_columns(
            (0, 2),
            [near_before, *plane_parts, down_zeros, up_zeros, cosines, sines, bank_rows],
        )
        column_parts = [own_columns, near_before, far_columns, near_after]
        low_shapes = [(rows, joint_rank)] + [(rows // 2, 2 * joint_rank)] * (seq_count - 1)
        lows = pl.pallas_call(
            functools.partial(low_kernel, seq_count),
            out_shape=[jax.ShapeDtypeStruct(shape, f32) for shape in low_shapes],
            in_specs=[in_smem()] + [in_vmem()] * (1 + seq_count),
            out_specs=[in_vmem()] * seq_count,
            compiler_params=pltpu.CompilerParams(vmem_limit_bytes=8 * mebibyte),
            cost_estimate=cost(
                4 * seq_count * rows * joint_rank * down_width, 2 * seq_count * rows * down_width
            ),
            name="low",
        )(document_lengths, down_block, *column_parts)
        lows = [lows[0]] + [
            shift(low, "seq", seq_count - 1 - steps) for steps, low in enumerate(lows[1:])
        ]
        arrays = [frozen_qkv_matrix, before, after, middle] + plane_parts + middle_parts
        arrays += column_parts

        def frozen_at(behind, batch_step, group_step):
            return frozen_place(seq_count, frozen_rows, share, behind, batch_step, group_step)

        entries = [
            (0, 0, frozen_rows, frozen_place(seq_count, frozen_rows, None, 0, 0, 0)),
            (1, 0, frozen_rows, frozen_at(1, 0, 0)),
            (2, 0, frozen_rows, frozen_at(3, 0, 0)),
            (3, 0, frozen_rows, frozen_at(2, 0, 0)),
        ]
        for number, (batch_step, group_step) in enumerate(((1, 0), (0, 1), (1, 1))):
            entries += [
                (4 + number, 0, frozen_rows, frozen_at(1, batch_step, group_step)),
                (4 + number, frozen_rows, frozen_rows, frozen_at(3, batch_step, group_step)),
                (7 + number, 0, frozen_rows, frozen_at(2, batch_step, group_step)),
            ]
        up_entries = [(10 + behind, rows, behind) for behind in range(seq_count)]
    else:
        bank_rows = sample_rows.reshape(-1)
        got_down = lax.all_to_all(
            down_bank[sample_rows], "batch", split_axis=0, concat_axis=0, tiled=True
        )
        got_up = lax.all_to_all(
            adapter_up_weight[sample_rows], "batch", split_axis=0, concat_axis=0, tiled=True
        )
        down_block = jnp.transpose(got_down, (1, 2, 0, 3)).reshape(SEGS * joint_rank, -1)
        up_block = jnp.transpose(got_up, (1, 2, 0, 3)).reshape(SEGS * low_width, -1)
        all_down = lax.all_gather(down_block, "seq", axis=0)
        all_up = lax.all_gather(up_block, "seq", axis=0)
        first = (seq_index >= half_count).astype(jnp.int32)
        merged = jnp.transpose(all_down, (1, 0, 2)).reshape(SEGS * joint_rank, -1)
        pair_rows = lax.dynamic_slice_in_dim(merged, first * joint_rank, 2 * joint_rank)
        arrays = [lax.all_gather(frozen_qkv_matrix, "seq", axis=0, tiled=True)]
        entries = [(0, 0, features, whole_place(0))]
        both_lows = lax.dot_general(
            local_tokens, pair_rows, (((1,), (1,)), ((), ())), preferred_element_type=f32
        )
        segments = (positions >= first_end).astype(jnp.int32) + (positions >= second_end)
        lows = [
            jnp.where(
                (segments == first)[:, None], both_lows[:, :joint_rank], both_lows[:, joint_rank:]
            )
        ]
        weight_parts, weight_places = [pair_rows], [whole_place(0)]
        up_rows = jnp.transpose(all_up, (1, 0, 2)).reshape(SEGS, low_width, -1)
        is_query = jnp.arange(up_rows.shape[2]) < query_columns
        up_blocks = jnp.concatenate(
            [
                jnp.where(is_query[None, None, :], up_rows, 0),
                jnp.where(is_query[None, None, :], 0, up_rows),
            ],
            axis=1,
        )
        column_blocks = [
            lax.dynamic_slice_in_dim(
                local_tokens,
                jnp.remainder(seq_index + steps, seq_count) * down_width,
                down_width,
                axis=1,
            )
            for steps in range(seq_count)
        ]

    if not direct:
        column_parts = [
            shift(block, "seq", steps) if steps else block
            for steps, block in enumerate(column_blocks)
        ]
    up_shape = (SEGS, joint_rank, query_columns + HEAD_WIDTH)
    part_width = features + 2 * joint_rank
    arrived = [pltpu.VMEM((seq_count, low_width // 2, down_width), bf16)] if direct else []
    part, matrix, *built = pl.pallas_call(
        functools.partial(
            project_kernel, len(arrays), entries, up_entries, len(lows), seq_count
        ),
        out_shape=[
            jax.ShapeDtypeStruct((rows, part_width), f32),
            jax.ShapeDtypeStruct((features, width), bf16),
        ]
        + ([jax.ShapeDtypeStruct(up_shape, bf16)] if direct else []),
        in_specs=[in_vmem()] + [in_place()] * len(arrays) + [in_vmem()] * len(lows),
        out_specs=[in_vmem(), in_place()] + ([by_block(up_shape)] if direct else []),
        scratch_shapes=arrived
        + [
            pltpu.VMEM((features, width), bf16),
            pltpu.SemaphoreType.DMA((len(entries) + len(up_entries) + 1,)),
        ],
        compiler_params=pltpu.CompilerParams(vmem_limit_bytes=20 * mebibyte),
        cost_estimate=cost(2 * rows * width * features, 2 * width * (features + rows)),
        name="project",
    )(local_tokens, *arrays, *lows)
    if direct:
        up_blocks = built[0]
        payloads = pl.pallas_call(
            functools.partial(pack_kernel, 1),
            out_shape=[jax.ShapeDtypeStruct((2 * joint_rank, down_width), bf16)] * seq_count,
            in_specs=[in_vmem()] + [in_place()],
            out_specs=[by_block((2 * joint_rank, down_width))] * seq_count,
            compiler_params=pltpu.CompilerParams(vmem_limit_bytes=8 * mebibyte),
            cost_estimate=cost(0, 16 * joint_rank * down_width),
            name="pack",
        )(down_block, part)
        weight_parts = [
            shift(part, "seq", steps) if steps else part for steps, part in enumerate(payloads)
        ]
        weight_places = [down_place(seq_count, 0, down_width, steps) for steps in range(seq_count)]

    other_part = shift(part, "tp", 1)
    queries, pairs, low_rank = pl.pallas_call(
        functools.partial(qkv_kernel, 0),
        out_shape=(
            jax.ShapeDtypeStruct((QHEADS * own_rows, HEAD_WIDTH), bf16),
            jax.ShapeDtypeStruct((rows, 2 * HEAD_WIDTH), bf16),
            jax.ShapeDtypeStruct((rows, joint_rank), bf16),
        ),
        in_specs=[in_smem()] + [in_vmem()] * 5,
        out_specs=(in_vmem(),) * 3,
        compiler_params=pltpu.CompilerParams(vmem_limit_bytes=8 * mebibyte),
        cost_estimate=cost(2 * rows * 3 * 64 * 640, 8 * rows * features),
        name="qkv",
    )(document_lengths, part, other_part, up_blocks, cosines, sines)

    blocks = [pairs] + [push(pairs, "seq", back) for back in range(1, half_count + 1)]
    block_count = len(blocks)
    incoming = output_gradient[0]
    early_columns = [weight_parts[1], weight_parts[-1]] if direct else []
    attention, query_grad, kept, sent = pl.pallas_call(
        functools.partial(attention_kernel, block_count, len(early_columns)),
        out_shape=(
            jax.ShapeDtypeStruct((own_rows, query_columns), bf16),
            jax.ShapeDtypeStruct((own_rows, query_columns), bf16),
            jax.ShapeDtypeStruct((block_count, own_rows, 2 * HEAD_WIDTH), f32),
            jax.ShapeDtypeStruct((block_count, own_rows, 2 * HEAD_WIDTH), f32),
        ),
        in_specs=[in_smem()]
        + [in_vmem()] * (4 + block_count)
        + [in_place()] * len(early_columns),
        out_specs=(in_vmem(),) * 4,
        scratch_shapes=[pltpu.VMEM((block_count, QHEADS * own_rows, rows), bf16)],
        compiler_params=pltpu.CompilerParams(vmem_limit_bytes=(8 + 4 * block_count) * mebibyte),
        cost_estimate=cost(
            10 * block_count * QHEADS * own_rows * rows * HEAD_WIDTH,
            4 * rows * features,
            block_count * QHEADS * own_rows * rows,
        ),
        name="attention",
    )(document_lengths, queries, incoming, cosines, sines, *blocks, *early_columns)

    other_query = shift(query_grad, "tp", 1)
    pair_sums = pl.pallas_call(
        sum_kernel,
        out_shape=[jax.ShapeDtypeStruct((own_rows, 2 * HEAD_WIDTH), f32)] * block_count,
        in_specs=[in_vmem()] * 2,
        out_specs=[in_vmem()] * block_count,
        compiler_params=pltpu.CompilerParams(vmem_limit_bytes=8 * mebibyte),
        cost_estimate=cost(0, 12 * block_count * own_rows * 2 * HEAD_WIDTH),
        name="pair_sums",
    )(kept, shift(sent, "tp", 1))
    pair_terms = [pair_sums[0]]
    pair_terms += [push(pair_sums[back], "seq", -back) for back in range(1, block_count)]
    pair_grad = pl.pallas_call(
        functools.partial(pair_kernel, block_count),
        out_shape=jax.ShapeDtypeStruct((own_rows, 2 * HEAD_WIDTH), bf16),
        in_specs=[in_vmem()] * (2 + block_count),
        out_specs=in_vmem(),
        compiler_params=pltpu.CompilerParams(vmem_limit_bytes=8 * mebibyte),
        cost_estimate=cost(0, 12 * block_count * own_rows * 2 * HEAD_WIDTH),
        name="pair_gradients",
    )(cosines, sines, *pair_terms)
    other_pair = shift(pair_grad, "tp", 1)

    split_shapes = [(SEGS * low_width, up_width)] * seq_count
    if direct:
        sent_rows = SEGS * low_width * up_width // 128
        split_shapes[1:] = [(sent_rows, 128)] * (seq_count - 1)
    gradients, rank_grad, packed_grad, *up_split = pl.pallas_call(
        functools.partial(rank_kernel, seq_count),
        out_shape=[
            jax.ShapeDtypeStruct((rows, part_width), bf16),
            jax.ShapeDtypeStruct((rows, joint_rank), bf16),
            jax.ShapeDtypeStruct((rows // 2, 2 * joint_rank), bf16),
        ]
        + [jax.ShapeDtypeStruct(shape, f32) for shape in split_shapes],
        in_specs=[in_smem()] + [in_vmem()] * 6,
        out_specs=[by_block((rows, part_width)), in_vmem(), in_vmem()]
        + [by_block(shape) for shape in split_shapes],
        scratch_shapes=[
            pltpu.VMEM((SEGS * low_width, features - HEAD_WIDTH), f32),
            pltpu.VMEM((seq_count, SEGS * low_width, held_up * batch_count), f32),
        ],
        compiler_params=pltpu.CompilerParams(vmem_limit_bytes=8 * mebibyte),
        cost_estimate=cost(4 * rows * 3 * 64 * 640, 4 * rows * features),
        name="rank_gradients",
    )(
        document_lengths, query_grad, other_query, pair_grad, other_pair, low_rank, up_blocks
    )

    rank_parts = [rank_grad]
    rank_parts += [shift(packed_grad, "seq", steps) for steps in range(1, seq_count)]
    up_sums = [
        shift(block, "seq", steps) if steps else block for steps, block in enumerate(up_split)
    ]

    chunk = 512
    token_grad = pl.pallas_call(
        functools.partial(token_kernel, weight_places),
        grid=(width // chunk,),
        out_shape=jax.ShapeDtypeStruct((rows, width), bf16),
        in_specs=[
            pl.BlockSpec((rows, part_width), lambda step: (0, 0)),
            pl.BlockSpec((features, chunk), lambda step: (0, step)),
        ]
        + [in_place()] * len(weight_parts),
        out_specs=pl.BlockSpec((rows, chunk), lambda step: (0, step)),
        scratch_shapes=[
            pltpu.VMEM((2 * joint_rank, width), bf16),
            pltpu.SemaphoreType.DMA((len(weight_parts),)),
        ],
        compiler_params=pltpu.CompilerParams(vmem_limit_bytes=12 * mebibyte),
        cost_estimate=cost(2 * rows * width * part_width, 2 * width * (part_width + rows)),
        name="token_gradient",
    )(gradients, matrix, *weight_parts)

    term_shapes = [(SEGS * joint_rank, held_down)] * 2
    up_shapes = [(SEGS * low_width, held_up)] * 2
    if not direct:
        term_shapes = [(SEGS * joint_rank, down_width)]
        up_shapes = [(SEGS * low_width, up_width)]
    ups = pl.pallas_call(
        functools.partial(up_kernel, seq_count),
        out_shape=[jax.ShapeDtypeStruct(shape, f32) for shape in up_shapes],
        in_specs=[in_vmem()] * seq_count,
        out_specs=[in_vmem()] * len(up_shapes),
        scratch_shapes=[pltpu.VMEM((SEGS * low_width, up_width), f32)] if direct else [],
        compiler_params=pltpu.CompilerParams(vmem_limit_bytes=8 * mebibyte),
        name="up_terms",
    )(*up_sums)
    terms = pl.pallas_call(
        functools.partial(down_kernel, seq_count),
        out_shape=[jax.ShapeDtypeStruct(shape, f32) for shape in term_shapes],
        in_specs=[in_smem()] + [in_vmem()] * (2 * seq_count) + [in_place()],
        out_specs=[in_vmem()] * len(term_shapes),
        compiler_params=pltpu.CompilerParams(vmem_limit_bytes=8 * mebibyte),
        cost_estimate=cost(
            2 * seq_count * rows * SEGS * joint_rank * down_width, 2 * seq_count * rows * down_width
        ),
        name="down_terms",
    )(document_lengths, *column_parts, *rank_parts, ups[0])
    if direct:
        bank_terms = [terms[0], shift(terms[1], "batch", 1), ups[0], shift(ups[1], "batch", 1)]
    else:
        down_send = jnp.transpose(
            terms[0].reshape(SEGS * joint_rank, batch_count, held_down), (1, 0, 2)
        )
        up_send = jnp.transpose(
            ups[0].reshape(SEGS * low_width, batch_count, held_up), (1, 0, 2)
        )
        back_down = lax.all_to_all(down_send, "batch", split_axis=0, concat_axis=0, tiled=True)
        back_up = lax.all_to_all(up_send, "batch", split_axis=0, concat_axis=0, tiled=True)
        bank_downs = [back_down[batch] for batch in range(batch_count)]
        bank_ups = [back_up[batch] for batch in range(batch_count)]
        bank_terms = bank_downs + bank_ups


    def whole(array):
        return pl.BlockSpec(array.shape, lambda step, bank: (0,) * array.ndim)

    term_count = len(bank_terms)
    down_grad, up_grad = pl.pallas_call(
        packed_bank_kernel if direct else functools.partial(bank_kernel, batch_count),
        out_shape=(
            jax.ShapeDtypeStruct(down_zeros.shape, f32),
            jax.ShapeDtypeStruct(up_zeros.shape, f32),
        ),
        grid_spec=pltpu.PrefetchScalarGridSpec(
            num_scalar_prefetch=1,
            grid=(batch_count * SEGS,),
            in_specs=[whole(array) for array in bank_terms] + [in_place()] * 2,
            out_specs=(
                pl.BlockSpec(
                    (1, joint_rank, 1, held_down),
                    lambda step, bank: (bank[step], 0, 0, 0),
                ),
                pl.BlockSpec(
                    (1, low_width, held_up),
                    lambda step, bank: (bank[step], 0, 0),
                ),
            ),
        ),
        input_output_aliases={1 + term_count: 0, 2 + term_count: 1},
        compiler_params=pltpu.CompilerParams(vmem_limit_bytes=16 * mebibyte),
        name="bank_rows",
    )(
        bank_rows,
        *bank_terms,
        down_zeros,
        up_zeros,
    )
    return (attention[None], token_grad[None], down_grad, up_grad)


def solution(mesh):
    in_specs = (
        P(("groups", "batch"), "seq", "tp"),
        P("seq", "tp"),
        P(None, None, "tp", ("seq", "batch")),
        P(None, None, ("seq", "batch")),
        P(),
        P("groups", None),
        P("groups", None),
        P(("groups", "batch"), ("seq", "tp"), None),
    )
    out_specs = (
        P(("groups", "batch"), ("seq", "tp"), None),
        P(("groups", "batch"), "seq", "tp"),
        P("groups", None, "tp", ("seq", "batch")),
        P("groups", None, ("seq", "batch")),
    )
    return jax.shard_map(shards, mesh=mesh, in_specs=in_specs, out_specs=out_specs, check_vma=False)
```

```python
import functools

import jax
import jax.numpy as jnp
from jax import lax
from jax.experimental import pallas as pl
from jax.experimental.pallas import tpu as pltpu
from jax.sharding import PartitionSpec as P

QHEADS = 4
HEAD_WIDTH = 128
ADAPTER_RANK = 32
SEGS = 3

adapter_scale = 2.0
rope_base = 5000000.0
masked_score = -1e30
mebibyte = 1024 * 1024


def shift(value, axis, steps):
    count = lax.axis_size(axis)
    return lax.ppermute(value, axis, [(at, (at + steps) % count) for at in range(count)])


def push(value, axis, steps):
    count = lax.axis_size(axis)
    pairs = [(at, at + steps) for at in range(count) if 0 <= at + steps < count]
    return lax.ppermute(value, axis, pairs)


def dot_nt(left, right):
    return lax.dot_general(
        left, right, (((1,), (1,)), ((), ())), preferred_element_type=jnp.float32
    )


def dot_nn(left, right):
    return jnp.dot(left, right, preferred_element_type=jnp.float32)


def dot_tn(left, right):
    return lax.dot_general(
        left, right, (((0,), (0,)), ((), ())), preferred_element_type=jnp.float32
    )


def lookup_rows(adapter_bank_row, document_adapter):
    matches = document_adapter[..., None] == jnp.arange(adapter_bank_row.shape[0], dtype=jnp.int32)
    return jnp.sum(jnp.where(matches, adapter_bank_row, 0), axis=-1)


def row_positions(first, count):
    return first + lax.broadcasted_iota(jnp.int32, (count, 1), 0)


def ring_index(index, count):
    return lax.rem(index + count, count)


def kernel_marks(lengths):
    batch = lax.axis_index("batch")
    first_end = lengths[batch, 0]
    return first_end, first_end + lengths[batch, 1]


def row_segments(ends, positions):
    return (positions >= ends[0]).astype(jnp.int32) + (positions >= ends[1]).astype(jnp.int32)


def cost(flops, bytes_accessed, transcendentals=0):
    return pl.CostEstimate(
        flops=flops, bytes_accessed=bytes_accessed, transcendentals=transcendentals
    )


def in_vmem():
    return pl.BlockSpec(memory_space=pltpu.VMEM)


def in_smem():
    return pl.BlockSpec(memory_space=pltpu.SMEM)


def by_block(shape):
    return pl.BlockSpec(shape, lambda: (0,) * len(shape))


def in_place():
    return pl.BlockSpec(memory_space=pl.ANY)


def fetch(piece, target, place, semaphore):
    height, width = piece.shape
    row, column = place()
    copy = pltpu.make_async_copy(
        piece,
        target.at[
            pl.ds(pl.multiple_of(row, 16), height), pl.ds(pl.multiple_of(column, 128), width)
        ],
        semaphore,
    )
    copy.start()
    return copy


def frozen_place(seq_count, rows, share, behind, batch_step, group_step):
    def place():
        holder = ring_index(lax.axis_index("seq") - behind, seq_count)
        if share is None:
            return holder * rows, 0
        batch = lax.rem(lax.axis_index("batch") + batch_step, 2)
        group = lax.rem(lax.axis_index("groups") + group_step, 2)
        return holder * rows, (group * 2 + batch) * share

    return place


def down_place(seq_count, features, width, behind):
    def place():
        return features, ring_index(lax.axis_index("seq") - behind, seq_count) * width

    return place


def whole_place(row):
    def place():
        return row, 0

    return place


def pack_kernel(own_down, far_down, own_up, far_up, before, after, *refs):
    plane, forward, payloads, (down, up) = refs[0], refs[1], refs[2:-2], refs[-2:]
    ahead = lax.axis_index("batch") == 0
    joint_rank, held = own_down.shape[1:]
    low_width, held_up = own_up.shape[1:]
    frozen_rows = before.shape[0]
    plane[:frozen_rows] = before[...]
    plane[frozen_rows:] = after[...]
    forward[:frozen_rows] = before[...]
    for document in range(SEGS):
        rows = slice(document * joint_rank, (document + 1) * joint_rank)
        down[rows, :held] = jnp.where(ahead, own_down[document], far_down[document])
        down[rows, held:] = jnp.where(ahead, far_down[document], own_down[document])
        up[document, :, :held_up] = jnp.where(ahead, own_up[document], far_up[document])
        up[document, :, held_up:] = jnp.where(ahead, far_up[document], own_up[document])
    half, slot = low_width // 2, down.shape[1] // 4
    targets = [(0, payloads[0], 0), (1, forward, frozen_rows)]
    targets += [(steps + 2, payload, 0) for steps, payload in enumerate(payloads[1:])]
    seq_count = len(targets)
    for steps, payload, base in targets:
        target = ring_index(lax.axis_index("seq") + steps - seq_count, seq_count)
        first = (target >= seq_count // 2).astype(jnp.int32)
        start = pl.multiple_of(first * joint_rank, joint_rank)
        payload[base : base + 2 * joint_rank] = down[pl.ds(start, 2 * joint_rank)]
        base = base + 2 * joint_rank
        for index in range(2):
            block = up[first + index]
            for part in range(2):
                column = (2 * index + part) * slot
                payload[base : base + half, column : column + 2 * held_up] = block[
                    part * half : (part + 1) * half
                ]


def cut_kernel(unused, seq_count, tokens, payload, *refs):
    blocks = refs[unused:]
    for steps, block in enumerate(blocks):
        target = ring_index(lax.axis_index("seq") + steps - seq_count, seq_count)
        width = block.shape[1]
        rows = block.shape[0] - tokens.shape[0]
        if rows:
            block[:rows] = payload[...]
        block[rows:] = tokens[:, pl.ds(pl.multiple_of(target * width, 128), width)]


def assemble_up(seq_count, arrived, up_blocks):
    low_width = up_blocks.shape[1] // 2
    query_columns = QHEADS * HEAD_WIDTH
    seq_index = lax.axis_index("seq")
    first = (seq_index >= seq_count // 2).astype(jnp.int32)
    held = up_blocks.shape[2] // seq_count
    half, slot = low_width // 2, arrived.shape[2] // 4
    up_blocks[...] = jnp.zeros_like(up_blocks)
    for holder in range(seq_count):
        block = arrived[ring_index(seq_index - holder, seq_count)]
        start, stop = holder * held, (holder + 1) * held
        middle = min(max(query_columns, start), stop)
        for index in range(2):
            for part in range(2):
                offset = (2 * index + part) * slot
                if middle > start:
                    up_blocks[first + index, part * half : (part + 1) * half, start:middle] = block[
                        :, offset : offset + middle - start
                    ]
                if stop > middle:
                    low = low_width + part * half
                    up_blocks[first + index, low : low + half, middle:stop] = block[
                        :, offset + middle - start : offset + held
                    ]


def project_kernel(array_count, entries, up_entries, unused, seq_count, tokens, *refs):
    arrays = refs[:array_count]
    refs = refs[array_count + unused :]
    own_query, sent_query, rest, matrix = refs[:4]
    weights, semaphore = refs[-2:]
    copies = []
    for number, start, height, place in entries:
        piece = arrays[number].at[pl.ds(start, height)]
        copies.append(fetch(piece, weights, place, semaphore.at[len(copies)]))
    for number, start, slot in up_entries:
        copy = pltpu.make_async_copy(
            arrays[number].at[pl.ds(start, refs[5].shape[1])],
            refs[5].at[slot],
            semaphore.at[len(copies)],
        )
        copy.start()
        copies.append(copy)
    for copy in copies:
        copy.wait()
    keep = pltpu.make_async_copy(weights, matrix, semaphore.at[len(copies)])
    keep.start()
    part = dot_nt(tokens[...], weights[...])
    own_rows, query_columns = own_query.shape
    first = lax.axis_index("tp") == 0
    upper, lower = part[:own_rows, :query_columns], part[own_rows:, :query_columns]
    own_query[...] = jnp.where(first, upper, lower)
    sent_query[...] = jnp.where(first, lower, upper)
    rest[...] = part[:, query_columns:]
    if up_entries:
        assemble_up(seq_count, refs[5], refs[4])
    keep.wait()


def rotated(values, cosines, sines):
    return values * cosines + pltpu.roll(values, values.shape[1] // 2, 1) * sines


def qkv_kernel(
    seq_count, unused, lengths, own_query, other_query, mine, theirs, up_blocks, cosines, sines, *refs
):
    queries, pairs, low_rank = refs[unused:]
    rows, joint_rank = low_rank.shape
    own_rows, query_columns = own_query.shape
    start_low, middle = 2 * HEAD_WIDTH, 2 * HEAD_WIDTH + joint_rank
    ends = kernel_marks(lengths)

    def low_rows(picked, second):
        first_low = mine[picked, start_low:middle] + theirs[picked, start_low:middle]
        second_low = mine[picked, middle:] + theirs[picked, middle:]
        return jnp.where(second, second_low, first_low).astype(jnp.bfloat16)

    first = (lax.axis_index("seq") >= seq_count // 2).astype(jnp.int32)
    first_row = lax.axis_index("seq") * rows
    segments = row_segments(ends, row_positions(first_row, rows))
    low = low_rows(slice(None), segments != first)
    low_rank[...] = low
    value_delta = jnp.zeros((rows, HEAD_WIDTH), jnp.float32)
    for document in range(SEGS):
        chosen = jnp.where(segments == document, low, jnp.zeros_like(low))
        value_delta += dot_nn(chosen, up_blocks[document, :, query_columns:])
    keys = mine[:, :HEAD_WIDTH] + theirs[:, :HEAD_WIDTH]
    pairs[:, :HEAD_WIDTH] = rotated(keys, cosines[...], sines[...]).astype(jnp.bfloat16)
    values = mine[:, HEAD_WIDTH:start_low] + theirs[:, HEAD_WIDTH:start_low]
    pairs[:, HEAD_WIDTH:] = (values + adapter_scale * value_delta).astype(jnp.bfloat16)
    start = pl.multiple_of(lax.axis_index("tp") * own_rows, own_rows)
    own = pl.ds(start, own_rows)
    own_segments = row_segments(ends, row_positions(first_row + start, own_rows))
    own_low = low_rows(own, own_segments != first)
    query_delta = jnp.zeros((own_rows, query_columns), jnp.float32)
    for document in range(SEGS):
        chosen = jnp.where(own_segments == document, own_low, jnp.zeros_like(own_low))
        query_delta += dot_nn(chosen, up_blocks[document, :, :query_columns])
    projected = own_query[...] + other_query[...]
    projected = projected + adapter_scale * query_delta
    for head in range(QHEADS):
        turned = rotated(
            projected[:, head * HEAD_WIDTH : (head + 1) * HEAD_WIDTH], cosines[own], sines[own]
        )
        queries[head * own_rows : (head + 1) * own_rows] = turned.astype(jnp.bfloat16)


def attention_kernel(block_count, unused, lengths, queries, incoming, cosines, sines, *refs):
    blocks = refs[:block_count]
    output, query_grad, kept, sent, low_probs = refs[block_count + unused :]
    own_rows, query_columns = incoming.shape
    rows = blocks[0].shape[0]
    score_scale = HEAD_WIDTH ** (-0.5)
    ends = kernel_marks(lengths)
    seq_index, tp_index = lax.axis_index("seq"), lax.axis_index("tp")
    positions = row_positions(seq_index * rows + tp_index * own_rows, own_rows)
    positions = jnp.concatenate([positions] * QHEADS, axis=0)
    segments = row_segments(ends, positions)
    starts = jnp.where(segments == 0, 0, jnp.where(segments == 1, ends[0], ends[1]))
    scores = []
    for back, block in enumerate(blocks):
        key_positions = (seq_index - back) * rows + lax.broadcasted_iota(jnp.int32, (1, rows), 1)
        allowed = (key_positions <= positions) & (key_positions >= starts)
        block_scores = dot_nt(queries[...], block[:, :HEAD_WIDTH]) * score_scale
        scores.append(jnp.where(allowed, block_scores, masked_score))
    row_max = functools.reduce(
        jnp.maximum, [jnp.max(part, axis=1, keepdims=True) for part in scores]
    )
    raised = [jnp.exp(part - row_max) for part in scores]
    row_total = sum(jnp.sum(part, axis=1, keepdims=True) for part in raised)
    inverse = 1.0 / row_total
    probs = [part * inverse for part in raised]
    weighted = jnp.zeros((QHEADS * own_rows, HEAD_WIDTH), jnp.float32)
    for back, block in enumerate(blocks):
        low_probs[back] = probs[back].astype(jnp.bfloat16)
        weighted += dot_nn(low_probs[back], block[:, HEAD_WIDTH:])
    attended = weighted.astype(jnp.bfloat16)
    gradients = jnp.concatenate(
        [incoming[:, head * HEAD_WIDTH : (head + 1) * HEAD_WIDTH] for head in range(QHEADS)],
        axis=0,
    )
    row_delta = jnp.sum(
        gradients.astype(jnp.float32) * attended.astype(jnp.float32), axis=1, keepdims=True
    )
    start = pl.multiple_of(tp_index * own_rows, own_rows)
    total = jnp.zeros((QHEADS * own_rows, HEAD_WIDTH), jnp.float32)
    for back, block in enumerate(blocks):
        prob_grad = dot_nt(gradients, block[:, HEAD_WIDTH:])
        score_grad = (probs[back] * (prob_grad - row_delta)).astype(jnp.bfloat16)
        total += dot_nn(score_grad, block[:, :HEAD_WIDTH])
        key_part = dot_tn(score_grad, queries[...]) * score_scale
        value_part = dot_tn(low_probs[back], gradients)
        mine = tp_index == 0
        kept[back, :, :HEAD_WIDTH] = jnp.where(mine, key_part[:own_rows], key_part[own_rows:])
        sent[back, :, :HEAD_WIDTH] = jnp.where(mine, key_part[own_rows:], key_part[:own_rows])
        kept[back, :, HEAD_WIDTH:] = jnp.where(mine, value_part[:own_rows], value_part[own_rows:])
        sent[back, :, HEAD_WIDTH:] = jnp.where(mine, value_part[own_rows:], value_part[:own_rows])
    own = pl.ds(start, own_rows)
    for head in range(QHEADS):
        picked = slice(head * own_rows, (head + 1) * own_rows)
        columns = slice(head * HEAD_WIDTH, (head + 1) * HEAD_WIDTH)
        output[:, columns] = attended[picked]
        query_grad[:, columns] = rotated(
            total[picked] * score_scale, cosines[own], -sines[own]
        ).astype(jnp.bfloat16)


def sum_kernel(unused, kept, arrived, *refs):
    for back, total in enumerate(refs[unused:]):
        total[...] = kept[back] + arrived[back]


def pair_kernel(terms, cosines, sines, *refs):
    parts, pair = refs[:terms], refs[-1]
    own_rows = pair.shape[0]
    total = sum(part[...] for part in parts)
    own = pl.ds(pl.multiple_of(lax.axis_index("tp") * own_rows, own_rows), own_rows)
    keys = rotated(total[:, :HEAD_WIDTH], cosines[own], -sines[own])
    pair[:, :HEAD_WIDTH] = keys.astype(jnp.bfloat16)
    pair[:, HEAD_WIDTH:] = total[:, HEAD_WIDTH:].astype(jnp.bfloat16)


def rank_kernel(
    seq_count, lengths, own_query, other_query, own_pair, other_pair, low_rank, up_blocks, *refs
):
    gradients, rank_grad = refs[:2]
    split_terms, (terms, blocks) = refs[2:-2], refs[-2:]
    own_rows, query_columns = own_query.shape
    rows = low_rank.shape[0]
    seq_index = lax.axis_index("seq")
    start = pl.multiple_of(lax.axis_index("tp") * own_rows, own_rows)
    other = pl.multiple_of(own_rows - start, own_rows)
    gradients[pl.ds(start, own_rows), :query_columns] = own_query[...]
    gradients[pl.ds(other, own_rows), :query_columns] = other_query[...]
    value_start = query_columns + HEAD_WIDTH
    features = value_start + HEAD_WIDTH
    gradients[pl.ds(start, own_rows), query_columns:features] = own_pair[...]
    gradients[pl.ds(other, own_rows), query_columns:features] = other_pair[...]
    query_grad = gradients[:, :query_columns]
    value_grad = gradients[:, value_start:features]
    low = low_rank[...]
    rank = low.shape[1] // 2
    segments = row_segments(kernel_marks(lengths), row_positions(seq_index * rows, rows))
    total = jnp.zeros((rows, low.shape[1]), jnp.float32)
    for document in range(SEGS):
        member = segments == document
        parts = dot_nt(query_grad, up_blocks[document, :, :query_columns])
        parts += dot_nt(value_grad, up_blocks[document, :, query_columns:])
        total = jnp.where(member, parts, total)
        chosen = jnp.where(member, low, jnp.zeros_like(low))
        query_terms = dot_tn(chosen, query_grad)
        value_terms = dot_tn(chosen, value_grad)
        place = slice(document * rank, (document + 1) * rank)
        terms[place, :query_columns] = adapter_scale * query_terms[:rank]
        terms[place, query_columns:] = adapter_scale * value_terms[rank:]
    turned = (adapter_scale * total).astype(jnp.bfloat16)
    rank_grad[...] = turned
    second = segments != (seq_index >= seq_count // 2).astype(jnp.int32)
    nothing = jnp.zeros_like(turned)
    middle = features + low.shape[1]
    gradients[:, features:middle] = jnp.where(second, nothing, turned)
    gradients[:, middle:] = jnp.where(second, turned, nothing)
    held = blocks.shape[2]
    for holder in range(seq_count):
        blocks[holder] = terms[:, holder * held : (holder + 1) * held]
    for steps, block in enumerate(split_terms):
        mine = blocks[ring_index(seq_index + steps - seq_count, seq_count)]
        if block.shape == mine.shape:
            block[...] = mine
            continue
        tail = held - 128
        count = 128 // tail
        height = mine.shape[0] // count
        first_low = mine.shape[0] + height
        block[: mine.shape[0]] = mine[:, :128]
        for part in range(count):
            block[mine.shape[0] : first_low, part * tail : (part + 1) * tail] = mine[
                part * height : (part + 1) * height, 128:
            ]
        block[first_low:, : low.shape[1]] = turned[: rows // 2].astype(jnp.float32)
        block[first_low:, low.shape[1] :] = turned[rows // 2 :].astype(jnp.float32)


def token_kernel(gradients, matrix, token_grad):
    token_grad[...] = dot_nn(gradients[...], matrix[...]).astype(jnp.bfloat16)


def down_kernel(block_count, lengths, *refs):
    columns = refs[:block_count]
    up_parts = refs[block_count : 2 * block_count]
    packed = up_parts[0].shape != up_parts[1].shape
    rank_count = 1 if packed else block_count
    ranks = refs[2 * block_count : 2 * block_count + rank_count]
    outputs = refs[2 * block_count + rank_count :]
    rows, joint_rank = ranks[0].shape
    ends = kernel_marks(lengths)
    up_rows, up_width = up_parts[0].shape
    lows, ups = [ranks[0][...]], [up_parts[0][...]]
    for behind in range(1, block_count):
        if not packed:
            lows.append(ranks[behind][...])
            ups.append(up_parts[behind][...])
            continue
        part = up_parts[behind]
        count = 128 // (up_width - 128)
        first_low = up_rows + up_rows // count
        halves = [part[first_low:, :joint_rank], part[first_low:, joint_rank:]]
        lows.append(jnp.concatenate(halves, axis=0).astype(jnp.bfloat16))
    all_terms = []
    for document in range(SEGS):
        total = jnp.zeros((joint_rank, columns[0].shape[1]), jnp.float32)
        for behind in range(block_count):
            holder = ring_index(lax.axis_index("seq") - behind, block_count)
            segments = row_segments(ends, row_positions(holder * rows, rows))
            chosen = jnp.where(segments == document, lows[behind], jnp.zeros_like(lows[behind]))
            first_row = columns[behind].shape[0] - rows
            total += dot_tn(chosen, columns[behind][first_row:])
        all_terms.append(total)
    down_terms = jnp.concatenate(all_terms, axis=0)
    if not packed:
        outputs[0][...] = down_terms
        outputs[1][...] = sum(ups)
        return
    own_down, far, own_up, up_terms = outputs
    tail = up_width - 128
    height = up_rows // (128 // tail)
    up_terms[...] = ups[0]
    for part in up_parts[1:]:
        up_terms[:, :128] += part[:up_rows]
        for piece in range(128 // tail):
            up_terms[piece * height : (piece + 1) * height, 128:] += part[
                up_rows : up_rows + height, piece * tail : (piece + 1) * tail
            ]
    held, held_up = own_down.shape[1], own_up.shape[1]
    ahead = lax.axis_index("batch") == 0
    own_down[...] = jnp.where(ahead, down_terms[:, :held], down_terms[:, held:])
    far[:, :held] = jnp.where(ahead, down_terms[:, held:], down_terms[:, :held])
    left, right = up_terms[:, :held_up], up_terms[:, held_up:]
    own_up[...] = jnp.where(ahead, left, right)
    far_up = jnp.where(ahead, right, left)
    spare = far.shape[1] - held
    far[:up_rows, held:] = far_up[:, :spare]
    far[up_rows:, held : held + held_up - spare] = far_up[:, spare:]


def packed_bank_kernel(bank_rows, own_down, far, own_up, down_zeros, up_zeros, down_out, up_out):
    step = pl.program_id(0)
    joint_rank, held = down_out.shape[1], down_out.shape[3]
    low_width, held_up = up_out.shape[1:]
    up_rows = own_up.shape[0]
    spare = far.shape[1] - held
    down_total = jnp.zeros((joint_rank, held), jnp.float32)
    head = jnp.zeros((low_width, spare), jnp.float32)
    rest = jnp.zeros((low_width, held_up - spare), jnp.float32)
    for document in range(SEGS):
        rows = slice(document * joint_rank, (document + 1) * joint_rank)
        lows = slice(document * low_width, (document + 1) * low_width)
        same = bank_rows[document] == bank_rows[step]
        down_total += jnp.where(same, own_down[rows], 0.0)
        head += jnp.where(same, own_up[lows, :spare], 0.0)
        rest += jnp.where(same, own_up[lows, spare:], 0.0)
        same = bank_rows[SEGS + document] == bank_rows[step]
        down_total += jnp.where(same, far[rows, :held], 0.0)
        head += jnp.where(same, far[lows, held:], 0.0)
        lows = slice(up_rows + document * low_width, up_rows + (document + 1) * low_width)
        rest += jnp.where(same, far[lows, held : held + held_up - spare], 0.0)
    down_out[0, :, 0, :] = down_total
    up_out[0, :, :spare] = head
    up_out[0, :, spare:] = rest


def bank_kernel(block_count, bank_rows, *refs):
    down_terms = refs[:block_count]
    up_terms = refs[block_count : 2 * block_count]
    down_out, up_out = refs[2 * block_count + 2 :]
    step = pl.program_id(0)
    row = bank_rows[step]
    joint_rank = down_out.shape[1]
    low_width = up_out.shape[1]
    down_total = jnp.zeros((joint_rank, down_out.shape[3]), jnp.float32)
    up_total = jnp.zeros((low_width, up_out.shape[2]), jnp.float32)
    for block in range(block_count):
        for document in range(SEGS):
            same = bank_rows[block * SEGS + document] == row
            down_rows = down_terms[block][document * joint_rank : (document + 1) * joint_rank]
            up_rows = up_terms[block][document * low_width : (document + 1) * low_width]
            down_total += jnp.where(same, down_rows, 0.0)
            up_total += jnp.where(same, up_rows, 0.0)
    down_out[0, :, 0, :] = down_total
    up_out[0] = up_total


def shards(
    tokens,
    frozen_qkv_matrix,
    adapter_down_weight,
    adapter_up_weight,
    adapter_bank_row,
    document_lengths,
    document_adapter,
    output_gradient,
):
    seq_count = lax.axis_size("seq")
    batch_count = lax.axis_size("batch")
    group_count = lax.axis_size("groups")
    chip_size = lax.axis_size("tp")
    seq_index = lax.axis_index("seq")
    batch_index = lax.axis_index("batch")
    group_index = lax.axis_index("groups")
    tp_index = lax.axis_index("tp")
    local_tokens = tokens[0]
    rows, width = local_tokens.shape
    own_rows = rows // chip_size
    query_columns = QHEADS * HEAD_WIDTH
    frozen_rows = frozen_qkv_matrix.shape[0]
    features = frozen_rows * seq_count
    low_width = ADAPTER_RANK
    joint_rank = adapter_down_weight.shape[1]
    adapters = adapter_bank_row.shape[0]
    bf16 = jnp.bfloat16
    f32 = jnp.float32

    lengths = lax.dynamic_index_in_dim(document_lengths, batch_index, 0, keepdims=False)
    first_end = lengths[0]
    second_end = first_end + lengths[1]
    half_count = seq_count // 2
    held_down = adapter_down_weight.shape[3]
    held_up = adapter_up_weight.shape[2]
    down_width = held_down * batch_count
    up_width = held_up * batch_count

    positions = seq_index * rows + jnp.arange(rows, dtype=jnp.int32)
    inside = positions - jnp.where(
        positions >= second_end, second_end, jnp.where(positions >= first_end, first_end, 0)
    )
    exponent = jnp.arange(HEAD_WIDTH // 2, dtype=f32) * (2.0 / HEAD_WIDTH)
    inverse = jnp.power(jnp.float32(rope_base), -exponent)
    angles = inside.astype(f32)[:, None] * jnp.concatenate([inverse, inverse])[None, :]
    signs = jnp.where(jnp.arange(HEAD_WIDTH) < HEAD_WIDTH // 2, -1.0, 1.0).astype(f32)
    cosines = jnp.cos(angles)
    sines = jnp.sin(angles) * signs[None, :]

    sample_rows = lookup_rows(adapter_bank_row, document_adapter)
    bank_rows = sample_rows.reshape(-1)
    if batch_count == 2:
        own_bank = jnp.where(batch_index == 0, sample_rows[0], sample_rows[1])
        far_bank = jnp.where(batch_index == 0, sample_rows[1], sample_rows[0])
        bank_rows = jnp.concatenate([own_bank, far_bank])
    down_bank = adapter_down_weight[:, :, 0, :]
    down_zeros = jnp.zeros((adapters, joint_rank, 1, held_down), f32)
    up_zeros = jnp.zeros((adapters, low_width, held_up), f32)

    plane_count = group_count * batch_count
    share = width // plane_count
    padded_down = (held_down + 127) // 128 * 128
    direct = (
        group_count == 2
        and seq_count == 4
        and share == down_width
        and batch_count == 2
        and share % 128 == 0
        and down_width % 128 == 0
        and frozen_rows % 16 == 0
        and 4 * up_width <= down_width
        and up_width > 128
        and 128 % (up_width - 128) == 0
        and 0 < held_up + held_down - padded_down <= padded_down - held_down
    )
    up_entries = []
    if direct:
        own_share = lax.dynamic_slice_in_dim(
            frozen_qkv_matrix, (group_index * batch_count + batch_index) * share, share, axis=1
        )
        before = shift(own_share, "seq", 1)
        after = shift(own_share, "seq", 3)
        far_down = shift(down_bank[far_bank], "batch", 1)
        far_up = shift(adapter_up_weight[far_bank], "batch", 1)
        own_down, own_up = down_bank[own_bank], adapter_up_weight[own_bank]
        payload_rows = 2 * joint_rank + low_width // 2
        pack_shapes = [(2 * frozen_rows, share), (frozen_rows + payload_rows, share)]
        pack_shapes += [(payload_rows, share)] * 3
        plane, forward, payload, *payloads = pl.pallas_call(
            pack_kernel,
            out_shape=[jax.ShapeDtypeStruct(shape, bf16) for shape in pack_shapes],
            in_specs=[in_vmem()] * 6,
            out_specs=[by_block(shape) for shape in pack_shapes],
            scratch_shapes=[
                pltpu.VMEM((SEGS * joint_rank, down_width), bf16),
                pltpu.VMEM((SEGS, low_width, 2 * held_up), bf16),
            ],
            compiler_params=pltpu.CompilerParams(vmem_limit_bytes=16 * mebibyte),
            cost_estimate=cost(0, 8 * frozen_rows * share),
            name="pack",
        )(own_down, far_down, own_up, far_up, before, after)

        def over_plane(value):
            over_both = [(at, plane_count - 1 - at) for at in range(plane_count)]
            return [
                shift(value, "batch", 1),
                shift(value, "groups", 1),
                lax.ppermute(value, ("groups", "batch"), over_both),
            ]

        plane_parts = over_plane(plane)
        forward = shift(forward, "seq", 1)
        middle = forward[:frozen_rows]
        middle_parts = over_plane(middle)
        near_payload = shift(payloads[1], "seq", 3)
        early = [plane, down_zeros, up_zeros, cosines, sines, bank_rows]
        block_shapes = [(rows, down_width)] * seq_count
        block_shapes[2] = (rows + payload_rows, down_width)
        column_blocks = pl.pallas_call(
            functools.partial(cut_kernel, len(early), seq_count),
            out_shape=[jax.ShapeDtypeStruct(shape, bf16) for shape in block_shapes],
            in_specs=[in_vmem()] * 2 + [in_place()] * len(early),
            out_specs=[by_block(shape) for shape in block_shapes],
            compiler_params=pltpu.CompilerParams(vmem_limit_bytes=16 * mebibyte),
            cost_estimate=cost(0, 4 * rows * width),
            name="cut",
        )(local_tokens, payloads[0], *early)
        column_parts = [
            shift(block, "seq", steps) if steps else block
            for steps, block in enumerate(column_blocks)
        ]
        arrays = [frozen_qkv_matrix, before, after, forward, payload]
        arrays += [column_parts[2], near_payload] + plane_parts + middle_parts

        def frozen_at(behind, batch_step, group_step):
            return frozen_place(seq_count, frozen_rows, share, behind, batch_step, group_step)

        def down_at(behind):
            return down_place(seq_count, features, down_width, behind)

        entries = [
            (0, 0, frozen_rows, frozen_place(seq_count, frozen_rows, None, 0, 0, 0)),
            (1, 0, frozen_rows, frozen_at(1, 0, 0)),
            (2, 0, frozen_rows, frozen_at(3, 0, 0)),
            (3, 0, frozen_rows, frozen_at(2, 0, 0)),
            (4, 0, 2 * joint_rank, down_at(0)),
            (3, frozen_rows, 2 * joint_rank, down_at(1)),
            (5, 0, 2 * joint_rank, down_at(2)),
            (6, 0, 2 * joint_rank, down_at(3)),
        ]
        up_entries = [(4, 2 * joint_rank, 0), (3, frozen_rows + 2 * joint_rank, 1)]
        up_entries += [(5, 2 * joint_rank, 2), (6, 2 * joint_rank, 3)]
        for number, (batch_step, group_step) in enumerate(((1, 0), (0, 1), (1, 1))):
            entries += [
                (7 + number, 0, frozen_rows, frozen_at(1, batch_step, group_step)),
                (7 + number, frozen_rows, frozen_rows, frozen_at(3, batch_step, group_step)),
                (10 + number, 0, frozen_rows, frozen_at(2, batch_step, group_step)),
            ]
    else:
        bank_rows = sample_rows.reshape(-1)
        got_down = lax.all_to_all(
            down_bank[sample_rows], "batch", split_axis=0, concat_axis=0, tiled=True
        )
        got_up = lax.all_to_all(
            adapter_up_weight[sample_rows], "batch", split_axis=0, concat_axis=0, tiled=True
        )
        down_block = jnp.transpose(got_down, (1, 2, 0, 3)).reshape(SEGS * joint_rank, -1)
        up_block = jnp.transpose(got_up, (1, 2, 0, 3)).reshape(SEGS * low_width, -1)
        all_down = lax.all_gather(down_block, "seq", axis=0)
        all_up = lax.all_gather(up_block, "seq", axis=0)
        first = (seq_index >= half_count).astype(jnp.int32)
        merged = jnp.transpose(all_down, (1, 0, 2)).reshape(SEGS * joint_rank, -1)
        arrays = [
            lax.all_gather(frozen_qkv_matrix, "seq", axis=0, tiled=True),
            lax.dynamic_slice_in_dim(merged, first * joint_rank, 2 * joint_rank),
        ]
        entries = [
            (0, 0, features, whole_place(0)),
            (1, 0, 2 * joint_rank, whole_place(features)),
        ]
        up_rows = jnp.transpose(all_up, (1, 0, 2)).reshape(SEGS, low_width, -1)
        is_query = jnp.arange(up_rows.shape[2]) < query_columns
        up_blocks = jnp.concatenate(
            [
                jnp.where(is_query[None, None, :], up_rows, 0),
                jnp.where(is_query[None, None, :], 0, up_rows),
            ],
            axis=1,
        )
        column_blocks = [
            lax.dynamic_slice_in_dim(
                local_tokens,
                jnp.remainder(seq_index + steps, seq_count) * down_width,
                down_width,
                axis=1,
            )
            for steps in range(seq_count)
        ]

    if not direct:
        column_parts = [
            shift(block, "seq", steps) if steps else block
            for steps, block in enumerate(column_blocks)
        ]
    up_shape = (SEGS, joint_rank, query_columns + HEAD_WIDTH)
    matrix_rows = features + 2 * joint_rank
    arrived = [pltpu.VMEM((seq_count, low_width // 2, down_width), bf16)] if direct else []
    own_part, sent_part, rest_part, matrix, *built = pl.pallas_call(
        functools.partial(
            project_kernel, len(arrays), entries, up_entries, 0, seq_count
        ),
        out_shape=[
            jax.ShapeDtypeStruct((own_rows, query_columns), f32),
            jax.ShapeDtypeStruct((own_rows, query_columns), f32),
            jax.ShapeDtypeStruct((rows, matrix_rows - query_columns), f32),
            jax.ShapeDtypeStruct((matrix_rows, width), bf16),
        ]
        + ([jax.ShapeDtypeStruct(up_shape, bf16)] if direct else []),
        in_specs=[in_vmem()] + [in_place()] * len(arrays),
        out_specs=[in_vmem()] * 3 + [in_place()] + ([by_block(up_shape)] if direct else []),
        scratch_shapes=arrived
        + [
            pltpu.VMEM((matrix_rows, width), bf16),
            pltpu.SemaphoreType.DMA((len(entries) + len(up_entries) + 1,)),
        ],
        compiler_params=pltpu.CompilerParams(vmem_limit_bytes=20 * mebibyte),
        cost_estimate=cost(2 * rows * width * matrix_rows, 2 * width * (matrix_rows + rows)),
        name="project",
    )(local_tokens, *arrays)
    if direct:
        up_blocks = built[0]

    other_part = shift(sent_part, "tp", 1)
    other_rest = shift(rest_part, "tp", 1)
    due = [column_parts[1]] if direct else []
    queries, pairs, low_rank = pl.pallas_call(
        functools.partial(qkv_kernel, seq_count, len(due)),
        out_shape=(
            jax.ShapeDtypeStruct((QHEADS * own_rows, HEAD_WIDTH), bf16),
            jax.ShapeDtypeStruct((rows, 2 * HEAD_WIDTH), bf16),
            jax.ShapeDtypeStruct((rows, joint_rank), bf16),
        ),
        in_specs=[in_smem()] + [in_vmem()] * 7 + [in_place()] * len(due),
        out_specs=(in_vmem(),) * 3,
        compiler_params=pltpu.CompilerParams(vmem_limit_bytes=8 * mebibyte),
        cost_estimate=cost(2 * rows * 3 * 64 * 640, 8 * rows * features),
        name="qkv",
    )(
        document_lengths, own_part, other_part, rest_part, other_rest, up_blocks, cosines, sines, *due
    )

    blocks = [pairs] + [push(pairs, "seq", back) for back in range(1, half_count + 1)]
    block_count = len(blocks)
    incoming = output_gradient[0]
    early_columns = []
    attention, query_grad, kept, sent = pl.pallas_call(
        functools.partial(attention_kernel, block_count, len(early_columns)),
        out_shape=(
            jax.ShapeDtypeStruct((own_rows, query_columns), bf16),
            jax.ShapeDtypeStruct((own_rows, query_columns), bf16),
            jax.ShapeDtypeStruct((block_count, own_rows, 2 * HEAD_WIDTH), f32),
            jax.ShapeDtypeStruct((block_count, own_rows, 2 * HEAD_WIDTH), f32),
        ),
        in_specs=[in_smem()]
        + [in_vmem()] * (4 + block_count)
        + [in_place()] * len(early_columns),
        out_specs=(in_vmem(),) * 4,
        scratch_shapes=[pltpu.VMEM((block_count, QHEADS * own_rows, rows), bf16)],
        compiler_params=pltpu.CompilerParams(vmem_limit_bytes=(8 + 4 * block_count) * mebibyte),
        cost_estimate=cost(
            10 * block_count * QHEADS * own_rows * rows * HEAD_WIDTH,
            4 * rows * features,
            block_count * QHEADS * own_rows * rows,
        ),
        name="attention",
    )(document_lengths, queries, incoming, cosines, sines, *blocks, *early_columns)

    other_query = shift(query_grad, "tp", 1)
    due = [column_parts[-1]] if direct else []
    pair_sums = pl.pallas_call(
        functools.partial(sum_kernel, len(due)),
        out_shape=[jax.ShapeDtypeStruct((own_rows, 2 * HEAD_WIDTH), f32)] * block_count,
        in_specs=[in_vmem()] * 2 + [in_place()] * len(due),
        out_specs=[in_vmem()] * block_count,
        compiler_params=pltpu.CompilerParams(vmem_limit_bytes=8 * mebibyte),
        cost_estimate=cost(0, 12 * block_count * own_rows * 2 * HEAD_WIDTH),
        name="pair_sums",
    )(kept, shift(sent, "tp", 1), *due)
    pair_terms = [pair_sums[0]]
    pair_terms += [push(pair_sums[back], "seq", -back) for back in range(1, block_count)]
    pair_grad = pl.pallas_call(
        functools.partial(pair_kernel, block_count),
        out_shape=jax.ShapeDtypeStruct((own_rows, 2 * HEAD_WIDTH), bf16),
        in_specs=[in_vmem()] * (2 + block_count),
        out_specs=in_vmem(),
        compiler_params=pltpu.CompilerParams(vmem_limit_bytes=8 * mebibyte),
        cost_estimate=cost(0, 12 * block_count * own_rows * 2 * HEAD_WIDTH),
        name="pair_gradients",
    )(cosines, sines, *pair_terms)
    other_pair = shift(pair_grad, "tp", 1)

    split_shapes = [(SEGS * low_width, up_width)] * seq_count
    if direct:
        sent_rows = SEGS * low_width * up_width // 128 + rows // 2
        split_shapes[1:] = [(sent_rows, 128)] * (seq_count - 1)
    gradients, rank_grad, *up_split = pl.pallas_call(
        functools.partial(rank_kernel, seq_count),
        out_shape=[
            jax.ShapeDtypeStruct((rows, matrix_rows), bf16),
            jax.ShapeDtypeStruct((rows, joint_rank), bf16),
        ]
        + [jax.ShapeDtypeStruct(shape, f32) for shape in split_shapes],
        in_specs=[in_smem()] + [in_vmem()] * 6,
        out_specs=[by_block((rows, matrix_rows)), in_vmem()]
        + [by_block(shape) for shape in split_shapes],
        scratch_shapes=[
            pltpu.VMEM((SEGS * low_width, features - HEAD_WIDTH), f32),
            pltpu.VMEM((seq_count, SEGS * low_width, held_up * batch_count), f32),
        ],
        compiler_params=pltpu.CompilerParams(vmem_limit_bytes=8 * mebibyte),
        cost_estimate=cost(4 * rows * 3 * 64 * 640, 4 * rows * features),
        name="rank_gradients",
    )(
        document_lengths, query_grad, other_query, pair_grad, other_pair, low_rank, up_blocks
    )

    rank_parts = [rank_grad]
    if not direct:
        rank_parts += [shift(rank_grad, "seq", steps) for steps in range(1, seq_count)]
    up_sums = [
        shift(block, "seq", steps) if steps else block for steps, block in enumerate(up_split)
    ]

    chunk = 512
    token_grad = pl.pallas_call(
        token_kernel,
        grid=(width // chunk,),
        out_shape=jax.ShapeDtypeStruct((rows, width), bf16),
        in_specs=[
            pl.BlockSpec((rows, matrix_rows), lambda step: (0, 0)),
            pl.BlockSpec((matrix_rows, chunk), lambda step: (0, step)),
        ],
        out_specs=pl.BlockSpec((rows, chunk), lambda step: (0, step)),
        compiler_params=pltpu.CompilerParams(vmem_limit_bytes=12 * mebibyte),
        cost_estimate=cost(2 * rows * width * matrix_rows, 2 * width * (matrix_rows + rows)),
        name="token_gradient",
    )(gradients, matrix)

    if direct:
        term_shapes = [(SEGS * joint_rank, held_down), (SEGS * joint_rank, padded_down)]
        term_shapes += [(SEGS * low_width, held_up)]
    else:
        term_shapes = [(SEGS * joint_rank, down_width), (SEGS * low_width, up_width)]
    terms = pl.pallas_call(
        functools.partial(down_kernel, seq_count),
        out_shape=[jax.ShapeDtypeStruct(shape, f32) for shape in term_shapes],
        in_specs=[in_smem()] + [in_vmem()] * (2 * seq_count + len(rank_parts)),
        out_specs=[in_vmem()] * len(term_shapes),
        scratch_shapes=[pltpu.VMEM((SEGS * low_width, up_width), f32)] if direct else [],
        compiler_params=pltpu.CompilerParams(vmem_limit_bytes=8 * mebibyte),
        cost_estimate=cost(
            2 * seq_count * rows * SEGS * joint_rank * down_width, 2 * seq_count * rows * down_width
        ),
        name="down_terms",
    )(document_lengths, *column_parts, *up_sums, *rank_parts)

    if direct:
        bank_terms = [terms[0], shift(terms[1], "batch", 1), terms[2]]
    else:
        down_send = jnp.transpose(
            terms[0].reshape(SEGS * joint_rank, batch_count, held_down), (1, 0, 2)
        )
        up_send = jnp.transpose(
            terms[1].reshape(SEGS * low_width, batch_count, held_up), (1, 0, 2)
        )
        back_down = lax.all_to_all(down_send, "batch", split_axis=0, concat_axis=0, tiled=True)
        back_up = lax.all_to_all(up_send, "batch", split_axis=0, concat_axis=0, tiled=True)
        bank_downs = [back_down[batch] for batch in range(batch_count)]
        bank_ups = [back_up[batch] for batch in range(batch_count)]
        bank_terms = bank_downs + bank_ups


    def whole(array):
        return pl.BlockSpec(array.shape, lambda step, bank: (0,) * array.ndim)

    term_count = len(bank_terms)
    down_grad, up_grad = pl.pallas_call(
        packed_bank_kernel if direct else functools.partial(bank_kernel, batch_count),
        out_shape=(
            jax.ShapeDtypeStruct(down_zeros.shape, f32),
            jax.ShapeDtypeStruct(up_zeros.shape, f32),
        ),
        grid_spec=pltpu.PrefetchScalarGridSpec(
            num_scalar_prefetch=1,
            grid=(batch_count * SEGS,),
            in_specs=[whole(array) for array in bank_terms] + [in_place()] * 2,
            out_specs=(
                pl.BlockSpec(
                    (1, joint_rank, 1, held_down),
                    lambda step, bank: (bank[step], 0, 0, 0),
                ),
                pl.BlockSpec(
                    (1, low_width, held_up),
                    lambda step, bank: (bank[step], 0, 0),
                ),
            ),
        ),
        input_output_aliases={1 + term_count: 0, 2 + term_count: 1},
        compiler_params=pltpu.CompilerParams(vmem_limit_bytes=16 * mebibyte),
        name="bank_rows",
    )(
        bank_rows,
        *bank_terms,
        down_zeros,
        up_zeros,
    )
    return (attention[None], token_grad[None], down_grad, up_grad)


def solution(mesh):
    in_specs = (
        P(("groups", "batch"), "seq", "tp"),
        P("seq", "tp"),
        P(None, None, "tp", ("seq", "batch")),
        P(None, None, ("seq", "batch")),
        P(),
        P("groups", None),
        P("groups", None),
        P(("groups", "batch"), ("seq", "tp"), None),
    )
    out_specs = (
        P(("groups", "batch"), ("seq", "tp"), None),
        P(("groups", "batch"), "seq", "tp"),
        P("groups", None, "tp", ("seq", "batch")),
        P("groups", None, ("seq", "batch")),
    )
    return jax.shard_map(shards, mesh=mesh, in_specs=in_specs, out_specs=out_specs, check_vma=False)
```

```python
import functools

import jax
import jax.numpy as jnp
from jax import lax
from jax.experimental import pallas as pl
from jax.experimental.pallas import tpu as pltpu
from jax.sharding import PartitionSpec as P

QHEADS = 4
HEAD_WIDTH = 128
ADAPTER_RANK = 32
SEGS = 3

adapter_scale = 2.0
rope_base = 5000000.0
masked_score = -1e30
mebibyte = 1024 * 1024


def shift(value, axis, steps):
    count = lax.axis_size(axis)
    return lax.ppermute(value, axis, [(at, (at + steps) % count) for at in range(count)])


def push(value, axis, steps):
    count = lax.axis_size(axis)
    pairs = [(at, at + steps) for at in range(count) if 0 <= at + steps < count]
    return lax.ppermute(value, axis, pairs)


def dot_nt(left, right):
    return lax.dot_general(
        left, right, (((1,), (1,)), ((), ())), preferred_element_type=jnp.float32
    )


def dot_nn(left, right):
    return jnp.dot(left, right, preferred_element_type=jnp.float32)


def dot_tn(left, right):
    return lax.dot_general(
        left, right, (((0,), (0,)), ((), ())), preferred_element_type=jnp.float32
    )


def lookup_rows(adapter_bank_row, document_adapter):
    matches = document_adapter[..., None] == jnp.arange(adapter_bank_row.shape[0], dtype=jnp.int32)
    return jnp.sum(jnp.where(matches, adapter_bank_row, 0), axis=-1)


def row_positions(first, count):
    return first + lax.broadcasted_iota(jnp.int32, (count, 1), 0)


def ring_index(index, count):
    return lax.rem(index + count, count)


def kernel_marks(lengths):
    batch = lax.axis_index("batch")
    first_end = lengths[batch, 0]
    return first_end, first_end + lengths[batch, 1]


def row_segments(ends, positions):
    return (positions >= ends[0]).astype(jnp.int32) + (positions >= ends[1]).astype(jnp.int32)


def cost(flops, bytes_accessed, transcendentals=0):
    return pl.CostEstimate(
        flops=flops, bytes_accessed=bytes_accessed, transcendentals=transcendentals
    )


def in_vmem():
    return pl.BlockSpec(memory_space=pltpu.VMEM)


def in_smem():
    return pl.BlockSpec(memory_space=pltpu.SMEM)


def by_block(shape):
    return pl.BlockSpec(shape, lambda: (0,) * len(shape))


def in_place():
    return pl.BlockSpec(memory_space=pl.ANY)


def fetch(piece, target, place, semaphore):
    height, width = piece.shape
    row, column = place()
    copy = pltpu.make_async_copy(
        piece,
        target.at[
            pl.ds(pl.multiple_of(row, 16), height), pl.ds(pl.multiple_of(column, 128), width)
        ],
        semaphore,
    )
    copy.start()
    return copy


def frozen_place(seq_count, rows, share, behind, batch_step, group_step):
    def place():
        holder = ring_index(lax.axis_index("seq") - behind, seq_count)
        if share is None:
            return holder * rows, 0
        batch = lax.rem(lax.axis_index("batch") + batch_step, 2)
        group = lax.rem(lax.axis_index("groups") + group_step, 2)
        return holder * rows, (group * 2 + batch) * share

    return place


def down_place(seq_count, features, width, behind):
    def place():
        return features, ring_index(lax.axis_index("seq") - behind, seq_count) * width

    return place


def whole_place(row):
    def place():
        return row, 0

    return place


def pack_kernel(own_down, far_down, own_up, far_up, before, after, *refs):
    plane, forward, payloads, (down, up) = refs[0], refs[1], refs[2:-2], refs[-2:]
    ahead = lax.axis_index("batch") == 0
    joint_rank, held = own_down.shape[1:]
    low_width, held_up = own_up.shape[1:]
    frozen_rows = before.shape[0]
    plane[:frozen_rows] = before[...]
    plane[frozen_rows:] = after[...]
    forward[:frozen_rows] = before[...]
    for document in range(SEGS):
        rows = slice(document * joint_rank, (document + 1) * joint_rank)
        down[rows, :held] = jnp.where(ahead, own_down[document], far_down[document])
        down[rows, held:] = jnp.where(ahead, far_down[document], own_down[document])
        up[document, :, :held_up] = jnp.where(ahead, own_up[document], far_up[document])
        up[document, :, held_up:] = jnp.where(ahead, far_up[document], own_up[document])
    half, slot = low_width // 2, down.shape[1] // 4
    targets = [(0, payloads[0], 0), (1, forward, frozen_rows)]
    targets += [(steps + 2, payload, 0) for steps, payload in enumerate(payloads[1:])]
    seq_count = len(targets)
    for steps, payload, base in targets:
        target = ring_index(lax.axis_index("seq") + steps - seq_count, seq_count)
        first = (target >= seq_count // 2).astype(jnp.int32)
        start = pl.multiple_of(first * joint_rank, joint_rank)
        payload[base : base + 2 * joint_rank] = down[pl.ds(start, 2 * joint_rank)]
        base = base + 2 * joint_rank
        for index in range(2):
            block = up[first + index]
            for part in range(2):
                column = (2 * index + part) * slot
                payload[base : base + half, column : column + 2 * held_up] = block[
                    part * half : (part + 1) * half
                ]


def cut_kernel(unused, seq_count, tokens, *refs):
    for steps, block in enumerate(refs[unused:]):
        target = ring_index(lax.axis_index("seq") + steps - seq_count, seq_count)
        width = block.shape[1]
        block[...] = tokens[:, pl.ds(pl.multiple_of(target * width, 128), width)]


def assemble_up(seq_count, arrived, up_blocks):
    low_width = up_blocks.shape[1] // 2
    query_columns = QHEADS * HEAD_WIDTH
    seq_index = lax.axis_index("seq")
    first = (seq_index >= seq_count // 2).astype(jnp.int32)
    held = up_blocks.shape[2] // seq_count
    half, slot = low_width // 2, arrived.shape[2] // 4
    up_blocks[...] = jnp.zeros_like(up_blocks)
    for holder in range(seq_count):
        block = arrived[ring_index(seq_index - holder, seq_count)]
        start, stop = holder * held, (holder + 1) * held
        middle = min(max(query_columns, start), stop)
        for index in range(2):
            for part in range(2):
                offset = (2 * index + part) * slot
                if middle > start:
                    up_blocks[first + index, part * half : (part + 1) * half, start:middle] = block[
                        :, offset : offset + middle - start
                    ]
                if stop > middle:
                    low = low_width + part * half
                    up_blocks[first + index, low : low + half, middle:stop] = block[
                        :, offset + middle - start : offset + held
                    ]


def project_kernel(array_count, entries, up_entries, unused, seq_count, tokens, *refs):
    arrays = refs[:array_count]
    refs = refs[array_count + unused :]
    own_query, sent_query, rest, matrix = refs[:4]
    weights, semaphore = refs[-2:]
    copies = []
    for number, start, height, place in entries:
        piece = arrays[number].at[pl.ds(start, height)]
        copies.append(fetch(piece, weights, place, semaphore.at[len(copies)]))
    for number, start, slot in up_entries:
        copy = pltpu.make_async_copy(
            arrays[number].at[pl.ds(start, refs[5].shape[1])],
            refs[5].at[slot],
            semaphore.at[len(copies)],
        )
        copy.start()
        copies.append(copy)
    for copy in copies:
        copy.wait()
    keep = pltpu.make_async_copy(weights, matrix, semaphore.at[len(copies)])
    keep.start()
    part = dot_nt(tokens[...], weights[...])
    own_rows, query_columns = own_query.shape
    first = lax.axis_index("tp") == 0
    upper, lower = part[:own_rows, :query_columns], part[own_rows:, :query_columns]
    own_query[...] = jnp.where(first, upper, lower)
    sent_query[...] = jnp.where(first, lower, upper)
    rest[...] = part[:, query_columns:]
    if up_entries:
        assemble_up(seq_count, refs[5], refs[4])
    keep.wait()


def rotated(values, cosines, sines):
    return values * cosines + pltpu.roll(values, values.shape[1] // 2, 1) * sines


def qkv_kernel(
    seq_count, unused, lengths, own_query, other_query, mine, theirs, up_blocks, cosines, sines, *refs
):
    queries, pairs, low_rank = refs[unused:]
    rows, joint_rank = low_rank.shape
    own_rows, query_columns = own_query.shape
    start_low, middle = 2 * HEAD_WIDTH, 2 * HEAD_WIDTH + joint_rank
    ends = kernel_marks(lengths)

    def low_rows(picked, second):
        first_low = mine[picked, start_low:middle] + theirs[picked, start_low:middle]
        second_low = mine[picked, middle:] + theirs[picked, middle:]
        return jnp.where(second, second_low, first_low).astype(jnp.bfloat16)

    first = (lax.axis_index("seq") >= seq_count // 2).astype(jnp.int32)
    first_row = lax.axis_index("seq") * rows
    segments = row_segments(ends, row_positions(first_row, rows))
    low = low_rows(slice(None), segments != first)
    low_rank[...] = low
    value_delta = jnp.zeros((rows, HEAD_WIDTH), jnp.float32)
    for document in range(SEGS):
        chosen = jnp.where(segments == document, low, jnp.zeros_like(low))
        value_delta += dot_nn(chosen, up_blocks[document, :, query_columns:])
    keys = mine[:, :HEAD_WIDTH] + theirs[:, :HEAD_WIDTH]
    pairs[:, :HEAD_WIDTH] = rotated(keys, cosines[...], sines[...]).astype(jnp.bfloat16)
    values = mine[:, HEAD_WIDTH:start_low] + theirs[:, HEAD_WIDTH:start_low]
    pairs[:, HEAD_WIDTH:] = (values + adapter_scale * value_delta).astype(jnp.bfloat16)
    start = pl.multiple_of(lax.axis_index("tp") * own_rows, own_rows)
    own = pl.ds(start, own_rows)
    own_segments = row_segments(ends, row_positions(first_row + start, own_rows))
    own_low = low_rows(own, own_segments != first)
    query_delta = jnp.zeros((own_rows, query_columns), jnp.float32)
    for document in range(SEGS):
        chosen = jnp.where(own_segments == document, own_low, jnp.zeros_like(own_low))
        query_delta += dot_nn(chosen, up_blocks[document, :, :query_columns])
    projected = own_query[...] + other_query[...]
    projected = projected + adapter_scale * query_delta
    for head in range(QHEADS):
        turned = rotated(
            projected[:, head * HEAD_WIDTH : (head + 1) * HEAD_WIDTH], cosines[own], sines[own]
        )
        queries[head * own_rows : (head + 1) * own_rows] = turned.astype(jnp.bfloat16)


def attention_kernel(block_count, unused, lengths, queries, incoming, cosines, sines, *refs):
    blocks = refs[:block_count]
    output, query_grad, kept, sent, low_probs = refs[block_count + unused :]
    own_rows, query_columns = incoming.shape
    rows = blocks[0].shape[0]
    score_scale = HEAD_WIDTH ** (-0.5)
    ends = kernel_marks(lengths)
    seq_index, tp_index = lax.axis_index("seq"), lax.axis_index("tp")
    positions = row_positions(seq_index * rows + tp_index * own_rows, own_rows)
    positions = jnp.concatenate([positions] * QHEADS, axis=0)
    segments = row_segments(ends, positions)
    starts = jnp.where(segments == 0, 0, jnp.where(segments == 1, ends[0], ends[1]))
    scores = []
    for back, block in enumerate(blocks):
        key_positions = (seq_index - back) * rows + lax.broadcasted_iota(jnp.int32, (1, rows), 1)
        allowed = (key_positions <= positions) & (key_positions >= starts)
        block_scores = dot_nt(queries[...], block[:, :HEAD_WIDTH]) * score_scale
        scores.append(jnp.where(allowed, block_scores, masked_score))
    row_max = functools.reduce(
        jnp.maximum, [jnp.max(part, axis=1, keepdims=True) for part in scores]
    )
    raised = [jnp.exp(part - row_max) for part in scores]
    row_total = sum(jnp.sum(part, axis=1, keepdims=True) for part in raised)
    inverse = 1.0 / row_total
    probs = [part * inverse for part in raised]
    weighted = jnp.zeros((QHEADS * own_rows, HEAD_WIDTH), jnp.float32)
    for back, block in enumerate(blocks):
        low_probs[back] = probs[back].astype(jnp.bfloat16)
        weighted += dot_nn(low_probs[back], block[:, HEAD_WIDTH:])
    attended = weighted.astype(jnp.bfloat16)
    gradients = jnp.concatenate(
        [incoming[:, head * HEAD_WIDTH : (head + 1) * HEAD_WIDTH] for head in range(QHEADS)],
        axis=0,
    )
    row_delta = jnp.sum(
        gradients.astype(jnp.float32) * attended.astype(jnp.float32), axis=1, keepdims=True
    )
    start = pl.multiple_of(tp_index * own_rows, own_rows)
    total = jnp.zeros((QHEADS * own_rows, HEAD_WIDTH), jnp.float32)
    for back, block in enumerate(blocks):
        prob_grad = dot_nt(gradients, block[:, HEAD_WIDTH:])
        score_grad = (probs[back] * (prob_grad - row_delta)).astype(jnp.bfloat16)
        total += dot_nn(score_grad, block[:, :HEAD_WIDTH])
        key_part = dot_tn(score_grad, queries[...]) * score_scale
        value_part = dot_tn(low_probs[back], gradients)
        mine = tp_index == 0
        kept[back, :, :HEAD_WIDTH] = jnp.where(mine, key_part[:own_rows], key_part[own_rows:])
        sent[back, :, :HEAD_WIDTH] = jnp.where(mine, key_part[own_rows:], key_part[:own_rows])
        kept[back, :, HEAD_WIDTH:] = jnp.where(mine, value_part[:own_rows], value_part[own_rows:])
        sent[back, :, HEAD_WIDTH:] = jnp.where(mine, value_part[own_rows:], value_part[:own_rows])
    own = pl.ds(start, own_rows)
    for head in range(QHEADS):
        picked = slice(head * own_rows, (head + 1) * own_rows)
        columns = slice(head * HEAD_WIDTH, (head + 1) * HEAD_WIDTH)
        output[:, columns] = attended[picked]
        query_grad[:, columns] = rotated(
            total[picked] * score_scale, cosines[own], -sines[own]
        ).astype(jnp.bfloat16)


def sum_kernel(kept, arrived, *sums):
    for back, total in enumerate(sums):
        total[...] = kept[back] + arrived[back]


def pair_kernel(terms, cosines, sines, *refs):
    parts, pair = refs[:terms], refs[-2]
    own_rows = pair.shape[0]
    total = sum(part[...] for part in parts)
    own = pl.ds(pl.multiple_of(lax.axis_index("tp") * own_rows, own_rows), own_rows)
    keys = rotated(total[:, :HEAD_WIDTH], cosines[own], -sines[own])
    pair[:, :HEAD_WIDTH] = keys.astype(jnp.bfloat16)
    pair[:, HEAD_WIDTH:] = total[:, HEAD_WIDTH:].astype(jnp.bfloat16)


def rank_kernel(
    seq_count, lengths, own_query, other_query, own_pair, other_pair, low_rank, up_blocks, *refs
):
    gradients, rank_grad = refs[:2]
    split_terms, (terms, blocks) = refs[2:-2], refs[-2:]
    own_rows, query_columns = own_query.shape
    rows = low_rank.shape[0]
    seq_index = lax.axis_index("seq")
    start = pl.multiple_of(lax.axis_index("tp") * own_rows, own_rows)
    other = pl.multiple_of(own_rows - start, own_rows)
    gradients[pl.ds(start, own_rows), :query_columns] = own_query[...]
    gradients[pl.ds(other, own_rows), :query_columns] = other_query[...]
    value_start = query_columns + HEAD_WIDTH
    features = value_start + HEAD_WIDTH
    gradients[pl.ds(start, own_rows), query_columns:features] = own_pair[...]
    gradients[pl.ds(other, own_rows), query_columns:features] = other_pair[...]
    query_grad = gradients[:, :query_columns]
    value_grad = gradients[:, value_start:features]
    low = low_rank[...]
    rank = low.shape[1] // 2
    segments = row_segments(kernel_marks(lengths), row_positions(seq_index * rows, rows))
    total = jnp.zeros((rows, low.shape[1]), jnp.float32)
    for document in range(SEGS):
        member = segments == document
        parts = dot_nt(query_grad, up_blocks[document, :, :query_columns])
        parts += dot_nt(value_grad, up_blocks[document, :, query_columns:])
        total = jnp.where(member, parts, total)
        chosen = jnp.where(member, low, jnp.zeros_like(low))
        query_terms = dot_tn(chosen, query_grad)
        value_terms = dot_tn(chosen, value_grad)
        place = slice(document * rank, (document + 1) * rank)
        terms[place, :query_columns] = adapter_scale * query_terms[:rank]
        terms[place, query_columns:] = adapter_scale * value_terms[rank:]
    turned = (adapter_scale * total).astype(jnp.bfloat16)
    rank_grad[...] = turned
    second = segments != (seq_index >= seq_count // 2).astype(jnp.int32)
    nothing = jnp.zeros_like(turned)
    middle = features + low.shape[1]
    gradients[:, features:middle] = jnp.where(second, nothing, turned)
    gradients[:, middle:] = jnp.where(second, turned, nothing)
    held = blocks.shape[2]
    for holder in range(seq_count):
        blocks[holder] = terms[:, holder * held : (holder + 1) * held]
    for steps, block in enumerate(split_terms):
        mine = blocks[ring_index(seq_index + steps - seq_count, seq_count)]
        if block.shape == mine.shape:
            block[...] = mine
            continue
        tail = held - 128
        count = 128 // tail
        height = mine.shape[0] // count
        first_low = mine.shape[0] + height
        block[: mine.shape[0]] = mine[:, :128]
        for part in range(count):
            block[mine.shape[0] : first_low, part * tail : (part + 1) * tail] = mine[
                part * height : (part + 1) * height, 128:
            ]
        block[first_low:, : low.shape[1]] = turned[: rows // 2].astype(jnp.float32)
        block[first_low:, low.shape[1] :] = turned[rows // 2 :].astype(jnp.float32)


def token_kernel(gradients, matrix, *refs):
    token_grad = refs[2]
    token_grad[...] = dot_nn(gradients[...], matrix[...]).astype(jnp.bfloat16)


def down_kernel(block_count, lengths, *refs):
    columns = refs[:block_count]
    up_parts = refs[block_count : 2 * block_count]
    packed = up_parts[0].shape != up_parts[1].shape
    rank_count = 1 if packed else block_count
    ranks = refs[2 * block_count : 2 * block_count + rank_count]
    outputs = refs[2 * block_count + rank_count :]
    rows, joint_rank = ranks[0].shape
    ends = kernel_marks(lengths)
    up_rows, up_width = up_parts[0].shape
    lows, ups = [ranks[0][...]], [up_parts[0][...]]
    for behind in range(1, block_count):
        if not packed:
            lows.append(ranks[behind][...])
            ups.append(up_parts[behind][...])
            continue
        part = up_parts[behind]
        count = 128 // (up_width - 128)
        first_low = up_rows + up_rows // count
        halves = [part[first_low:, :joint_rank], part[first_low:, joint_rank:]]
        lows.append(jnp.concatenate(halves, axis=0).astype(jnp.bfloat16))
    all_terms = []
    for document in range(SEGS):
        total = jnp.zeros((joint_rank, columns[0].shape[1]), jnp.float32)
        for behind in range(block_count):
            holder = ring_index(lax.axis_index("seq") - behind, block_count)
            segments = row_segments(ends, row_positions(holder * rows, rows))
            chosen = jnp.where(segments == document, lows[behind], jnp.zeros_like(lows[behind]))
            total += dot_tn(chosen, columns[behind][...])
        all_terms.append(total)
    down_terms = jnp.concatenate(all_terms, axis=0)
    if not packed:
        outputs[0][...] = down_terms
        outputs[1][...] = sum(ups)
        return
    own_down, far, own_up, up_terms = outputs
    tail = up_width - 128
    height = up_rows // (128 // tail)
    up_terms[...] = ups[0]
    for part in up_parts[1:]:
        up_terms[:, :128] += part[:up_rows]
        for piece in range(128 // tail):
            up_terms[piece * height : (piece + 1) * height, 128:] += part[
                up_rows : up_rows + height, piece * tail : (piece + 1) * tail
            ]
    held, held_up = own_down.shape[1], own_up.shape[1]
    ahead = lax.axis_index("batch") == 0
    own_down[...] = jnp.where(ahead, down_terms[:, :held], down_terms[:, held:])
    far[:, :held] = jnp.where(ahead, down_terms[:, held:], down_terms[:, :held])
    left, right = up_terms[:, :held_up], up_terms[:, held_up:]
    own_up[...] = jnp.where(ahead, left, right)
    far_up = jnp.where(ahead, right, left)
    spare = far.shape[1] - held
    far[:up_rows, held:] = far_up[:, :spare]
    far[up_rows:, held : held + held_up - spare] = far_up[:, spare:]


def packed_bank_kernel(bank_rows, own_down, far, own_up, down_zeros, up_zeros, down_out, up_out):
    step = pl.program_id(0)
    joint_rank, held = down_out.shape[1], down_out.shape[3]
    low_width, held_up = up_out.shape[1:]
    up_rows = own_up.shape[0]
    spare = far.shape[1] - held
    down_total = jnp.zeros((joint_rank, held), jnp.float32)
    head = jnp.zeros((low_width, spare), jnp.float32)
    rest = jnp.zeros((low_width, held_up - spare), jnp.float32)
    for document in range(SEGS):
        rows = slice(document * joint_rank, (document + 1) * joint_rank)
        lows = slice(document * low_width, (document + 1) * low_width)
        same = bank_rows[document] == bank_rows[step]
        down_total += jnp.where(same, own_down[rows], 0.0)
        head += jnp.where(same, own_up[lows, :spare], 0.0)
        rest += jnp.where(same, own_up[lows, spare:], 0.0)
        same = bank_rows[SEGS + document] == bank_rows[step]
        down_total += jnp.where(same, far[rows, :held], 0.0)
        head += jnp.where(same, far[lows, held:], 0.0)
        lows = slice(up_rows + document * low_width, up_rows + (document + 1) * low_width)
        rest += jnp.where(same, far[lows, held : held + held_up - spare], 0.0)
    down_out[0, :, 0, :] = down_total
    up_out[0, :, :spare] = head
    up_out[0, :, spare:] = rest


def bank_kernel(block_count, bank_rows, *refs):
    down_terms = refs[:block_count]
    up_terms = refs[block_count : 2 * block_count]
    down_out, up_out = refs[2 * block_count + 2 :]
    step = pl.program_id(0)
    row = bank_rows[step]
    joint_rank = down_out.shape[1]
    low_width = up_out.shape[1]
    down_total = jnp.zeros((joint_rank, down_out.shape[3]), jnp.float32)
    up_total = jnp.zeros((low_width, up_out.shape[2]), jnp.float32)
    for block in range(block_count):
        for document in range(SEGS):
            same = bank_rows[block * SEGS + document] == row
            down_rows = down_terms[block][document * joint_rank : (document + 1) * joint_rank]
            up_rows = up_terms[block][document * low_width : (document + 1) * low_width]
            down_total += jnp.where(same, down_rows, 0.0)
            up_total += jnp.where(same, up_rows, 0.0)
    down_out[0, :, 0, :] = down_total
    up_out[0] = up_total


def shards(
    tokens,
    frozen_qkv_matrix,
    adapter_down_weight,
    adapter_up_weight,
    adapter_bank_row,
    document_lengths,
    document_adapter,
    output_gradient,
):
    seq_count = lax.axis_size("seq")
    batch_count = lax.axis_size("batch")
    group_count = lax.axis_size("groups")
    chip_size = lax.axis_size("tp")
    seq_index = lax.axis_index("seq")
    batch_index = lax.axis_index("batch")
    group_index = lax.axis_index("groups")
    tp_index = lax.axis_index("tp")
    local_tokens = tokens[0]
    rows, width = local_tokens.shape
    own_rows = rows // chip_size
    query_columns = QHEADS * HEAD_WIDTH
    frozen_rows = frozen_qkv_matrix.shape[0]
    features = frozen_rows * seq_count
    low_width = ADAPTER_RANK
    joint_rank = adapter_down_weight.shape[1]
    adapters = adapter_bank_row.shape[0]
    bf16 = jnp.bfloat16
    f32 = jnp.float32

    lengths = lax.dynamic_index_in_dim(document_lengths, batch_index, 0, keepdims=False)
    first_end = lengths[0]
    second_end = first_end + lengths[1]
    half_count = seq_count // 2
    held_down = adapter_down_weight.shape[3]
    held_up = adapter_up_weight.shape[2]
    down_width = held_down * batch_count
    up_width = held_up * batch_count

    positions = seq_index * rows + jnp.arange(rows, dtype=jnp.int32)
    inside = positions - jnp.where(
        positions >= second_end, second_end, jnp.where(positions >= first_end, first_end, 0)
    )
    exponent = jnp.arange(HEAD_WIDTH // 2, dtype=f32) * (2.0 / HEAD_WIDTH)
    inverse = jnp.power(jnp.float32(rope_base), -exponent)
    angles = inside.astype(f32)[:, None] * jnp.concatenate([inverse, inverse])[None, :]
    signs = jnp.where(jnp.arange(HEAD_WIDTH) < HEAD_WIDTH // 2, -1.0, 1.0).astype(f32)
    cosines = jnp.cos(angles)
    sines = jnp.sin(angles) * signs[None, :]

    sample_rows = lookup_rows(adapter_bank_row, document_adapter)
    bank_rows = sample_rows.reshape(-1)
    if batch_count == 2:
        own_bank = jnp.where(batch_index == 0, sample_rows[0], sample_rows[1])
        far_bank = jnp.where(batch_index == 0, sample_rows[1], sample_rows[0])
        bank_rows = jnp.concatenate([own_bank, far_bank])
    down_bank = adapter_down_weight[:, :, 0, :]
    down_zeros = jnp.zeros((adapters, joint_rank, 1, held_down), f32)
    up_zeros = jnp.zeros((adapters, low_width, held_up), f32)

    plane_count = group_count * batch_count
    share = width // plane_count
    padded_down = (held_down + 127) // 128 * 128
    direct = (
        group_count == 2
        and seq_count == 4
        and share == down_width
        and batch_count == 2
        and share % 128 == 0
        and down_width % 128 == 0
        and frozen_rows % 16 == 0
        and 4 * up_width <= down_width
        and up_width > 128
        and 128 % (up_width - 128) == 0
        and 0 < held_up + held_down - padded_down <= padded_down - held_down
    )
    up_entries = []
    if direct:
        own_share = lax.dynamic_slice_in_dim(
            frozen_qkv_matrix, (group_index * batch_count + batch_index) * share, share, axis=1
        )
        before = shift(own_share, "seq", 1)
        after = shift(own_share, "seq", 3)
        far_down = shift(down_bank[far_bank], "batch", 1)
        far_up = shift(adapter_up_weight[far_bank], "batch", 1)
        own_down, own_up = down_bank[own_bank], adapter_up_weight[own_bank]
        payload_rows = 2 * joint_rank + low_width // 2
        pack_shapes = [(2 * frozen_rows, share), (frozen_rows + payload_rows, share)]
        pack_shapes += [(payload_rows, share)] * 3
        plane, forward, payload, *payloads = pl.pallas_call(
            pack_kernel,
            out_shape=[jax.ShapeDtypeStruct(shape, bf16) for shape in pack_shapes],
            in_specs=[in_vmem()] * 6,
            out_specs=[by_block(shape) for shape in pack_shapes],
            scratch_shapes=[
                pltpu.VMEM((SEGS * joint_rank, down_width), bf16),
                pltpu.VMEM((SEGS, low_width, 2 * held_up), bf16),
            ],
            compiler_params=pltpu.CompilerParams(vmem_limit_bytes=16 * mebibyte),
            cost_estimate=cost(0, 8 * frozen_rows * share),
            name="pack",
        )(own_down, far_down, own_up, far_up, before, after)

        def over_plane(value):
            over_both = [(at, plane_count - 1 - at) for at in range(plane_count)]
            return [
                shift(value, "batch", 1),
                shift(value, "groups", 1),
                lax.ppermute(value, ("groups", "batch"), over_both),
            ]

        plane_parts = over_plane(plane)
        forward = shift(forward, "seq", 1)
        middle = forward[:frozen_rows]
        middle_parts = over_plane(middle)
        payloads = [shift(part, "seq", steps + 2) for steps, part in enumerate(payloads)]
        arrays = [frozen_qkv_matrix, before, after, forward, payload] + payloads
        arrays += plane_parts + middle_parts

        def frozen_at(behind, batch_step, group_step):
            return frozen_place(seq_count, frozen_rows, share, behind, batch_step, group_step)

        def down_at(behind):
            return down_place(seq_count, features, down_width, behind)

        entries = [
            (0, 0, frozen_rows, frozen_place(seq_count, frozen_rows, None, 0, 0, 0)),
            (1, 0, frozen_rows, frozen_at(1, 0, 0)),
            (2, 0, frozen_rows, frozen_at(3, 0, 0)),
            (3, 0, frozen_rows, frozen_at(2, 0, 0)),
            (4, 0, 2 * joint_rank, down_at(0)),
            (3, frozen_rows, 2 * joint_rank, down_at(1)),
            (5, 0, 2 * joint_rank, down_at(2)),
            (6, 0, 2 * joint_rank, down_at(3)),
        ]
        up_entries = [(4, 2 * joint_rank, 0), (3, frozen_rows + 2 * joint_rank, 1)]
        up_entries += [(5, 2 * joint_rank, 2), (6, 2 * joint_rank, 3)]
        for number, (batch_step, group_step) in enumerate(((1, 0), (0, 1), (1, 1))):
            entries += [
                (7 + number, 0, frozen_rows, frozen_at(1, batch_step, group_step)),
                (7 + number, frozen_rows, frozen_rows, frozen_at(3, batch_step, group_step)),
                (10 + number, 0, frozen_rows, frozen_at(2, batch_step, group_step)),
            ]
        early = [forward, cosines, sines, bank_rows]
        column_blocks = pl.pallas_call(
            functools.partial(cut_kernel, len(early), seq_count),
            out_shape=[jax.ShapeDtypeStruct((rows, down_width), bf16)] * seq_count,
            in_specs=[in_vmem()] + [in_place()] * len(early),
            out_specs=[by_block((rows, down_width))] * seq_count,
            compiler_params=pltpu.CompilerParams(vmem_limit_bytes=16 * mebibyte),
            cost_estimate=cost(0, 4 * rows * width),
            name="cut",
        )(local_tokens, *early)
    else:
        bank_rows = sample_rows.reshape(-1)
        got_down = lax.all_to_all(
            down_bank[sample_rows], "batch", split_axis=0, concat_axis=0, tiled=True
        )
        got_up = lax.all_to_all(
            adapter_up_weight[sample_rows], "batch", split_axis=0, concat_axis=0, tiled=True
        )
        down_block = jnp.transpose(got_down, (1, 2, 0, 3)).reshape(SEGS * joint_rank, -1)
        up_block = jnp.transpose(got_up, (1, 2, 0, 3)).reshape(SEGS * low_width, -1)
        all_down = lax.all_gather(down_block, "seq", axis=0)
        all_up = lax.all_gather(up_block, "seq", axis=0)
        first = (seq_index >= half_count).astype(jnp.int32)
        merged = jnp.transpose(all_down, (1, 0, 2)).reshape(SEGS * joint_rank, -1)
        arrays = [
            lax.all_gather(frozen_qkv_matrix, "seq", axis=0, tiled=True),
            lax.dynamic_slice_in_dim(merged, first * joint_rank, 2 * joint_rank),
        ]
        entries = [
            (0, 0, features, whole_place(0)),
            (1, 0, 2 * joint_rank, whole_place(features)),
        ]
        up_rows = jnp.transpose(all_up, (1, 0, 2)).reshape(SEGS, low_width, -1)
        is_query = jnp.arange(up_rows.shape[2]) < query_columns
        up_blocks = jnp.concatenate(
            [
                jnp.where(is_query[None, None, :], up_rows, 0),
                jnp.where(is_query[None, None, :], 0, up_rows),
            ],
            axis=1,
        )
        column_blocks = [
            lax.dynamic_slice_in_dim(
                local_tokens,
                jnp.remainder(seq_index + steps, seq_count) * down_width,
                down_width,
                axis=1,
            )
            for steps in range(seq_count)
        ]

    column_parts = [
        shift(block, "seq", steps) if steps else block
        for steps, block in enumerate(column_blocks)
    ]
    early = [column_parts[2]] if direct and seq_count > 3 else []
    up_shape = (SEGS, joint_rank, query_columns + HEAD_WIDTH)
    matrix_rows = features + 2 * joint_rank
    arrived = [pltpu.VMEM((seq_count, low_width // 2, down_width), bf16)] if direct else []
    own_part, sent_part, rest_part, matrix, *built = pl.pallas_call(
        functools.partial(
            project_kernel, len(arrays), entries, up_entries, len(early), seq_count
        ),
        out_shape=[
            jax.ShapeDtypeStruct((own_rows, query_columns), f32),
            jax.ShapeDtypeStruct((own_rows, query_columns), f32),
            jax.ShapeDtypeStruct((rows, matrix_rows - query_columns), f32),
            jax.ShapeDtypeStruct((matrix_rows, width), bf16),
        ]
        + ([jax.ShapeDtypeStruct(up_shape, bf16)] if direct else []),
        in_specs=[in_vmem()] + [in_place()] * (len(arrays) + len(early)),
        out_specs=[in_vmem()] * 3 + [in_place()] + ([by_block(up_shape)] if direct else []),
        scratch_shapes=arrived
        + [
            pltpu.VMEM((matrix_rows, width), bf16),
            pltpu.SemaphoreType.DMA((len(entries) + len(up_entries) + 1,)),
        ],
        compiler_params=pltpu.CompilerParams(vmem_limit_bytes=20 * mebibyte),
        cost_estimate=cost(2 * rows * width * matrix_rows, 2 * width * (matrix_rows + rows)),
        name="project",
    )(local_tokens, *arrays, *early)
    if direct:
        up_blocks = built[0]

    other_part = shift(sent_part, "tp", 1)
    other_rest = shift(rest_part, "tp", 1)
    queries, pairs, low_rank = pl.pallas_call(
        functools.partial(qkv_kernel, seq_count, 1),
        out_shape=(
            jax.ShapeDtypeStruct((QHEADS * own_rows, HEAD_WIDTH), bf16),
            jax.ShapeDtypeStruct((rows, 2 * HEAD_WIDTH), bf16),
            jax.ShapeDtypeStruct((rows, joint_rank), bf16),
        ),
        in_specs=[in_smem()] + [in_vmem()] * 7 + [in_place()],
        out_specs=(in_vmem(),) * 3,
        compiler_params=pltpu.CompilerParams(vmem_limit_bytes=8 * mebibyte),
        cost_estimate=cost(2 * rows * 3 * 64 * 640, 8 * rows * features),
        name="qkv",
    )(
        document_lengths, own_part, other_part, rest_part, other_rest, up_blocks, cosines, sines,
        column_parts[1],
    )

    blocks = [pairs] + [push(pairs, "seq", back) for back in range(1, half_count + 1)]
    block_count = len(blocks)
    incoming = output_gradient[0]
    early_columns = []
    attention, query_grad, kept, sent = pl.pallas_call(
        functools.partial(attention_kernel, block_count, len(early_columns)),
        out_shape=(
            jax.ShapeDtypeStruct((own_rows, query_columns), bf16),
            jax.ShapeDtypeStruct((own_rows, query_columns), bf16),
            jax.ShapeDtypeStruct((block_count, own_rows, 2 * HEAD_WIDTH), f32),
            jax.ShapeDtypeStruct((block_count, own_rows, 2 * HEAD_WIDTH), f32),
        ),
        in_specs=[in_smem()]
        + [in_vmem()] * (4 + block_count)
        + [in_place()] * len(early_columns),
        out_specs=(in_vmem(),) * 4,
        scratch_shapes=[pltpu.VMEM((block_count, QHEADS * own_rows, rows), bf16)],
        compiler_params=pltpu.CompilerParams(vmem_limit_bytes=(8 + 4 * block_count) * mebibyte),
        cost_estimate=cost(
            10 * block_count * QHEADS * own_rows * rows * HEAD_WIDTH,
            4 * rows * features,
            block_count * QHEADS * own_rows * rows,
        ),
        name="attention",
    )(document_lengths, queries, incoming, cosines, sines, *blocks, *early_columns)

    other_query = shift(query_grad, "tp", 1)
    pair_sums = pl.pallas_call(
        sum_kernel,
        out_shape=[jax.ShapeDtypeStruct((own_rows, 2 * HEAD_WIDTH), f32)] * block_count,
        in_specs=[in_vmem()] * 2,
        out_specs=[in_vmem()] * block_count,
        compiler_params=pltpu.CompilerParams(vmem_limit_bytes=8 * mebibyte),
        cost_estimate=cost(0, 12 * block_count * own_rows * 2 * HEAD_WIDTH),
        name="pair_sums",
    )(kept, shift(sent, "tp", 1))
    pair_terms = [pair_sums[0]]
    pair_terms += [push(pair_sums[back], "seq", -back) for back in range(1, block_count)]
    pair_grad, late_block = pl.pallas_call(
        functools.partial(pair_kernel, block_count),
        out_shape=[
            jax.ShapeDtypeStruct((own_rows, 2 * HEAD_WIDTH), bf16),
            jax.ShapeDtypeStruct((rows, down_width), bf16),
        ],
        in_specs=[in_vmem()] * (2 + block_count) + [in_place()],
        out_specs=[in_vmem(), in_place()],
        input_output_aliases={2 + block_count: 1},
        compiler_params=pltpu.CompilerParams(vmem_limit_bytes=8 * mebibyte),
        cost_estimate=cost(0, 12 * block_count * own_rows * 2 * HEAD_WIDTH),
        name="pair_gradients",
    )(cosines, sines, *pair_terms, column_blocks[-1])
    column_parts[-1] = shift(late_block, "seq", seq_count - 1)
    other_pair = shift(pair_grad, "tp", 1)

    split_shapes = [(SEGS * low_width, up_width)] * seq_count
    if direct:
        sent_rows = SEGS * low_width * up_width // 128 + rows // 2
        split_shapes[1:] = [(sent_rows, 128)] * (seq_count - 1)
    gradients, rank_grad, *up_split = pl.pallas_call(
        functools.partial(rank_kernel, seq_count),
        out_shape=[
            jax.ShapeDtypeStruct((rows, matrix_rows), bf16),
            jax.ShapeDtypeStruct((rows, joint_rank), bf16),
        ]
        + [jax.ShapeDtypeStruct(shape, f32) for shape in split_shapes],
        in_specs=[in_smem()] + [in_vmem()] * 6,
        out_specs=[by_block((rows, matrix_rows)), in_vmem()]
        + [by_block(shape) for shape in split_shapes],
        scratch_shapes=[
            pltpu.VMEM((SEGS * low_width, features - HEAD_WIDTH), f32),
            pltpu.VMEM((seq_count, SEGS * low_width, held_up * batch_count), f32),
        ],
        compiler_params=pltpu.CompilerParams(vmem_limit_bytes=8 * mebibyte),
        cost_estimate=cost(4 * rows * 3 * 64 * 640, 4 * rows * features),
        name="rank_gradients",
    )(
        document_lengths, query_grad, other_query, pair_grad, other_pair, low_rank, up_blocks
    )

    rank_parts = [rank_grad]
    if not direct:
        rank_parts += [shift(rank_grad, "seq", steps) for steps in range(1, seq_count)]
    up_sums = [
        shift(block, "seq", steps) if steps else block for steps, block in enumerate(up_split)
    ]

    chunk = 512
    token_grad, down_zeros, up_zeros = pl.pallas_call(
        token_kernel,
        grid=(width // chunk,),
        out_shape=[
            jax.ShapeDtypeStruct((rows, width), bf16),
            jax.ShapeDtypeStruct(down_zeros.shape, f32),
            jax.ShapeDtypeStruct(up_zeros.shape, f32),
        ],
        in_specs=[
            pl.BlockSpec((rows, matrix_rows), lambda step: (0, 0)),
            pl.BlockSpec((matrix_rows, chunk), lambda step: (0, step)),
            in_place(),
            in_place(),
        ],
        out_specs=[
            pl.BlockSpec((rows, chunk), lambda step: (0, step)),
            in_place(),
            in_place(),
        ],
        input_output_aliases={2: 1, 3: 2},
        compiler_params=pltpu.CompilerParams(vmem_limit_bytes=12 * mebibyte),
        cost_estimate=cost(2 * rows * width * matrix_rows, 2 * width * (matrix_rows + rows)),
        name="token_gradient",
    )(gradients, matrix, down_zeros, up_zeros)

    if direct:
        term_shapes = [(SEGS * joint_rank, held_down), (SEGS * joint_rank, padded_down)]
        term_shapes += [(SEGS * low_width, held_up)]
    else:
        term_shapes = [(SEGS * joint_rank, down_width), (SEGS * low_width, up_width)]
    terms = pl.pallas_call(
        functools.partial(down_kernel, seq_count),
        out_shape=[jax.ShapeDtypeStruct(shape, f32) for shape in term_shapes],
        in_specs=[in_smem()] + [in_vmem()] * (2 * seq_count + len(rank_parts)),
        out_specs=[in_vmem()] * len(term_shapes),
        scratch_shapes=[pltpu.VMEM((SEGS * low_width, up_width), f32)] if direct else [],
        compiler_params=pltpu.CompilerParams(vmem_limit_bytes=8 * mebibyte),
        cost_estimate=cost(
            2 * seq_count * rows * SEGS * joint_rank * down_width, 2 * seq_count * rows * down_width
        ),
        name="down_terms",
    )(document_lengths, *column_parts, *up_sums, *rank_parts)

    if direct:
        bank_terms = [terms[0], shift(terms[1], "batch", 1), terms[2]]
    else:
        down_send = jnp.transpose(
            terms[0].reshape(SEGS * joint_rank, batch_count, held_down), (1, 0, 2)
        )
        up_send = jnp.transpose(
            terms[1].reshape(SEGS * low_width, batch_count, held_up), (1, 0, 2)
        )
        back_down = lax.all_to_all(down_send, "batch", split_axis=0, concat_axis=0, tiled=True)
        back_up = lax.all_to_all(up_send, "batch", split_axis=0, concat_axis=0, tiled=True)
        bank_downs = [back_down[batch] for batch in range(batch_count)]
        bank_ups = [back_up[batch] for batch in range(batch_count)]
        bank_terms = bank_downs + bank_ups


    def whole(array):
        return pl.BlockSpec(array.shape, lambda step, bank: (0,) * array.ndim)

    term_count = len(bank_terms)
    down_grad, up_grad = pl.pallas_call(
        packed_bank_kernel if direct else functools.partial(bank_kernel, batch_count),
        out_shape=(
            jax.ShapeDtypeStruct(down_zeros.shape, f32),
            jax.ShapeDtypeStruct(up_zeros.shape, f32),
        ),
        grid_spec=pltpu.PrefetchScalarGridSpec(
            num_scalar_prefetch=1,
            grid=(batch_count * SEGS,),
            in_specs=[whole(array) for array in bank_terms] + [in_place()] * 2,
            out_specs=(
                pl.BlockSpec(
                    (1, joint_rank, 1, held_down),
                    lambda step, bank: (bank[step], 0, 0, 0),
                ),
                pl.BlockSpec(
                    (1, low_width, held_up),
                    lambda step, bank: (bank[step], 0, 0),
                ),
            ),
        ),
        input_output_aliases={1 + term_count: 0, 2 + term_count: 1},
        compiler_params=pltpu.CompilerParams(vmem_limit_bytes=16 * mebibyte),
        name="bank_rows",
    )(
        bank_rows,
        *bank_terms,
        down_zeros,
        up_zeros,
    )
    return (attention[None], token_grad[None], down_grad, up_grad)


def solution(mesh):
    in_specs = (
        P(("groups", "batch"), "seq", "tp"),
        P("seq", "tp"),
        P(None, None, "tp", ("seq", "batch")),
        P(None, None, ("seq", "batch")),
        P(),
        P("groups", None),
        P("groups", None),
        P(("groups", "batch"), ("seq", "tp"), None),
    )
    out_specs = (
        P(("groups", "batch"), ("seq", "tp"), None),
        P(("groups", "batch"), "seq", "tp"),
        P("groups", None, "tp", ("seq", "batch")),
        P("groups", None, ("seq", "batch")),
    )
    return jax.shard_map(shards, mesh=mesh, in_specs=in_specs, out_specs=out_specs, check_vma=False)
```

```python
import functools

import jax
import jax.numpy as jnp
from jax import lax
from jax.experimental import pallas as pl
from jax.experimental.pallas import tpu as pltpu
from jax.sharding import PartitionSpec as P

QHEADS = 4
HEAD_WIDTH = 128
ADAPTER_RANK = 32
SEGS = 3

adapter_scale = 2.0
rope_base = 5000000.0
masked_score = -1e30
mebibyte = 1024 * 1024


def shift(value, axis, steps):
    count = lax.axis_size(axis)
    return lax.ppermute(value, axis, [(at, (at + steps) % count) for at in range(count)])


def push(value, axis, steps):
    count = lax.axis_size(axis)
    pairs = [(at, at + steps) for at in range(count) if 0 <= at + steps < count]
    return lax.ppermute(value, axis, pairs)


def dot_nt(left, right):
    return lax.dot_general(
        left, right, (((1,), (1,)), ((), ())), preferred_element_type=jnp.float32
    )


def dot_nn(left, right):
    return jnp.dot(left, right, preferred_element_type=jnp.float32)


def dot_tn(left, right):
    return lax.dot_general(
        left, right, (((0,), (0,)), ((), ())), preferred_element_type=jnp.float32
    )


def lookup_rows(adapter_bank_row, document_adapter):
    matches = document_adapter[..., None] == jnp.arange(adapter_bank_row.shape[0], dtype=jnp.int32)
    return jnp.sum(jnp.where(matches, adapter_bank_row, 0), axis=-1)


def row_positions(first, count):
    return first + lax.broadcasted_iota(jnp.int32, (count, 1), 0)


def ring_index(index, count):
    return lax.rem(index + count, count)


def kernel_marks(lengths):
    batch = lax.axis_index("batch")
    first_end = lengths[batch, 0]
    return first_end, first_end + lengths[batch, 1]


def row_segments(ends, positions):
    return (positions >= ends[0]).astype(jnp.int32) + (positions >= ends[1]).astype(jnp.int32)


def cost(flops, bytes_accessed, transcendentals=0):
    return pl.CostEstimate(
        flops=flops, bytes_accessed=bytes_accessed, transcendentals=transcendentals
    )


def in_vmem():
    return pl.BlockSpec(memory_space=pltpu.VMEM)


def in_smem():
    return pl.BlockSpec(memory_space=pltpu.SMEM)


def by_block(shape):
    return pl.BlockSpec(shape, lambda: (0,) * len(shape))


def in_place():
    return pl.BlockSpec(memory_space=pl.ANY)


def fetch(piece, target, place, semaphore):
    height, width = piece.shape
    row, column = place()
    copy = pltpu.make_async_copy(
        piece,
        target.at[
            pl.ds(pl.multiple_of(row, 16), height), pl.ds(pl.multiple_of(column, 128), width)
        ],
        semaphore,
    )
    copy.start()
    return copy


def frozen_place(seq_count, rows, share, behind, batch_step, group_step):
    def place():
        holder = ring_index(lax.axis_index("seq") - behind, seq_count)
        if share is None:
            return holder * rows, 0
        batch = lax.rem(lax.axis_index("batch") + batch_step, 2)
        group = lax.rem(lax.axis_index("groups") + group_step, 2)
        return holder * rows, (group * 2 + batch) * share

    return place


def down_place(seq_count, features, width, behind):
    def place():
        return features, ring_index(lax.axis_index("seq") - behind, seq_count) * width

    return place


def whole_place(row):
    def place():
        return row, 0

    return place


def pack_kernel(own_down, far_down, own_up, far_up, before, after, *refs):
    plane, forward, payloads, (down, up) = refs[0], refs[1], refs[2:-2], refs[-2:]
    ahead = lax.axis_index("batch") == 0
    joint_rank, held = own_down.shape[1:]
    low_width, held_up = own_up.shape[1:]
    frozen_rows = before.shape[0]
    plane[:frozen_rows] = before[...]
    plane[frozen_rows:] = after[...]
    forward[:frozen_rows] = before[...]
    for document in range(SEGS):
        rows = slice(document * joint_rank, (document + 1) * joint_rank)
        down[rows, :held] = jnp.where(ahead, own_down[document], far_down[document])
        down[rows, held:] = jnp.where(ahead, far_down[document], own_down[document])
        up[document, :, :held_up] = jnp.where(ahead, own_up[document], far_up[document])
        up[document, :, held_up:] = jnp.where(ahead, far_up[document], own_up[document])
    half, slot = low_width // 2, down.shape[1] // 4
    targets = [(0, payloads[0], 0), (1, forward, frozen_rows)]
    targets += [(steps + 2, payload, 0) for steps, payload in enumerate(payloads[1:])]
    seq_count = len(targets)
    for steps, payload, base in targets:
        target = ring_index(lax.axis_index("seq") + steps - seq_count, seq_count)
        first = (target >= seq_count // 2).astype(jnp.int32)
        start = pl.multiple_of(first * joint_rank, joint_rank)
        payload[base : base + 2 * joint_rank] = down[pl.ds(start, 2 * joint_rank)]
        base = base + 2 * joint_rank
        for index in range(2):
            block = up[first + index]
            for part in range(2):
                column = (2 * index + part) * slot
                payload[base : base + half, column : column + 2 * held_up] = block[
                    part * half : (part + 1) * half
                ]


def pass_kernel(*refs):
    del refs


def pass_after(value, *earlier):
    return pl.pallas_call(
        pass_kernel,
        out_shape=jax.ShapeDtypeStruct(value.shape, value.dtype),
        in_specs=[in_place()] * (1 + len(earlier)),
        out_specs=in_place(),
        input_output_aliases={0: 0},
        name="pass_after",
    )(value, *earlier)


def pick_kernel(forward, *refs):
    middle = refs[-1]
    middle[...] = forward[: middle.shape[0]]


def cut_kernel(unused, seq_count, tokens, *refs):
    for steps, block in enumerate(refs[unused:]):
        target = ring_index(lax.axis_index("seq") + steps - seq_count, seq_count)
        width = block.shape[1]
        block[...] = tokens[:, pl.ds(pl.multiple_of(target * width, 128), width)]


def assemble_up(seq_count, arrived, up_blocks):
    low_width = up_blocks.shape[1] // 2
    query_columns = QHEADS * HEAD_WIDTH
    seq_index = lax.axis_index("seq")
    first = (seq_index >= seq_count // 2).astype(jnp.int32)
    held = up_blocks.shape[2] // seq_count
    half, slot = low_width // 2, arrived.shape[2] // 4
    up_blocks[...] = jnp.zeros_like(up_blocks)
    for holder in range(seq_count):
        block = arrived[ring_index(seq_index - holder, seq_count)]
        start, stop = holder * held, (holder + 1) * held
        middle = min(max(query_columns, start), stop)
        for index in range(2):
            for part in range(2):
                offset = (2 * index + part) * slot
                if middle > start:
                    up_blocks[first + index, part * half : (part + 1) * half, start:middle] = block[
                        :, offset : offset + middle - start
                    ]
                if stop > middle:
                    low = low_width + part * half
                    up_blocks[first + index, low : low + half, middle:stop] = block[
                        :, offset + middle - start : offset + held
                    ]


def project_kernel(array_count, entries, up_entries, unused, seq_count, tokens, *refs):
    arrays = refs[:array_count]
    refs = refs[array_count + unused :]
    own_query, sent_query, rest, matrix = refs[:4]
    weights, semaphore = refs[-2:]
    copies = []
    for number, start, height, place in entries:
        piece = arrays[number].at[pl.ds(start, height)]
        copies.append(fetch(piece, weights, place, semaphore.at[len(copies)]))
    for number, start, slot in up_entries:
        copy = pltpu.make_async_copy(
            arrays[number].at[pl.ds(start, refs[5].shape[1])],
            refs[5].at[slot],
            semaphore.at[len(copies)],
        )
        copy.start()
        copies.append(copy)
    for copy in copies:
        copy.wait()
    keep = pltpu.make_async_copy(weights, matrix, semaphore.at[len(copies)])
    keep.start()
    part = dot_nt(tokens[...], weights[...])
    own_rows, query_columns = own_query.shape
    first = lax.axis_index("tp") == 0
    upper, lower = part[:own_rows, :query_columns], part[own_rows:, :query_columns]
    own_query[...] = jnp.where(first, upper, lower)
    sent_query[...] = jnp.where(first, lower, upper)
    rest[...] = part[:, query_columns:]
    if up_entries:
        assemble_up(seq_count, refs[5], refs[4])
    keep.wait()


def rotated(values, cosines, sines):
    return values * cosines + pltpu.roll(values, values.shape[1] // 2, 1) * sines


def qkv_kernel(
    seq_count, unused, lengths, own_query, other_query, mine, theirs, up_blocks, cosines, sines, *refs
):
    queries, pairs, low_rank = refs[unused:]
    rows, joint_rank = low_rank.shape
    own_rows, query_columns = own_query.shape
    start_low, middle = 2 * HEAD_WIDTH, 2 * HEAD_WIDTH + joint_rank
    ends = kernel_marks(lengths)

    def low_rows(picked, second):
        first_low = mine[picked, start_low:middle] + theirs[picked, start_low:middle]
        second_low = mine[picked, middle:] + theirs[picked, middle:]
        return jnp.where(second, second_low, first_low).astype(jnp.bfloat16)

    first = (lax.axis_index("seq") >= seq_count // 2).astype(jnp.int32)
    first_row = lax.axis_index("seq") * rows
    segments = row_segments(ends, row_positions(first_row, rows))
    low = low_rows(slice(None), segments != first)
    low_rank[...] = low
    value_delta = jnp.zeros((rows, HEAD_WIDTH), jnp.float32)
    for document in range(SEGS):
        chosen = jnp.where(segments == document, low, jnp.zeros_like(low))
        value_delta += dot_nn(chosen, up_blocks[document, :, query_columns:])
    keys = mine[:, :HEAD_WIDTH] + theirs[:, :HEAD_WIDTH]
    pairs[:, :HEAD_WIDTH] = rotated(keys, cosines[...], sines[...]).astype(jnp.bfloat16)
    values = mine[:, HEAD_WIDTH:start_low] + theirs[:, HEAD_WIDTH:start_low]
    pairs[:, HEAD_WIDTH:] = (values + adapter_scale * value_delta).astype(jnp.bfloat16)
    start = pl.multiple_of(lax.axis_index("tp") * own_rows, own_rows)
    own = pl.ds(start, own_rows)
    own_segments = row_segments(ends, row_positions(first_row + start, own_rows))
    own_low = low_rows(own, own_segments != first)
    query_delta = jnp.zeros((own_rows, query_columns), jnp.float32)
    for document in range(SEGS):
        chosen = jnp.where(own_segments == document, own_low, jnp.zeros_like(own_low))
        query_delta += dot_nn(chosen, up_blocks[document, :, :query_columns])
    projected = own_query[...] + other_query[...]
    projected = projected + adapter_scale * query_delta
    for head in range(QHEADS):
        turned = rotated(
            projected[:, head * HEAD_WIDTH : (head + 1) * HEAD_WIDTH], cosines[own], sines[own]
        )
        queries[head * own_rows : (head + 1) * own_rows] = turned.astype(jnp.bfloat16)


def attention_kernel(block_count, unused, lengths, queries, incoming, cosines, sines, *refs):
    blocks = refs[:block_count]
    output, query_grad, kept, sent, low_probs = refs[block_count + unused :]
    own_rows, query_columns = incoming.shape
    rows = blocks[0].shape[0]
    score_scale = HEAD_WIDTH ** (-0.5)
    ends = kernel_marks(lengths)
    seq_index, tp_index = lax.axis_index("seq"), lax.axis_index("tp")
    positions = row_positions(seq_index * rows + tp_index * own_rows, own_rows)
    positions = jnp.concatenate([positions] * QHEADS, axis=0)
    segments = row_segments(ends, positions)
    starts = jnp.where(segments == 0, 0, jnp.where(segments == 1, ends[0], ends[1]))
    scores = []
    for back, block in enumerate(blocks):
        key_positions = (seq_index - back) * rows + lax.broadcasted_iota(jnp.int32, (1, rows), 1)
        allowed = (key_positions <= positions) & (key_positions >= starts)
        block_scores = dot_nt(queries[...], block[:, :HEAD_WIDTH]) * score_scale
        scores.append(jnp.where(allowed, block_scores, masked_score))
    row_max = functools.reduce(
        jnp.maximum, [jnp.max(part, axis=1, keepdims=True) for part in scores]
    )
    raised = [jnp.exp(part - row_max) for part in scores]
    row_total = sum(jnp.sum(part, axis=1, keepdims=True) for part in raised)
    inverse = 1.0 / row_total
    probs = [part * inverse for part in raised]
    weighted = jnp.zeros((QHEADS * own_rows, HEAD_WIDTH), jnp.float32)
    for back, block in enumerate(blocks):
        low_probs[back] = probs[back].astype(jnp.bfloat16)
        weighted += dot_nn(low_probs[back], block[:, HEAD_WIDTH:])
    attended = weighted.astype(jnp.bfloat16)
    gradients = jnp.concatenate(
        [incoming[:, head * HEAD_WIDTH : (head + 1) * HEAD_WIDTH] for head in range(QHEADS)],
        axis=0,
    )
    row_delta = jnp.sum(
        gradients.astype(jnp.float32) * attended.astype(jnp.float32), axis=1, keepdims=True
    )
    start = pl.multiple_of(tp_index * own_rows, own_rows)
    total = jnp.zeros((QHEADS * own_rows, HEAD_WIDTH), jnp.float32)
    for back, block in enumerate(blocks):
        prob_grad = dot_nt(gradients, block[:, HEAD_WIDTH:])
        score_grad = (probs[back] * (prob_grad - row_delta)).astype(jnp.bfloat16)
        total += dot_nn(score_grad, block[:, :HEAD_WIDTH])
        key_part = dot_tn(score_grad, queries[...]) * score_scale
        value_part = dot_tn(low_probs[back], gradients)
        mine = tp_index == 0
        kept[back, :, :HEAD_WIDTH] = jnp.where(mine, key_part[:own_rows], key_part[own_rows:])
        sent[back, :, :HEAD_WIDTH] = jnp.where(mine, key_part[own_rows:], key_part[:own_rows])
        kept[back, :, HEAD_WIDTH:] = jnp.where(mine, value_part[:own_rows], value_part[own_rows:])
        sent[back, :, HEAD_WIDTH:] = jnp.where(mine, value_part[own_rows:], value_part[:own_rows])
    own = pl.ds(start, own_rows)
    for head in range(QHEADS):
        picked = slice(head * own_rows, (head + 1) * own_rows)
        columns = slice(head * HEAD_WIDTH, (head + 1) * HEAD_WIDTH)
        output[:, columns] = attended[picked]
        query_grad[:, columns] = rotated(
            total[picked] * score_scale, cosines[own], -sines[own]
        ).astype(jnp.bfloat16)


def sum_kernel(unused, kept, arrived, *refs):
    for back, total in enumerate(refs[unused:]):
        total[...] = kept[back] + arrived[back]


def pair_kernel(terms, cosines, sines, *refs):
    parts, pair = refs[:terms], refs[-1]
    own_rows = pair.shape[0]
    total = sum(part[...] for part in parts)
    own = pl.ds(pl.multiple_of(lax.axis_index("tp") * own_rows, own_rows), own_rows)
    keys = rotated(total[:, :HEAD_WIDTH], cosines[own], -sines[own])
    pair[:, :HEAD_WIDTH] = keys.astype(jnp.bfloat16)
    pair[:, HEAD_WIDTH:] = total[:, HEAD_WIDTH:].astype(jnp.bfloat16)


def rank_kernel(
    seq_count, lengths, own_query, other_query, own_pair, other_pair, low_rank, up_blocks, *refs
):
    gradients, rank_grad = refs[:2]
    split_terms, (terms, blocks) = refs[2:-2], refs[-2:]
    own_rows, query_columns = own_query.shape
    rows = low_rank.shape[0]
    seq_index = lax.axis_index("seq")
    start = pl.multiple_of(lax.axis_index("tp") * own_rows, own_rows)
    other = pl.multiple_of(own_rows - start, own_rows)
    gradients[pl.ds(start, own_rows), :query_columns] = own_query[...]
    gradients[pl.ds(other, own_rows), :query_columns] = other_query[...]
    value_start = query_columns + HEAD_WIDTH
    features = value_start + HEAD_WIDTH
    gradients[pl.ds(start, own_rows), query_columns:features] = own_pair[...]
    gradients[pl.ds(other, own_rows), query_columns:features] = other_pair[...]
    query_grad = gradients[:, :query_columns]
    value_grad = gradients[:, value_start:features]
    low = low_rank[...]
    rank = low.shape[1] // 2
    segments = row_segments(kernel_marks(lengths), row_positions(seq_index * rows, rows))
    total = jnp.zeros((rows, low.shape[1]), jnp.float32)
    for document in range(SEGS):
        member = segments == document
        parts = dot_nt(query_grad, up_blocks[document, :, :query_columns])
        parts += dot_nt(value_grad, up_blocks[document, :, query_columns:])
        total = jnp.where(member, parts, total)
        chosen = jnp.where(member, low, jnp.zeros_like(low))
        query_terms = dot_tn(chosen, query_grad)
        value_terms = dot_tn(chosen, value_grad)
        place = slice(document * rank, (document + 1) * rank)
        terms[place, :query_columns] = adapter_scale * query_terms[:rank]
        terms[place, query_columns:] = adapter_scale * value_terms[rank:]
    turned = (adapter_scale * total).astype(jnp.bfloat16)
    rank_grad[...] = turned
    second = segments != (seq_index >= seq_count // 2).astype(jnp.int32)
    nothing = jnp.zeros_like(turned)
    middle = features + low.shape[1]
    gradients[:, features:middle] = jnp.where(second, nothing, turned)
    gradients[:, middle:] = jnp.where(second, turned, nothing)
    held = blocks.shape[2]
    for holder in range(seq_count):
        blocks[holder] = terms[:, holder * held : (holder + 1) * held]
    for steps, block in enumerate(split_terms):
        mine = blocks[ring_index(seq_index + steps - seq_count, seq_count)]
        if block.shape == mine.shape:
            block[...] = mine
            continue
        tail = held - 128
        count = 128 // tail
        height = mine.shape[0] // count
        first_low = mine.shape[0] + height
        block[: mine.shape[0]] = mine[:, :128]
        for part in range(count):
            block[mine.shape[0] : first_low, part * tail : (part + 1) * tail] = mine[
                part * height : (part + 1) * height, 128:
            ]
        block[first_low:, : low.shape[1]] = turned[: rows // 2].astype(jnp.float32)
        block[first_low:, low.shape[1] :] = turned[rows // 2 :].astype(jnp.float32)


def token_kernel(gradients, matrix, token_grad):
    token_grad[...] = dot_nn(gradients[...], matrix[...]).astype(jnp.bfloat16)


def down_kernel(block_count, lengths, *refs):
    columns = refs[:block_count]
    up_parts = refs[block_count : 2 * block_count]
    packed = up_parts[0].shape != up_parts[1].shape
    rank_count = 1 if packed else block_count
    ranks = refs[2 * block_count : 2 * block_count + rank_count]
    outputs = refs[2 * block_count + rank_count :]
    rows, joint_rank = ranks[0].shape
    ends = kernel_marks(lengths)
    up_rows, up_width = up_parts[0].shape
    lows, ups = [ranks[0][...]], [up_parts[0][...]]
    for behind in range(1, block_count):
        if not packed:
            lows.append(ranks[behind][...])
            ups.append(up_parts[behind][...])
            continue
        part = up_parts[behind]
        count = 128 // (up_width - 128)
        first_low = up_rows + up_rows // count
        halves = [part[first_low:, :joint_rank], part[first_low:, joint_rank:]]
        lows.append(jnp.concatenate(halves, axis=0).astype(jnp.bfloat16))
    all_terms = []
    for document in range(SEGS):
        total = jnp.zeros((joint_rank, columns[0].shape[1]), jnp.float32)
        for behind in range(block_count):
            holder = ring_index(lax.axis_index("seq") - behind, block_count)
            segments = row_segments(ends, row_positions(holder * rows, rows))
            chosen = jnp.where(segments == document, lows[behind], jnp.zeros_like(lows[behind]))
            total += dot_tn(chosen, columns[behind][...])
        all_terms.append(total)
    down_terms = jnp.concatenate(all_terms, axis=0)
    if not packed:
        outputs[0][...] = down_terms
        outputs[1][...] = sum(ups)
        return
    own_down, far, own_up, up_terms = outputs
    tail = up_width - 128
    height = up_rows // (128 // tail)
    up_terms[...] = ups[0]
    for part in up_parts[1:]:
        up_terms[:, :128] += part[:up_rows]
        for piece in range(128 // tail):
            up_terms[piece * height : (piece + 1) * height, 128:] += part[
                up_rows : up_rows + height, piece * tail : (piece + 1) * tail
            ]
    held, held_up = own_down.shape[1], own_up.shape[1]
    ahead = lax.axis_index("batch") == 0
    own_down[...] = jnp.where(ahead, down_terms[:, :held], down_terms[:, held:])
    far[:, :held] = jnp.where(ahead, down_terms[:, held:], down_terms[:, :held])
    left, right = up_terms[:, :held_up], up_terms[:, held_up:]
    own_up[...] = jnp.where(ahead, left, right)
    far_up = jnp.where(ahead, right, left)
    spare = far.shape[1] - held
    far[:up_rows, held:] = far_up[:, :spare]
    far[up_rows:, held : held + held_up - spare] = far_up[:, spare:]


def packed_bank_kernel(bank_rows, own_down, far, own_up, down_zeros, up_zeros, down_out, up_out):
    step = pl.program_id(0)
    joint_rank, held = down_out.shape[1], down_out.shape[3]
    low_width, held_up = up_out.shape[1:]
    up_rows = own_up.shape[0]
    spare = far.shape[1] - held
    down_total = jnp.zeros((joint_rank, held), jnp.float32)
    head = jnp.zeros((low_width, spare), jnp.float32)
    rest = jnp.zeros((low_width, held_up - spare), jnp.float32)
    for document in range(SEGS):
        rows = slice(document * joint_rank, (document + 1) * joint_rank)
        lows = slice(document * low_width, (document + 1) * low_width)
        same = bank_rows[document] == bank_rows[step]
        down_total += jnp.where(same, own_down[rows], 0.0)
        head += jnp.where(same, own_up[lows, :spare], 0.0)
        rest += jnp.where(same, own_up[lows, spare:], 0.0)
        same = bank_rows[SEGS + document] == bank_rows[step]
        down_total += jnp.where(same, far[rows, :held], 0.0)
        head += jnp.where(same, far[lows, held:], 0.0)
        lows = slice(up_rows + document * low_width, up_rows + (document + 1) * low_width)
        rest += jnp.where(same, far[lows, held : held + held_up - spare], 0.0)
    down_out[0, :, 0, :] = down_total
    up_out[0, :, :spare] = head
    up_out[0, :, spare:] = rest


def bank_kernel(block_count, bank_rows, *refs):
    down_terms = refs[:block_count]
    up_terms = refs[block_count : 2 * block_count]
    down_out, up_out = refs[2 * block_count + 2 :]
    step = pl.program_id(0)
    row = bank_rows[step]
    joint_rank = down_out.shape[1]
    low_width = up_out.shape[1]
    down_total = jnp.zeros((joint_rank, down_out.shape[3]), jnp.float32)
    up_total = jnp.zeros((low_width, up_out.shape[2]), jnp.float32)
    for block in range(block_count):
        for document in range(SEGS):
            same = bank_rows[block * SEGS + document] == row
            down_rows = down_terms[block][document * joint_rank : (document + 1) * joint_rank]
            up_rows = up_terms[block][document * low_width : (document + 1) * low_width]
            down_total += jnp.where(same, down_rows, 0.0)
            up_total += jnp.where(same, up_rows, 0.0)
    down_out[0, :, 0, :] = down_total
    up_out[0] = up_total


def shards(
    tokens,
    frozen_qkv_matrix,
    adapter_down_weight,
    adapter_up_weight,
    adapter_bank_row,
    document_lengths,
    document_adapter,
    output_gradient,
):
    seq_count = lax.axis_size("seq")
    batch_count = lax.axis_size("batch")
    group_count = lax.axis_size("groups")
    chip_size = lax.axis_size("tp")
    seq_index = lax.axis_index("seq")
    batch_index = lax.axis_index("batch")
    group_index = lax.axis_index("groups")
    tp_index = lax.axis_index("tp")
    local_tokens = tokens[0]
    rows, width = local_tokens.shape
    own_rows = rows // chip_size
    query_columns = QHEADS * HEAD_WIDTH
    frozen_rows = frozen_qkv_matrix.shape[0]
    features = frozen_rows * seq_count
    low_width = ADAPTER_RANK
    joint_rank = adapter_down_weight.shape[1]
    adapters = adapter_bank_row.shape[0]
    bf16 = jnp.bfloat16
    f32 = jnp.float32

    lengths = lax.dynamic_index_in_dim(document_lengths, batch_index, 0, keepdims=False)
    first_end = lengths[0]
    second_end = first_end + lengths[1]
    half_count = seq_count // 2
    held_down = adapter_down_weight.shape[3]
    held_up = adapter_up_weight.shape[2]
    down_width = held_down * batch_count
    up_width = held_up * batch_count

    positions = seq_index * rows + jnp.arange(rows, dtype=jnp.int32)
    inside = positions - jnp.where(
        positions >= second_end, second_end, jnp.where(positions >= first_end, first_end, 0)
    )
    exponent = jnp.arange(HEAD_WIDTH // 2, dtype=f32) * (2.0 / HEAD_WIDTH)
    inverse = jnp.power(jnp.float32(rope_base), -exponent)
    angles = inside.astype(f32)[:, None] * jnp.concatenate([inverse, inverse])[None, :]
    signs = jnp.where(jnp.arange(HEAD_WIDTH) < HEAD_WIDTH // 2, -1.0, 1.0).astype(f32)
    cosines = jnp.cos(angles)
    sines = jnp.sin(angles) * signs[None, :]

    sample_rows = lookup_rows(adapter_bank_row, document_adapter)
    bank_rows = sample_rows.reshape(-1)
    if batch_count == 2:
        own_bank = jnp.where(batch_index == 0, sample_rows[0], sample_rows[1])
        far_bank = jnp.where(batch_index == 0, sample_rows[1], sample_rows[0])
        bank_rows = jnp.concatenate([own_bank, far_bank])
    down_bank = adapter_down_weight[:, :, 0, :]
    down_zeros = jnp.zeros((adapters, joint_rank, 1, held_down), f32)
    up_zeros = jnp.zeros((adapters, low_width, held_up), f32)

    plane_count = group_count * batch_count
    share = width // plane_count
    padded_down = (held_down + 127) // 128 * 128
    direct = (
        group_count == 2
        and seq_count == 4
        and share == down_width
        and batch_count == 2
        and share % 128 == 0
        and down_width % 128 == 0
        and frozen_rows % 16 == 0
        and 4 * up_width <= down_width
        and up_width > 128
        and 128 % (up_width - 128) == 0
        and 0 < held_up + held_down - padded_down <= padded_down - held_down
    )
    up_entries = []
    if direct:
        own_share = lax.dynamic_slice_in_dim(
            frozen_qkv_matrix, (group_index * batch_count + batch_index) * share, share, axis=1
        )
        before = shift(own_share, "seq", 1)
        after = shift(own_share, "seq", 3)
        far_down = shift(down_bank[far_bank], "batch", 1)
        far_up = shift(adapter_up_weight[far_bank], "batch", 1)
        own_down, own_up = down_bank[own_bank], adapter_up_weight[own_bank]
        payload_rows = 2 * joint_rank + low_width // 2
        pack_shapes = [(2 * frozen_rows, share), (frozen_rows + payload_rows, share)]
        pack_shapes += [(payload_rows, share)] * 3
        plane, forward, payload, *payloads = pl.pallas_call(
            pack_kernel,
            out_shape=[jax.ShapeDtypeStruct(shape, bf16) for shape in pack_shapes],
            in_specs=[in_vmem()] * 6,
            out_specs=[by_block(shape) for shape in pack_shapes],
            scratch_shapes=[
                pltpu.VMEM((SEGS * joint_rank, down_width), bf16),
                pltpu.VMEM((SEGS, low_width, 2 * held_up), bf16),
            ],
            compiler_params=pltpu.CompilerParams(vmem_limit_bytes=16 * mebibyte),
            cost_estimate=cost(0, 8 * frozen_rows * share),
            name="pack",
        )(own_down, far_down, own_up, far_up, before, after)

        def over_plane(value):
            over_both = [(at, plane_count - 1 - at) for at in range(plane_count)]
            return [
                shift(value, "batch", 1),
                shift(value, "groups", 1),
                lax.ppermute(value, ("groups", "batch"), over_both),
            ]

        plane_parts = over_plane(plane)
        forward = shift(forward, "seq", 1)
        middle = pl.pallas_call(
            pick_kernel,
            out_shape=jax.ShapeDtypeStruct((frozen_rows, share), bf16),
            in_specs=[in_vmem()] + [in_place()] * 2,
            out_specs=in_vmem(),
            compiler_params=pltpu.CompilerParams(vmem_limit_bytes=8 * mebibyte),
            cost_estimate=cost(0, 4 * frozen_rows * share),
            name="pick",
        )(forward, down_zeros, up_zeros)
        middle_parts = over_plane(middle)
        payloads = [shift(part, "seq", steps + 2) for steps, part in enumerate(payloads)]
        arrays = [frozen_qkv_matrix, before, after, forward, payload] + payloads
        arrays += plane_parts + middle_parts

        def frozen_at(behind, batch_step, group_step):
            return frozen_place(seq_count, frozen_rows, share, behind, batch_step, group_step)

        def down_at(behind):
            return down_place(seq_count, features, down_width, behind)

        entries = [
            (0, 0, frozen_rows, frozen_place(seq_count, frozen_rows, None, 0, 0, 0)),
            (1, 0, frozen_rows, frozen_at(1, 0, 0)),
            (2, 0, frozen_rows, frozen_at(3, 0, 0)),
            (3, 0, frozen_rows, frozen_at(2, 0, 0)),
            (4, 0, 2 * joint_rank, down_at(0)),
            (3, frozen_rows, 2 * joint_rank, down_at(1)),
            (5, 0, 2 * joint_rank, down_at(2)),
            (6, 0, 2 * joint_rank, down_at(3)),
        ]
        up_entries = [(4, 2 * joint_rank, 0), (3, frozen_rows + 2 * joint_rank, 1)]
        up_entries += [(5, 2 * joint_rank, 2), (6, 2 * joint_rank, 3)]
        for number, (batch_step, group_step) in enumerate(((1, 0), (0, 1), (1, 1))):
            entries += [
                (7 + number, 0, frozen_rows, frozen_at(1, batch_step, group_step)),
                (7 + number, frozen_rows, frozen_rows, frozen_at(3, batch_step, group_step)),
                (10 + number, 0, frozen_rows, frozen_at(2, batch_step, group_step)),
            ]
        early = [forward, *plane_parts, *payloads, cosines, sines, bank_rows]
        column_blocks = pl.pallas_call(
            functools.partial(cut_kernel, len(early), seq_count),
            out_shape=[jax.ShapeDtypeStruct((rows, down_width), bf16)] * seq_count,
            in_specs=[in_vmem()] + [in_place()] * len(early),
            out_specs=[by_block((rows, down_width))] * seq_count,
            compiler_params=pltpu.CompilerParams(vmem_limit_bytes=16 * mebibyte),
            cost_estimate=cost(0, 4 * rows * width),
            name="cut",
        )(local_tokens, *early)
    else:
        bank_rows = sample_rows.reshape(-1)
        got_down = lax.all_to_all(
            down_bank[sample_rows], "batch", split_axis=0, concat_axis=0, tiled=True
        )
        got_up = lax.all_to_all(
            adapter_up_weight[sample_rows], "batch", split_axis=0, concat_axis=0, tiled=True
        )
        down_block = jnp.transpose(got_down, (1, 2, 0, 3)).reshape(SEGS * joint_rank, -1)
        up_block = jnp.transpose(got_up, (1, 2, 0, 3)).reshape(SEGS * low_width, -1)
        all_down = lax.all_gather(down_block, "seq", axis=0)
        all_up = lax.all_gather(up_block, "seq", axis=0)
        first = (seq_index >= half_count).astype(jnp.int32)
        merged = jnp.transpose(all_down, (1, 0, 2)).reshape(SEGS * joint_rank, -1)
        arrays = [
            lax.all_gather(frozen_qkv_matrix, "seq", axis=0, tiled=True),
            lax.dynamic_slice_in_dim(merged, first * joint_rank, 2 * joint_rank),
        ]
        entries = [
            (0, 0, features, whole_place(0)),
            (1, 0, 2 * joint_rank, whole_place(features)),
        ]
        up_rows = jnp.transpose(all_up, (1, 0, 2)).reshape(SEGS, low_width, -1)
        is_query = jnp.arange(up_rows.shape[2]) < query_columns
        up_blocks = jnp.concatenate(
            [
                jnp.where(is_query[None, None, :], up_rows, 0),
                jnp.where(is_query[None, None, :], 0, up_rows),
            ],
            axis=1,
        )
        column_blocks = [
            lax.dynamic_slice_in_dim(
                local_tokens,
                jnp.remainder(seq_index + steps, seq_count) * down_width,
                down_width,
                axis=1,
            )
            for steps in range(seq_count)
        ]

    if direct:
        column_parts = [column_blocks[0], None, shift(column_blocks[2], "seq", 2), None]
        column_parts[1] = shift(pass_after(column_blocks[1], column_parts[2]), "seq", 1)
    else:
        column_parts = [
            shift(block, "seq", steps) if steps else block
            for steps, block in enumerate(column_blocks)
        ]
    early = [column_parts[2]] if direct and seq_count > 3 else []
    up_shape = (SEGS, joint_rank, query_columns + HEAD_WIDTH)
    matrix_rows = features + 2 * joint_rank
    arrived = [pltpu.VMEM((seq_count, low_width // 2, down_width), bf16)] if direct else []
    own_part, sent_part, rest_part, matrix, *built = pl.pallas_call(
        functools.partial(
            project_kernel, len(arrays), entries, up_entries, len(early), seq_count
        ),
        out_shape=[
            jax.ShapeDtypeStruct((own_rows, query_columns), f32),
            jax.ShapeDtypeStruct((own_rows, query_columns), f32),
            jax.ShapeDtypeStruct((rows, matrix_rows - query_columns), f32),
            jax.ShapeDtypeStruct((matrix_rows, width), bf16),
        ]
        + ([jax.ShapeDtypeStruct(up_shape, bf16)] if direct else []),
        in_specs=[in_vmem()] + [in_place()] * (len(arrays) + len(early)),
        out_specs=[in_vmem()] * 3 + [in_place()] + ([by_block(up_shape)] if direct else []),
        scratch_shapes=arrived
        + [
            pltpu.VMEM((matrix_rows, width), bf16),
            pltpu.SemaphoreType.DMA((len(entries) + len(up_entries) + 1,)),
        ],
        compiler_params=pltpu.CompilerParams(vmem_limit_bytes=20 * mebibyte),
        cost_estimate=cost(2 * rows * width * matrix_rows, 2 * width * (matrix_rows + rows)),
        name="project",
    )(local_tokens, *arrays, *early)
    if direct:
        up_blocks = built[0]

    other_part = shift(sent_part, "tp", 1)
    other_rest = shift(rest_part, "tp", 1)
    queries, pairs, low_rank = pl.pallas_call(
        functools.partial(qkv_kernel, seq_count, 1),
        out_shape=(
            jax.ShapeDtypeStruct((QHEADS * own_rows, HEAD_WIDTH), bf16),
            jax.ShapeDtypeStruct((rows, 2 * HEAD_WIDTH), bf16),
            jax.ShapeDtypeStruct((rows, joint_rank), bf16),
        ),
        in_specs=[in_smem()] + [in_vmem()] * 7 + [in_place()],
        out_specs=(in_vmem(),) * 3,
        compiler_params=pltpu.CompilerParams(vmem_limit_bytes=8 * mebibyte),
        cost_estimate=cost(2 * rows * 3 * 64 * 640, 8 * rows * features),
        name="qkv",
    )(
        document_lengths, own_part, other_part, rest_part, other_rest, up_blocks, cosines, sines,
        column_parts[1],
    )

    blocks = [pairs] + [push(pairs, "seq", back) for back in range(1, half_count + 1)]
    block_count = len(blocks)
    if direct:
        column_parts[3] = shift(pass_after(column_blocks[3], *blocks[1:]), "seq", 3)
    incoming = output_gradient[0]
    early_columns = []
    attention, query_grad, kept, sent = pl.pallas_call(
        functools.partial(attention_kernel, block_count, len(early_columns)),
        out_shape=(
            jax.ShapeDtypeStruct((own_rows, query_columns), bf16),
            jax.ShapeDtypeStruct((own_rows, query_columns), bf16),
            jax.ShapeDtypeStruct((block_count, own_rows, 2 * HEAD_WIDTH), f32),
            jax.ShapeDtypeStruct((block_count, own_rows, 2 * HEAD_WIDTH), f32),
        ),
        in_specs=[in_smem()]
        + [in_vmem()] * (4 + block_count)
        + [in_place()] * len(early_columns),
        out_specs=(in_vmem(),) * 4,
        scratch_shapes=[pltpu.VMEM((block_count, QHEADS * own_rows, rows), bf16)],
        compiler_params=pltpu.CompilerParams(vmem_limit_bytes=(8 + 4 * block_count) * mebibyte),
        cost_estimate=cost(
            10 * block_count * QHEADS * own_rows * rows * HEAD_WIDTH,
            4 * rows * features,
            block_count * QHEADS * own_rows * rows,
        ),
        name="attention",
    )(document_lengths, queries, incoming, cosines, sines, *blocks, *early_columns)

    other_query = shift(query_grad, "tp", 1)
    due = [column_parts[-1]] if direct else []
    pair_sums = pl.pallas_call(
        functools.partial(sum_kernel, len(due)),
        out_shape=[jax.ShapeDtypeStruct((own_rows, 2 * HEAD_WIDTH), f32)] * block_count,
        in_specs=[in_vmem()] * 2 + [in_place()] * len(due),
        out_specs=[in_vmem()] * block_count,
        compiler_params=pltpu.CompilerParams(vmem_limit_bytes=8 * mebibyte),
        cost_estimate=cost(0, 12 * block_count * own_rows * 2 * HEAD_WIDTH),
        name="pair_sums",
    )(kept, shift(sent, "tp", 1), *due)
    pair_terms = [pair_sums[0]]
    pair_terms += [push(pair_sums[back], "seq", -back) for back in range(1, block_count)]
    pair_grad = pl.pallas_call(
        functools.partial(pair_kernel, block_count),
        out_shape=jax.ShapeDtypeStruct((own_rows, 2 * HEAD_WIDTH), bf16),
        in_specs=[in_vmem()] * (2 + block_count),
        out_specs=in_vmem(),
        compiler_params=pltpu.CompilerParams(vmem_limit_bytes=8 * mebibyte),
        cost_estimate=cost(0, 12 * block_count * own_rows * 2 * HEAD_WIDTH),
        name="pair_gradients",
    )(cosines, sines, *pair_terms)
    other_pair = shift(pair_grad, "tp", 1)

    split_shapes = [(SEGS * low_width, up_width)] * seq_count
    if direct:
        sent_rows = SEGS * low_width * up_width // 128 + rows // 2
        split_shapes[1:] = [(sent_rows, 128)] * (seq_count - 1)
    gradients, rank_grad, *up_split = pl.pallas_call(
        functools.partial(rank_kernel, seq_count),
        out_shape=[
            jax.ShapeDtypeStruct((rows, matrix_rows), bf16),
            jax.ShapeDtypeStruct((rows, joint_rank), bf16),
        ]
        + [jax.ShapeDtypeStruct(shape, f32) for shape in split_shapes],
        in_specs=[in_smem()] + [in_vmem()] * 6,
        out_specs=[by_block((rows, matrix_rows)), in_vmem()]
        + [by_block(shape) for shape in split_shapes],
        scratch_shapes=[
            pltpu.VMEM((SEGS * low_width, features - HEAD_WIDTH), f32),
            pltpu.VMEM((seq_count, SEGS * low_width, held_up * batch_count), f32),
        ],
        compiler_params=pltpu.CompilerParams(vmem_limit_bytes=8 * mebibyte),
        cost_estimate=cost(4 * rows * 3 * 64 * 640, 4 * rows * features),
        name="rank_gradients",
    )(
        document_lengths, query_grad, other_query, pair_grad, other_pair, low_rank, up_blocks
    )

    rank_parts = [rank_grad]
    if not direct:
        rank_parts += [shift(rank_grad, "seq", steps) for steps in range(1, seq_count)]
    up_sums = [
        shift(block, "seq", steps) if steps else block for steps, block in enumerate(up_split)
    ]

    chunk = 512
    token_grad = pl.pallas_call(
        token_kernel,
        grid=(width // chunk,),
        out_shape=jax.ShapeDtypeStruct((rows, width), bf16),
        in_specs=[
            pl.BlockSpec((rows, matrix_rows), lambda step: (0, 0)),
            pl.BlockSpec((matrix_rows, chunk), lambda step: (0, step)),
        ],
        out_specs=pl.BlockSpec((rows, chunk), lambda step: (0, step)),
        compiler_params=pltpu.CompilerParams(vmem_limit_bytes=12 * mebibyte),
        cost_estimate=cost(2 * rows * width * matrix_rows, 2 * width * (matrix_rows + rows)),
        name="token_gradient",
    )(gradients, matrix)

    if direct:
        term_shapes = [(SEGS * joint_rank, held_down), (SEGS * joint_rank, padded_down)]
        term_shapes += [(SEGS * low_width, held_up)]
    else:
        term_shapes = [(SEGS * joint_rank, down_width), (SEGS * low_width, up_width)]
    terms = pl.pallas_call(
        functools.partial(down_kernel, seq_count),
        out_shape=[jax.ShapeDtypeStruct(shape, f32) for shape in term_shapes],
        in_specs=[in_smem()] + [in_vmem()] * (2 * seq_count + len(rank_parts)),
        out_specs=[in_vmem()] * len(term_shapes),
        scratch_shapes=[pltpu.VMEM((SEGS * low_width, up_width), f32)] if direct else [],
        compiler_params=pltpu.CompilerParams(vmem_limit_bytes=8 * mebibyte),
        cost_estimate=cost(
            2 * seq_count * rows * SEGS * joint_rank * down_width, 2 * seq_count * rows * down_width
        ),
        name="down_terms",
    )(document_lengths, *column_parts, *up_sums, *rank_parts)

    if direct:
        bank_terms = [terms[0], shift(terms[1], "batch", 1), terms[2]]
    else:
        down_send = jnp.transpose(
            terms[0].reshape(SEGS * joint_rank, batch_count, held_down), (1, 0, 2)
        )
        up_send = jnp.transpose(
            terms[1].reshape(SEGS * low_width, batch_count, held_up), (1, 0, 2)
        )
        back_down = lax.all_to_all(down_send, "batch", split_axis=0, concat_axis=0, tiled=True)
        back_up = lax.all_to_all(up_send, "batch", split_axis=0, concat_axis=0, tiled=True)
        bank_downs = [back_down[batch] for batch in range(batch_count)]
        bank_ups = [back_up[batch] for batch in range(batch_count)]
        bank_terms = bank_downs + bank_ups


    def whole(array):
        return pl.BlockSpec(array.shape, lambda step, bank: (0,) * array.ndim)

    term_count = len(bank_terms)
    down_grad, up_grad = pl.pallas_call(
        packed_bank_kernel if direct else functools.partial(bank_kernel, batch_count),
        out_shape=(
            jax.ShapeDtypeStruct(down_zeros.shape, f32),
            jax.ShapeDtypeStruct(up_zeros.shape, f32),
        ),
        grid_spec=pltpu.PrefetchScalarGridSpec(
            num_scalar_prefetch=1,
            grid=(batch_count * SEGS,),
            in_specs=[whole(array) for array in bank_terms] + [in_place()] * 2,
            out_specs=(
                pl.BlockSpec(
                    (1, joint_rank, 1, held_down),
                    lambda step, bank: (bank[step], 0, 0, 0),
                ),
                pl.BlockSpec(
                    (1, low_width, held_up),
                    lambda step, bank: (bank[step], 0, 0),
                ),
            ),
        ),
        input_output_aliases={1 + term_count: 0, 2 + term_count: 1},
        compiler_params=pltpu.CompilerParams(vmem_limit_bytes=16 * mebibyte),
        name="bank_rows",
    )(
        bank_rows,
        *bank_terms,
        down_zeros,
        up_zeros,
    )
    return (attention[None], token_grad[None], down_grad, up_grad)


def solution(mesh):
    in_specs = (
        P(("groups", "batch"), "seq", "tp"),
        P("seq", "tp"),
        P(None, None, "tp", ("seq", "batch")),
        P(None, None, ("seq", "batch")),
        P(),
        P("groups", None),
        P("groups", None),
        P(("groups", "batch"), ("seq", "tp"), None),
    )
    out_specs = (
        P(("groups", "batch"), ("seq", "tp"), None),
        P(("groups", "batch"), "seq", "tp"),
        P("groups", None, "tp", ("seq", "batch")),
        P("groups", None, ("seq", "batch")),
    )
    return jax.shard_map(shards, mesh=mesh, in_specs=in_specs, out_specs=out_specs, check_vma=False)
```

```python
import functools

import jax
import jax.numpy as jnp
from jax import lax
from jax.experimental import pallas as pl
from jax.experimental.pallas import tpu as pltpu
from jax.sharding import PartitionSpec as P

QHEADS = 4
HEAD_WIDTH = 128
ADAPTER_RANK = 32
SEGS = 3

adapter_scale = 2.0
rope_base = 5000000.0
masked_score = -1e30
mebibyte = 1024 * 1024


def shift(value, axis, steps):
    count = lax.axis_size(axis)
    return lax.ppermute(value, axis, [(at, (at + steps) % count) for at in range(count)])


def push(value, axis, steps):
    count = lax.axis_size(axis)
    pairs = [(at, at + steps) for at in range(count) if 0 <= at + steps < count]
    return lax.ppermute(value, axis, pairs)


def dot_nt(left, right):
    return lax.dot_general(
        left, right, (((1,), (1,)), ((), ())), preferred_element_type=jnp.float32
    )


def dot_nn(left, right):
    return jnp.dot(left, right, preferred_element_type=jnp.float32)


def dot_tn(left, right):
    return lax.dot_general(
        left, right, (((0,), (0,)), ((), ())), preferred_element_type=jnp.float32
    )


def lookup_rows(adapter_bank_row, document_adapter):
    matches = document_adapter[..., None] == jnp.arange(adapter_bank_row.shape[0], dtype=jnp.int32)
    return jnp.sum(jnp.where(matches, adapter_bank_row, 0), axis=-1)


def row_positions(first, count):
    return first + lax.broadcasted_iota(jnp.int32, (count, 1), 0)


def ring_index(index, count):
    return lax.rem(index + count, count)


def kernel_marks(lengths):
    batch = lax.axis_index("batch")
    first_end = lengths[batch, 0]
    return first_end, first_end + lengths[batch, 1]


def row_segments(ends, positions):
    return (positions >= ends[0]).astype(jnp.int32) + (positions >= ends[1]).astype(jnp.int32)


def cost(flops, bytes_accessed, transcendentals=0):
    return pl.CostEstimate(
        flops=flops, bytes_accessed=bytes_accessed, transcendentals=transcendentals
    )


def in_vmem():
    return pl.BlockSpec(memory_space=pltpu.VMEM)


def in_smem():
    return pl.BlockSpec(memory_space=pltpu.SMEM)


def by_block(shape):
    return pl.BlockSpec(shape, lambda: (0,) * len(shape))


def in_place():
    return pl.BlockSpec(memory_space=pl.ANY)


def fetch(piece, target, place, semaphore):
    height, width = piece.shape
    row, column = place()
    copy = pltpu.make_async_copy(
        piece,
        target.at[
            pl.ds(pl.multiple_of(row, 16), height), pl.ds(pl.multiple_of(column, 128), width)
        ],
        semaphore,
    )
    copy.start()
    return copy


def frozen_place(seq_count, rows, share, behind, batch_step, group_step):
    def place():
        holder = ring_index(lax.axis_index("seq") - behind, seq_count)
        if share is None:
            return holder * rows, 0
        batch = lax.rem(lax.axis_index("batch") + batch_step, 2)
        group = lax.rem(lax.axis_index("groups") + group_step, 2)
        return holder * rows, (group * 2 + batch) * share

    return place


def down_place(seq_count, features, width, behind):
    def place():
        return features, ring_index(lax.axis_index("seq") - behind, seq_count) * width

    return place


def whole_place(row):
    def place():
        return row, 0

    return place


def pack_kernel(own_down, far_down, own_up, far_up, before, after, *refs):
    plane, forward, payloads, (down, up) = refs[0], refs[1], refs[2:-2], refs[-2:]
    ahead = lax.axis_index("batch") == 0
    joint_rank, held = own_down.shape[1:]
    low_width, held_up = own_up.shape[1:]
    frozen_rows = before.shape[0]
    plane[:frozen_rows] = before[...]
    plane[frozen_rows:] = after[...]
    forward[:frozen_rows] = before[...]
    for document in range(SEGS):
        rows = slice(document * joint_rank, (document + 1) * joint_rank)
        down[rows, :held] = jnp.where(ahead, own_down[document], far_down[document])
        down[rows, held:] = jnp.where(ahead, far_down[document], own_down[document])
        up[document, :, :held_up] = jnp.where(ahead, own_up[document], far_up[document])
        up[document, :, held_up:] = jnp.where(ahead, far_up[document], own_up[document])
    half, slot = low_width // 2, down.shape[1] // 4
    targets = [(0, payloads[0], 0), (1, forward, frozen_rows)]
    targets += [(steps + 2, payload, 0) for steps, payload in enumerate(payloads[1:])]
    seq_count = len(targets)
    for steps, payload, base in targets:
        target = ring_index(lax.axis_index("seq") + steps - seq_count, seq_count)
        first = (target >= seq_count // 2).astype(jnp.int32)
        start = pl.multiple_of(first * joint_rank, joint_rank)
        payload[base : base + 2 * joint_rank] = down[pl.ds(start, 2 * joint_rank)]
        base = base + 2 * joint_rank
        for index in range(2):
            block = up[first + index]
            for part in range(2):
                column = (2 * index + part) * slot
                payload[base : base + half, column : column + 2 * held_up] = block[
                    part * half : (part + 1) * half
                ]


def pass_kernel(*refs):
    del refs


def pass_after(value, *earlier):
    return pl.pallas_call(
        pass_kernel,
        out_shape=jax.ShapeDtypeStruct(value.shape, value.dtype),
        in_specs=[in_place()] * (1 + len(earlier)),
        out_specs=in_place(),
        input_output_aliases={0: 0},
        name="pass_after",
    )(value, *earlier)


def cut_kernel(unused, seq_count, tokens, *refs):
    for steps, block in enumerate(refs[unused:]):
        target = ring_index(lax.axis_index("seq") + steps - seq_count, seq_count)
        width = block.shape[1]
        block[...] = tokens[:, pl.ds(pl.multiple_of(target * width, 128), width)]


def assemble_up(seq_count, arrived, up_blocks):
    low_width = up_blocks.shape[1] // 2
    query_columns = QHEADS * HEAD_WIDTH
    seq_index = lax.axis_index("seq")
    first = (seq_index >= seq_count // 2).astype(jnp.int32)
    held = up_blocks.shape[2] // seq_count
    half, slot = low_width // 2, arrived.shape[2] // 4
    up_blocks[...] = jnp.zeros_like(up_blocks)
    for holder in range(seq_count):
        block = arrived[ring_index(seq_index - holder, seq_count)]
        start, stop = holder * held, (holder + 1) * held
        middle = min(max(query_columns, start), stop)
        for index in range(2):
            for part in range(2):
                offset = (2 * index + part) * slot
                if middle > start:
                    up_blocks[first + index, part * half : (part + 1) * half, start:middle] = block[
                        :, offset : offset + middle - start
                    ]
                if stop > middle:
                    low = low_width + part * half
                    up_blocks[first + index, low : low + half, middle:stop] = block[
                        :, offset + middle - start : offset + held
                    ]


def project_kernel(array_count, entries, up_entries, unused, seq_count, tokens, *refs):
    arrays = refs[:array_count]
    refs = refs[array_count + unused :]
    part, matrix = refs[:2]
    weights, semaphore = refs[-2:]
    copies = []
    for number, start, height, place in entries:
        piece = arrays[number].at[pl.ds(start, height)]
        copies.append(fetch(piece, weights, place, semaphore.at[len(copies)]))
    for number, start, slot in up_entries:
        copy = pltpu.make_async_copy(
            arrays[number].at[pl.ds(start, refs[3].shape[1])],
            refs[3].at[slot],
            semaphore.at[len(copies)],
        )
        copy.start()
        copies.append(copy)
    for copy in copies:
        copy.wait()
    keep = pltpu.make_async_copy(weights, matrix, semaphore.at[len(copies)])
    keep.start()
    part[...] = dot_nt(tokens[...], weights[...])
    if up_entries:
        assemble_up(seq_count, refs[3], refs[2])
    keep.wait()


def rotated(values, cosines, sines):
    return values * cosines + pltpu.roll(values, values.shape[1] // 2, 1) * sines


def qkv_kernel(seq_count, unused, lengths, mine, theirs, up_blocks, cosines, sines, *refs):
    queries, pairs, low_rank = refs[unused:]
    rows = mine.shape[0]
    own_rows = queries.shape[0] // QHEADS
    query_columns = QHEADS * HEAD_WIDTH
    value_start = query_columns + HEAD_WIDTH
    features = value_start + HEAD_WIDTH
    joint_rank = low_rank.shape[1]
    middle = features + joint_rank
    ends = kernel_marks(lengths)

    def low_rows(picked, second):
        first_low = mine[picked, features:middle] + theirs[picked, features:middle]
        second_low = mine[picked, middle:] + theirs[picked, middle:]
        return jnp.where(second, second_low, first_low).astype(jnp.bfloat16)

    first = (lax.axis_index("seq") >= seq_count // 2).astype(jnp.int32)
    first_row = lax.axis_index("seq") * rows
    segments = row_segments(ends, row_positions(first_row, rows))
    low = low_rows(slice(None), segments != first)
    low_rank[...] = low
    value_delta = jnp.zeros((rows, HEAD_WIDTH), jnp.float32)
    for document in range(SEGS):
        chosen = jnp.where(segments == document, low, jnp.zeros_like(low))
        value_delta += dot_nn(chosen, up_blocks[document, :, query_columns:])
    keys = mine[:, query_columns:value_start] + theirs[:, query_columns:value_start]
    pairs[:, :HEAD_WIDTH] = rotated(keys, cosines[...], sines[...]).astype(jnp.bfloat16)
    values = mine[:, value_start:features] + theirs[:, value_start:features]
    pairs[:, HEAD_WIDTH:] = (values + adapter_scale * value_delta).astype(jnp.bfloat16)
    start = pl.multiple_of(lax.axis_index("tp") * own_rows, own_rows)
    own = pl.ds(start, own_rows)
    own_segments = row_segments(ends, row_positions(first_row + start, own_rows))
    own_low = low_rows(own, own_segments != first)
    query_delta = jnp.zeros((own_rows, query_columns), jnp.float32)
    for document in range(SEGS):
        chosen = jnp.where(own_segments == document, own_low, jnp.zeros_like(own_low))
        query_delta += dot_nn(chosen, up_blocks[document, :, :query_columns])
    projected = mine[own, :query_columns] + theirs[own, :query_columns]
    projected = projected + adapter_scale * query_delta
    for head in range(QHEADS):
        turned = rotated(
            projected[:, head * HEAD_WIDTH : (head + 1) * HEAD_WIDTH], cosines[own], sines[own]
        )
        queries[head * own_rows : (head + 1) * own_rows] = turned.astype(jnp.bfloat16)


def attention_kernel(block_count, unused, lengths, queries, incoming, cosines, sines, *refs):
    blocks = refs[:block_count]
    output, query_grad, kept, sent, low_probs = refs[block_count + unused :]
    own_rows, query_columns = incoming.shape
    rows = blocks[0].shape[0]
    score_scale = HEAD_WIDTH ** (-0.5)
    ends = kernel_marks(lengths)
    seq_index, tp_index = lax.axis_index("seq"), lax.axis_index("tp")
    positions = row_positions(seq_index * rows + tp_index * own_rows, own_rows)
    positions = jnp.concatenate([positions] * QHEADS, axis=0)
    segments = row_segments(ends, positions)
    starts = jnp.where(segments == 0, 0, jnp.where(segments == 1, ends[0], ends[1]))
    scores = []
    for back, block in enumerate(blocks):
        key_positions = (seq_index - back) * rows + lax.broadcasted_iota(jnp.int32, (1, rows), 1)
        allowed = (key_positions <= positions) & (key_positions >= starts)
        block_scores = dot_nt(queries[...], block[:, :HEAD_WIDTH]) * score_scale
        scores.append(jnp.where(allowed, block_scores, masked_score))
    row_max = functools.reduce(
        jnp.maximum, [jnp.max(part, axis=1, keepdims=True) for part in scores]
    )
    raised = [jnp.exp(part - row_max) for part in scores]
    row_total = sum(jnp.sum(part, axis=1, keepdims=True) for part in raised)
    inverse = 1.0 / row_total
    probs = [part * inverse for part in raised]
    weighted = jnp.zeros((QHEADS * own_rows, HEAD_WIDTH), jnp.float32)
    for back, block in enumerate(blocks):
        low_probs[back] = probs[back].astype(jnp.bfloat16)
        weighted += dot_nn(low_probs[back], block[:, HEAD_WIDTH:])
    attended = weighted.astype(jnp.bfloat16)
    gradients = jnp.concatenate(
        [incoming[:, head * HEAD_WIDTH : (head + 1) * HEAD_WIDTH] for head in range(QHEADS)],
        axis=0,
    )
    row_delta = jnp.sum(
        gradients.astype(jnp.float32) * attended.astype(jnp.float32), axis=1, keepdims=True
    )
    start = pl.multiple_of(tp_index * own_rows, own_rows)
    total = jnp.zeros((QHEADS * own_rows, HEAD_WIDTH), jnp.float32)
    for back, block in enumerate(blocks):
        prob_grad = dot_nt(gradients, block[:, HEAD_WIDTH:])
        score_grad = (probs[back] * (prob_grad - row_delta)).astype(jnp.bfloat16)
        total += dot_nn(score_grad, block[:, :HEAD_WIDTH])
        key_part = dot_tn(score_grad, queries[...]) * score_scale
        value_part = dot_tn(low_probs[back], gradients)
        mine = tp_index == 0
        kept[back, :, :HEAD_WIDTH] = jnp.where(mine, key_part[:own_rows], key_part[own_rows:])
        sent[back, :, :HEAD_WIDTH] = jnp.where(mine, key_part[own_rows:], key_part[:own_rows])
        kept[back, :, HEAD_WIDTH:] = jnp.where(mine, value_part[:own_rows], value_part[own_rows:])
        sent[back, :, HEAD_WIDTH:] = jnp.where(mine, value_part[own_rows:], value_part[:own_rows])
    own = pl.ds(start, own_rows)
    for head in range(QHEADS):
        picked = slice(head * own_rows, (head + 1) * own_rows)
        columns = slice(head * HEAD_WIDTH, (head + 1) * HEAD_WIDTH)
        output[:, columns] = attended[picked]
        query_grad[:, columns] = rotated(
            total[picked] * score_scale, cosines[own], -sines[own]
        ).astype(jnp.bfloat16)


def sum_kernel(unused, kept, arrived, *refs):
    for back, total in enumerate(refs[unused:]):
        total[...] = kept[back] + arrived[back]


def pair_kernel(terms, cosines, sines, *refs):
    parts, pair = refs[:terms], refs[-2]
    own_rows = pair.shape[0]
    total = sum(part[...] for part in parts)
    own = pl.ds(pl.multiple_of(lax.axis_index("tp") * own_rows, own_rows), own_rows)
    keys = rotated(total[:, :HEAD_WIDTH], cosines[own], -sines[own])
    pair[:, :HEAD_WIDTH] = keys.astype(jnp.bfloat16)
    pair[:, HEAD_WIDTH:] = total[:, HEAD_WIDTH:].astype(jnp.bfloat16)


def rank_kernel(
    seq_count, lengths, own_query, other_query, own_pair, other_pair, low_rank, up_blocks, *refs
):
    gradients, rank_grad = refs[:2]
    split_terms, (terms, blocks) = refs[2:-2], refs[-2:]
    own_rows, query_columns = own_query.shape
    rows = low_rank.shape[0]
    seq_index = lax.axis_index("seq")
    start = pl.multiple_of(lax.axis_index("tp") * own_rows, own_rows)
    other = pl.multiple_of(own_rows - start, own_rows)
    gradients[pl.ds(start, own_rows), :query_columns] = own_query[...]
    gradients[pl.ds(other, own_rows), :query_columns] = other_query[...]
    value_start = query_columns + HEAD_WIDTH
    features = value_start + HEAD_WIDTH
    gradients[pl.ds(start, own_rows), query_columns:features] = own_pair[...]
    gradients[pl.ds(other, own_rows), query_columns:features] = other_pair[...]
    query_grad = gradients[:, :query_columns]
    value_grad = gradients[:, value_start:features]
    low = low_rank[...]
    rank = low.shape[1] // 2
    segments = row_segments(kernel_marks(lengths), row_positions(seq_index * rows, rows))
    total = jnp.zeros((rows, low.shape[1]), jnp.float32)
    for document in range(SEGS):
        member = segments == document
        parts = dot_nt(query_grad, up_blocks[document, :, :query_columns])
        parts += dot_nt(value_grad, up_blocks[document, :, query_columns:])
        total = jnp.where(member, parts, total)
        chosen = jnp.where(member, low, jnp.zeros_like(low))
        query_terms = dot_tn(chosen, query_grad)
        value_terms = dot_tn(chosen, value_grad)
        place = slice(document * rank, (document + 1) * rank)
        terms[place, :query_columns] = adapter_scale * query_terms[:rank]
        terms[place, query_columns:] = adapter_scale * value_terms[rank:]
    turned = (adapter_scale * total).astype(jnp.bfloat16)
    rank_grad[...] = turned
    second = segments != (seq_index >= seq_count // 2).astype(jnp.int32)
    nothing = jnp.zeros_like(turned)
    middle = features + low.shape[1]
    gradients[:, features:middle] = jnp.where(second, nothing, turned)
    gradients[:, middle:] = jnp.where(second, turned, nothing)
    held = blocks.shape[2]
    for holder in range(seq_count):
        blocks[holder] = terms[:, holder * held : (holder + 1) * held]
    for steps, block in enumerate(split_terms):
        mine = blocks[ring_index(seq_index + steps - seq_count, seq_count)]
        if block.shape == mine.shape:
            block[...] = mine
            continue
        tail = held - 128
        count = 128 // tail
        height = mine.shape[0] // count
        first_low = mine.shape[0] + height
        block[: mine.shape[0]] = mine[:, :128]
        for part in range(count):
            block[mine.shape[0] : first_low, part * tail : (part + 1) * tail] = mine[
                part * height : (part + 1) * height, 128:
            ]
        block[first_low:, : low.shape[1]] = turned[: rows // 2].astype(jnp.float32)
        block[first_low:, low.shape[1] :] = turned[rows // 2 :].astype(jnp.float32)


def token_kernel(gradients, matrix, token_grad):
    token_grad[...] = dot_nn(gradients[...], matrix[...]).astype(jnp.bfloat16)


def down_kernel(block_count, lengths, *refs):
    columns = refs[:block_count]
    up_parts = refs[block_count : 2 * block_count]
    packed = up_parts[0].shape != up_parts[1].shape
    rank_count = 1 if packed else block_count
    ranks = refs[2 * block_count : 2 * block_count + rank_count]
    outputs = refs[2 * block_count + rank_count :]
    rows, joint_rank = ranks[0].shape
    ends = kernel_marks(lengths)
    up_rows, up_width = up_parts[0].shape
    lows, ups = [ranks[0][...]], [up_parts[0][...]]
    for behind in range(1, block_count):
        if not packed:
            lows.append(ranks[behind][...])
            ups.append(up_parts[behind][...])
            continue
        part = up_parts[behind]
        count = 128 // (up_width - 128)
        first_low = up_rows + up_rows // count
        halves = [part[first_low:, :joint_rank], part[first_low:, joint_rank:]]
        lows.append(jnp.concatenate(halves, axis=0).astype(jnp.bfloat16))
    all_terms = []
    for document in range(SEGS):
        total = jnp.zeros((joint_rank, columns[0].shape[1]), jnp.float32)
        for behind in range(block_count):
            holder = ring_index(lax.axis_index("seq") - behind, block_count)
            segments = row_segments(ends, row_positions(holder * rows, rows))
            chosen = jnp.where(segments == document, lows[behind], jnp.zeros_like(lows[behind]))
            total += dot_tn(chosen, columns[behind][...])
        all_terms.append(total)
    down_terms = jnp.concatenate(all_terms, axis=0)
    if not packed:
        outputs[0][...] = down_terms
        outputs[1][...] = sum(ups)
        return
    own_down, far, own_up, up_terms = outputs
    tail = up_width - 128
    height = up_rows // (128 // tail)
    up_terms[...] = ups[0]
    for part in up_parts[1:]:
        up_terms[:, :128] += part[:up_rows]
        for piece in range(128 // tail):
            up_terms[piece * height : (piece + 1) * height, 128:] += part[
                up_rows : up_rows + height, piece * tail : (piece + 1) * tail
            ]
    held, held_up = own_down.shape[1], own_up.shape[1]
    ahead = lax.axis_index("batch") == 0
    own_down[...] = jnp.where(ahead, down_terms[:, :held], down_terms[:, held:])
    far[:, :held] = jnp.where(ahead, down_terms[:, held:], down_terms[:, :held])
    left, right = up_terms[:, :held_up], up_terms[:, held_up:]
    own_up[...] = jnp.where(ahead, left, right)
    far_up = jnp.where(ahead, right, left)
    spare = far.shape[1] - held
    far[:up_rows, held:] = far_up[:, :spare]
    far[up_rows:, held : held + held_up - spare] = far_up[:, spare:]


def packed_bank_kernel(bank_rows, own_down, far, own_up, down_zeros, up_zeros, down_out, up_out):
    step = pl.program_id(0)
    joint_rank, held = down_out.shape[1], down_out.shape[3]
    low_width, held_up = up_out.shape[1:]
    up_rows = own_up.shape[0]
    spare = far.shape[1] - held
    down_total = jnp.zeros((joint_rank, held), jnp.float32)
    head = jnp.zeros((low_width, spare), jnp.float32)
    rest = jnp.zeros((low_width, held_up - spare), jnp.float32)
    for document in range(SEGS):
        rows = slice(document * joint_rank, (document + 1) * joint_rank)
        lows = slice(document * low_width, (document + 1) * low_width)
        same = bank_rows[document] == bank_rows[step]
        down_total += jnp.where(same, own_down[rows], 0.0)
        head += jnp.where(same, own_up[lows, :spare], 0.0)
        rest += jnp.where(same, own_up[lows, spare:], 0.0)
        same = bank_rows[SEGS + document] == bank_rows[step]
        down_total += jnp.where(same, far[rows, :held], 0.0)
        head += jnp.where(same, far[lows, held:], 0.0)
        lows = slice(up_rows + document * low_width, up_rows + (document + 1) * low_width)
        rest += jnp.where(same, far[lows, held : held + held_up - spare], 0.0)
    down_out[0, :, 0, :] = down_total
    up_out[0, :, :spare] = head
    up_out[0, :, spare:] = rest


def bank_kernel(block_count, bank_rows, *refs):
    down_terms = refs[:block_count]
    up_terms = refs[block_count : 2 * block_count]
    down_out, up_out = refs[2 * block_count + 2 :]
    step = pl.program_id(0)
    row = bank_rows[step]
    joint_rank = down_out.shape[1]
    low_width = up_out.shape[1]
    down_total = jnp.zeros((joint_rank, down_out.shape[3]), jnp.float32)
    up_total = jnp.zeros((low_width, up_out.shape[2]), jnp.float32)
    for block in range(block_count):
        for document in range(SEGS):
            same = bank_rows[block * SEGS + document] == row
            down_rows = down_terms[block][document * joint_rank : (document + 1) * joint_rank]
            up_rows = up_terms[block][document * low_width : (document + 1) * low_width]
            down_total += jnp.where(same, down_rows, 0.0)
            up_total += jnp.where(same, up_rows, 0.0)
    down_out[0, :, 0, :] = down_total
    up_out[0] = up_total


def shards(
    tokens,
    frozen_qkv_matrix,
    adapter_down_weight,
    adapter_up_weight,
    adapter_bank_row,
    document_lengths,
    document_adapter,
    output_gradient,
):
    seq_count = lax.axis_size("seq")
    batch_count = lax.axis_size("batch")
    group_count = lax.axis_size("groups")
    chip_size = lax.axis_size("tp")
    seq_index = lax.axis_index("seq")
    batch_index = lax.axis_index("batch")
    group_index = lax.axis_index("groups")
    tp_index = lax.axis_index("tp")
    local_tokens = tokens[0]
    rows, width = local_tokens.shape
    own_rows = rows // chip_size
    query_columns = QHEADS * HEAD_WIDTH
    frozen_rows = frozen_qkv_matrix.shape[0]
    features = frozen_rows * seq_count
    low_width = ADAPTER_RANK
    joint_rank = adapter_down_weight.shape[1]
    adapters = adapter_bank_row.shape[0]
    bf16 = jnp.bfloat16
    f32 = jnp.float32

    lengths = lax.dynamic_index_in_dim(document_lengths, batch_index, 0, keepdims=False)
    first_end = lengths[0]
    second_end = first_end + lengths[1]
    half_count = seq_count // 2
    held_down = adapter_down_weight.shape[3]
    held_up = adapter_up_weight.shape[2]
    down_width = held_down * batch_count
    up_width = held_up * batch_count

    positions = seq_index * rows + jnp.arange(rows, dtype=jnp.int32)
    inside = positions - jnp.where(
        positions >= second_end, second_end, jnp.where(positions >= first_end, first_end, 0)
    )
    exponent = jnp.arange(HEAD_WIDTH // 2, dtype=f32) * (2.0 / HEAD_WIDTH)
    inverse = jnp.power(jnp.float32(rope_base), -exponent)
    angles = inside.astype(f32)[:, None] * jnp.concatenate([inverse, inverse])[None, :]
    signs = jnp.where(jnp.arange(HEAD_WIDTH) < HEAD_WIDTH // 2, -1.0, 1.0).astype(f32)
    cosines = jnp.cos(angles)
    sines = jnp.sin(angles) * signs[None, :]

    sample_rows = lookup_rows(adapter_bank_row, document_adapter)
    bank_rows = sample_rows.reshape(-1)
    if batch_count == 2:
        own_bank = jnp.where(batch_index == 0, sample_rows[0], sample_rows[1])
        far_bank = jnp.where(batch_index == 0, sample_rows[1], sample_rows[0])
        bank_rows = jnp.concatenate([own_bank, far_bank])
    down_bank = adapter_down_weight[:, :, 0, :]
    down_zeros = jnp.zeros((adapters, joint_rank, 1, held_down), f32)
    up_zeros = jnp.zeros((adapters, low_width, held_up), f32)

    plane_count = group_count * batch_count
    share = width // plane_count
    padded_down = (held_down + 127) // 128 * 128
    direct = (
        group_count == 2
        and seq_count == 4
        and share == down_width
        and batch_count == 2
        and share % 128 == 0
        and down_width % 128 == 0
        and frozen_rows % 16 == 0
        and 4 * up_width <= down_width
        and up_width > 128
        and 128 % (up_width - 128) == 0
        and 0 < held_up + held_down - padded_down <= padded_down - held_down
    )
    up_entries = []
    if direct:
        own_share = lax.dynamic_slice_in_dim(
            frozen_qkv_matrix, (group_index * batch_count + batch_index) * share, share, axis=1
        )
        before = shift(own_share, "seq", 1)
        after = shift(own_share, "seq", 3)
        far_down = shift(down_bank[far_bank], "batch", 1)
        far_up = shift(adapter_up_weight[far_bank], "batch", 1)
        own_down, own_up = down_bank[own_bank], adapter_up_weight[own_bank]
        payload_rows = 2 * joint_rank + low_width // 2
        pack_shapes = [(2 * frozen_rows, share), (frozen_rows + payload_rows, share)]
        pack_shapes += [(payload_rows, share)] * 3
        plane, forward, payload, *payloads = pl.pallas_call(
            pack_kernel,
            out_shape=[jax.ShapeDtypeStruct(shape, bf16) for shape in pack_shapes],
            in_specs=[in_vmem()] * 6,
            out_specs=[by_block(shape) for shape in pack_shapes],
            scratch_shapes=[
                pltpu.VMEM((SEGS * joint_rank, down_width), bf16),
                pltpu.VMEM((SEGS, low_width, 2 * held_up), bf16),
            ],
            compiler_params=pltpu.CompilerParams(vmem_limit_bytes=8 * mebibyte),
            cost_estimate=cost(0, 8 * frozen_rows * share),
            name="pack",
        )(own_down, far_down, own_up, far_up, before, after)

        def over_plane(value):
            over_both = [(at, plane_count - 1 - at) for at in range(plane_count)]
            return [
                shift(value, "batch", 1),
                shift(value, "groups", 1),
                lax.ppermute(value, ("groups", "batch"), over_both),
            ]

        plane_parts = over_plane(plane)
        forward = shift(forward, "seq", 1)
        middle = forward[:frozen_rows]
        middle_parts = over_plane(middle)
        payloads = [shift(part, "seq", steps + 2) for steps, part in enumerate(payloads)]
        arrays = [frozen_qkv_matrix, before, after, forward, payload] + payloads
        arrays += plane_parts + middle_parts

        def frozen_at(behind, batch_step, group_step):
            return frozen_place(seq_count, frozen_rows, share, behind, batch_step, group_step)

        def down_at(behind):
            return down_place(seq_count, features, down_width, behind)

        entries = [
            (0, 0, frozen_rows, frozen_place(seq_count, frozen_rows, None, 0, 0, 0)),
            (1, 0, frozen_rows, frozen_at(1, 0, 0)),
            (2, 0, frozen_rows, frozen_at(3, 0, 0)),
            (3, 0, frozen_rows, frozen_at(2, 0, 0)),
            (4, 0, 2 * joint_rank, down_at(0)),
            (3, frozen_rows, 2 * joint_rank, down_at(1)),
            (5, 0, 2 * joint_rank, down_at(2)),
            (6, 0, 2 * joint_rank, down_at(3)),
        ]
        up_entries = [(4, 2 * joint_rank, 0), (3, frozen_rows + 2 * joint_rank, 1)]
        up_entries += [(5, 2 * joint_rank, 2), (6, 2 * joint_rank, 3)]
        for number, (batch_step, group_step) in enumerate(((1, 0), (0, 1), (1, 1))):
            entries += [
                (7 + number, 0, frozen_rows, frozen_at(1, batch_step, group_step)),
                (7 + number, frozen_rows, frozen_rows, frozen_at(3, batch_step, group_step)),
                (10 + number, 0, frozen_rows, frozen_at(2, batch_step, group_step)),
            ]
        early = [forward, down_zeros, up_zeros, cosines, sines, bank_rows]
        column_blocks = pl.pallas_call(
            functools.partial(cut_kernel, len(early), seq_count),
            out_shape=[jax.ShapeDtypeStruct((rows, down_width), bf16)] * seq_count,
            in_specs=[in_vmem()] + [in_place()] * len(early),
            out_specs=[by_block((rows, down_width))] * seq_count,
            compiler_params=pltpu.CompilerParams(vmem_limit_bytes=8 * mebibyte),
            cost_estimate=cost(0, 4 * rows * width),
            name="cut",
        )(local_tokens, *early)
    else:
        bank_rows = sample_rows.reshape(-1)
        got_down = lax.all_to_all(
            down_bank[sample_rows], "batch", split_axis=0, concat_axis=0, tiled=True
        )
        got_up = lax.all_to_all(
            adapter_up_weight[sample_rows], "batch", split_axis=0, concat_axis=0, tiled=True
        )
        down_block = jnp.transpose(got_down, (1, 2, 0, 3)).reshape(SEGS * joint_rank, -1)
        up_block = jnp.transpose(got_up, (1, 2, 0, 3)).reshape(SEGS * low_width, -1)
        all_down = lax.all_gather(down_block, "seq", axis=0)
        all_up = lax.all_gather(up_block, "seq", axis=0)
        first = (seq_index >= half_count).astype(jnp.int32)
        merged = jnp.transpose(all_down, (1, 0, 2)).reshape(SEGS * joint_rank, -1)
        arrays = [
            lax.all_gather(frozen_qkv_matrix, "seq", axis=0, tiled=True),
            lax.dynamic_slice_in_dim(merged, first * joint_rank, 2 * joint_rank),
        ]
        entries = [
            (0, 0, features, whole_place(0)),
            (1, 0, 2 * joint_rank, whole_place(features)),
        ]
        up_rows = jnp.transpose(all_up, (1, 0, 2)).reshape(SEGS, low_width, -1)
        is_query = jnp.arange(up_rows.shape[2]) < query_columns
        up_blocks = jnp.concatenate(
            [
                jnp.where(is_query[None, None, :], up_rows, 0),
                jnp.where(is_query[None, None, :], 0, up_rows),
            ],
            axis=1,
        )
        column_blocks = [
            lax.dynamic_slice_in_dim(
                local_tokens,
                jnp.remainder(seq_index + steps, seq_count) * down_width,
                down_width,
                axis=1,
            )
            for steps in range(seq_count)
        ]

    column_parts = [
        shift(block, "seq", steps) if steps else block
        for steps, block in enumerate(column_blocks)
    ]
    early = [column_parts[2]] if direct and seq_count > 3 else []
    up_shape = (SEGS, joint_rank, query_columns + HEAD_WIDTH)
    matrix_rows = features + 2 * joint_rank
    arrived = [pltpu.VMEM((seq_count, low_width // 2, down_width), bf16)] if direct else []
    part, matrix, *built = pl.pallas_call(
        functools.partial(
            project_kernel, len(arrays), entries, up_entries, len(early), seq_count
        ),
        out_shape=[
            jax.ShapeDtypeStruct((rows, matrix_rows), f32),
            jax.ShapeDtypeStruct((matrix_rows, width), bf16),
        ]
        + ([jax.ShapeDtypeStruct(up_shape, bf16)] if direct else []),
        in_specs=[in_vmem()] + [in_place()] * (len(arrays) + len(early)),
        out_specs=[in_vmem(), in_place()] + ([by_block(up_shape)] if direct else []),
        scratch_shapes=arrived
        + [
            pltpu.VMEM((matrix_rows, width), bf16),
            pltpu.SemaphoreType.DMA((len(entries) + len(up_entries) + 1,)),
        ],
        compiler_params=pltpu.CompilerParams(vmem_limit_bytes=12 * mebibyte),
        cost_estimate=cost(2 * rows * width * matrix_rows, 2 * width * (matrix_rows + rows)),
        name="project",
    )(local_tokens, *arrays, *early)
    if direct:
        up_blocks = built[0]

    other_part = shift(part, "tp", 1)
    queries, pairs, low_rank = pl.pallas_call(
        functools.partial(qkv_kernel, seq_count, 0),
        out_shape=(
            jax.ShapeDtypeStruct((QHEADS * own_rows, HEAD_WIDTH), bf16),
            jax.ShapeDtypeStruct((rows, 2 * HEAD_WIDTH), bf16),
            jax.ShapeDtypeStruct((rows, joint_rank), bf16),
        ),
        in_specs=[in_smem()] + [in_vmem()] * 5,
        out_specs=(in_vmem(),) * 3,
        compiler_params=pltpu.CompilerParams(vmem_limit_bytes=8 * mebibyte),
        cost_estimate=cost(2 * rows * 3 * 64 * 640, 8 * rows * features),
        name="qkv",
    )(document_lengths, part, other_part, up_blocks, cosines, sines)

    blocks = [pairs] + [push(pairs, "seq", back) for back in range(1, half_count + 1)]
    block_count = len(blocks)
    column_parts[1] = shift(pass_after(column_blocks[1], *blocks[1:]), "seq", 1)
    incoming = output_gradient[0]
    early_columns = []
    attention, query_grad, kept, sent = pl.pallas_call(
        functools.partial(attention_kernel, block_count, len(early_columns)),
        out_shape=(
            jax.ShapeDtypeStruct((own_rows, query_columns), bf16),
            jax.ShapeDtypeStruct((own_rows, query_columns), bf16),
            jax.ShapeDtypeStruct((block_count, own_rows, 2 * HEAD_WIDTH), f32),
            jax.ShapeDtypeStruct((block_count, own_rows, 2 * HEAD_WIDTH), f32),
        ),
        in_specs=[in_smem()]
        + [in_vmem()] * (4 + block_count)
        + [in_place()] * len(early_columns),
        out_specs=(in_vmem(),) * 4,
        scratch_shapes=[pltpu.VMEM((block_count, QHEADS * own_rows, rows), bf16)],
        compiler_params=pltpu.CompilerParams(vmem_limit_bytes=(8 + 4 * block_count) * mebibyte),
        cost_estimate=cost(
            10 * block_count * QHEADS * own_rows * rows * HEAD_WIDTH,
            4 * rows * features,
            block_count * QHEADS * own_rows * rows,
        ),
        name="attention",
    )(document_lengths, queries, incoming, cosines, sines, *blocks, *early_columns)

    other_query = shift(query_grad, "tp", 1)
    due = [column_parts[1]]
    pair_sums = pl.pallas_call(
        functools.partial(sum_kernel, len(due)),
        out_shape=[jax.ShapeDtypeStruct((own_rows, 2 * HEAD_WIDTH), f32)] * block_count,
        in_specs=[in_vmem()] * 2 + [in_place()] * len(due),
        out_specs=[in_vmem()] * block_count,
        compiler_params=pltpu.CompilerParams(vmem_limit_bytes=8 * mebibyte),
        cost_estimate=cost(0, 12 * block_count * own_rows * 2 * HEAD_WIDTH),
        name="pair_sums",
    )(kept, shift(sent, "tp", 1), *due)
    pair_terms = [pair_sums[0]]
    pair_terms += [push(pair_sums[back], "seq", -back) for back in range(1, block_count)]
    pair_grad, late_block = pl.pallas_call(
        functools.partial(pair_kernel, block_count),
        out_shape=[
            jax.ShapeDtypeStruct((own_rows, 2 * HEAD_WIDTH), bf16),
            jax.ShapeDtypeStruct((rows, down_width), bf16),
        ],
        in_specs=[in_vmem()] * (2 + block_count) + [in_place()],
        out_specs=[in_vmem(), in_place()],
        input_output_aliases={2 + block_count: 1},
        compiler_params=pltpu.CompilerParams(vmem_limit_bytes=8 * mebibyte),
        cost_estimate=cost(0, 12 * block_count * own_rows * 2 * HEAD_WIDTH),
        name="pair_gradients",
    )(cosines, sines, *pair_terms, column_blocks[-1])
    column_parts[-1] = shift(late_block, "seq", seq_count - 1)
    other_pair = shift(pair_grad, "tp", 1)

    split_shapes = [(SEGS * low_width, up_width)] * seq_count
    if direct:
        sent_rows = SEGS * low_width * up_width // 128 + rows // 2
        split_shapes[1:] = [(sent_rows, 128)] * (seq_count - 1)
    gradients, rank_grad, *up_split = pl.pallas_call(
        functools.partial(rank_kernel, seq_count),
        out_shape=[
            jax.ShapeDtypeStruct((rows, matrix_rows), bf16),
            jax.ShapeDtypeStruct((rows, joint_rank), bf16),
        ]
        + [jax.ShapeDtypeStruct(shape, f32) for shape in split_shapes],
        in_specs=[in_smem()] + [in_vmem()] * 6,
        out_specs=[by_block((rows, matrix_rows)), in_vmem()]
        + [by_block(shape) for shape in split_shapes],
        scratch_shapes=[
            pltpu.VMEM((SEGS * low_width, features - HEAD_WIDTH), f32),
            pltpu.VMEM((seq_count, SEGS * low_width, held_up * batch_count), f32),
        ],
        compiler_params=pltpu.CompilerParams(vmem_limit_bytes=8 * mebibyte),
        cost_estimate=cost(4 * rows * 3 * 64 * 640, 4 * rows * features),
        name="rank_gradients",
    )(
        document_lengths, query_grad, other_query, pair_grad, other_pair, low_rank, up_blocks
    )

    rank_parts = [rank_grad]
    if not direct:
        rank_parts += [shift(rank_grad, "seq", steps) for steps in range(1, seq_count)]
    up_sums = [
        shift(block, "seq", steps) if steps else block for steps, block in enumerate(up_split)
    ]

    chunk = 512
    token_grad = pl.pallas_call(
        token_kernel,
        grid=(width // chunk,),
        out_shape=jax.ShapeDtypeStruct((rows, width), bf16),
        in_specs=[
            pl.BlockSpec((rows, matrix_rows), lambda step: (0, 0)),
            pl.BlockSpec((matrix_rows, chunk), lambda step: (0, step)),
        ],
        out_specs=pl.BlockSpec((rows, chunk), lambda step: (0, step)),
        compiler_params=pltpu.CompilerParams(vmem_limit_bytes=12 * mebibyte),
        cost_estimate=cost(2 * rows * width * matrix_rows, 2 * width * (matrix_rows + rows)),
        name="token_gradient",
    )(gradients, matrix)

    if direct:
        term_shapes = [(SEGS * joint_rank, held_down), (SEGS * joint_rank, padded_down)]
        term_shapes += [(SEGS * low_width, held_up)]
    else:
        term_shapes = [(SEGS * joint_rank, down_width), (SEGS * low_width, up_width)]
    terms = pl.pallas_call(
        functools.partial(down_kernel, seq_count),
        out_shape=[jax.ShapeDtypeStruct(shape, f32) for shape in term_shapes],
        in_specs=[in_smem()] + [in_vmem()] * (2 * seq_count + len(rank_parts)),
        out_specs=[in_vmem()] * len(term_shapes),
        scratch_shapes=[pltpu.VMEM((SEGS * low_width, up_width), f32)] if direct else [],
        compiler_params=pltpu.CompilerParams(vmem_limit_bytes=8 * mebibyte),
        cost_estimate=cost(
            2 * seq_count * rows * SEGS * joint_rank * down_width, 2 * seq_count * rows * down_width
        ),
        name="down_terms",
    )(document_lengths, *column_parts, *up_sums, *rank_parts)

    if direct:
        bank_terms = [terms[0], shift(terms[1], "batch", 1), terms[2]]
    else:
        down_send = jnp.transpose(
            terms[0].reshape(SEGS * joint_rank, batch_count, held_down), (1, 0, 2)
        )
        up_send = jnp.transpose(
            terms[1].reshape(SEGS * low_width, batch_count, held_up), (1, 0, 2)
        )
        back_down = lax.all_to_all(down_send, "batch", split_axis=0, concat_axis=0, tiled=True)
        back_up = lax.all_to_all(up_send, "batch", split_axis=0, concat_axis=0, tiled=True)
        bank_downs = [back_down[batch] for batch in range(batch_count)]
        bank_ups = [back_up[batch] for batch in range(batch_count)]
        bank_terms = bank_downs + bank_ups


    def whole(array):
        return pl.BlockSpec(array.shape, lambda step, bank: (0,) * array.ndim)

    term_count = len(bank_terms)
    down_grad, up_grad = pl.pallas_call(
        packed_bank_kernel if direct else functools.partial(bank_kernel, batch_count),
        out_shape=(
            jax.ShapeDtypeStruct(down_zeros.shape, f32),
            jax.ShapeDtypeStruct(up_zeros.shape, f32),
        ),
        grid_spec=pltpu.PrefetchScalarGridSpec(
            num_scalar_prefetch=1,
            grid=(batch_count * SEGS,),
            in_specs=[whole(array) for array in bank_terms] + [in_place()] * 2,
            out_specs=(
                pl.BlockSpec(
                    (1, joint_rank, 1, held_down),
                    lambda step, bank: (bank[step], 0, 0, 0),
                ),
                pl.BlockSpec(
                    (1, low_width, held_up),
                    lambda step, bank: (bank[step], 0, 0),
                ),
            ),
        ),
        input_output_aliases={1 + term_count: 0, 2 + term_count: 1},
        compiler_params=pltpu.CompilerParams(vmem_limit_bytes=8 * mebibyte),
        name="bank_rows",
    )(
        bank_rows,
        *bank_terms,
        down_zeros,
        up_zeros,
    )
    return (attention[None], token_grad[None], down_grad, up_grad)


def solution(mesh):
    in_specs = (
        P(("groups", "batch"), "seq", "tp"),
        P("seq", "tp"),
        P(None, None, "tp", ("seq", "batch")),
        P(None, None, ("seq", "batch")),
        P(),
        P("groups", None),
        P("groups", None),
        P(("groups", "batch"), ("seq", "tp"), None),
    )
    out_specs = (
        P(("groups", "batch"), ("seq", "tp"), None),
        P(("groups", "batch"), "seq", "tp"),
        P("groups", None, "tp", ("seq", "batch")),
        P("groups", None, ("seq", "batch")),
    )
    return jax.shard_map(shards, mesh=mesh, in_specs=in_specs, out_specs=out_specs, check_vma=False)
```

```python
import functools

import jax
import jax.numpy as jnp
from jax import lax
from jax.experimental import pallas as pl
from jax.experimental.pallas import tpu as pltpu
from jax.sharding import PartitionSpec as P

QHEADS = 4
HEAD_WIDTH = 128
ADAPTER_RANK = 32
SEGS = 3

adapter_scale = 2.0
rope_base = 5000000.0
masked_score = -1e30
mebibyte = 1024 * 1024


def shift(value, axis, steps):
    count = lax.axis_size(axis)
    return lax.ppermute(value, axis, [(at, (at + steps) % count) for at in range(count)])


def push(value, axis, steps):
    count = lax.axis_size(axis)
    pairs = [(at, at + steps) for at in range(count) if 0 <= at + steps < count]
    return lax.ppermute(value, axis, pairs)


def dot_nt(left, right):
    return lax.dot_general(
        left, right, (((1,), (1,)), ((), ())), preferred_element_type=jnp.float32
    )


def dot_nn(left, right):
    return jnp.dot(left, right, preferred_element_type=jnp.float32)


def dot_tn(left, right):
    return lax.dot_general(
        left, right, (((0,), (0,)), ((), ())), preferred_element_type=jnp.float32
    )


def lookup_rows(adapter_bank_row, document_adapter):
    matches = document_adapter[..., None] == jnp.arange(adapter_bank_row.shape[0], dtype=jnp.int32)
    return jnp.sum(jnp.where(matches, adapter_bank_row, 0), axis=-1)


def row_positions(first, count):
    return first + lax.broadcasted_iota(jnp.int32, (count, 1), 0)


def ring_index(index, count):
    return lax.rem(index + count, count)


def kernel_marks(lengths):
    batch = lax.axis_index("batch")
    first_end = lengths[batch, 0]
    return first_end, first_end + lengths[batch, 1]


def row_segments(ends, positions):
    return (positions >= ends[0]).astype(jnp.int32) + (positions >= ends[1]).astype(jnp.int32)


def cost(flops, bytes_accessed, transcendentals=0):
    return pl.CostEstimate(
        flops=flops, bytes_accessed=bytes_accessed, transcendentals=transcendentals
    )


def in_vmem():
    return pl.BlockSpec(memory_space=pltpu.VMEM)


def in_smem():
    return pl.BlockSpec(memory_space=pltpu.SMEM)


def by_block(shape):
    return pl.BlockSpec(shape, lambda: (0,) * len(shape))


def in_place():
    return pl.BlockSpec(memory_space=pl.ANY)


def fetch(piece, target, place, semaphore):
    height, width = piece.shape
    row, column = place()
    copy = pltpu.make_async_copy(
        piece,
        target.at[
            pl.ds(pl.multiple_of(row, 16), height), pl.ds(pl.multiple_of(column, 128), width)
        ],
        semaphore,
    )
    copy.start()
    return copy


def frozen_place(seq_count, rows, share, behind, batch_step, group_step):
    def place():
        holder = ring_index(lax.axis_index("seq") - behind, seq_count)
        if share is None:
            return holder * rows, 0
        batch = lax.rem(lax.axis_index("batch") + batch_step, 2)
        group = lax.rem(lax.axis_index("groups") + group_step, 2)
        return holder * rows, (group * 2 + batch) * share

    return place


def down_place(seq_count, features, width, behind):
    def place():
        return features, ring_index(lax.axis_index("seq") - behind, seq_count) * width

    return place


def whole_place(row):
    def place():
        return row, 0

    return place


def pack_kernel(own_down, far_down, own_up, far_up, before, after, *refs):
    plane, forward, payloads, (down, up) = refs[0], refs[1], refs[2:-2], refs[-2:]
    ahead = lax.axis_index("batch") == 0
    joint_rank, held = own_down.shape[1:]
    low_width, held_up = own_up.shape[1:]
    frozen_rows = before.shape[0]
    plane[:frozen_rows] = before[...]
    plane[frozen_rows:] = after[...]
    forward[:frozen_rows] = before[...]
    for document in range(SEGS):
        rows = slice(document * joint_rank, (document + 1) * joint_rank)
        down[rows, :held] = jnp.where(ahead, own_down[document], far_down[document])
        down[rows, held:] = jnp.where(ahead, far_down[document], own_down[document])
        up[document, :, :held_up] = jnp.where(ahead, own_up[document], far_up[document])
        up[document, :, held_up:] = jnp.where(ahead, far_up[document], own_up[document])
    half, slot = low_width // 2, down.shape[1] // 4
    targets = [(0, payloads[0], 0), (1, forward, frozen_rows)]
    targets += [(steps + 2, payload, 0) for steps, payload in enumerate(payloads[1:])]
    seq_count = len(targets)
    for steps, payload, base in targets:
        target = ring_index(lax.axis_index("seq") + steps - seq_count, seq_count)
        first = (target >= seq_count // 2).astype(jnp.int32)
        start = pl.multiple_of(first * joint_rank, joint_rank)
        payload[base : base + 2 * joint_rank] = down[pl.ds(start, 2 * joint_rank)]
        base = base + 2 * joint_rank
        for index in range(2):
            block = up[first + index]
            for part in range(2):
                column = (2 * index + part) * slot
                payload[base : base + half, column : column + 2 * held_up] = block[
                    part * half : (part + 1) * half
                ]


def pass_kernel(*refs):
    del refs


def pass_after(value, *earlier):
    return pl.pallas_call(
        pass_kernel,
        out_shape=jax.ShapeDtypeStruct(value.shape, value.dtype),
        in_specs=[in_place()] + [in_vmem()] * len(earlier),
        out_specs=in_place(),
        input_output_aliases={0: 0},
        name="pass_after",
    )(value, *earlier)


def cut_kernel(unused, seq_count, tokens, *refs):
    for steps, block in enumerate(refs[unused:]):
        target = ring_index(lax.axis_index("seq") + steps - seq_count, seq_count)
        width = block.shape[1]
        block[...] = tokens[:, pl.ds(pl.multiple_of(target * width, 128), width)]


def assemble_up(seq_count, arrived, up_blocks):
    low_width = up_blocks.shape[1] // 2
    query_columns = QHEADS * HEAD_WIDTH
    seq_index = lax.axis_index("seq")
    first = (seq_index >= seq_count // 2).astype(jnp.int32)
    held = up_blocks.shape[2] // seq_count
    half, slot = low_width // 2, arrived.shape[2] // 4
    up_blocks[...] = jnp.zeros_like(up_blocks)
    for holder in range(seq_count):
        block = arrived[ring_index(seq_index - holder, seq_count)]
        start, stop = holder * held, (holder + 1) * held
        middle = min(max(query_columns, start), stop)
        for index in range(2):
            for part in range(2):
                offset = (2 * index + part) * slot
                if middle > start:
                    up_blocks[first + index, part * half : (part + 1) * half, start:middle] = block[
                        :, offset : offset + middle - start
                    ]
                if stop > middle:
                    low = low_width + part * half
                    up_blocks[first + index, low : low + half, middle:stop] = block[
                        :, offset + middle - start : offset + held
                    ]


def project_kernel(array_count, entries, up_entries, unused, seq_count, tokens, *refs):
    arrays = refs[:array_count]
    refs = refs[array_count + unused :]
    part, matrix = refs[:2]
    weights, semaphore = refs[-2:]
    copies = []
    for number, start, height, place in entries:
        piece = arrays[number].at[pl.ds(start, height)]
        copies.append(fetch(piece, weights, place, semaphore.at[len(copies)]))
    for number, start, slot in up_entries:
        copy = pltpu.make_async_copy(
            arrays[number].at[pl.ds(start, refs[3].shape[1])],
            refs[3].at[slot],
            semaphore.at[len(copies)],
        )
        copy.start()
        copies.append(copy)
    for copy in copies:
        copy.wait()
    keep = pltpu.make_async_copy(weights, matrix, semaphore.at[len(copies)])
    keep.start()
    part[...] = dot_nt(tokens[...], weights[...])
    if up_entries:
        assemble_up(seq_count, refs[3], refs[2])
    keep.wait()


def rotated(values, cosines, sines):
    return values * cosines + pltpu.roll(values, values.shape[1] // 2, 1) * sines


def qkv_kernel(seq_count, unused, lengths, mine, theirs, up_blocks, cosines, sines, *refs):
    queries, pairs, low_rank = refs[unused:]
    rows = mine.shape[0]
    own_rows = queries.shape[0] // QHEADS
    query_columns = QHEADS * HEAD_WIDTH
    value_start = query_columns + HEAD_WIDTH
    features = value_start + HEAD_WIDTH
    joint_rank = low_rank.shape[1]
    middle = features + joint_rank
    ends = kernel_marks(lengths)

    def low_rows(picked, second):
        first_low = mine[picked, features:middle] + theirs[picked, features:middle]
        second_low = mine[picked, middle:] + theirs[picked, middle:]
        return jnp.where(second, second_low, first_low).astype(jnp.bfloat16)

    first = (lax.axis_index("seq") >= seq_count // 2).astype(jnp.int32)
    first_row = lax.axis_index("seq") * rows
    segments = row_segments(ends, row_positions(first_row, rows))
    low = low_rows(slice(None), segments != first)
    low_rank[...] = low
    value_delta = jnp.zeros((rows, HEAD_WIDTH), jnp.float32)
    for document in range(SEGS):
        chosen = jnp.where(segments == document, low, jnp.zeros_like(low))
        value_delta += dot_nn(chosen, up_blocks[document, :, query_columns:])
    keys = mine[:, query_columns:value_start] + theirs[:, query_columns:value_start]
    pairs[:, :HEAD_WIDTH] = rotated(keys, cosines[...], sines[...]).astype(jnp.bfloat16)
    values = mine[:, value_start:features] + theirs[:, value_start:features]
    pairs[:, HEAD_WIDTH:] = (values + adapter_scale * value_delta).astype(jnp.bfloat16)
    start = pl.multiple_of(lax.axis_index("tp") * own_rows, own_rows)
    own = pl.ds(start, own_rows)
    own_segments = row_segments(ends, row_positions(first_row + start, own_rows))
    own_low = low_rows(own, own_segments != first)
    query_delta = jnp.zeros((own_rows, query_columns), jnp.float32)
    for document in range(SEGS):
        chosen = jnp.where(own_segments == document, own_low, jnp.zeros_like(own_low))
        query_delta += dot_nn(chosen, up_blocks[document, :, :query_columns])
    projected = mine[own, :query_columns] + theirs[own, :query_columns]
    projected = projected + adapter_scale * query_delta
    for head in range(QHEADS):
        turned = rotated(
            projected[:, head * HEAD_WIDTH : (head + 1) * HEAD_WIDTH], cosines[own], sines[own]
        )
        queries[head * own_rows : (head + 1) * own_rows] = turned.astype(jnp.bfloat16)


def attention_kernel(block_count, unused, lengths, queries, incoming, cosines, sines, *refs):
    blocks = refs[:block_count]
    output, query_grad, kept, sent, low_probs = refs[block_count + unused :]
    own_rows, query_columns = incoming.shape
    rows = blocks[0].shape[0]
    score_scale = HEAD_WIDTH ** (-0.5)
    ends = kernel_marks(lengths)
    seq_index, tp_index = lax.axis_index("seq"), lax.axis_index("tp")
    positions = row_positions(seq_index * rows + tp_index * own_rows, own_rows)
    positions = jnp.concatenate([positions] * QHEADS, axis=0)
    segments = row_segments(ends, positions)
    starts = jnp.where(segments == 0, 0, jnp.where(segments == 1, ends[0], ends[1]))
    scores = []
    for back, block in enumerate(blocks):
        key_positions = (seq_index - back) * rows + lax.broadcasted_iota(jnp.int32, (1, rows), 1)
        allowed = (key_positions <= positions) & (key_positions >= starts)
        block_scores = dot_nt(queries[...], block[:, :HEAD_WIDTH]) * score_scale
        scores.append(jnp.where(allowed, block_scores, masked_score))
    row_max = functools.reduce(
        jnp.maximum, [jnp.max(part, axis=1, keepdims=True) for part in scores]
    )
    raised = [jnp.exp(part - row_max) for part in scores]
    row_total = sum(jnp.sum(part, axis=1, keepdims=True) for part in raised)
    inverse = 1.0 / row_total
    probs = [part * inverse for part in raised]
    weighted = jnp.zeros((QHEADS * own_rows, HEAD_WIDTH), jnp.float32)
    for back, block in enumerate(blocks):
        low_probs[back] = probs[back].astype(jnp.bfloat16)
        weighted += dot_nn(low_probs[back], block[:, HEAD_WIDTH:])
    attended = weighted.astype(jnp.bfloat16)
    gradients = jnp.concatenate(
        [incoming[:, head * HEAD_WIDTH : (head + 1) * HEAD_WIDTH] for head in range(QHEADS)],
        axis=0,
    )
    row_delta = jnp.sum(
        gradients.astype(jnp.float32) * attended.astype(jnp.float32), axis=1, keepdims=True
    )
    start = pl.multiple_of(tp_index * own_rows, own_rows)
    total = jnp.zeros((QHEADS * own_rows, HEAD_WIDTH), jnp.float32)
    for back, block in enumerate(blocks):
        prob_grad = dot_nt(gradients, block[:, HEAD_WIDTH:])
        score_grad = (probs[back] * (prob_grad - row_delta)).astype(jnp.bfloat16)
        total += dot_nn(score_grad, block[:, :HEAD_WIDTH])
        key_part = dot_tn(score_grad, queries[...]) * score_scale
        value_part = dot_tn(low_probs[back], gradients)
        mine = tp_index == 0
        kept[back, :, :HEAD_WIDTH] = jnp.where(mine, key_part[:own_rows], key_part[own_rows:])
        sent[back, :, :HEAD_WIDTH] = jnp.where(mine, key_part[own_rows:], key_part[:own_rows])
        kept[back, :, HEAD_WIDTH:] = jnp.where(mine, value_part[:own_rows], value_part[own_rows:])
        sent[back, :, HEAD_WIDTH:] = jnp.where(mine, value_part[own_rows:], value_part[:own_rows])
    own = pl.ds(start, own_rows)
    for head in range(QHEADS):
        picked = slice(head * own_rows, (head + 1) * own_rows)
        columns = slice(head * HEAD_WIDTH, (head + 1) * HEAD_WIDTH)
        output[:, columns] = attended[picked]
        query_grad[:, columns] = rotated(
            total[picked] * score_scale, cosines[own], -sines[own]
        ).astype(jnp.bfloat16)


def sum_kernel(unused, kept, arrived, *refs):
    for back, total in enumerate(refs[unused:]):
        total[...] = kept[back] + arrived[back]


def pair_kernel(terms, cosines, sines, *refs):
    parts, pair = refs[:terms], refs[-2]
    own_rows = pair.shape[0]
    total = sum(part[...] for part in parts)
    own = pl.ds(pl.multiple_of(lax.axis_index("tp") * own_rows, own_rows), own_rows)
    keys = rotated(total[:, :HEAD_WIDTH], cosines[own], -sines[own])
    pair[:, :HEAD_WIDTH] = keys.astype(jnp.bfloat16)
    pair[:, HEAD_WIDTH:] = total[:, HEAD_WIDTH:].astype(jnp.bfloat16)


def rank_kernel(
    seq_count, lengths, own_query, other_query, own_pair, other_pair, low_rank, up_blocks, *refs
):
    gradients, rank_grad = refs[:2]
    split_terms, (terms, blocks) = refs[2:-2], refs[-2:]
    own_rows, query_columns = own_query.shape
    rows = low_rank.shape[0]
    seq_index = lax.axis_index("seq")
    start = pl.multiple_of(lax.axis_index("tp") * own_rows, own_rows)
    other = pl.multiple_of(own_rows - start, own_rows)
    gradients[pl.ds(start, own_rows), :query_columns] = own_query[...]
    gradients[pl.ds(other, own_rows), :query_columns] = other_query[...]
    value_start = query_columns + HEAD_WIDTH
    features = value_start + HEAD_WIDTH
    gradients[pl.ds(start, own_rows), query_columns:features] = own_pair[...]
    gradients[pl.ds(other, own_rows), query_columns:features] = other_pair[...]
    query_grad = gradients[:, :query_columns]
    value_grad = gradients[:, value_start:features]
    low = low_rank[...]
    rank = low.shape[1] // 2
    segments = row_segments(kernel_marks(lengths), row_positions(seq_index * rows, rows))
    total = jnp.zeros((rows, low.shape[1]), jnp.float32)
    for document in range(SEGS):
        member = segments == document
        parts = dot_nt(query_grad, up_blocks[document, :, :query_columns])
        parts += dot_nt(value_grad, up_blocks[document, :, query_columns:])
        total = jnp.where(member, parts, total)
        chosen = jnp.where(member, low, jnp.zeros_like(low))
        query_terms = dot_tn(chosen, query_grad)
        value_terms = dot_tn(chosen, value_grad)
        place = slice(document * rank, (document + 1) * rank)
        terms[place, :query_columns] = adapter_scale * query_terms[:rank]
        terms[place, query_columns:] = adapter_scale * value_terms[rank:]
    turned = (adapter_scale * total).astype(jnp.bfloat16)
    rank_grad[...] = turned
    second = segments != (seq_index >= seq_count // 2).astype(jnp.int32)
    nothing = jnp.zeros_like(turned)
    middle = features + low.shape[1]
    gradients[:, features:middle] = jnp.where(second, nothing, turned)
    gradients[:, middle:] = jnp.where(second, turned, nothing)
    held = blocks.shape[2]
    for holder in range(seq_count):
        blocks[holder] = terms[:, holder * held : (holder + 1) * held]
    for steps, block in enumerate(split_terms):
        mine = blocks[ring_index(seq_index + steps - seq_count, seq_count)]
        if block.shape == mine.shape:
            block[...] = mine
            continue
        tail = held - 128
        count = 128 // tail
        height = mine.shape[0] // count
        first_low = mine.shape[0] + height
        block[: mine.shape[0]] = mine[:, :128]
        for part in range(count):
            block[mine.shape[0] : first_low, part * tail : (part + 1) * tail] = mine[
                part * height : (part + 1) * height, 128:
            ]
        block[first_low:, : low.shape[1]] = turned[: rows // 2].astype(jnp.float32)
        block[first_low:, low.shape[1] :] = turned[rows // 2 :].astype(jnp.float32)


def token_kernel(gradients, matrix, token_grad):
    token_grad[...] = dot_nn(gradients[...], matrix[...]).astype(jnp.bfloat16)


def down_kernel(block_count, lengths, *refs):
    columns = refs[:block_count]
    up_parts = refs[block_count : 2 * block_count]
    packed = up_parts[0].shape != up_parts[1].shape
    rank_count = 1 if packed else block_count
    ranks = refs[2 * block_count : 2 * block_count + rank_count]
    outputs = refs[2 * block_count + rank_count :]
    rows, joint_rank = ranks[0].shape
    ends = kernel_marks(lengths)
    up_rows, up_width = up_parts[0].shape
    lows, ups = [ranks[0][...]], [up_parts[0][...]]
    for behind in range(1, block_count):
        if not packed:
            lows.append(ranks[behind][...])
            ups.append(up_parts[behind][...])
            continue
        part = up_parts[behind]
        count = 128 // (up_width - 128)
        first_low = up_rows + up_rows // count
        halves = [part[first_low:, :joint_rank], part[first_low:, joint_rank:]]
        lows.append(jnp.concatenate(halves, axis=0).astype(jnp.bfloat16))
    all_terms = []
    for document in range(SEGS):
        total = jnp.zeros((joint_rank, columns[0].shape[1]), jnp.float32)
        for behind in range(block_count):
            holder = ring_index(lax.axis_index("seq") - behind, block_count)
            segments = row_segments(ends, row_positions(holder * rows, rows))
            chosen = jnp.where(segments == document, lows[behind], jnp.zeros_like(lows[behind]))
            total += dot_tn(chosen, columns[behind][...])
        all_terms.append(total)
    down_terms = jnp.concatenate(all_terms, axis=0)
    if not packed:
        outputs[0][...] = down_terms
        outputs[1][...] = sum(ups)
        return
    own_down, far, own_up, up_terms = outputs
    tail = up_width - 128
    height = up_rows // (128 // tail)
    up_terms[...] = ups[0]
    for part in up_parts[1:]:
        up_terms[:, :128] += part[:up_rows]
        for piece in range(128 // tail):
            up_terms[piece * height : (piece + 1) * height, 128:] += part[
                up_rows : up_rows + height, piece * tail : (piece + 1) * tail
            ]
    held, held_up = own_down.shape[1], own_up.shape[1]
    ahead = lax.axis_index("batch") == 0
    own_down[...] = jnp.where(ahead, down_terms[:, :held], down_terms[:, held:])
    far[:, :held] = jnp.where(ahead, down_terms[:, held:], down_terms[:, :held])
    left, right = up_terms[:, :held_up], up_terms[:, held_up:]
    own_up[...] = jnp.where(ahead, left, right)
    far_up = jnp.where(ahead, right, left)
    spare = far.shape[1] - held
    far[:up_rows, held:] = far_up[:, :spare]
    far[up_rows:, held : held + held_up - spare] = far_up[:, spare:]


def packed_bank_kernel(bank_rows, own_down, far, own_up, down_zeros, up_zeros, down_out, up_out):
    step = pl.program_id(0)
    joint_rank, held = down_out.shape[1], down_out.shape[3]
    low_width, held_up = up_out.shape[1:]
    up_rows = own_up.shape[0]
    spare = far.shape[1] - held
    down_total = jnp.zeros((joint_rank, held), jnp.float32)
    head = jnp.zeros((low_width, spare), jnp.float32)
    rest = jnp.zeros((low_width, held_up - spare), jnp.float32)
    for document in range(SEGS):
        rows = slice(document * joint_rank, (document + 1) * joint_rank)
        lows = slice(document * low_width, (document + 1) * low_width)
        same = bank_rows[document] == bank_rows[step]
        down_total += jnp.where(same, own_down[rows], 0.0)
        head += jnp.where(same, own_up[lows, :spare], 0.0)
        rest += jnp.where(same, own_up[lows, spare:], 0.0)
        same = bank_rows[SEGS + document] == bank_rows[step]
        down_total += jnp.where(same, far[rows, :held], 0.0)
        head += jnp.where(same, far[lows, held:], 0.0)
        lows = slice(up_rows + document * low_width, up_rows + (document + 1) * low_width)
        rest += jnp.where(same, far[lows, held : held + held_up - spare], 0.0)
    down_out[0, :, 0, :] = down_total
    up_out[0, :, :spare] = head
    up_out[0, :, spare:] = rest


def bank_kernel(block_count, bank_rows, *refs):
    down_terms = refs[:block_count]
    up_terms = refs[block_count : 2 * block_count]
    down_out, up_out = refs[2 * block_count + 2 :]
    step = pl.program_id(0)
    row = bank_rows[step]
    joint_rank = down_out.shape[1]
    low_width = up_out.shape[1]
    down_total = jnp.zeros((joint_rank, down_out.shape[3]), jnp.float32)
    up_total = jnp.zeros((low_width, up_out.shape[2]), jnp.float32)
    for block in range(block_count):
        for document in range(SEGS):
            same = bank_rows[block * SEGS + document] == row
            down_rows = down_terms[block][document * joint_rank : (document + 1) * joint_rank]
            up_rows = up_terms[block][document * low_width : (document + 1) * low_width]
            down_total += jnp.where(same, down_rows, 0.0)
            up_total += jnp.where(same, up_rows, 0.0)
    down_out[0, :, 0, :] = down_total
    up_out[0] = up_total


def shards(
    tokens,
    frozen_qkv_matrix,
    adapter_down_weight,
    adapter_up_weight,
    adapter_bank_row,
    document_lengths,
    document_adapter,
    output_gradient,
):
    seq_count = lax.axis_size("seq")
    batch_count = lax.axis_size("batch")
    group_count = lax.axis_size("groups")
    chip_size = lax.axis_size("tp")
    seq_index = lax.axis_index("seq")
    batch_index = lax.axis_index("batch")
    group_index = lax.axis_index("groups")
    tp_index = lax.axis_index("tp")
    local_tokens = tokens[0]
    rows, width = local_tokens.shape
    own_rows = rows // chip_size
    query_columns = QHEADS * HEAD_WIDTH
    frozen_rows = frozen_qkv_matrix.shape[0]
    features = frozen_rows * seq_count
    low_width = ADAPTER_RANK
    joint_rank = adapter_down_weight.shape[1]
    adapters = adapter_bank_row.shape[0]
    bf16 = jnp.bfloat16
    f32 = jnp.float32

    lengths = lax.dynamic_index_in_dim(document_lengths, batch_index, 0, keepdims=False)
    first_end = lengths[0]
    second_end = first_end + lengths[1]
    half_count = seq_count // 2
    held_down = adapter_down_weight.shape[3]
    held_up = adapter_up_weight.shape[2]
    down_width = held_down * batch_count
    up_width = held_up * batch_count

    positions = seq_index * rows + jnp.arange(rows, dtype=jnp.int32)
    inside = positions - jnp.where(
        positions >= second_end, second_end, jnp.where(positions >= first_end, first_end, 0)
    )
    exponent = jnp.arange(HEAD_WIDTH // 2, dtype=f32) * (2.0 / HEAD_WIDTH)
    inverse = jnp.power(jnp.float32(rope_base), -exponent)
    angles = inside.astype(f32)[:, None] * jnp.concatenate([inverse, inverse])[None, :]
    signs = jnp.where(jnp.arange(HEAD_WIDTH) < HEAD_WIDTH // 2, -1.0, 1.0).astype(f32)
    cosines = jnp.cos(angles)
    sines = jnp.sin(angles) * signs[None, :]

    sample_rows = lookup_rows(adapter_bank_row, document_adapter)
    bank_rows = sample_rows.reshape(-1)
    if batch_count == 2:
        own_bank = jnp.where(batch_index == 0, sample_rows[0], sample_rows[1])
        far_bank = jnp.where(batch_index == 0, sample_rows[1], sample_rows[0])
        bank_rows = jnp.concatenate([own_bank, far_bank])
    down_bank = adapter_down_weight[:, :, 0, :]
    down_zeros = jnp.zeros((adapters, joint_rank, 1, held_down), f32)
    up_zeros = jnp.zeros((adapters, low_width, held_up), f32)

    plane_count = group_count * batch_count
    share = width // plane_count
    padded_down = (held_down + 127) // 128 * 128
    direct = (
        group_count == 2
        and seq_count == 4
        and share == down_width
        and batch_count == 2
        and share % 128 == 0
        and down_width % 128 == 0
        and frozen_rows % 16 == 0
        and 4 * up_width <= down_width
        and up_width > 128
        and 128 % (up_width - 128) == 0
        and 0 < held_up + held_down - padded_down <= padded_down - held_down
    )
    up_entries = []
    if direct:
        own_share = lax.dynamic_slice_in_dim(
            frozen_qkv_matrix, (group_index * batch_count + batch_index) * share, share, axis=1
        )
        before = shift(own_share, "seq", 1)
        after = shift(own_share, "seq", 3)
        far_down = shift(down_bank[far_bank], "batch", 1)
        far_up = shift(adapter_up_weight[far_bank], "batch", 1)
        own_down, own_up = down_bank[own_bank], adapter_up_weight[own_bank]
        payload_rows = 2 * joint_rank + low_width // 2
        pack_shapes = [(2 * frozen_rows, share), (frozen_rows + payload_rows, share)]
        pack_shapes += [(payload_rows, share)] * 3
        plane, forward, payload, *payloads = pl.pallas_call(
            pack_kernel,
            out_shape=[jax.ShapeDtypeStruct(shape, bf16) for shape in pack_shapes],
            in_specs=[in_vmem()] * 6,
            out_specs=[by_block(shape) for shape in pack_shapes],
            scratch_shapes=[
                pltpu.VMEM((SEGS * joint_rank, down_width), bf16),
                pltpu.VMEM((SEGS, low_width, 2 * held_up), bf16),
            ],
            compiler_params=pltpu.CompilerParams(vmem_limit_bytes=16 * mebibyte),
            cost_estimate=cost(0, 8 * frozen_rows * share),
            name="pack",
        )(own_down, far_down, own_up, far_up, before, after)

        def over_plane(value):
            over_both = [(at, plane_count - 1 - at) for at in range(plane_count)]
            return [
                shift(value, "batch", 1),
                shift(value, "groups", 1),
                lax.ppermute(value, ("groups", "batch"), over_both),
            ]

        plane_parts = over_plane(plane)
        forward = shift(forward, "seq", 1)
        middle = forward[:frozen_rows]
        middle_parts = over_plane(middle)
        payloads = [shift(part, "seq", steps + 2) for steps, part in enumerate(payloads)]
        arrays = [frozen_qkv_matrix, before, after, forward, payload] + payloads
        arrays += plane_parts + middle_parts

        def frozen_at(behind, batch_step, group_step):
            return frozen_place(seq_count, frozen_rows, share, behind, batch_step, group_step)

        def down_at(behind):
            return down_place(seq_count, features, down_width, behind)

        entries = [
            (0, 0, frozen_rows, frozen_place(seq_count, frozen_rows, None, 0, 0, 0)),
            (1, 0, frozen_rows, frozen_at(1, 0, 0)),
            (2, 0, frozen_rows, frozen_at(3, 0, 0)),
            (3, 0, frozen_rows, frozen_at(2, 0, 0)),
            (4, 0, 2 * joint_rank, down_at(0)),
            (3, frozen_rows, 2 * joint_rank, down_at(1)),
            (5, 0, 2 * joint_rank, down_at(2)),
            (6, 0, 2 * joint_rank, down_at(3)),
        ]
        up_entries = [(4, 2 * joint_rank, 0), (3, frozen_rows + 2 * joint_rank, 1)]
        up_entries += [(5, 2 * joint_rank, 2), (6, 2 * joint_rank, 3)]
        for number, (batch_step, group_step) in enumerate(((1, 0), (0, 1), (1, 1))):
            entries += [
                (7 + number, 0, frozen_rows, frozen_at(1, batch_step, group_step)),
                (7 + number, frozen_rows, frozen_rows, frozen_at(3, batch_step, group_step)),
                (10 + number, 0, frozen_rows, frozen_at(2, batch_step, group_step)),
            ]
        early = [forward, down_zeros, up_zeros, cosines, sines, bank_rows]
        column_blocks = pl.pallas_call(
            functools.partial(cut_kernel, len(early), seq_count),
            out_shape=[jax.ShapeDtypeStruct((rows, down_width), bf16)] * seq_count,
            in_specs=[in_vmem()] + [in_place()] * len(early),
            out_specs=[by_block((rows, down_width))] * seq_count,
            compiler_params=pltpu.CompilerParams(vmem_limit_bytes=16 * mebibyte),
            cost_estimate=cost(0, 4 * rows * width),
            name="cut",
        )(local_tokens, *early)
    else:
        bank_rows = sample_rows.reshape(-1)
        got_down = lax.all_to_all(
            down_bank[sample_rows], "batch", split_axis=0, concat_axis=0, tiled=True
        )
        got_up = lax.all_to_all(
            adapter_up_weight[sample_rows], "batch", split_axis=0, concat_axis=0, tiled=True
        )
        down_block = jnp.transpose(got_down, (1, 2, 0, 3)).reshape(SEGS * joint_rank, -1)
        up_block = jnp.transpose(got_up, (1, 2, 0, 3)).reshape(SEGS * low_width, -1)
        all_down = lax.all_gather(down_block, "seq", axis=0)
        all_up = lax.all_gather(up_block, "seq", axis=0)
        first = (seq_index >= half_count).astype(jnp.int32)
        merged = jnp.transpose(all_down, (1, 0, 2)).reshape(SEGS * joint_rank, -1)
        arrays = [
            lax.all_gather(frozen_qkv_matrix, "seq", axis=0, tiled=True),
            lax.dynamic_slice_in_dim(merged, first * joint_rank, 2 * joint_rank),
        ]
        entries = [
            (0, 0, features, whole_place(0)),
            (1, 0, 2 * joint_rank, whole_place(features)),
        ]
        up_rows = jnp.transpose(all_up, (1, 0, 2)).reshape(SEGS, low_width, -1)
        is_query = jnp.arange(up_rows.shape[2]) < query_columns
        up_blocks = jnp.concatenate(
            [
                jnp.where(is_query[None, None, :], up_rows, 0),
                jnp.where(is_query[None, None, :], 0, up_rows),
            ],
            axis=1,
        )
        column_blocks = [
            lax.dynamic_slice_in_dim(
                local_tokens,
                jnp.remainder(seq_index + steps, seq_count) * down_width,
                down_width,
                axis=1,
            )
            for steps in range(seq_count)
        ]

    column_parts = [
        shift(block, "seq", steps) if steps else block
        for steps, block in enumerate(column_blocks)
    ]
    early = [column_parts[2]] if direct and seq_count > 3 else []
    up_shape = (SEGS, joint_rank, query_columns + HEAD_WIDTH)
    matrix_rows = features + 2 * joint_rank
    arrived = [pltpu.VMEM((seq_count, low_width // 2, down_width), bf16)] if direct else []
    part, matrix, *built = pl.pallas_call(
        functools.partial(
            project_kernel, len(arrays), entries, up_entries, len(early), seq_count
        ),
        out_shape=[
            jax.ShapeDtypeStruct((rows, matrix_rows), f32),
            jax.ShapeDtypeStruct((matrix_rows, width), bf16),
        ]
        + ([jax.ShapeDtypeStruct(up_shape, bf16)] if direct else []),
        in_specs=[in_vmem()] + [in_place()] * (len(arrays) + len(early)),
        out_specs=[in_vmem(), in_place()] + ([by_block(up_shape)] if direct else []),
        scratch_shapes=arrived
        + [
            pltpu.VMEM((matrix_rows, width), bf16),
            pltpu.SemaphoreType.DMA((len(entries) + len(up_entries) + 1,)),
        ],
        compiler_params=pltpu.CompilerParams(vmem_limit_bytes=20 * mebibyte),
        cost_estimate=cost(2 * rows * width * matrix_rows, 2 * width * (matrix_rows + rows)),
        name="project",
    )(local_tokens, *arrays, *early)
    if direct:
        up_blocks = built[0]

    other_part = shift(part, "tp", 1)
    queries, pairs, low_rank = pl.pallas_call(
        functools.partial(qkv_kernel, seq_count, 0),
        out_shape=(
            jax.ShapeDtypeStruct((QHEADS * own_rows, HEAD_WIDTH), bf16),
            jax.ShapeDtypeStruct((rows, 2 * HEAD_WIDTH), bf16),
            jax.ShapeDtypeStruct((rows, joint_rank), bf16),
        ),
        in_specs=[in_smem()] + [in_vmem()] * 5,
        out_specs=(in_vmem(),) * 3,
        compiler_params=pltpu.CompilerParams(vmem_limit_bytes=8 * mebibyte),
        cost_estimate=cost(2 * rows * 3 * 64 * 640, 8 * rows * features),
        name="qkv",
    )(document_lengths, part, other_part, up_blocks, cosines, sines)

    blocks = [pairs] + [push(pairs, "seq", back) for back in range(1, half_count + 1)]
    block_count = len(blocks)
    column_parts[1] = shift(pass_after(column_blocks[1], *blocks[1:]), "seq", 1)
    incoming = output_gradient[0]
    early_columns = []
    attention, query_grad, kept, sent = pl.pallas_call(
        functools.partial(attention_kernel, block_count, len(early_columns)),
        out_shape=(
            jax.ShapeDtypeStruct((own_rows, query_columns), bf16),
            jax.ShapeDtypeStruct((own_rows, query_columns), bf16),
            jax.ShapeDtypeStruct((block_count, own_rows, 2 * HEAD_WIDTH), f32),
            jax.ShapeDtypeStruct((block_count, own_rows, 2 * HEAD_WIDTH), f32),
        ),
        in_specs=[in_smem()]
        + [in_vmem()] * (4 + block_count)
        + [in_place()] * len(early_columns),
        out_specs=(in_vmem(),) * 4,
        scratch_shapes=[pltpu.VMEM((block_count, QHEADS * own_rows, rows), bf16)],
        compiler_params=pltpu.CompilerParams(vmem_limit_bytes=(8 + 4 * block_count) * mebibyte),
        cost_estimate=cost(
            10 * block_count * QHEADS * own_rows * rows * HEAD_WIDTH,
            4 * rows * features,
            block_count * QHEADS * own_rows * rows,
        ),
        name="attention",
    )(document_lengths, queries, incoming, cosines, sines, *blocks, *early_columns)

    other_query = shift(query_grad, "tp", 1)
    due = [column_parts[1]]
    pair_sums = pl.pallas_call(
        functools.partial(sum_kernel, len(due)),
        out_shape=[jax.ShapeDtypeStruct((own_rows, 2 * HEAD_WIDTH), f32)] * block_count,
        in_specs=[in_vmem()] * 2 + [in_place()] * len(due),
        out_specs=[in_vmem()] * block_count,
        compiler_params=pltpu.CompilerParams(vmem_limit_bytes=8 * mebibyte),
        cost_estimate=cost(0, 12 * block_count * own_rows * 2 * HEAD_WIDTH),
        name="pair_sums",
    )(kept, shift(sent, "tp", 1), *due)
    pair_terms = [pair_sums[0]]
    pair_terms += [push(pair_sums[back], "seq", -back) for back in range(1, block_count)]
    pair_grad, late_block = pl.pallas_call(
        functools.partial(pair_kernel, block_count),
        out_shape=[
            jax.ShapeDtypeStruct((own_rows, 2 * HEAD_WIDTH), bf16),
            jax.ShapeDtypeStruct((rows, down_width), bf16),
        ],
        in_specs=[in_vmem()] * (2 + block_count) + [in_place()],
        out_specs=[in_vmem(), in_place()],
        input_output_aliases={2 + block_count: 1},
        compiler_params=pltpu.CompilerParams(vmem_limit_bytes=8 * mebibyte),
        cost_estimate=cost(0, 12 * block_count * own_rows * 2 * HEAD_WIDTH),
        name="pair_gradients",
    )(cosines, sines, *pair_terms, column_blocks[-1])
    column_parts[-1] = shift(late_block, "seq", seq_count - 1)
    other_pair = shift(pair_grad, "tp", 1)

    split_shapes = [(SEGS * low_width, up_width)] * seq_count
    if direct:
        sent_rows = SEGS * low_width * up_width // 128 + rows // 2
        split_shapes[1:] = [(sent_rows, 128)] * (seq_count - 1)
    gradients, rank_grad, *up_split = pl.pallas_call(
        functools.partial(rank_kernel, seq_count),
        out_shape=[
            jax.ShapeDtypeStruct((rows, matrix_rows), bf16),
            jax.ShapeDtypeStruct((rows, joint_rank), bf16),
        ]
        + [jax.ShapeDtypeStruct(shape, f32) for shape in split_shapes],
        in_specs=[in_smem()] + [in_vmem()] * 6,
        out_specs=[by_block((rows, matrix_rows)), in_vmem()]
        + [by_block(shape) for shape in split_shapes],
        scratch_shapes=[
            pltpu.VMEM((SEGS * low_width, features - HEAD_WIDTH), f32),
            pltpu.VMEM((seq_count, SEGS * low_width, held_up * batch_count), f32),
        ],
        compiler_params=pltpu.CompilerParams(vmem_limit_bytes=8 * mebibyte),
        cost_estimate=cost(4 * rows * 3 * 64 * 640, 4 * rows * features),
        name="rank_gradients",
    )(
        document_lengths, query_grad, other_query, pair_grad, other_pair, low_rank, up_blocks
    )

    rank_parts = [rank_grad]
    if not direct:
        rank_parts += [shift(rank_grad, "seq", steps) for steps in range(1, seq_count)]
    up_sums = [
        shift(block, "seq", steps) if steps else block for steps, block in enumerate(up_split)
    ]

    chunk = 512
    token_grad = pl.pallas_call(
        token_kernel,
        grid=(width // chunk,),
        out_shape=jax.ShapeDtypeStruct((rows, width), bf16),
        in_specs=[
            pl.BlockSpec((rows, matrix_rows), lambda step: (0, 0)),
            pl.BlockSpec((matrix_rows, chunk), lambda step: (0, step)),
        ],
        out_specs=pl.BlockSpec((rows, chunk), lambda step: (0, step)),
        compiler_params=pltpu.CompilerParams(vmem_limit_bytes=12 * mebibyte),
        cost_estimate=cost(2 * rows * width * matrix_rows, 2 * width * (matrix_rows + rows)),
        name="token_gradient",
    )(gradients, matrix)

    if direct:
        term_shapes = [(SEGS * joint_rank, held_down), (SEGS * joint_rank, padded_down)]
        term_shapes += [(SEGS * low_width, held_up)]
    else:
        term_shapes = [(SEGS * joint_rank, down_width), (SEGS * low_width, up_width)]
    terms = pl.pallas_call(
        functools.partial(down_kernel, seq_count),
        out_shape=[jax.ShapeDtypeStruct(shape, f32) for shape in term_shapes],
        in_specs=[in_smem()] + [in_vmem()] * (2 * seq_count + len(rank_parts)),
        out_specs=[in_vmem()] * len(term_shapes),
        scratch_shapes=[pltpu.VMEM((SEGS * low_width, up_width), f32)] if direct else [],
        compiler_params=pltpu.CompilerParams(vmem_limit_bytes=8 * mebibyte),
        cost_estimate=cost(
            2 * seq_count * rows * SEGS * joint_rank * down_width, 2 * seq_count * rows * down_width
        ),
        name="down_terms",
    )(document_lengths, *column_parts, *up_sums, *rank_parts)

    if direct:
        bank_terms = [terms[0], shift(terms[1], "batch", 1), terms[2]]
    else:
        down_send = jnp.transpose(
            terms[0].reshape(SEGS * joint_rank, batch_count, held_down), (1, 0, 2)
        )
        up_send = jnp.transpose(
            terms[1].reshape(SEGS * low_width, batch_count, held_up), (1, 0, 2)
        )
        back_down = lax.all_to_all(down_send, "batch", split_axis=0, concat_axis=0, tiled=True)
        back_up = lax.all_to_all(up_send, "batch", split_axis=0, concat_axis=0, tiled=True)
        bank_downs = [back_down[batch] for batch in range(batch_count)]
        bank_ups = [back_up[batch] for batch in range(batch_count)]
        bank_terms = bank_downs + bank_ups


    def whole(array):
        return pl.BlockSpec(array.shape, lambda step, bank: (0,) * array.ndim)

    term_count = len(bank_terms)
    down_grad, up_grad = pl.pallas_call(
        packed_bank_kernel if direct else functools.partial(bank_kernel, batch_count),
        out_shape=(
            jax.ShapeDtypeStruct(down_zeros.shape, f32),
            jax.ShapeDtypeStruct(up_zeros.shape, f32),
        ),
        grid_spec=pltpu.PrefetchScalarGridSpec(
            num_scalar_prefetch=1,
            grid=(batch_count * SEGS,),
            in_specs=[whole(array) for array in bank_terms] + [in_place()] * 2,
            out_specs=(
                pl.BlockSpec(
                    (1, joint_rank, 1, held_down),
                    lambda step, bank: (bank[step], 0, 0, 0),
                ),
                pl.BlockSpec(
                    (1, low_width, held_up),
                    lambda step, bank: (bank[step], 0, 0),
                ),
            ),
        ),
        input_output_aliases={1 + term_count: 0, 2 + term_count: 1},
        compiler_params=pltpu.CompilerParams(vmem_limit_bytes=16 * mebibyte),
        name="bank_rows",
    )(
        bank_rows,
        *bank_terms,
        down_zeros,
        up_zeros,
    )
    return (attention[None], token_grad[None], down_grad, up_grad)


def solution(mesh):
    in_specs = (
        P(("groups", "batch"), "seq", "tp"),
        P("seq", "tp"),
        P(None, None, "tp", ("seq", "batch")),
        P(None, None, ("seq", "batch")),
        P(),
        P("groups", None),
        P("groups", None),
        P(("groups", "batch"), ("seq", "tp"), None),
    )
    out_specs = (
        P(("groups", "batch"), ("seq", "tp"), None),
        P(("groups", "batch"), "seq", "tp"),
        P("groups", None, "tp", ("seq", "batch")),
        P("groups", None, ("seq", "batch")),
    )
    return jax.shard_map(shards, mesh=mesh, in_specs=in_specs, out_specs=out_specs, check_vma=False)
```

```python
import functools

import jax
import jax.numpy as jnp
from jax import lax
from jax.experimental import pallas as pl
from jax.experimental.pallas import tpu as pltpu
from jax.sharding import PartitionSpec as P

QHEADS = 4
HEAD_WIDTH = 128
ADAPTER_RANK = 32
SEGS = 3

adapter_scale = 2.0
rope_base = 5000000.0
masked_score = -1e30
mebibyte = 1024 * 1024


def shift(value, axis, steps):
    count = lax.axis_size(axis)
    return lax.ppermute(value, axis, [(at, (at + steps) % count) for at in range(count)])


def push(value, axis, steps):
    count = lax.axis_size(axis)
    pairs = [(at, at + steps) for at in range(count) if 0 <= at + steps < count]
    return lax.ppermute(value, axis, pairs)


def dot_nt(left, right):
    return lax.dot_general(
        left, right, (((1,), (1,)), ((), ())), preferred_element_type=jnp.float32
    )


def dot_nn(left, right):
    return jnp.dot(left, right, preferred_element_type=jnp.float32)


def dot_tn(left, right):
    return lax.dot_general(
        left, right, (((0,), (0,)), ((), ())), preferred_element_type=jnp.float32
    )


def lookup_rows(adapter_bank_row, document_adapter):
    matches = document_adapter[..., None] == jnp.arange(adapter_bank_row.shape[0], dtype=jnp.int32)
    return jnp.sum(jnp.where(matches, adapter_bank_row, 0), axis=-1)


def row_positions(first, count):
    return first + lax.broadcasted_iota(jnp.int32, (count, 1), 0)


def ring_index(index, count):
    return lax.rem(index + count, count)


def kernel_marks(lengths):
    batch = lax.axis_index("batch")
    first_end = lengths[batch, 0]
    return first_end, first_end + lengths[batch, 1]


def row_segments(ends, positions):
    return (positions >= ends[0]).astype(jnp.int32) + (positions >= ends[1]).astype(jnp.int32)


def cost(flops, bytes_accessed, transcendentals=0):
    return pl.CostEstimate(
        flops=flops, bytes_accessed=bytes_accessed, transcendentals=transcendentals
    )


def in_vmem():
    return pl.BlockSpec(memory_space=pltpu.VMEM)


def in_smem():
    return pl.BlockSpec(memory_space=pltpu.SMEM)


def by_block(shape):
    return pl.BlockSpec(shape, lambda: (0,) * len(shape))


def in_place():
    return pl.BlockSpec(memory_space=pl.ANY)


def fetch(piece, target, place, semaphore):
    height, width = piece.shape
    row, column = place()
    copy = pltpu.make_async_copy(
        piece,
        target.at[
            pl.ds(pl.multiple_of(row, 16), height), pl.ds(pl.multiple_of(column, 128), width)
        ],
        semaphore,
    )
    copy.start()
    return copy


def frozen_place(seq_count, rows, share, behind, batch_step, group_step):
    def place():
        holder = ring_index(lax.axis_index("seq") - behind, seq_count)
        if share is None:
            return holder * rows, 0
        batch = lax.rem(lax.axis_index("batch") + batch_step, 2)
        group = lax.rem(lax.axis_index("groups") + group_step, 2)
        return holder * rows, (group * 2 + batch) * share

    return place


def down_place(seq_count, features, width, behind):
    def place():
        return features, ring_index(lax.axis_index("seq") - behind, seq_count) * width

    return place


def whole_place(row):
    def place():
        return row, 0

    return place


def pack_kernel(own_down, far_down, own_up, far_up, before, after, *refs):
    plane, forward, payloads, (down, up) = refs[0], refs[1], refs[2:-2], refs[-2:]
    ahead = lax.axis_index("batch") == 0
    joint_rank, held = own_down.shape[1:]
    low_width, held_up = own_up.shape[1:]
    frozen_rows = before.shape[0]
    plane[:frozen_rows] = before[...]
    plane[frozen_rows:] = after[...]
    forward[:frozen_rows] = before[...]
    for document in range(SEGS):
        rows = slice(document * joint_rank, (document + 1) * joint_rank)
        down[rows, :held] = jnp.where(ahead, own_down[document], far_down[document])
        down[rows, held:] = jnp.where(ahead, far_down[document], own_down[document])
        up[document, :, :held_up] = jnp.where(ahead, own_up[document], far_up[document])
        up[document, :, held_up:] = jnp.where(ahead, far_up[document], own_up[document])
    half, slot = low_width // 2, down.shape[1] // 4
    targets = [(0, payloads[0], 0), (1, forward, frozen_rows)]
    targets += [(steps + 2, payload, 0) for steps, payload in enumerate(payloads[1:])]
    seq_count = len(targets)
    for steps, payload, base in targets:
        target = ring_index(lax.axis_index("seq") + steps - seq_count, seq_count)
        first = (target >= seq_count // 2).astype(jnp.int32)
        start = pl.multiple_of(first * joint_rank, joint_rank)
        payload[base : base + 2 * joint_rank] = down[pl.ds(start, 2 * joint_rank)]
        base = base + 2 * joint_rank
        for index in range(2):
            block = up[first + index]
            for part in range(2):
                column = (2 * index + part) * slot
                payload[base : base + half, column : column + 2 * held_up] = block[
                    part * half : (part + 1) * half
                ]


def pass_kernel(*refs):
    del refs


def pass_after(value, *earlier):
    return pl.pallas_call(
        pass_kernel,
        out_shape=jax.ShapeDtypeStruct(value.shape, value.dtype),
        in_specs=[in_place()] + [in_vmem()] * len(earlier),
        out_specs=in_place(),
        input_output_aliases={0: 0},
        compiler_params=pltpu.CompilerParams(vmem_limit_bytes=2 * mebibyte),
        name="pass_after",
    )(value, *earlier)


def cut_kernel(unused, seq_count, tokens, *refs):
    for steps, block in enumerate(refs[unused:]):
        target = ring_index(lax.axis_index("seq") + steps - seq_count, seq_count)
        width = block.shape[1]
        block[...] = tokens[:, pl.ds(pl.multiple_of(target * width, 128), width)]


def assemble_up(seq_count, arrived, up_blocks):
    low_width = up_blocks.shape[1] // 2
    query_columns = QHEADS * HEAD_WIDTH
    seq_index = lax.axis_index("seq")
    first = (seq_index >= seq_count // 2).astype(jnp.int32)
    held = up_blocks.shape[2] // seq_count
    half, slot = low_width // 2, arrived.shape[2] // 4
    up_blocks[...] = jnp.zeros_like(up_blocks)
    for holder in range(seq_count):
        block = arrived[ring_index(seq_index - holder, seq_count)]
        start, stop = holder * held, (holder + 1) * held
        middle = min(max(query_columns, start), stop)
        for index in range(2):
            for part in range(2):
                offset = (2 * index + part) * slot
                if middle > start:
                    up_blocks[first + index, part * half : (part + 1) * half, start:middle] = block[
                        :, offset : offset + middle - start
                    ]
                if stop > middle:
                    low = low_width + part * half
                    up_blocks[first + index, low : low + half, middle:stop] = block[
                        :, offset + middle - start : offset + held
                    ]


def project_kernel(array_count, entries, up_entries, unused, seq_count, tokens, *refs):
    arrays = refs[:array_count]
    refs = refs[array_count + unused :]
    part, matrix = refs[:2]
    weights, semaphore = refs[-2:]
    copies = []
    for number, start, height, place in entries:
        piece = arrays[number].at[pl.ds(start, height)]
        copies.append(fetch(piece, weights, place, semaphore.at[len(copies)]))
    for number, start, slot in up_entries:
        copy = pltpu.make_async_copy(
            arrays[number].at[pl.ds(start, refs[3].shape[1])],
            refs[3].at[slot],
            semaphore.at[len(copies)],
        )
        copy.start()
        copies.append(copy)
    for copy in copies:
        copy.wait()
    keep = pltpu.make_async_copy(weights, matrix, semaphore.at[len(copies)])
    keep.start()
    part[...] = dot_nt(tokens[...], weights[...])
    if up_entries:
        assemble_up(seq_count, refs[3], refs[2])
    keep.wait()


def rotated(values, cosines, sines):
    return values * cosines + pltpu.roll(values, values.shape[1] // 2, 1) * sines


def qkv_kernel(seq_count, unused, lengths, mine, theirs, up_blocks, cosines, sines, *refs):
    queries, pairs, low_rank = refs[unused:]
    rows = mine.shape[0]
    own_rows = queries.shape[0] // QHEADS
    query_columns = QHEADS * HEAD_WIDTH
    value_start = query_columns + HEAD_WIDTH
    features = value_start + HEAD_WIDTH
    joint_rank = low_rank.shape[1]
    middle = features + joint_rank
    ends = kernel_marks(lengths)

    def low_rows(picked, second):
        first_low = mine[picked, features:middle] + theirs[picked, features:middle]
        second_low = mine[picked, middle:] + theirs[picked, middle:]
        return jnp.where(second, second_low, first_low).astype(jnp.bfloat16)

    first = (lax.axis_index("seq") >= seq_count // 2).astype(jnp.int32)
    first_row = lax.axis_index("seq") * rows
    segments = row_segments(ends, row_positions(first_row, rows))
    low = low_rows(slice(None), segments != first)
    low_rank[...] = low
    value_delta = jnp.zeros((rows, HEAD_WIDTH), jnp.float32)
    for document in range(SEGS):
        chosen = jnp.where(segments == document, low, jnp.zeros_like(low))
        value_delta += dot_nn(chosen, up_blocks[document, :, query_columns:])
    keys = mine[:, query_columns:value_start] + theirs[:, query_columns:value_start]
    pairs[:, :HEAD_WIDTH] = rotated(keys, cosines[...], sines[...]).astype(jnp.bfloat16)
    values = mine[:, value_start:features] + theirs[:, value_start:features]
    pairs[:, HEAD_WIDTH:] = (values + adapter_scale * value_delta).astype(jnp.bfloat16)
    start = pl.multiple_of(lax.axis_index("tp") * own_rows, own_rows)
    own = pl.ds(start, own_rows)
    own_segments = row_segments(ends, row_positions(first_row + start, own_rows))
    own_low = low_rows(own, own_segments != first)
    query_delta = jnp.zeros((own_rows, query_columns), jnp.float32)
    for document in range(SEGS):
        chosen = jnp.where(own_segments == document, own_low, jnp.zeros_like(own_low))
        query_delta += dot_nn(chosen, up_blocks[document, :, :query_columns])
    projected = mine[own, :query_columns] + theirs[own, :query_columns]
    projected = projected + adapter_scale * query_delta
    for head in range(QHEADS):
        turned = rotated(
            projected[:, head * HEAD_WIDTH : (head + 1) * HEAD_WIDTH], cosines[own], sines[own]
        )
        queries[head * own_rows : (head + 1) * own_rows] = turned.astype(jnp.bfloat16)


def attention_kernel(block_count, unused, lengths, queries, incoming, cosines, sines, *refs):
    blocks = refs[:block_count]
    output, query_grad, kept, sent, low_probs = refs[block_count + unused :]
    own_rows, query_columns = incoming.shape
    rows = blocks[0].shape[0]
    score_scale = HEAD_WIDTH ** (-0.5)
    ends = kernel_marks(lengths)
    seq_index, tp_index = lax.axis_index("seq"), lax.axis_index("tp")
    positions = row_positions(seq_index * rows + tp_index * own_rows, own_rows)
    positions = jnp.concatenate([positions] * QHEADS, axis=0)
    segments = row_segments(ends, positions)
    starts = jnp.where(segments == 0, 0, jnp.where(segments == 1, ends[0], ends[1]))
    scores = []
    for back, block in enumerate(blocks):
        key_positions = (seq_index - back) * rows + lax.broadcasted_iota(jnp.int32, (1, rows), 1)
        allowed = (key_positions <= positions) & (key_positions >= starts)
        block_scores = dot_nt(queries[...], block[:, :HEAD_WIDTH]) * score_scale
        scores.append(jnp.where(allowed, block_scores, masked_score))
    row_max = functools.reduce(
        jnp.maximum, [jnp.max(part, axis=1, keepdims=True) for part in scores]
    )
    raised = [jnp.exp(part - row_max) for part in scores]
    row_total = sum(jnp.sum(part, axis=1, keepdims=True) for part in raised)
    inverse = 1.0 / row_total
    probs = [part * inverse for part in raised]
    weighted = jnp.zeros((QHEADS * own_rows, HEAD_WIDTH), jnp.float32)
    for back, block in enumerate(blocks):
        low_probs[back] = probs[back].astype(jnp.bfloat16)
        weighted += dot_nn(low_probs[back], block[:, HEAD_WIDTH:])
    attended = weighted.astype(jnp.bfloat16)
    gradients = jnp.concatenate(
        [incoming[:, head * HEAD_WIDTH : (head + 1) * HEAD_WIDTH] for head in range(QHEADS)],
        axis=0,
    )
    row_delta = jnp.sum(
        gradients.astype(jnp.float32) * attended.astype(jnp.float32), axis=1, keepdims=True
    )
    start = pl.multiple_of(tp_index * own_rows, own_rows)
    total = jnp.zeros((QHEADS * own_rows, HEAD_WIDTH), jnp.float32)
    for back, block in enumerate(blocks):
        prob_grad = dot_nt(gradients, block[:, HEAD_WIDTH:])
        score_grad = (probs[back] * (prob_grad - row_delta)).astype(jnp.bfloat16)
        total += dot_nn(score_grad, block[:, :HEAD_WIDTH])
        key_part = dot_tn(score_grad, queries[...]) * score_scale
        value_part = dot_tn(low_probs[back], gradients)
        mine = tp_index == 0
        kept[back, :, :HEAD_WIDTH] = jnp.where(mine, key_part[:own_rows], key_part[own_rows:])
        sent[back, :, :HEAD_WIDTH] = jnp.where(mine, key_part[own_rows:], key_part[:own_rows])
        kept[back, :, HEAD_WIDTH:] = jnp.where(mine, value_part[:own_rows], value_part[own_rows:])
        sent[back, :, HEAD_WIDTH:] = jnp.where(mine, value_part[own_rows:], value_part[:own_rows])
    own = pl.ds(start, own_rows)
    for head in range(QHEADS):
        picked = slice(head * own_rows, (head + 1) * own_rows)
        columns = slice(head * HEAD_WIDTH, (head + 1) * HEAD_WIDTH)
        output[:, columns] = attended[picked]
        query_grad[:, columns] = rotated(
            total[picked] * score_scale, cosines[own], -sines[own]
        ).astype(jnp.bfloat16)


def sum_kernel(unused, kept, arrived, *refs):
    for back, total in enumerate(refs[unused:]):
        total[...] = kept[back] + arrived[back]


def pair_kernel(terms, cosines, sines, *refs):
    parts, pair = refs[:terms], refs[-2]
    own_rows = pair.shape[0]
    total = sum(part[...] for part in parts)
    own = pl.ds(pl.multiple_of(lax.axis_index("tp") * own_rows, own_rows), own_rows)
    keys = rotated(total[:, :HEAD_WIDTH], cosines[own], -sines[own])
    pair[:, :HEAD_WIDTH] = keys.astype(jnp.bfloat16)
    pair[:, HEAD_WIDTH:] = total[:, HEAD_WIDTH:].astype(jnp.bfloat16)


def rank_kernel(
    seq_count, lengths, own_query, other_query, own_pair, other_pair, low_rank, up_blocks, *refs
):
    gradients, rank_grad = refs[:2]
    split_terms, (terms, blocks) = refs[2:-2], refs[-2:]
    own_rows, query_columns = own_query.shape
    rows = low_rank.shape[0]
    seq_index = lax.axis_index("seq")
    start = pl.multiple_of(lax.axis_index("tp") * own_rows, own_rows)
    other = pl.multiple_of(own_rows - start, own_rows)
    gradients[pl.ds(start, own_rows), :query_columns] = own_query[...]
    gradients[pl.ds(other, own_rows), :query_columns] = other_query[...]
    value_start = query_columns + HEAD_WIDTH
    features = value_start + HEAD_WIDTH
    gradients[pl.ds(start, own_rows), query_columns:features] = own_pair[...]
    gradients[pl.ds(other, own_rows), query_columns:features] = other_pair[...]
    query_grad = gradients[:, :query_columns]
    value_grad = gradients[:, value_start:features]
    low = low_rank[...]
    rank = low.shape[1] // 2
    segments = row_segments(kernel_marks(lengths), row_positions(seq_index * rows, rows))
    total = jnp.zeros((rows, low.shape[1]), jnp.float32)
    for document in range(SEGS):
        member = segments == document
        parts = dot_nt(query_grad, up_blocks[document, :, :query_columns])
        parts += dot_nt(value_grad, up_blocks[document, :, query_columns:])
        total = jnp.where(member, parts, total)
        chosen = jnp.where(member, low, jnp.zeros_like(low))
        query_terms = dot_tn(chosen, query_grad)
        value_terms = dot_tn(chosen, value_grad)
        place = slice(document * rank, (document + 1) * rank)
        terms[place, :query_columns] = adapter_scale * query_terms[:rank]
        terms[place, query_columns:] = adapter_scale * value_terms[rank:]
    turned = (adapter_scale * total).astype(jnp.bfloat16)
    rank_grad[...] = turned
    second = segments != (seq_index >= seq_count // 2).astype(jnp.int32)
    nothing = jnp.zeros_like(turned)
    middle = features + low.shape[1]
    gradients[:, features:middle] = jnp.where(second, nothing, turned)
    gradients[:, middle:] = jnp.where(second, turned, nothing)
    held = blocks.shape[2]
    for holder in range(seq_count):
        blocks[holder] = terms[:, holder * held : (holder + 1) * held]
    for steps, block in enumerate(split_terms):
        mine = blocks[ring_index(seq_index + steps - seq_count, seq_count)]
        if block.shape == mine.shape:
            block[...] = mine
            continue
        tail = held - 128
        count = 128 // tail
        height = mine.shape[0] // count
        first_low = mine.shape[0] + height
        block[: mine.shape[0]] = mine[:, :128]
        for part in range(count):
            block[mine.shape[0] : first_low, part * tail : (part + 1) * tail] = mine[
                part * height : (part + 1) * height, 128:
            ]
        block[first_low:, : low.shape[1]] = turned[: rows // 2].astype(jnp.float32)
        block[first_low:, low.shape[1] :] = turned[rows // 2 :].astype(jnp.float32)


def token_kernel(gradients, matrix, token_grad):
    token_grad[...] = dot_nn(gradients[...], matrix[...]).astype(jnp.bfloat16)


def down_kernel(block_count, lengths, *refs):
    columns = refs[:block_count]
    up_parts = refs[block_count : 2 * block_count]
    packed = up_parts[0].shape != up_parts[1].shape
    rank_count = 1 if packed else block_count
    ranks = refs[2 * block_count : 2 * block_count + rank_count]
    outputs = refs[2 * block_count + rank_count :]
    rows, joint_rank = ranks[0].shape
    ends = kernel_marks(lengths)
    up_rows, up_width = up_parts[0].shape
    lows, ups = [ranks[0][...]], [up_parts[0][...]]
    for behind in range(1, block_count):
        if not packed:
            lows.append(ranks[behind][...])
            ups.append(up_parts[behind][...])
            continue
        part = up_parts[behind]
        count = 128 // (up_width - 128)
        first_low = up_rows + up_rows // count
        halves = [part[first_low:, :joint_rank], part[first_low:, joint_rank:]]
        lows.append(jnp.concatenate(halves, axis=0).astype(jnp.bfloat16))
    all_terms = []
    for document in range(SEGS):
        total = jnp.zeros((joint_rank, columns[0].shape[1]), jnp.float32)
        for behind in range(block_count):
            holder = ring_index(lax.axis_index("seq") - behind, block_count)
            segments = row_segments(ends, row_positions(holder * rows, rows))
            chosen = jnp.where(segments == document, lows[behind], jnp.zeros_like(lows[behind]))
            total += dot_tn(chosen, columns[behind][...])
        all_terms.append(total)
    down_terms = jnp.concatenate(all_terms, axis=0)
    if not packed:
        outputs[0][...] = down_terms
        outputs[1][...] = sum(ups)
        return
    own_down, far, own_up, up_terms = outputs
    tail = up_width - 128
    height = up_rows // (128 // tail)
    up_terms[...] = ups[0]
    for part in up_parts[1:]:
        up_terms[:, :128] += part[:up_rows]
        for piece in range(128 // tail):
            up_terms[piece * height : (piece + 1) * height, 128:] += part[
                up_rows : up_rows + height, piece * tail : (piece + 1) * tail
            ]
    held, held_up = own_down.shape[1], own_up.shape[1]
    ahead = lax.axis_index("batch") == 0
    own_down[...] = jnp.where(ahead, down_terms[:, :held], down_terms[:, held:])
    far[:, :held] = jnp.where(ahead, down_terms[:, held:], down_terms[:, :held])
    left, right = up_terms[:, :held_up], up_terms[:, held_up:]
    own_up[...] = jnp.where(ahead, left, right)
    far_up = jnp.where(ahead, right, left)
    spare = far.shape[1] - held
    far[:up_rows, held:] = far_up[:, :spare]
    far[up_rows:, held : held + held_up - spare] = far_up[:, spare:]


def packed_bank_kernel(bank_rows, own_down, far, own_up, down_zeros, up_zeros, down_out, up_out):
    step = pl.program_id(0)
    joint_rank, held = down_out.shape[1], down_out.shape[3]
    low_width, held_up = up_out.shape[1:]
    up_rows = own_up.shape[0]
    spare = far.shape[1] - held
    down_total = jnp.zeros((joint_rank, held), jnp.float32)
    head = jnp.zeros((low_width, spare), jnp.float32)
    rest = jnp.zeros((low_width, held_up - spare), jnp.float32)
    for document in range(SEGS):
        rows = slice(document * joint_rank, (document + 1) * joint_rank)
        lows = slice(document * low_width, (document + 1) * low_width)
        same = bank_rows[document] == bank_rows[step]
        down_total += jnp.where(same, own_down[rows], 0.0)
        head += jnp.where(same, own_up[lows, :spare], 0.0)
        rest += jnp.where(same, own_up[lows, spare:], 0.0)
        same = bank_rows[SEGS + document] == bank_rows[step]
        down_total += jnp.where(same, far[rows, :held], 0.0)
        head += jnp.where(same, far[lows, held:], 0.0)
        lows = slice(up_rows + document * low_width, up_rows + (document + 1) * low_width)
        rest += jnp.where(same, far[lows, held : held + held_up - spare], 0.0)
    down_out[0, :, 0, :] = down_total
    up_out[0, :, :spare] = head
    up_out[0, :, spare:] = rest


def bank_kernel(block_count, bank_rows, *refs):
    down_terms = refs[:block_count]
    up_terms = refs[block_count : 2 * block_count]
    down_out, up_out = refs[2 * block_count + 2 :]
    step = pl.program_id(0)
    row = bank_rows[step]
    joint_rank = down_out.shape[1]
    low_width = up_out.shape[1]
    down_total = jnp.zeros((joint_rank, down_out.shape[3]), jnp.float32)
    up_total = jnp.zeros((low_width, up_out.shape[2]), jnp.float32)
    for block in range(block_count):
        for document in range(SEGS):
            same = bank_rows[block * SEGS + document] == row
            down_rows = down_terms[block][document * joint_rank : (document + 1) * joint_rank]
            up_rows = up_terms[block][document * low_width : (document + 1) * low_width]
            down_total += jnp.where(same, down_rows, 0.0)
            up_total += jnp.where(same, up_rows, 0.0)
    down_out[0, :, 0, :] = down_total
    up_out[0] = up_total


def shards(
    tokens,
    frozen_qkv_matrix,
    adapter_down_weight,
    adapter_up_weight,
    adapter_bank_row,
    document_lengths,
    document_adapter,
    output_gradient,
):
    seq_count = lax.axis_size("seq")
    batch_count = lax.axis_size("batch")
    group_count = lax.axis_size("groups")
    chip_size = lax.axis_size("tp")
    seq_index = lax.axis_index("seq")
    batch_index = lax.axis_index("batch")
    group_index = lax.axis_index("groups")
    tp_index = lax.axis_index("tp")
    local_tokens = tokens[0]
    rows, width = local_tokens.shape
    own_rows = rows // chip_size
    query_columns = QHEADS * HEAD_WIDTH
    frozen_rows = frozen_qkv_matrix.shape[0]
    features = frozen_rows * seq_count
    low_width = ADAPTER_RANK
    joint_rank = adapter_down_weight.shape[1]
    adapters = adapter_bank_row.shape[0]
    bf16 = jnp.bfloat16
    f32 = jnp.float32

    lengths = lax.dynamic_index_in_dim(document_lengths, batch_index, 0, keepdims=False)
    first_end = lengths[0]
    second_end = first_end + lengths[1]
    half_count = seq_count // 2
    held_down = adapter_down_weight.shape[3]
    held_up = adapter_up_weight.shape[2]
    down_width = held_down * batch_count
    up_width = held_up * batch_count

    positions = seq_index * rows + jnp.arange(rows, dtype=jnp.int32)
    inside = positions - jnp.where(
        positions >= second_end, second_end, jnp.where(positions >= first_end, first_end, 0)
    )
    exponent = jnp.arange(HEAD_WIDTH // 2, dtype=f32) * (2.0 / HEAD_WIDTH)
    inverse = jnp.power(jnp.float32(rope_base), -exponent)
    angles = inside.astype(f32)[:, None] * jnp.concatenate([inverse, inverse])[None, :]
    signs = jnp.where(jnp.arange(HEAD_WIDTH) < HEAD_WIDTH // 2, -1.0, 1.0).astype(f32)
    cosines = jnp.cos(angles)
    sines = jnp.sin(angles) * signs[None, :]

    sample_rows = lookup_rows(adapter_bank_row, document_adapter)
    bank_rows = sample_rows.reshape(-1)
    if batch_count == 2:
        own_bank = jnp.where(batch_index == 0, sample_rows[0], sample_rows[1])
        far_bank = jnp.where(batch_index == 0, sample_rows[1], sample_rows[0])
        bank_rows = jnp.concatenate([own_bank, far_bank])
    down_bank = adapter_down_weight[:, :, 0, :]
    down_zeros = jnp.zeros((adapters, joint_rank, 1, held_down), f32)
    up_zeros = jnp.zeros((adapters, low_width, held_up), f32)

    plane_count = group_count * batch_count
    share = width // plane_count
    padded_down = (held_down + 127) // 128 * 128
    direct = (
        group_count == 2
        and seq_count == 4
        and share == down_width
        and batch_count == 2
        and share % 128 == 0
        and down_width % 128 == 0
        and frozen_rows % 16 == 0
        and 4 * up_width <= down_width
        and up_width > 128
        and 128 % (up_width - 128) == 0
        and 0 < held_up + held_down - padded_down <= padded_down - held_down
    )
    up_entries = []
    if direct:
        own_share = lax.dynamic_slice_in_dim(
            frozen_qkv_matrix, (group_index * batch_count + batch_index) * share, share, axis=1
        )
        before = shift(own_share, "seq", 1)
        after = shift(own_share, "seq", 3)
        far_down = shift(down_bank[far_bank], "batch", 1)
        far_up = shift(adapter_up_weight[far_bank], "batch", 1)
        own_down, own_up = down_bank[own_bank], adapter_up_weight[own_bank]
        payload_rows = 2 * joint_rank + low_width // 2
        pack_shapes = [(2 * frozen_rows, share), (frozen_rows + payload_rows, share)]
        pack_shapes += [(payload_rows, share)] * 3
        plane, forward, payload, *payloads = pl.pallas_call(
            pack_kernel,
            out_shape=[jax.ShapeDtypeStruct(shape, bf16) for shape in pack_shapes],
            in_specs=[in_vmem()] * 6,
            out_specs=[by_block(shape) for shape in pack_shapes],
            scratch_shapes=[
                pltpu.VMEM((SEGS * joint_rank, down_width), bf16),
                pltpu.VMEM((SEGS, low_width, 2 * held_up), bf16),
            ],
            compiler_params=pltpu.CompilerParams(vmem_limit_bytes=16 * mebibyte),
            cost_estimate=cost(0, 8 * frozen_rows * share),
            name="pack",
        )(own_down, far_down, own_up, far_up, before, after)

        def over_plane(value):
            over_both = [(at, plane_count - 1 - at) for at in range(plane_count)]
            return [
                shift(value, "batch", 1),
                shift(value, "groups", 1),
                lax.ppermute(value, ("groups", "batch"), over_both),
            ]

        plane_parts = over_plane(plane)
        forward = shift(forward, "seq", 1)
        middle = forward[:frozen_rows]
        middle_parts = over_plane(middle)
        payloads = [shift(part, "seq", steps + 2) for steps, part in enumerate(payloads)]
        arrays = [frozen_qkv_matrix, before, after, forward, payload] + payloads
        arrays += plane_parts + middle_parts

        def frozen_at(behind, batch_step, group_step):
            return frozen_place(seq_count, frozen_rows, share, behind, batch_step, group_step)

        def down_at(behind):
            return down_place(seq_count, features, down_width, behind)

        entries = [
            (0, 0, frozen_rows, frozen_place(seq_count, frozen_rows, None, 0, 0, 0)),
            (1, 0, frozen_rows, frozen_at(1, 0, 0)),
            (2, 0, frozen_rows, frozen_at(3, 0, 0)),
            (3, 0, frozen_rows, frozen_at(2, 0, 0)),
            (4, 0, 2 * joint_rank, down_at(0)),
            (3, frozen_rows, 2 * joint_rank, down_at(1)),
            (5, 0, 2 * joint_rank, down_at(2)),
            (6, 0, 2 * joint_rank, down_at(3)),
        ]
        up_entries = [(4, 2 * joint_rank, 0), (3, frozen_rows + 2 * joint_rank, 1)]
        up_entries += [(5, 2 * joint_rank, 2), (6, 2 * joint_rank, 3)]
        for number, (batch_step, group_step) in enumerate(((1, 0), (0, 1), (1, 1))):
            entries += [
                (7 + number, 0, frozen_rows, frozen_at(1, batch_step, group_step)),
                (7 + number, frozen_rows, frozen_rows, frozen_at(3, batch_step, group_step)),
                (10 + number, 0, frozen_rows, frozen_at(2, batch_step, group_step)),
            ]
        early = [forward, down_zeros, up_zeros, cosines, sines, bank_rows]
        column_blocks = pl.pallas_call(
            functools.partial(cut_kernel, len(early), seq_count),
            out_shape=[jax.ShapeDtypeStruct((rows, down_width), bf16)] * seq_count,
            in_specs=[in_vmem()] + [in_place()] * len(early),
            out_specs=[by_block((rows, down_width))] * seq_count,
            compiler_params=pltpu.CompilerParams(vmem_limit_bytes=16 * mebibyte),
            cost_estimate=cost(0, 4 * rows * width),
            name="cut",
        )(local_tokens, *early)
    else:
        bank_rows = sample_rows.reshape(-1)
        got_down = lax.all_to_all(
            down_bank[sample_rows], "batch", split_axis=0, concat_axis=0, tiled=True
        )
        got_up = lax.all_to_all(
            adapter_up_weight[sample_rows], "batch", split_axis=0, concat_axis=0, tiled=True
        )
        down_block = jnp.transpose(got_down, (1, 2, 0, 3)).reshape(SEGS * joint_rank, -1)
        up_block = jnp.transpose(got_up, (1, 2, 0, 3)).reshape(SEGS * low_width, -1)
        all_down = lax.all_gather(down_block, "seq", axis=0)
        all_up = lax.all_gather(up_block, "seq", axis=0)
        first = (seq_index >= half_count).astype(jnp.int32)
        merged = jnp.transpose(all_down, (1, 0, 2)).reshape(SEGS * joint_rank, -1)
        arrays = [
            lax.all_gather(frozen_qkv_matrix, "seq", axis=0, tiled=True),
            lax.dynamic_slice_in_dim(merged, first * joint_rank, 2 * joint_rank),
        ]
        entries = [
            (0, 0, features, whole_place(0)),
            (1, 0, 2 * joint_rank, whole_place(features)),
        ]
        up_rows = jnp.transpose(all_up, (1, 0, 2)).reshape(SEGS, low_width, -1)
        is_query = jnp.arange(up_rows.shape[2]) < query_columns
        up_blocks = jnp.concatenate(
            [
                jnp.where(is_query[None, None, :], up_rows, 0),
                jnp.where(is_query[None, None, :], 0, up_rows),
            ],
            axis=1,
        )
        column_blocks = [
            lax.dynamic_slice_in_dim(
                local_tokens,
                jnp.remainder(seq_index + steps, seq_count) * down_width,
                down_width,
                axis=1,
            )
            for steps in range(seq_count)
        ]

    column_parts = [
        shift(block, "seq", steps) if steps else block
        for steps, block in enumerate(column_blocks)
    ]
    early = [column_parts[2]] if direct and seq_count > 3 else []
    up_shape = (SEGS, joint_rank, query_columns + HEAD_WIDTH)
    matrix_rows = features + 2 * joint_rank
    arrived = [pltpu.VMEM((seq_count, low_width // 2, down_width), bf16)] if direct else []
    part, matrix, *built = pl.pallas_call(
        functools.partial(
            project_kernel, len(arrays), entries, up_entries, len(early), seq_count
        ),
        out_shape=[
            jax.ShapeDtypeStruct((rows, matrix_rows), f32),
            jax.ShapeDtypeStruct((matrix_rows, width), bf16),
        ]
        + ([jax.ShapeDtypeStruct(up_shape, bf16)] if direct else []),
        in_specs=[in_vmem()] + [in_place()] * (len(arrays) + len(early)),
        out_specs=[in_vmem(), in_place()] + ([by_block(up_shape)] if direct else []),
        scratch_shapes=arrived
        + [
            pltpu.VMEM((matrix_rows, width), bf16),
            pltpu.SemaphoreType.DMA((len(entries) + len(up_entries) + 1,)),
        ],
        compiler_params=pltpu.CompilerParams(vmem_limit_bytes=20 * mebibyte),
        cost_estimate=cost(2 * rows * width * matrix_rows, 2 * width * (matrix_rows + rows)),
        name="project",
    )(local_tokens, *arrays, *early)
    if direct:
        up_blocks = built[0]

    other_part = shift(part, "tp", 1)
    queries, pairs, low_rank = pl.pallas_call(
        functools.partial(qkv_kernel, seq_count, 0),
        out_shape=(
            jax.ShapeDtypeStruct((QHEADS * own_rows, HEAD_WIDTH), bf16),
            jax.ShapeDtypeStruct((rows, 2 * HEAD_WIDTH), bf16),
            jax.ShapeDtypeStruct((rows, joint_rank), bf16),
        ),
        in_specs=[in_smem()] + [in_vmem()] * 5,
        out_specs=(in_vmem(),) * 3,
        compiler_params=pltpu.CompilerParams(vmem_limit_bytes=8 * mebibyte),
        cost_estimate=cost(2 * rows * 3 * 64 * 640, 8 * rows * features),
        name="qkv",
    )(document_lengths, part, other_part, up_blocks, cosines, sines)

    blocks = [pairs] + [push(pairs, "seq", back) for back in range(1, half_count + 1)]
    block_count = len(blocks)
    column_parts[1] = shift(pass_after(column_blocks[1], *blocks[1:]), "seq", 1)
    incoming = output_gradient[0]
    early_columns = []
    attention, query_grad, kept, sent = pl.pallas_call(
        functools.partial(attention_kernel, block_count, len(early_columns)),
        out_shape=(
            jax.ShapeDtypeStruct((own_rows, query_columns), bf16),
            jax.ShapeDtypeStruct((own_rows, query_columns), bf16),
            jax.ShapeDtypeStruct((block_count, own_rows, 2 * HEAD_WIDTH), f32),
            jax.ShapeDtypeStruct((block_count, own_rows, 2 * HEAD_WIDTH), f32),
        ),
        in_specs=[in_smem()]
        + [in_vmem()] * (4 + block_count)
        + [in_place()] * len(early_columns),
        out_specs=(in_vmem(),) * 4,
        scratch_shapes=[pltpu.VMEM((block_count, QHEADS * own_rows, rows), bf16)],
        compiler_params=pltpu.CompilerParams(vmem_limit_bytes=(8 + 4 * block_count) * mebibyte),
        cost_estimate=cost(
            10 * block_count * QHEADS * own_rows * rows * HEAD_WIDTH,
            4 * rows * features,
            block_count * QHEADS * own_rows * rows,
        ),
        name="attention",
    )(document_lengths, queries, incoming, cosines, sines, *blocks, *early_columns)

    other_query = shift(query_grad, "tp", 1)
    due = [column_parts[1]]
    pair_sums = pl.pallas_call(
        functools.partial(sum_kernel, len(due)),
        out_shape=[jax.ShapeDtypeStruct((own_rows, 2 * HEAD_WIDTH), f32)] * block_count,
        in_specs=[in_vmem()] * 2 + [in_place()] * len(due),
        out_specs=[in_vmem()] * block_count,
        compiler_params=pltpu.CompilerParams(vmem_limit_bytes=8 * mebibyte),
        cost_estimate=cost(0, 12 * block_count * own_rows * 2 * HEAD_WIDTH),
        name="pair_sums",
    )(kept, shift(sent, "tp", 1), *due)
    pair_terms = [pair_sums[0]]
    pair_terms += [push(pair_sums[back], "seq", -back) for back in range(1, block_count)]
    pair_grad, late_block = pl.pallas_call(
        functools.partial(pair_kernel, block_count),
        out_shape=[
            jax.ShapeDtypeStruct((own_rows, 2 * HEAD_WIDTH), bf16),
            jax.ShapeDtypeStruct((rows, down_width), bf16),
        ],
        in_specs=[in_vmem()] * (2 + block_count) + [in_place()],
        out_specs=[in_vmem(), in_place()],
        input_output_aliases={2 + block_count: 1},
        compiler_params=pltpu.CompilerParams(vmem_limit_bytes=8 * mebibyte),
        cost_estimate=cost(0, 12 * block_count * own_rows * 2 * HEAD_WIDTH),
        name="pair_gradients",
    )(cosines, sines, *pair_terms, column_blocks[-1])
    column_parts[-1] = shift(late_block, "seq", seq_count - 1)
    other_pair = shift(pair_grad, "tp", 1)

    split_shapes = [(SEGS * low_width, up_width)] * seq_count
    if direct:
        sent_rows = SEGS * low_width * up_width // 128 + rows // 2
        split_shapes[1:] = [(sent_rows, 128)] * (seq_count - 1)
    gradients, rank_grad, *up_split = pl.pallas_call(
        functools.partial(rank_kernel, seq_count),
        out_shape=[
            jax.ShapeDtypeStruct((rows, matrix_rows), bf16),
            jax.ShapeDtypeStruct((rows, joint_rank), bf16),
        ]
        + [jax.ShapeDtypeStruct(shape, f32) for shape in split_shapes],
        in_specs=[in_smem()] + [in_vmem()] * 6,
        out_specs=[by_block((rows, matrix_rows)), in_vmem()]
        + [by_block(shape) for shape in split_shapes],
        scratch_shapes=[
            pltpu.VMEM((SEGS * low_width, features - HEAD_WIDTH), f32),
            pltpu.VMEM((seq_count, SEGS * low_width, held_up * batch_count), f32),
        ],
        compiler_params=pltpu.CompilerParams(vmem_limit_bytes=8 * mebibyte),
        cost_estimate=cost(4 * rows * 3 * 64 * 640, 4 * rows * features),
        name="rank_gradients",
    )(
        document_lengths, query_grad, other_query, pair_grad, other_pair, low_rank, up_blocks
    )

    rank_parts = [rank_grad]
    if not direct:
        rank_parts += [shift(rank_grad, "seq", steps) for steps in range(1, seq_count)]
    up_sums = [
        shift(block, "seq", steps) if steps else block for steps, block in enumerate(up_split)
    ]

    chunk = 512
    token_grad = pl.pallas_call(
        token_kernel,
        grid=(width // chunk,),
        out_shape=jax.ShapeDtypeStruct((rows, width), bf16),
        in_specs=[
            pl.BlockSpec((rows, matrix_rows), lambda step: (0, 0)),
            pl.BlockSpec((matrix_rows, chunk), lambda step: (0, step)),
        ],
        out_specs=pl.BlockSpec((rows, chunk), lambda step: (0, step)),
        compiler_params=pltpu.CompilerParams(vmem_limit_bytes=12 * mebibyte),
        cost_estimate=cost(2 * rows * width * matrix_rows, 2 * width * (matrix_rows + rows)),
        name="token_gradient",
    )(gradients, matrix)

    if direct:
        term_shapes = [(SEGS * joint_rank, held_down), (SEGS * joint_rank, padded_down)]
        term_shapes += [(SEGS * low_width, held_up)]
    else:
        term_shapes = [(SEGS * joint_rank, down_width), (SEGS * low_width, up_width)]
    terms = pl.pallas_call(
        functools.partial(down_kernel, seq_count),
        out_shape=[jax.ShapeDtypeStruct(shape, f32) for shape in term_shapes],
        in_specs=[in_smem()] + [in_vmem()] * (2 * seq_count + len(rank_parts)),
        out_specs=[in_vmem()] * len(term_shapes),
        scratch_shapes=[pltpu.VMEM((SEGS * low_width, up_width), f32)] if direct else [],
        compiler_params=pltpu.CompilerParams(vmem_limit_bytes=8 * mebibyte),
        cost_estimate=cost(
            2 * seq_count * rows * SEGS * joint_rank * down_width, 2 * seq_count * rows * down_width
        ),
        name="down_terms",
    )(document_lengths, *column_parts, *up_sums, *rank_parts)

    if direct:
        bank_terms = [terms[0], shift(terms[1], "batch", 1), terms[2]]
    else:
        down_send = jnp.transpose(
            terms[0].reshape(SEGS * joint_rank, batch_count, held_down), (1, 0, 2)
        )
        up_send = jnp.transpose(
            terms[1].reshape(SEGS * low_width, batch_count, held_up), (1, 0, 2)
        )
        back_down = lax.all_to_all(down_send, "batch", split_axis=0, concat_axis=0, tiled=True)
        back_up = lax.all_to_all(up_send, "batch", split_axis=0, concat_axis=0, tiled=True)
        bank_downs = [back_down[batch] for batch in range(batch_count)]
        bank_ups = [back_up[batch] for batch in range(batch_count)]
        bank_terms = bank_downs + bank_ups


    def whole(array):
        return pl.BlockSpec(array.shape, lambda step, bank: (0,) * array.ndim)

    term_count = len(bank_terms)
    down_grad, up_grad = pl.pallas_call(
        packed_bank_kernel if direct else functools.partial(bank_kernel, batch_count),
        out_shape=(
            jax.ShapeDtypeStruct(down_zeros.shape, f32),
            jax.ShapeDtypeStruct(up_zeros.shape, f32),
        ),
        grid_spec=pltpu.PrefetchScalarGridSpec(
            num_scalar_prefetch=1,
            grid=(batch_count * SEGS,),
            in_specs=[whole(array) for array in bank_terms] + [in_place()] * 2,
            out_specs=(
                pl.BlockSpec(
                    (1, joint_rank, 1, held_down),
                    lambda step, bank: (bank[step], 0, 0, 0),
                ),
                pl.BlockSpec(
                    (1, low_width, held_up),
                    lambda step, bank: (bank[step], 0, 0),
                ),
            ),
        ),
        input_output_aliases={1 + term_count: 0, 2 + term_count: 1},
        compiler_params=pltpu.CompilerParams(vmem_limit_bytes=16 * mebibyte),
        name="bank_rows",
    )(
        bank_rows,
        *bank_terms,
        down_zeros,
        up_zeros,
    )
    return (attention[None], token_grad[None], down_grad, up_grad)


def solution(mesh):
    in_specs = (
        P(("groups", "batch"), "seq", "tp"),
        P("seq", "tp"),
        P(None, None, "tp", ("seq", "batch")),
        P(None, None, ("seq", "batch")),
        P(),
        P("groups", None),
        P("groups", None),
        P(("groups", "batch"), ("seq", "tp"), None),
    )
    out_specs = (
        P(("groups", "batch"), ("seq", "tp"), None),
        P(("groups", "batch"), "seq", "tp"),
        P("groups", None, "tp", ("seq", "batch")),
        P("groups", None, ("seq", "batch")),
    )
    return jax.shard_map(shards, mesh=mesh, in_specs=in_specs, out_specs=out_specs, check_vma=False)
```

```python
import functools

import jax
import jax.numpy as jnp
from jax import lax
from jax.experimental import pallas as pl
from jax.experimental.pallas import tpu as pltpu
from jax.sharding import PartitionSpec as P

QHEADS = 4
HEAD_WIDTH = 128
ADAPTER_RANK = 32
SEGS = 3

adapter_scale = 2.0
rope_base = 5000000.0
masked_score = -1e30
mebibyte = 1024 * 1024


def shift(value, axis, steps):
    count = lax.axis_size(axis)
    return lax.ppermute(value, axis, [(at, (at + steps) % count) for at in range(count)])


def push(value, axis, steps):
    count = lax.axis_size(axis)
    pairs = [(at, at + steps) for at in range(count) if 0 <= at + steps < count]
    return lax.ppermute(value, axis, pairs)


def dot_nt(left, right):
    return lax.dot_general(
        left, right, (((1,), (1,)), ((), ())), preferred_element_type=jnp.float32
    )


def dot_nn(left, right):
    return jnp.dot(left, right, preferred_element_type=jnp.float32)


def dot_tn(left, right):
    return lax.dot_general(
        left, right, (((0,), (0,)), ((), ())), preferred_element_type=jnp.float32
    )


def lookup_rows(adapter_bank_row, document_adapter):
    matches = document_adapter[..., None] == jnp.arange(adapter_bank_row.shape[0], dtype=jnp.int32)
    return jnp.sum(jnp.where(matches, adapter_bank_row, 0), axis=-1)


def row_positions(first, count):
    return first + lax.broadcasted_iota(jnp.int32, (count, 1), 0)


def ring_index(index, count):
    return lax.rem(index + count, count)


def kernel_marks(lengths):
    batch = lax.axis_index("batch")
    first_end = lengths[batch, 0]
    return first_end, first_end + lengths[batch, 1]


def row_segments(ends, positions):
    return (positions >= ends[0]).astype(jnp.int32) + (positions >= ends[1]).astype(jnp.int32)


def cost(flops, bytes_accessed, transcendentals=0):
    return pl.CostEstimate(
        flops=flops, bytes_accessed=bytes_accessed, transcendentals=transcendentals
    )


def in_vmem():
    return pl.BlockSpec(memory_space=pltpu.VMEM)


def in_smem():
    return pl.BlockSpec(memory_space=pltpu.SMEM)


def by_block(shape):
    return pl.BlockSpec(shape, lambda: (0,) * len(shape))


def in_place():
    return pl.BlockSpec(memory_space=pl.ANY)


def fetch(piece, target, place, semaphore):
    height, width = piece.shape
    row, column = place()
    copy = pltpu.make_async_copy(
        piece,
        target.at[
            pl.ds(pl.multiple_of(row, 16), height), pl.ds(pl.multiple_of(column, 128), width)
        ],
        semaphore,
    )
    copy.start()
    return copy


def frozen_place(seq_count, rows, share, behind, batch_step, group_step):
    def place():
        holder = ring_index(lax.axis_index("seq") - behind, seq_count)
        if share is None:
            return holder * rows, 0
        batch = lax.rem(lax.axis_index("batch") + batch_step, 2)
        group = lax.rem(lax.axis_index("groups") + group_step, 2)
        return holder * rows, (group * 2 + batch) * share

    return place


def down_place(seq_count, features, width, behind):
    def place():
        return features, ring_index(lax.axis_index("seq") - behind, seq_count) * width

    return place


def whole_place(row):
    def place():
        return row, 0

    return place


def pack_kernel(own_down, far_down, own_up, far_up, before, after, *refs):
    plane, forward, payloads, (down, up) = refs[0], refs[1], refs[2:-2], refs[-2:]
    ahead = lax.axis_index("batch") == 0
    joint_rank, held = own_down.shape[1:]
    low_width, held_up = own_up.shape[1:]
    frozen_rows = before.shape[0]
    plane[:frozen_rows] = before[...]
    plane[frozen_rows:] = after[...]
    forward[:frozen_rows] = before[...]
    for document in range(SEGS):
        rows = slice(document * joint_rank, (document + 1) * joint_rank)
        down[rows, :held] = jnp.where(ahead, own_down[document], far_down[document])
        down[rows, held:] = jnp.where(ahead, far_down[document], own_down[document])
        up[document, :, :held_up] = jnp.where(ahead, own_up[document], far_up[document])
        up[document, :, held_up:] = jnp.where(ahead, far_up[document], own_up[document])
    half, slot = low_width // 2, down.shape[1] // 4
    targets = [(0, payloads[0], 0), (1, forward, frozen_rows)]
    targets += [(steps + 2, payload, 0) for steps, payload in enumerate(payloads[1:])]
    seq_count = len(targets)
    for steps, payload, base in targets:
        target = ring_index(lax.axis_index("seq") + steps - seq_count, seq_count)
        first = (target >= seq_count // 2).astype(jnp.int32)
        start = pl.multiple_of(first * joint_rank, joint_rank)
        payload[base : base + 2 * joint_rank] = down[pl.ds(start, 2 * joint_rank)]
        base = base + 2 * joint_rank
        for index in range(2):
            block = up[first + index]
            for part in range(2):
                column = (2 * index + part) * slot
                payload[base : base + half, column : column + 2 * held_up] = block[
                    part * half : (part + 1) * half
                ]


def pass_kernel(*refs):
    del refs


def pass_after(value, *earlier):
    return pl.pallas_call(
        pass_kernel,
        out_shape=jax.ShapeDtypeStruct(value.shape, value.dtype),
        in_specs=[in_place()] + [in_vmem()] * len(earlier),
        out_specs=in_place(),
        input_output_aliases={0: 0},
        compiler_params=pltpu.CompilerParams(vmem_limit_bytes=2 * mebibyte),
        name="pass_after",
    )(value, *earlier)


def cut_kernel(unused, seq_count, tokens, *refs):
    for steps, block in enumerate(refs[unused:]):
        target = ring_index(lax.axis_index("seq") + steps - seq_count, seq_count)
        width = block.shape[1]
        block[...] = tokens[:, pl.ds(pl.multiple_of(target * width, 128), width)]


def assemble_up(seq_count, arrived, up_blocks):
    low_width = up_blocks.shape[1] // 2
    query_columns = QHEADS * HEAD_WIDTH
    seq_index = lax.axis_index("seq")
    first = (seq_index >= seq_count // 2).astype(jnp.int32)
    held = up_blocks.shape[2] // seq_count
    half, slot = low_width // 2, arrived.shape[2] // 4
    up_blocks[...] = jnp.zeros_like(up_blocks)
    for holder in range(seq_count):
        block = arrived[ring_index(seq_index - holder, seq_count)]
        start, stop = holder * held, (holder + 1) * held
        middle = min(max(query_columns, start), stop)
        for index in range(2):
            for part in range(2):
                offset = (2 * index + part) * slot
                if middle > start:
                    up_blocks[first + index, part * half : (part + 1) * half, start:middle] = block[
                        :, offset : offset + middle - start
                    ]
                if stop > middle:
                    low = low_width + part * half
                    up_blocks[first + index, low : low + half, middle:stop] = block[
                        :, offset + middle - start : offset + held
                    ]


def project_kernel(array_count, entries, up_entries, unused, seq_count, tokens, *refs):
    arrays = refs[:array_count]
    refs = refs[array_count + unused :]
    part, matrix = refs[:2]
    weights, semaphore = refs[-2:]
    copies = []
    for number, start, height, place in entries:
        piece = arrays[number].at[pl.ds(start, height)]
        copies.append(fetch(piece, weights, place, semaphore.at[len(copies)]))
    for number, start, slot in up_entries:
        copy = pltpu.make_async_copy(
            arrays[number].at[pl.ds(start, refs[3].shape[1])],
            refs[3].at[slot],
            semaphore.at[len(copies)],
        )
        copy.start()
        copies.append(copy)
    for copy in copies:
        copy.wait()
    keep = pltpu.make_async_copy(weights, matrix, semaphore.at[len(copies)])
    keep.start()
    part[...] = dot_nt(tokens[...], weights[...])
    if up_entries:
        assemble_up(seq_count, refs[3], refs[2])
    keep.wait()


def rotated(values, cosines, sines):
    return values * cosines + pltpu.roll(values, values.shape[1] // 2, 1) * sines


def qkv_kernel(seq_count, unused, lengths, mine, theirs, up_blocks, cosines, sines, *refs):
    queries, pairs, low_rank = refs[unused:]
    rows = mine.shape[0]
    own_rows = queries.shape[0] // QHEADS
    query_columns = QHEADS * HEAD_WIDTH
    value_start = query_columns + HEAD_WIDTH
    features = value_start + HEAD_WIDTH
    joint_rank = low_rank.shape[1]
    middle = features + joint_rank
    ends = kernel_marks(lengths)

    def low_rows(picked, second):
        first_low = mine[picked, features:middle] + theirs[picked, features:middle]
        second_low = mine[picked, middle:] + theirs[picked, middle:]
        return jnp.where(second, second_low, first_low).astype(jnp.bfloat16)

    first = (lax.axis_index("seq") >= seq_count // 2).astype(jnp.int32)
    first_row = lax.axis_index("seq") * rows
    segments = row_segments(ends, row_positions(first_row, rows))
    low = low_rows(slice(None), segments != first)
    low_rank[...] = low
    value_delta = jnp.zeros((rows, HEAD_WIDTH), jnp.float32)
    for document in range(SEGS):
        chosen = jnp.where(segments == document, low, jnp.zeros_like(low))
        value_delta += dot_nn(chosen, up_blocks[document, :, query_columns:])
    keys = mine[:, query_columns:value_start] + theirs[:, query_columns:value_start]
    pairs[:, :HEAD_WIDTH] = rotated(keys, cosines[...], sines[...]).astype(jnp.bfloat16)
    values = mine[:, value_start:features] + theirs[:, value_start:features]
    pairs[:, HEAD_WIDTH:] = (values + adapter_scale * value_delta).astype(jnp.bfloat16)
    start = pl.multiple_of(lax.axis_index("tp") * own_rows, own_rows)
    own = pl.ds(start, own_rows)
    own_segments = row_segments(ends, row_positions(first_row + start, own_rows))
    own_low = low_rows(own, own_segments != first)
    query_delta = jnp.zeros((own_rows, query_columns), jnp.float32)
    for document in range(SEGS):
        chosen = jnp.where(own_segments == document, own_low, jnp.zeros_like(own_low))
        query_delta += dot_nn(chosen, up_blocks[document, :, :query_columns])
    projected = mine[own, :query_columns] + theirs[own, :query_columns]
    projected = projected + adapter_scale * query_delta
    for head in range(QHEADS):
        turned = rotated(
            projected[:, head * HEAD_WIDTH : (head + 1) * HEAD_WIDTH], cosines[own], sines[own]
        )
        queries[head * own_rows : (head + 1) * own_rows] = turned.astype(jnp.bfloat16)


def attention_kernel(block_count, unused, lengths, queries, incoming, cosines, sines, *refs):
    blocks = refs[:block_count]
    output, query_grad, kept, sent, low_probs = refs[block_count + unused :]
    own_rows, query_columns = incoming.shape
    rows = blocks[0].shape[0]
    score_scale = HEAD_WIDTH ** (-0.5)
    ends = kernel_marks(lengths)
    seq_index, tp_index = lax.axis_index("seq"), lax.axis_index("tp")
    positions = row_positions(seq_index * rows + tp_index * own_rows, own_rows)
    positions = jnp.concatenate([positions] * QHEADS, axis=0)
    segments = row_segments(ends, positions)
    starts = jnp.where(segments == 0, 0, jnp.where(segments == 1, ends[0], ends[1]))
    scores = []
    for back, block in enumerate(blocks):
        key_positions = (seq_index - back) * rows + lax.broadcasted_iota(jnp.int32, (1, rows), 1)
        allowed = (key_positions <= positions) & (key_positions >= starts)
        block_scores = dot_nt(queries[...], block[:, :HEAD_WIDTH]) * score_scale
        scores.append(jnp.where(allowed, block_scores, masked_score))
    row_max = functools.reduce(
        jnp.maximum, [jnp.max(part, axis=1, keepdims=True) for part in scores]
    )
    raised = [jnp.exp(part - row_max) for part in scores]
    row_total = sum(jnp.sum(part, axis=1, keepdims=True) for part in raised)
    inverse = 1.0 / row_total
    probs = [part * inverse for part in raised]
    weighted = jnp.zeros((QHEADS * own_rows, HEAD_WIDTH), jnp.float32)
    for back, block in enumerate(blocks):
        low_probs[back] = probs[back].astype(jnp.bfloat16)
        weighted += dot_nn(low_probs[back], block[:, HEAD_WIDTH:])
    attended = weighted.astype(jnp.bfloat16)
    gradients = jnp.concatenate(
        [incoming[:, head * HEAD_WIDTH : (head + 1) * HEAD_WIDTH] for head in range(QHEADS)],
        axis=0,
    )
    row_delta = jnp.sum(
        gradients.astype(jnp.float32) * attended.astype(jnp.float32), axis=1, keepdims=True
    )
    start = pl.multiple_of(tp_index * own_rows, own_rows)
    total = jnp.zeros((QHEADS * own_rows, HEAD_WIDTH), jnp.float32)
    for back, block in enumerate(blocks):
        prob_grad = dot_nt(gradients, block[:, HEAD_WIDTH:])
        score_grad = (probs[back] * (prob_grad - row_delta)).astype(jnp.bfloat16)
        total += dot_nn(score_grad, block[:, :HEAD_WIDTH])
        key_part = dot_tn(score_grad, queries[...]) * score_scale
        value_part = dot_tn(low_probs[back], gradients)
        mine = tp_index == 0
        kept[back, :, :HEAD_WIDTH] = jnp.where(mine, key_part[:own_rows], key_part[own_rows:])
        sent[back, :, :HEAD_WIDTH] = jnp.where(mine, key_part[own_rows:], key_part[:own_rows])
        kept[back, :, HEAD_WIDTH:] = jnp.where(mine, value_part[:own_rows], value_part[own_rows:])
        sent[back, :, HEAD_WIDTH:] = jnp.where(mine, value_part[own_rows:], value_part[:own_rows])
    own = pl.ds(start, own_rows)
    for head in range(QHEADS):
        picked = slice(head * own_rows, (head + 1) * own_rows)
        columns = slice(head * HEAD_WIDTH, (head + 1) * HEAD_WIDTH)
        output[:, columns] = attended[picked]
        query_grad[:, columns] = rotated(
            total[picked] * score_scale, cosines[own], -sines[own]
        ).astype(jnp.bfloat16)


def sum_kernel(kept, arrived, *sums):
    for back, total in enumerate(sums):
        total[...] = kept[back] + arrived[back]


def pair_kernel(terms, cosines, sines, *refs):
    parts, pair = refs[:terms], refs[-2]
    own_rows = pair.shape[0]
    total = sum(part[...] for part in parts)
    own = pl.ds(pl.multiple_of(lax.axis_index("tp") * own_rows, own_rows), own_rows)
    keys = rotated(total[:, :HEAD_WIDTH], cosines[own], -sines[own])
    pair[:, :HEAD_WIDTH] = keys.astype(jnp.bfloat16)
    pair[:, HEAD_WIDTH:] = total[:, HEAD_WIDTH:].astype(jnp.bfloat16)


def rank_kernel(
    seq_count, lengths, own_query, other_query, own_pair, other_pair, low_rank, up_blocks, *refs
):
    gradients, rank_grad = refs[:2]
    split_terms, (terms, blocks) = refs[2:-2], refs[-2:]
    own_rows, query_columns = own_query.shape
    rows = low_rank.shape[0]
    seq_index = lax.axis_index("seq")
    start = pl.multiple_of(lax.axis_index("tp") * own_rows, own_rows)
    other = pl.multiple_of(own_rows - start, own_rows)
    gradients[pl.ds(start, own_rows), :query_columns] = own_query[...]
    gradients[pl.ds(other, own_rows), :query_columns] = other_query[...]
    value_start = query_columns + HEAD_WIDTH
    features = value_start + HEAD_WIDTH
    gradients[pl.ds(start, own_rows), query_columns:features] = own_pair[...]
    gradients[pl.ds(other, own_rows), query_columns:features] = other_pair[...]
    query_grad = gradients[:, :query_columns]
    value_grad = gradients[:, value_start:features]
    low = low_rank[...]
    rank = low.shape[1] // 2
    segments = row_segments(kernel_marks(lengths), row_positions(seq_index * rows, rows))
    total = jnp.zeros((rows, low.shape[1]), jnp.float32)
    for document in range(SEGS):
        member = segments == document
        parts = dot_nt(query_grad, up_blocks[document, :, :query_columns])
        parts += dot_nt(value_grad, up_blocks[document, :, query_columns:])
        total = jnp.where(member, parts, total)
        chosen = jnp.where(member, low, jnp.zeros_like(low))
        query_terms = dot_tn(chosen, query_grad)
        value_terms = dot_tn(chosen, value_grad)
        place = slice(document * rank, (document + 1) * rank)
        terms[place, :query_columns] = adapter_scale * query_terms[:rank]
        terms[place, query_columns:] = adapter_scale * value_terms[rank:]
    turned = (adapter_scale * total).astype(jnp.bfloat16)
    rank_grad[...] = turned
    second = segments != (seq_index >= seq_count // 2).astype(jnp.int32)
    nothing = jnp.zeros_like(turned)
    middle = features + low.shape[1]
    gradients[:, features:middle] = jnp.where(second, nothing, turned)
    gradients[:, middle:] = jnp.where(second, turned, nothing)
    held = blocks.shape[2]
    for holder in range(seq_count):
        blocks[holder] = terms[:, holder * held : (holder + 1) * held]
    for steps, block in enumerate(split_terms):
        mine = blocks[ring_index(seq_index + steps - seq_count, seq_count)]
        if block.shape == mine.shape:
            block[...] = mine
            continue
        tail = held - 128
        count = 128 // tail
        height = mine.shape[0] // count
        first_low = mine.shape[0] + height
        block[: mine.shape[0]] = mine[:, :128]
        for part in range(count):
            block[mine.shape[0] : first_low, part * tail : (part + 1) * tail] = mine[
                part * height : (part + 1) * height, 128:
            ]
        block[first_low:, : low.shape[1]] = turned[: rows // 2].astype(jnp.float32)
        block[first_low:, low.shape[1] :] = turned[rows // 2 :].astype(jnp.float32)


def token_kernel(gradients, matrix, token_grad):
    token_grad[...] = dot_nn(gradients[...], matrix[...]).astype(jnp.bfloat16)


def down_kernel(block_count, lengths, *refs):
    columns = refs[:block_count]
    up_parts = refs[block_count : 2 * block_count]
    packed = up_parts[0].shape != up_parts[1].shape
    rank_count = 1 if packed else block_count
    ranks = refs[2 * block_count : 2 * block_count + rank_count]
    outputs = refs[2 * block_count + rank_count :]
    rows, joint_rank = ranks[0].shape
    ends = kernel_marks(lengths)
    up_rows, up_width = up_parts[0].shape
    lows, ups = [ranks[0][...]], [up_parts[0][...]]
    for behind in range(1, block_count):
        if not packed:
            lows.append(ranks[behind][...])
            ups.append(up_parts[behind][...])
            continue
        part = up_parts[behind]
        count = 128 // (up_width - 128)
        first_low = up_rows + up_rows // count
        halves = [part[first_low:, :joint_rank], part[first_low:, joint_rank:]]
        lows.append(jnp.concatenate(halves, axis=0).astype(jnp.bfloat16))
    all_terms = []
    for document in range(SEGS):
        total = jnp.zeros((joint_rank, columns[0].shape[1]), jnp.float32)
        for behind in range(block_count):
            holder = ring_index(lax.axis_index("seq") - behind, block_count)
            segments = row_segments(ends, row_positions(holder * rows, rows))
            chosen = jnp.where(segments == document, lows[behind], jnp.zeros_like(lows[behind]))
            total += dot_tn(chosen, columns[behind][...])
        all_terms.append(total)
    down_terms = jnp.concatenate(all_terms, axis=0)
    if not packed:
        outputs[0][...] = down_terms
        outputs[1][...] = sum(ups)
        return
    own_down, far, own_up, up_terms = outputs
    tail = up_width - 128
    height = up_rows // (128 // tail)
    up_terms[...] = ups[0]
    for part in up_parts[1:]:
        up_terms[:, :128] += part[:up_rows]
        for piece in range(128 // tail):
            up_terms[piece * height : (piece + 1) * height, 128:] += part[
                up_rows : up_rows + height, piece * tail : (piece + 1) * tail
            ]
    held, held_up = own_down.shape[1], own_up.shape[1]
    ahead = lax.axis_index("batch") == 0
    own_down[...] = jnp.where(ahead, down_terms[:, :held], down_terms[:, held:])
    far[:, :held] = jnp.where(ahead, down_terms[:, held:], down_terms[:, :held])
    left, right = up_terms[:, :held_up], up_terms[:, held_up:]
    own_up[...] = jnp.where(ahead, left, right)
    far_up = jnp.where(ahead, right, left)
    spare = far.shape[1] - held
    far[:up_rows, held:] = far_up[:, :spare]
    far[up_rows:, held : held + held_up - spare] = far_up[:, spare:]


def packed_bank_kernel(bank_rows, own_down, far, own_up, down_zeros, up_zeros, down_out, up_out):
    step = pl.program_id(0)
    joint_rank, held = down_out.shape[1], down_out.shape[3]
    low_width, held_up = up_out.shape[1:]
    up_rows = own_up.shape[0]
    spare = far.shape[1] - held
    down_total = jnp.zeros((joint_rank, held), jnp.float32)
    head = jnp.zeros((low_width, spare), jnp.float32)
    rest = jnp.zeros((low_width, held_up - spare), jnp.float32)
    for document in range(SEGS):
        rows = slice(document * joint_rank, (document + 1) * joint_rank)
        lows = slice(document * low_width, (document + 1) * low_width)
        same = bank_rows[document] == bank_rows[step]
        down_total += jnp.where(same, own_down[rows], 0.0)
        head += jnp.where(same, own_up[lows, :spare], 0.0)
        rest += jnp.where(same, own_up[lows, spare:], 0.0)
        same = bank_rows[SEGS + document] == bank_rows[step]
        down_total += jnp.where(same, far[rows, :held], 0.0)
        head += jnp.where(same, far[lows, held:], 0.0)
        lows = slice(up_rows + document * low_width, up_rows + (document + 1) * low_width)
        rest += jnp.where(same, far[lows, held : held + held_up - spare], 0.0)
    down_out[0, :, 0, :] = down_total
    up_out[0, :, :spare] = head
    up_out[0, :, spare:] = rest


def bank_kernel(block_count, bank_rows, *refs):
    down_terms = refs[:block_count]
    up_terms = refs[block_count : 2 * block_count]
    down_out, up_out = refs[2 * block_count + 2 :]
    step = pl.program_id(0)
    row = bank_rows[step]
    joint_rank = down_out.shape[1]
    low_width = up_out.shape[1]
    down_total = jnp.zeros((joint_rank, down_out.shape[3]), jnp.float32)
    up_total = jnp.zeros((low_width, up_out.shape[2]), jnp.float32)
    for block in range(block_count):
        for document in range(SEGS):
            same = bank_rows[block * SEGS + document] == row
            down_rows = down_terms[block][document * joint_rank : (document + 1) * joint_rank]
            up_rows = up_terms[block][document * low_width : (document + 1) * low_width]
            down_total += jnp.where(same, down_rows, 0.0)
            up_total += jnp.where(same, up_rows, 0.0)
    down_out[0, :, 0, :] = down_total
    up_out[0] = up_total


def shards(
    tokens,
    frozen_qkv_matrix,
    adapter_down_weight,
    adapter_up_weight,
    adapter_bank_row,
    document_lengths,
    document_adapter,
    output_gradient,
):
    seq_count = lax.axis_size("seq")
    batch_count = lax.axis_size("batch")
    group_count = lax.axis_size("groups")
    chip_size = lax.axis_size("tp")
    seq_index = lax.axis_index("seq")
    batch_index = lax.axis_index("batch")
    group_index = lax.axis_index("groups")
    tp_index = lax.axis_index("tp")
    local_tokens = tokens[0]
    rows, width = local_tokens.shape
    own_rows = rows // chip_size
    query_columns = QHEADS * HEAD_WIDTH
    frozen_rows = frozen_qkv_matrix.shape[0]
    features = frozen_rows * seq_count
    low_width = ADAPTER_RANK
    joint_rank = adapter_down_weight.shape[1]
    adapters = adapter_bank_row.shape[0]
    bf16 = jnp.bfloat16
    f32 = jnp.float32

    lengths = lax.dynamic_index_in_dim(document_lengths, batch_index, 0, keepdims=False)
    first_end = lengths[0]
    second_end = first_end + lengths[1]
    half_count = seq_count // 2
    held_down = adapter_down_weight.shape[3]
    held_up = adapter_up_weight.shape[2]
    down_width = held_down * batch_count
    up_width = held_up * batch_count

    positions = seq_index * rows + jnp.arange(rows, dtype=jnp.int32)
    inside = positions - jnp.where(
        positions >= second_end, second_end, jnp.where(positions >= first_end, first_end, 0)
    )
    exponent = jnp.arange(HEAD_WIDTH // 2, dtype=f32) * (2.0 / HEAD_WIDTH)
    inverse = jnp.power(jnp.float32(rope_base), -exponent)
    angles = inside.astype(f32)[:, None] * jnp.concatenate([inverse, inverse])[None, :]
    signs = jnp.where(jnp.arange(HEAD_WIDTH) < HEAD_WIDTH // 2, -1.0, 1.0).astype(f32)
    cosines = jnp.cos(angles)
    sines = jnp.sin(angles) * signs[None, :]

    sample_rows = lookup_rows(adapter_bank_row, document_adapter)
    bank_rows = sample_rows.reshape(-1)
    if batch_count == 2:
        own_bank = jnp.where(batch_index == 0, sample_rows[0], sample_rows[1])
        far_bank = jnp.where(batch_index == 0, sample_rows[1], sample_rows[0])
        bank_rows = jnp.concatenate([own_bank, far_bank])
    down_bank = adapter_down_weight[:, :, 0, :]
    down_zeros = jnp.zeros((adapters, joint_rank, 1, held_down), f32)
    up_zeros = jnp.zeros((adapters, low_width, held_up), f32)

    plane_count = group_count * batch_count
    share = width // plane_count
    padded_down = (held_down + 127) // 128 * 128
    direct = (
        group_count == 2
        and seq_count == 4
        and share == down_width
        and batch_count == 2
        and share % 128 == 0
        and down_width % 128 == 0
        and frozen_rows % 16 == 0
        and 4 * up_width <= down_width
        and up_width > 128
        and 128 % (up_width - 128) == 0
        and 0 < held_up + held_down - padded_down <= padded_down - held_down
    )
    up_entries = []
    if direct:
        own_share = lax.dynamic_slice_in_dim(
            frozen_qkv_matrix, (group_index * batch_count + batch_index) * share, share, axis=1
        )
        before = shift(own_share, "seq", 1)
        after = shift(own_share, "seq", 3)
        far_down = shift(down_bank[far_bank], "batch", 1)
        far_up = shift(adapter_up_weight[far_bank], "batch", 1)
        own_down, own_up = down_bank[own_bank], adapter_up_weight[own_bank]
        payload_rows = 2 * joint_rank + low_width // 2
        pack_shapes = [(2 * frozen_rows, share), (frozen_rows + payload_rows, share)]
        pack_shapes += [(payload_rows, share)] * 3
        plane, forward, payload, *payloads = pl.pallas_call(
            pack_kernel,
            out_shape=[jax.ShapeDtypeStruct(shape, bf16) for shape in pack_shapes],
            in_specs=[in_vmem()] * 6,
            out_specs=[by_block(shape) for shape in pack_shapes],
            scratch_shapes=[
                pltpu.VMEM((SEGS * joint_rank, down_width), bf16),
                pltpu.VMEM((SEGS, low_width, 2 * held_up), bf16),
            ],
            compiler_params=pltpu.CompilerParams(vmem_limit_bytes=16 * mebibyte),
            cost_estimate=cost(0, 8 * frozen_rows * share),
            name="pack",
        )(own_down, far_down, own_up, far_up, before, after)

        def over_plane(value):
            over_both = [(at, plane_count - 1 - at) for at in range(plane_count)]
            return [
                shift(value, "batch", 1),
                shift(value, "groups", 1),
                lax.ppermute(value, ("groups", "batch"), over_both),
            ]

        plane_parts = over_plane(plane)
        forward = shift(forward, "seq", 1)
        middle = forward[:frozen_rows]
        middle_parts = over_plane(middle)
        payloads = [shift(part, "seq", steps + 2) for steps, part in enumerate(payloads)]
        arrays = [frozen_qkv_matrix, before, after, forward, payload] + payloads
        arrays += plane_parts + middle_parts

        def frozen_at(behind, batch_step, group_step):
            return frozen_place(seq_count, frozen_rows, share, behind, batch_step, group_step)

        def down_at(behind):
            return down_place(seq_count, features, down_width, behind)

        entries = [
            (0, 0, frozen_rows, frozen_place(seq_count, frozen_rows, None, 0, 0, 0)),
            (1, 0, frozen_rows, frozen_at(1, 0, 0)),
            (2, 0, frozen_rows, frozen_at(3, 0, 0)),
            (3, 0, frozen_rows, frozen_at(2, 0, 0)),
            (4, 0, 2 * joint_rank, down_at(0)),
            (3, frozen_rows, 2 * joint_rank, down_at(1)),
            (5, 0, 2 * joint_rank, down_at(2)),
            (6, 0, 2 * joint_rank, down_at(3)),
        ]
        up_entries = [(4, 2 * joint_rank, 0), (3, frozen_rows + 2 * joint_rank, 1)]
        up_entries += [(5, 2 * joint_rank, 2), (6, 2 * joint_rank, 3)]
        for number, (batch_step, group_step) in enumerate(((1, 0), (0, 1), (1, 1))):
            entries += [
                (7 + number, 0, frozen_rows, frozen_at(1, batch_step, group_step)),
                (7 + number, frozen_rows, frozen_rows, frozen_at(3, batch_step, group_step)),
                (10 + number, 0, frozen_rows, frozen_at(2, batch_step, group_step)),
            ]
        early = [forward, down_zeros, up_zeros, cosines, sines, bank_rows]
        column_blocks = pl.pallas_call(
            functools.partial(cut_kernel, len(early), seq_count),
            out_shape=[jax.ShapeDtypeStruct((rows, down_width), bf16)] * seq_count,
            in_specs=[in_vmem()] + [in_place()] * len(early),
            out_specs=[by_block((rows, down_width))] * seq_count,
            compiler_params=pltpu.CompilerParams(vmem_limit_bytes=16 * mebibyte),
            cost_estimate=cost(0, 4 * rows * width),
            name="cut",
        )(local_tokens, *early)
    else:
        bank_rows = sample_rows.reshape(-1)
        got_down = lax.all_to_all(
            down_bank[sample_rows], "batch", split_axis=0, concat_axis=0, tiled=True
        )
        got_up = lax.all_to_all(
            adapter_up_weight[sample_rows], "batch", split_axis=0, concat_axis=0, tiled=True
        )
        down_block = jnp.transpose(got_down, (1, 2, 0, 3)).reshape(SEGS * joint_rank, -1)
        up_block = jnp.transpose(got_up, (1, 2, 0, 3)).reshape(SEGS * low_width, -1)
        all_down = lax.all_gather(down_block, "seq", axis=0)
        all_up = lax.all_gather(up_block, "seq", axis=0)
        first = (seq_index >= half_count).astype(jnp.int32)
        merged = jnp.transpose(all_down, (1, 0, 2)).reshape(SEGS * joint_rank, -1)
        arrays = [
            lax.all_gather(frozen_qkv_matrix, "seq", axis=0, tiled=True),
            lax.dynamic_slice_in_dim(merged, first * joint_rank, 2 * joint_rank),
        ]
        entries = [
            (0, 0, features, whole_place(0)),
            (1, 0, 2 * joint_rank, whole_place(features)),
        ]
        up_rows = jnp.transpose(all_up, (1, 0, 2)).reshape(SEGS, low_width, -1)
        is_query = jnp.arange(up_rows.shape[2]) < query_columns
        up_blocks = jnp.concatenate(
            [
                jnp.where(is_query[None, None, :], up_rows, 0),
                jnp.where(is_query[None, None, :], 0, up_rows),
            ],
            axis=1,
        )
        column_blocks = [
            lax.dynamic_slice_in_dim(
                local_tokens,
                jnp.remainder(seq_index + steps, seq_count) * down_width,
                down_width,
                axis=1,
            )
            for steps in range(seq_count)
        ]

    column_parts = [
        shift(block, "seq", steps) if steps else block
        for steps, block in enumerate(column_blocks)
    ]
    early = [column_parts[2]] if direct and seq_count > 3 else []
    up_shape = (SEGS, joint_rank, query_columns + HEAD_WIDTH)
    matrix_rows = features + 2 * joint_rank
    arrived = [pltpu.VMEM((seq_count, low_width // 2, down_width), bf16)] if direct else []
    part, matrix, *built = pl.pallas_call(
        functools.partial(
            project_kernel, len(arrays), entries, up_entries, len(early), seq_count
        ),
        out_shape=[
            jax.ShapeDtypeStruct((rows, matrix_rows), f32),
            jax.ShapeDtypeStruct((matrix_rows, width), bf16),
        ]
        + ([jax.ShapeDtypeStruct(up_shape, bf16)] if direct else []),
        in_specs=[in_vmem()] + [in_place()] * (len(arrays) + len(early)),
        out_specs=[in_vmem(), in_place()] + ([by_block(up_shape)] if direct else []),
        scratch_shapes=arrived
        + [
            pltpu.VMEM((matrix_rows, width), bf16),
            pltpu.SemaphoreType.DMA((len(entries) + len(up_entries) + 1,)),
        ],
        compiler_params=pltpu.CompilerParams(vmem_limit_bytes=20 * mebibyte),
        cost_estimate=cost(2 * rows * width * matrix_rows, 2 * width * (matrix_rows + rows)),
        name="project",
    )(local_tokens, *arrays, *early)
    if direct:
        up_blocks = built[0]

    other_part = shift(part, "tp", 1)
    queries, pairs, low_rank = pl.pallas_call(
        functools.partial(qkv_kernel, seq_count, 0),
        out_shape=(
            jax.ShapeDtypeStruct((QHEADS * own_rows, HEAD_WIDTH), bf16),
            jax.ShapeDtypeStruct((rows, 2 * HEAD_WIDTH), bf16),
            jax.ShapeDtypeStruct((rows, joint_rank), bf16),
        ),
        in_specs=[in_smem()] + [in_vmem()] * 5,
        out_specs=(in_vmem(),) * 3,
        compiler_params=pltpu.CompilerParams(vmem_limit_bytes=8 * mebibyte),
        cost_estimate=cost(2 * rows * 3 * 64 * 640, 8 * rows * features),
        name="qkv",
    )(document_lengths, part, other_part, up_blocks, cosines, sines)

    blocks = [pairs] + [push(pairs, "seq", back) for back in range(1, half_count + 1)]
    block_count = len(blocks)
    column_parts[1] = shift(pass_after(column_blocks[1], *blocks[1:]), "seq", 1)
    incoming = output_gradient[0]
    early_columns = []
    attention, query_grad, kept, sent = pl.pallas_call(
        functools.partial(attention_kernel, block_count, len(early_columns)),
        out_shape=(
            jax.ShapeDtypeStruct((own_rows, query_columns), bf16),
            jax.ShapeDtypeStruct((own_rows, query_columns), bf16),
            jax.ShapeDtypeStruct((block_count, own_rows, 2 * HEAD_WIDTH), f32),
            jax.ShapeDtypeStruct((block_count, own_rows, 2 * HEAD_WIDTH), f32),
        ),
        in_specs=[in_smem()]
        + [in_vmem()] * (4 + block_count)
        + [in_place()] * len(early_columns),
        out_specs=(in_vmem(),) * 4,
        scratch_shapes=[pltpu.VMEM((block_count, QHEADS * own_rows, rows), bf16)],
        compiler_params=pltpu.CompilerParams(vmem_limit_bytes=(8 + 4 * block_count) * mebibyte),
        cost_estimate=cost(
            10 * block_count * QHEADS * own_rows * rows * HEAD_WIDTH,
            4 * rows * features,
            block_count * QHEADS * own_rows * rows,
        ),
        name="attention",
    )(document_lengths, queries, incoming, cosines, sines, *blocks, *early_columns)

    other_query = shift(query_grad, "tp", 1)
    pair_sums = pl.pallas_call(
        sum_kernel,
        out_shape=[jax.ShapeDtypeStruct((own_rows, 2 * HEAD_WIDTH), f32)] * block_count,
        in_specs=[in_vmem()] * 2,
        out_specs=[in_vmem()] * block_count,
        compiler_params=pltpu.CompilerParams(vmem_limit_bytes=8 * mebibyte),
        cost_estimate=cost(0, 12 * block_count * own_rows * 2 * HEAD_WIDTH),
        name="pair_sums",
    )(kept, shift(sent, "tp", 1))
    pair_terms = [pair_sums[0]]
    pair_terms += [push(pair_sums[back], "seq", -back) for back in range(1, block_count)]
    pair_grad, late_block = pl.pallas_call(
        functools.partial(pair_kernel, block_count),
        out_shape=[
            jax.ShapeDtypeStruct((own_rows, 2 * HEAD_WIDTH), bf16),
            jax.ShapeDtypeStruct((rows, down_width), bf16),
        ],
        in_specs=[in_vmem()] * (2 + block_count) + [in_place()] * 2,
        out_specs=[in_vmem(), in_place()],
        input_output_aliases={2 + block_count: 1},
        compiler_params=pltpu.CompilerParams(vmem_limit_bytes=8 * mebibyte),
        cost_estimate=cost(0, 12 * block_count * own_rows * 2 * HEAD_WIDTH),
        name="pair_gradients",
    )(cosines, sines, *pair_terms, column_blocks[-1], column_parts[1])
    column_parts[-1] = shift(late_block, "seq", seq_count - 1)
    other_pair = shift(pair_grad, "tp", 1)

    split_shapes = [(SEGS * low_width, up_width)] * seq_count
    if direct:
        sent_rows = SEGS * low_width * up_width // 128 + rows // 2
        split_shapes[1:] = [(sent_rows, 128)] * (seq_count - 1)
    gradients, rank_grad, *up_split = pl.pallas_call(
        functools.partial(rank_kernel, seq_count),
        out_shape=[
            jax.ShapeDtypeStruct((rows, matrix_rows), bf16),
            jax.ShapeDtypeStruct((rows, joint_rank), bf16),
        ]
        + [jax.ShapeDtypeStruct(shape, f32) for shape in split_shapes],
        in_specs=[in_smem()] + [in_vmem()] * 6,
        out_specs=[by_block((rows, matrix_rows)), in_vmem()]
        + [by_block(shape) for shape in split_shapes],
        scratch_shapes=[
            pltpu.VMEM((SEGS * low_width, features - HEAD_WIDTH), f32),
            pltpu.VMEM((seq_count, SEGS * low_width, held_up * batch_count), f32),
        ],
        compiler_params=pltpu.CompilerParams(vmem_limit_bytes=8 * mebibyte),
        cost_estimate=cost(4 * rows * 3 * 64 * 640, 4 * rows * features),
        name="rank_gradients",
    )(
        document_lengths, query_grad, other_query, pair_grad, other_pair, low_rank, up_blocks
    )

    rank_parts = [rank_grad]
    if not direct:
        rank_parts += [shift(rank_grad, "seq", steps) for steps in range(1, seq_count)]
    up_sums = [
        shift(block, "seq", steps) if steps else block for steps, block in enumerate(up_split)
    ]

    chunk = 512
    token_grad = pl.pallas_call(
        token_kernel,
        grid=(width // chunk,),
        out_shape=jax.ShapeDtypeStruct((rows, width), bf16),
        in_specs=[
            pl.BlockSpec((rows, matrix_rows), lambda step: (0, 0)),
            pl.BlockSpec((matrix_rows, chunk), lambda step: (0, step)),
        ],
        out_specs=pl.BlockSpec((rows, chunk), lambda step: (0, step)),
        compiler_params=pltpu.CompilerParams(vmem_limit_bytes=12 * mebibyte),
        cost_estimate=cost(2 * rows * width * matrix_rows, 2 * width * (matrix_rows + rows)),
        name="token_gradient",
    )(gradients, matrix)

    if direct:
        term_shapes = [(SEGS * joint_rank, held_down), (SEGS * joint_rank, padded_down)]
        term_shapes += [(SEGS * low_width, held_up)]
    else:
        term_shapes = [(SEGS * joint_rank, down_width), (SEGS * low_width, up_width)]
    terms = pl.pallas_call(
        functools.partial(down_kernel, seq_count),
        out_shape=[jax.ShapeDtypeStruct(shape, f32) for shape in term_shapes],
        in_specs=[in_smem()] + [in_vmem()] * (2 * seq_count + len(rank_parts)),
        out_specs=[in_vmem()] * len(term_shapes),
        scratch_shapes=[pltpu.VMEM((SEGS * low_width, up_width), f32)] if direct else [],
        compiler_params=pltpu.CompilerParams(vmem_limit_bytes=8 * mebibyte),
        cost_estimate=cost(
            2 * seq_count * rows * SEGS * joint_rank * down_width, 2 * seq_count * rows * down_width
        ),
        name="down_terms",
    )(document_lengths, *column_parts, *up_sums, *rank_parts)

    if direct:
        bank_terms = [terms[0], shift(terms[1], "batch", 1), terms[2]]
    else:
        down_send = jnp.transpose(
            terms[0].reshape(SEGS * joint_rank, batch_count, held_down), (1, 0, 2)
        )
        up_send = jnp.transpose(
            terms[1].reshape(SEGS * low_width, batch_count, held_up), (1, 0, 2)
        )
        back_down = lax.all_to_all(down_send, "batch", split_axis=0, concat_axis=0, tiled=True)
        back_up = lax.all_to_all(up_send, "batch", split_axis=0, concat_axis=0, tiled=True)
        bank_downs = [back_down[batch] for batch in range(batch_count)]
        bank_ups = [back_up[batch] for batch in range(batch_count)]
        bank_terms = bank_downs + bank_ups


    def whole(array):
        return pl.BlockSpec(array.shape, lambda step, bank: (0,) * array.ndim)

    term_count = len(bank_terms)
    down_grad, up_grad = pl.pallas_call(
        packed_bank_kernel if direct else functools.partial(bank_kernel, batch_count),
        out_shape=(
            jax.ShapeDtypeStruct(down_zeros.shape, f32),
            jax.ShapeDtypeStruct(up_zeros.shape, f32),
        ),
        grid_spec=pltpu.PrefetchScalarGridSpec(
            num_scalar_prefetch=1,
            grid=(batch_count * SEGS,),
            in_specs=[whole(array) for array in bank_terms] + [in_place()] * 2,
            out_specs=(
                pl.BlockSpec(
                    (1, joint_rank, 1, held_down),
                    lambda step, bank: (bank[step], 0, 0, 0),
                ),
                pl.BlockSpec(
                    (1, low_width, held_up),
                    lambda step, bank: (bank[step], 0, 0),
                ),
            ),
        ),
        input_output_aliases={1 + term_count: 0, 2 + term_count: 1},
        compiler_params=pltpu.CompilerParams(vmem_limit_bytes=16 * mebibyte),
        name="bank_rows",
    )(
        bank_rows,
        *bank_terms,
        down_zeros,
        up_zeros,
    )
    return (attention[None], token_grad[None], down_grad, up_grad)


def solution(mesh):
    in_specs = (
        P(("groups", "batch"), "seq", "tp"),
        P("seq", "tp"),
        P(None, None, "tp", ("seq", "batch")),
        P(None, None, ("seq", "batch")),
        P(),
        P("groups", None),
        P("groups", None),
        P(("groups", "batch"), ("seq", "tp"), None),
    )
    out_specs = (
        P(("groups", "batch"), ("seq", "tp"), None),
        P(("groups", "batch"), "seq", "tp"),
        P("groups", None, "tp", ("seq", "batch")),
        P("groups", None, ("seq", "batch")),
    )
    return jax.shard_map(shards, mesh=mesh, in_specs=in_specs, out_specs=out_specs, check_vma=False)
```

```python
import functools

import jax
import jax.numpy as jnp
from jax import lax
from jax.experimental import pallas as pl
from jax.experimental.pallas import tpu as pltpu
from jax.sharding import PartitionSpec as P

QHEADS = 4
HEAD_WIDTH = 128
ADAPTER_RANK = 32
SEGS = 3

adapter_scale = 2.0
rope_base = 5000000.0
masked_score = -1e30
mebibyte = 1024 * 1024


def shift(value, axis, steps):
    count = lax.axis_size(axis)
    return lax.ppermute(value, axis, [(at, (at + steps) % count) for at in range(count)])


def push(value, axis, steps):
    count = lax.axis_size(axis)
    pairs = [(at, at + steps) for at in range(count) if 0 <= at + steps < count]
    return lax.ppermute(value, axis, pairs)


def dot_nt(left, right):
    return lax.dot_general(
        left, right, (((1,), (1,)), ((), ())), preferred_element_type=jnp.float32
    )


def dot_nn(left, right):
    return jnp.dot(left, right, preferred_element_type=jnp.float32)


def dot_tn(left, right):
    return lax.dot_general(
        left, right, (((0,), (0,)), ((), ())), preferred_element_type=jnp.float32
    )


def lookup_rows(adapter_bank_row, document_adapter):
    matches = document_adapter[..., None] == jnp.arange(adapter_bank_row.shape[0], dtype=jnp.int32)
    return jnp.sum(jnp.where(matches, adapter_bank_row, 0), axis=-1)


def row_positions(first, count):
    return first + lax.broadcasted_iota(jnp.int32, (count, 1), 0)


def ring_index(index, count):
    return lax.rem(index + count, count)


def kernel_marks(lengths):
    batch = lax.axis_index("batch")
    first_end = lengths[batch, 0]
    return first_end, first_end + lengths[batch, 1]


def row_segments(ends, positions):
    return (positions >= ends[0]).astype(jnp.int32) + (positions >= ends[1]).astype(jnp.int32)


def cost(flops, bytes_accessed, transcendentals=0):
    return pl.CostEstimate(
        flops=flops, bytes_accessed=bytes_accessed, transcendentals=transcendentals
    )


def in_vmem():
    return pl.BlockSpec(memory_space=pltpu.VMEM)


def in_smem():
    return pl.BlockSpec(memory_space=pltpu.SMEM)


def by_block(shape):
    return pl.BlockSpec(shape, lambda: (0,) * len(shape))


def in_place():
    return pl.BlockSpec(memory_space=pl.ANY)


def fetch(piece, target, place, semaphore):
    height, width = piece.shape
    row, column = place()
    copy = pltpu.make_async_copy(
        piece,
        target.at[
            pl.ds(pl.multiple_of(row, 16), height), pl.ds(pl.multiple_of(column, 128), width)
        ],
        semaphore,
    )
    copy.start()
    return copy


def frozen_place(seq_count, rows, share, behind, batch_step, group_step):
    def place():
        holder = ring_index(lax.axis_index("seq") - behind, seq_count)
        if share is None:
            return holder * rows, 0
        batch = lax.rem(lax.axis_index("batch") + batch_step, 2)
        group = lax.rem(lax.axis_index("groups") + group_step, 2)
        return holder * rows, (group * 2 + batch) * share

    return place


def down_place(seq_count, features, width, behind):
    def place():
        return features, ring_index(lax.axis_index("seq") - behind, seq_count) * width

    return place


def whole_place(row):
    def place():
        return row, 0

    return place


def pack_kernel(own_down, far_down, own_up, far_up, before, after, *refs):
    plane, forward, payloads, (down, up) = refs[0], refs[1], refs[2:-2], refs[-2:]
    ahead = lax.axis_index("batch") == 0
    joint_rank, held = own_down.shape[1:]
    low_width, held_up = own_up.shape[1:]
    frozen_rows = before.shape[0]
    plane[:frozen_rows] = before[...]
    plane[frozen_rows:] = after[...]
    forward[:frozen_rows] = before[...]
    for document in range(SEGS):
        rows = slice(document * joint_rank, (document + 1) * joint_rank)
        down[rows, :held] = jnp.where(ahead, own_down[document], far_down[document])
        down[rows, held:] = jnp.where(ahead, far_down[document], own_down[document])
        up[document, :, :held_up] = jnp.where(ahead, own_up[document], far_up[document])
        up[document, :, held_up:] = jnp.where(ahead, far_up[document], own_up[document])
    half, slot = low_width // 2, down.shape[1] // 4
    targets = [(0, payloads[0], 0), (1, forward, frozen_rows)]
    targets += [(steps + 2, payload, 0) for steps, payload in enumerate(payloads[1:])]
    seq_count = len(targets)
    for steps, payload, base in targets:
        target = ring_index(lax.axis_index("seq") + steps - seq_count, seq_count)
        first = (target >= seq_count // 2).astype(jnp.int32)
        start = pl.multiple_of(first * joint_rank, joint_rank)
        payload[base : base + 2 * joint_rank] = down[pl.ds(start, 2 * joint_rank)]
        base = base + 2 * joint_rank
        for index in range(2):
            block = up[first + index]
            for part in range(2):
                column = (2 * index + part) * slot
                payload[base : base + half, column : column + 2 * held_up] = block[
                    part * half : (part + 1) * half
                ]


def pass_kernel(*refs):
    del refs


def pass_after(value, *earlier):
    return pl.pallas_call(
        pass_kernel,
        out_shape=jax.ShapeDtypeStruct(value.shape, value.dtype),
        in_specs=[in_place()] + [in_vmem()] * len(earlier),
        out_specs=in_place(),
        input_output_aliases={0: 0},
        compiler_params=pltpu.CompilerParams(vmem_limit_bytes=2 * mebibyte),
        name="pass_after",
    )(value, *earlier)


def cut_kernel(unused, seq_count, tokens, *refs):
    for steps, block in enumerate(refs[unused:]):
        target = ring_index(lax.axis_index("seq") + steps - seq_count, seq_count)
        width = block.shape[1]
        block[...] = tokens[:, pl.ds(pl.multiple_of(target * width, 128), width)]


def assemble_up(seq_count, arrived, up_blocks):
    low_width = up_blocks.shape[1] // 2
    query_columns = QHEADS * HEAD_WIDTH
    seq_index = lax.axis_index("seq")
    first = (seq_index >= seq_count // 2).astype(jnp.int32)
    held = up_blocks.shape[2] // seq_count
    half, slot = low_width // 2, arrived.shape[2] // 4
    up_blocks[...] = jnp.zeros_like(up_blocks)
    for holder in range(seq_count):
        block = arrived[ring_index(seq_index - holder, seq_count)]
        start, stop = holder * held, (holder + 1) * held
        middle = min(max(query_columns, start), stop)
        for index in range(2):
            for part in range(2):
                offset = (2 * index + part) * slot
                if middle > start:
                    up_blocks[first + index, part * half : (part + 1) * half, start:middle] = block[
                        :, offset : offset + middle - start
                    ]
                if stop > middle:
                    low = low_width + part * half
                    up_blocks[first + index, low : low + half, middle:stop] = block[
                        :, offset + middle - start : offset + held
                    ]


def project_kernel(array_count, entries, up_entries, unused, seq_count, tokens, *refs):
    arrays = refs[:array_count]
    refs = refs[array_count + unused :]
    part, matrix = refs[:2]
    weights, semaphore = refs[-2:]
    copies = []
    for number, start, height, place in entries:
        piece = arrays[number].at[pl.ds(start, height)]
        copies.append(fetch(piece, weights, place, semaphore.at[len(copies)]))
    for number, start, slot in up_entries:
        copy = pltpu.make_async_copy(
            arrays[number].at[pl.ds(start, refs[3].shape[1])],
            refs[3].at[slot],
            semaphore.at[len(copies)],
        )
        copy.start()
        copies.append(copy)
    for copy in copies:
        copy.wait()
    keep = pltpu.make_async_copy(weights, matrix, semaphore.at[len(copies)])
    keep.start()
    part[...] = dot_nt(tokens[...], weights[...])
    if up_entries:
        assemble_up(seq_count, refs[3], refs[2])
    keep.wait()


def rotated(values, cosines, sines):
    return values * cosines + pltpu.roll(values, values.shape[1] // 2, 1) * sines


def qkv_kernel(seq_count, unused, lengths, mine, theirs, up_blocks, cosines, sines, *refs):
    queries, pairs, low_rank = refs[unused:]
    rows = mine.shape[0]
    own_rows = queries.shape[0] // QHEADS
    query_columns = QHEADS * HEAD_WIDTH
    value_start = query_columns + HEAD_WIDTH
    features = value_start + HEAD_WIDTH
    joint_rank = low_rank.shape[1]
    middle = features + joint_rank
    ends = kernel_marks(lengths)

    def low_rows(picked, second):
        first_low = mine[picked, features:middle] + theirs[picked, features:middle]
        second_low = mine[picked, middle:] + theirs[picked, middle:]
        return jnp.where(second, second_low, first_low).astype(jnp.bfloat16)

    first = (lax.axis_index("seq") >= seq_count // 2).astype(jnp.int32)
    first_row = lax.axis_index("seq") * rows
    segments = row_segments(ends, row_positions(first_row, rows))
    low = low_rows(slice(None), segments != first)
    low_rank[...] = low
    value_delta = jnp.zeros((rows, HEAD_WIDTH), jnp.float32)
    for document in range(SEGS):
        chosen = jnp.where(segments == document, low, jnp.zeros_like(low))
        value_delta += dot_nn(chosen, up_blocks[document, :, query_columns:])
    keys = mine[:, query_columns:value_start] + theirs[:, query_columns:value_start]
    pairs[:, :HEAD_WIDTH] = rotated(keys, cosines[...], sines[...]).astype(jnp.bfloat16)
    values = mine[:, value_start:features] + theirs[:, value_start:features]
    pairs[:, HEAD_WIDTH:] = (values + adapter_scale * value_delta).astype(jnp.bfloat16)
    start = pl.multiple_of(lax.axis_index("tp") * own_rows, own_rows)
    own = pl.ds(start, own_rows)
    own_segments = row_segments(ends, row_positions(first_row + start, own_rows))
    own_low = low_rows(own, own_segments != first)
    query_delta = jnp.zeros((own_rows, query_columns), jnp.float32)
    for document in range(SEGS):
        chosen = jnp.where(own_segments == document, own_low, jnp.zeros_like(own_low))
        query_delta += dot_nn(chosen, up_blocks[document, :, :query_columns])
    projected = mine[own, :query_columns] + theirs[own, :query_columns]
    projected = projected + adapter_scale * query_delta
    for head in range(QHEADS):
        turned = rotated(
            projected[:, head * HEAD_WIDTH : (head + 1) * HEAD_WIDTH], cosines[own], sines[own]
        )
        queries[head * own_rows : (head + 1) * own_rows] = turned.astype(jnp.bfloat16)


def attention_kernel(block_count, unused, lengths, queries, incoming, cosines, sines, *refs):
    blocks = refs[:block_count]
    output, query_grad, kept, sent, low_probs = refs[block_count + unused :]
    own_rows, query_columns = incoming.shape
    rows = blocks[0].shape[0]
    score_scale = HEAD_WIDTH ** (-0.5)
    ends = kernel_marks(lengths)
    seq_index, tp_index = lax.axis_index("seq"), lax.axis_index("tp")
    positions = row_positions(seq_index * rows + tp_index * own_rows, own_rows)
    positions = jnp.concatenate([positions] * QHEADS, axis=0)
    segments = row_segments(ends, positions)
    starts = jnp.where(segments == 0, 0, jnp.where(segments == 1, ends[0], ends[1]))
    scores = []
    for back, block in enumerate(blocks):
        key_positions = (seq_index - back) * rows + lax.broadcasted_iota(jnp.int32, (1, rows), 1)
        allowed = (key_positions <= positions) & (key_positions >= starts)
        block_scores = dot_nt(queries[...], block[:, :HEAD_WIDTH]) * score_scale
        scores.append(jnp.where(allowed, block_scores, masked_score))
    row_max = functools.reduce(
        jnp.maximum, [jnp.max(part, axis=1, keepdims=True) for part in scores]
    )
    raised = [jnp.exp(part - row_max) for part in scores]
    row_total = sum(jnp.sum(part, axis=1, keepdims=True) for part in raised)
    inverse = 1.0 / row_total
    probs = [part * inverse for part in raised]
    weighted = jnp.zeros((QHEADS * own_rows, HEAD_WIDTH), jnp.float32)
    for back, block in enumerate(blocks):
        low_probs[back] = probs[back].astype(jnp.bfloat16)
        weighted += dot_nn(low_probs[back], block[:, HEAD_WIDTH:])
    attended = weighted.astype(jnp.bfloat16)
    gradients = jnp.concatenate(
        [incoming[:, head * HEAD_WIDTH : (head + 1) * HEAD_WIDTH] for head in range(QHEADS)],
        axis=0,
    )
    row_delta = jnp.sum(
        gradients.astype(jnp.float32) * attended.astype(jnp.float32), axis=1, keepdims=True
    )
    start = pl.multiple_of(tp_index * own_rows, own_rows)
    total = jnp.zeros((QHEADS * own_rows, HEAD_WIDTH), jnp.float32)
    for back, block in enumerate(blocks):
        prob_grad = dot_nt(gradients, block[:, HEAD_WIDTH:])
        score_grad = (probs[back] * (prob_grad - row_delta)).astype(jnp.bfloat16)
        total += dot_nn(score_grad, block[:, :HEAD_WIDTH])
        key_part = dot_tn(score_grad, queries[...]) * score_scale
        value_part = dot_tn(low_probs[back], gradients)
        mine = tp_index == 0
        kept[back, :, :HEAD_WIDTH] = jnp.where(mine, key_part[:own_rows], key_part[own_rows:])
        sent[back, :, :HEAD_WIDTH] = jnp.where(mine, key_part[own_rows:], key_part[:own_rows])
        kept[back, :, HEAD_WIDTH:] = jnp.where(mine, value_part[:own_rows], value_part[own_rows:])
        sent[back, :, HEAD_WIDTH:] = jnp.where(mine, value_part[own_rows:], value_part[:own_rows])
    own = pl.ds(start, own_rows)
    for head in range(QHEADS):
        picked = slice(head * own_rows, (head + 1) * own_rows)
        columns = slice(head * HEAD_WIDTH, (head + 1) * HEAD_WIDTH)
        output[:, columns] = attended[picked]
        query_grad[:, columns] = rotated(
            total[picked] * score_scale, cosines[own], -sines[own]
        ).astype(jnp.bfloat16)


def sum_kernel(unused, kept, arrived, *refs):
    for back, total in enumerate(refs[unused:]):
        total[...] = kept[back] + arrived[back]


def pair_kernel(terms, cosines, sines, *refs):
    parts, pair = refs[:terms], refs[-2]
    own_rows = pair.shape[0]
    total = sum(part[...] for part in parts)
    own = pl.ds(pl.multiple_of(lax.axis_index("tp") * own_rows, own_rows), own_rows)
    keys = rotated(total[:, :HEAD_WIDTH], cosines[own], -sines[own])
    pair[:, :HEAD_WIDTH] = keys.astype(jnp.bfloat16)
    pair[:, HEAD_WIDTH:] = total[:, HEAD_WIDTH:].astype(jnp.bfloat16)


def rank_kernel(
    seq_count, lengths, own_query, other_query, own_pair, other_pair, low_rank, up_blocks, *refs
):
    gradients, rank_grad = refs[:2]
    split_terms, (terms, blocks) = refs[2:-2], refs[-2:]
    own_rows, query_columns = own_query.shape
    rows = low_rank.shape[0]
    seq_index = lax.axis_index("seq")
    start = pl.multiple_of(lax.axis_index("tp") * own_rows, own_rows)
    other = pl.multiple_of(own_rows - start, own_rows)
    gradients[pl.ds(start, own_rows), :query_columns] = own_query[...]
    gradients[pl.ds(other, own_rows), :query_columns] = other_query[...]
    value_start = query_columns + HEAD_WIDTH
    features = value_start + HEAD_WIDTH
    gradients[pl.ds(start, own_rows), query_columns:features] = own_pair[...]
    gradients[pl.ds(other, own_rows), query_columns:features] = other_pair[...]
    query_grad = gradients[:, :query_columns]
    value_grad = gradients[:, value_start:features]
    low = low_rank[...]
    rank = low.shape[1] // 2
    segments = row_segments(kernel_marks(lengths), row_positions(seq_index * rows, rows))
    total = jnp.zeros((rows, low.shape[1]), jnp.float32)
    for document in range(SEGS):
        member = segments == document
        parts = dot_nt(query_grad, up_blocks[document, :, :query_columns])
        parts += dot_nt(value_grad, up_blocks[document, :, query_columns:])
        total = jnp.where(member, parts, total)
        chosen = jnp.where(member, low, jnp.zeros_like(low))
        query_terms = dot_tn(chosen, query_grad)
        value_terms = dot_tn(chosen, value_grad)
        place = slice(document * rank, (document + 1) * rank)
        terms[place, :query_columns] = adapter_scale * query_terms[:rank]
        terms[place, query_columns:] = adapter_scale * value_terms[rank:]
    turned = (adapter_scale * total).astype(jnp.bfloat16)
    rank_grad[...] = turned
    second = segments != (seq_index >= seq_count // 2).astype(jnp.int32)
    nothing = jnp.zeros_like(turned)
    middle = features + low.shape[1]
    gradients[:, features:middle] = jnp.where(second, nothing, turned)
    gradients[:, middle:] = jnp.where(second, turned, nothing)
    held = blocks.shape[2]
    for holder in range(seq_count):
        blocks[holder] = terms[:, holder * held : (holder + 1) * held]
    for steps, block in enumerate(split_terms):
        mine = blocks[ring_index(seq_index + steps - seq_count, seq_count)]
        if block.shape == mine.shape:
            block[...] = mine
            continue
        tail = held - 128
        count = 128 // tail
        height = mine.shape[0] // count
        first_low = mine.shape[0] + height
        block[: mine.shape[0]] = mine[:, :128]
        for part in range(count):
            block[mine.shape[0] : first_low, part * tail : (part + 1) * tail] = mine[
                part * height : (part + 1) * height, 128:
            ]
        block[first_low:, : low.shape[1]] = turned[: rows // 2].astype(jnp.float32)
        block[first_low:, low.shape[1] :] = turned[rows // 2 :].astype(jnp.float32)


def token_kernel(gradients, matrix, token_grad):
    token_grad[...] = dot_nn(gradients[...], matrix[...]).astype(jnp.bfloat16)


def down_kernel(block_count, lengths, *refs):
    columns = refs[:block_count]
    up_parts = refs[block_count : 2 * block_count]
    packed = up_parts[0].shape != up_parts[1].shape
    rank_count = 1 if packed else block_count
    ranks = refs[2 * block_count : 2 * block_count + rank_count]
    outputs = refs[2 * block_count + rank_count :]
    rows, joint_rank = ranks[0].shape
    ends = kernel_marks(lengths)
    up_rows, up_width = up_parts[0].shape
    lows, ups = [ranks[0][...]], [up_parts[0][...]]
    for behind in range(1, block_count):
        if not packed:
            lows.append(ranks[behind][...])
            ups.append(up_parts[behind][...])
            continue
        part = up_parts[behind]
        count = 128 // (up_width - 128)
        first_low = up_rows + up_rows // count
        halves = [part[first_low:, :joint_rank], part[first_low:, joint_rank:]]
        lows.append(jnp.concatenate(halves, axis=0).astype(jnp.bfloat16))
    all_terms = []
    for document in range(SEGS):
        total = jnp.zeros((joint_rank, columns[0].shape[1]), jnp.float32)
        for behind in range(block_count):
            holder = ring_index(lax.axis_index("seq") - behind, block_count)
            segments = row_segments(ends, row_positions(holder * rows, rows))
            chosen = jnp.where(segments == document, lows[behind], jnp.zeros_like(lows[behind]))
            total += dot_tn(chosen, columns[behind][...])
        all_terms.append(total)
    down_terms = jnp.concatenate(all_terms, axis=0)
    if not packed:
        outputs[0][...] = down_terms
        outputs[1][...] = sum(ups)
        return
    own_down, far, own_up, up_terms = outputs
    tail = up_width - 128
    height = up_rows // (128 // tail)
    up_terms[...] = ups[0]
    for part in up_parts[1:]:
        up_terms[:, :128] += part[:up_rows]
        for piece in range(128 // tail):
            up_terms[piece * height : (piece + 1) * height, 128:] += part[
                up_rows : up_rows + height, piece * tail : (piece + 1) * tail
            ]
    held, held_up = own_down.shape[1], own_up.shape[1]
    ahead = lax.axis_index("batch") == 0
    own_down[...] = jnp.where(ahead, down_terms[:, :held], down_terms[:, held:])
    far[:, :held] = jnp.where(ahead, down_terms[:, held:], down_terms[:, :held])
    left, right = up_terms[:, :held_up], up_terms[:, held_up:]
    own_up[...] = jnp.where(ahead, left, right)
    far_up = jnp.where(ahead, right, left)
    spare = far.shape[1] - held
    far[:up_rows, held:] = far_up[:, :spare]
    far[up_rows:, held : held + held_up - spare] = far_up[:, spare:]


def packed_bank_kernel(bank_rows, own_down, far, own_up, down_zeros, up_zeros, down_out, up_out):
    step = pl.program_id(0)
    joint_rank, held = down_out.shape[1], down_out.shape[3]
    low_width, held_up = up_out.shape[1:]
    up_rows = own_up.shape[0]
    spare = far.shape[1] - held
    down_total = jnp.zeros((joint_rank, held), jnp.float32)
    head = jnp.zeros((low_width, spare), jnp.float32)
    rest = jnp.zeros((low_width, held_up - spare), jnp.float32)
    for document in range(SEGS):
        rows = slice(document * joint_rank, (document + 1) * joint_rank)
        lows = slice(document * low_width, (document + 1) * low_width)
        same = bank_rows[document] == bank_rows[step]
        down_total += jnp.where(same, own_down[rows], 0.0)
        head += jnp.where(same, own_up[lows, :spare], 0.0)
        rest += jnp.where(same, own_up[lows, spare:], 0.0)
        same = bank_rows[SEGS + document] == bank_rows[step]
        down_total += jnp.where(same, far[rows, :held], 0.0)
        head += jnp.where(same, far[lows, held:], 0.0)
        lows = slice(up_rows + document * low_width, up_rows + (document + 1) * low_width)
        rest += jnp.where(same, far[lows, held : held + held_up - spare], 0.0)
    down_out[0, :, 0, :] = down_total
    up_out[0, :, :spare] = head
    up_out[0, :, spare:] = rest


def bank_kernel(block_count, bank_rows, *refs):
    down_terms = refs[:block_count]
    up_terms = refs[block_count : 2 * block_count]
    down_out, up_out = refs[2 * block_count + 2 :]
    step = pl.program_id(0)
    row = bank_rows[step]
    joint_rank = down_out.shape[1]
    low_width = up_out.shape[1]
    down_total = jnp.zeros((joint_rank, down_out.shape[3]), jnp.float32)
    up_total = jnp.zeros((low_width, up_out.shape[2]), jnp.float32)
    for block in range(block_count):
        for document in range(SEGS):
            same = bank_rows[block * SEGS + document] == row
            down_rows = down_terms[block][document * joint_rank : (document + 1) * joint_rank]
            up_rows = up_terms[block][document * low_width : (document + 1) * low_width]
            down_total += jnp.where(same, down_rows, 0.0)
            up_total += jnp.where(same, up_rows, 0.0)
    down_out[0, :, 0, :] = down_total
    up_out[0] = up_total


def shards(
    tokens,
    frozen_qkv_matrix,
    adapter_down_weight,
    adapter_up_weight,
    adapter_bank_row,
    document_lengths,
    document_adapter,
    output_gradient,
):
    seq_count = lax.axis_size("seq")
    batch_count = lax.axis_size("batch")
    group_count = lax.axis_size("groups")
    chip_size = lax.axis_size("tp")
    seq_index = lax.axis_index("seq")
    batch_index = lax.axis_index("batch")
    group_index = lax.axis_index("groups")
    tp_index = lax.axis_index("tp")
    local_tokens = tokens[0]
    rows, width = local_tokens.shape
    own_rows = rows // chip_size
    query_columns = QHEADS * HEAD_WIDTH
    frozen_rows = frozen_qkv_matrix.shape[0]
    features = frozen_rows * seq_count
    low_width = ADAPTER_RANK
    joint_rank = adapter_down_weight.shape[1]
    adapters = adapter_bank_row.shape[0]
    bf16 = jnp.bfloat16
    f32 = jnp.float32

    lengths = lax.dynamic_index_in_dim(document_lengths, batch_index, 0, keepdims=False)
    first_end = lengths[0]
    second_end = first_end + lengths[1]
    half_count = seq_count // 2
    held_down = adapter_down_weight.shape[3]
    held_up = adapter_up_weight.shape[2]
    down_width = held_down * batch_count
    up_width = held_up * batch_count

    positions = seq_index * rows + jnp.arange(rows, dtype=jnp.int32)
    inside = positions - jnp.where(
        positions >= second_end, second_end, jnp.where(positions >= first_end, first_end, 0)
    )
    exponent = jnp.arange(HEAD_WIDTH // 2, dtype=f32) * (2.0 / HEAD_WIDTH)
    inverse = jnp.power(jnp.float32(rope_base), -exponent)
    angles = inside.astype(f32)[:, None] * jnp.concatenate([inverse, inverse])[None, :]
    signs = jnp.where(jnp.arange(HEAD_WIDTH) < HEAD_WIDTH // 2, -1.0, 1.0).astype(f32)
    cosines = jnp.cos(angles)
    sines = jnp.sin(angles) * signs[None, :]

    sample_rows = lookup_rows(adapter_bank_row, document_adapter)
    bank_rows = sample_rows.reshape(-1)
    if batch_count == 2:
        own_bank = jnp.where(batch_index == 0, sample_rows[0], sample_rows[1])
        far_bank = jnp.where(batch_index == 0, sample_rows[1], sample_rows[0])
        bank_rows = jnp.concatenate([own_bank, far_bank])
    down_bank = adapter_down_weight[:, :, 0, :]
    down_zeros = jnp.zeros((adapters, joint_rank, 1, held_down), f32)
    up_zeros = jnp.zeros((adapters, low_width, held_up), f32)

    plane_count = group_count * batch_count
    share = width // plane_count
    padded_down = (held_down + 127) // 128 * 128
    direct = (
        group_count == 2
        and seq_count == 4
        and share == down_width
        and batch_count == 2
        and share % 128 == 0
        and down_width % 128 == 0
        and frozen_rows % 16 == 0
        and 4 * up_width <= down_width
        and up_width > 128
        and 128 % (up_width - 128) == 0
        and 0 < held_up + held_down - padded_down <= padded_down - held_down
    )
    up_entries = []
    if direct:
        own_share = lax.dynamic_slice_in_dim(
            frozen_qkv_matrix, (group_index * batch_count + batch_index) * share, share, axis=1
        )
        before = shift(own_share, "seq", 1)
        after = shift(own_share, "seq", 3)
        far_down = shift(down_bank[far_bank], "batch", 1)
        far_up = shift(adapter_up_weight[far_bank], "batch", 1)
        own_down, own_up = down_bank[own_bank], adapter_up_weight[own_bank]
        payload_rows = 2 * joint_rank + low_width // 2
        pack_shapes = [(2 * frozen_rows, share), (frozen_rows + payload_rows, share)]
        pack_shapes += [(payload_rows, share)] * 3
        plane, forward, payload, *payloads = pl.pallas_call(
            pack_kernel,
            out_shape=[jax.ShapeDtypeStruct(shape, bf16) for shape in pack_shapes],
            in_specs=[in_vmem()] * 6,
            out_specs=[by_block(shape) for shape in pack_shapes],
            scratch_shapes=[
                pltpu.VMEM((SEGS * joint_rank, down_width), bf16),
                pltpu.VMEM((SEGS, low_width, 2 * held_up), bf16),
            ],
            compiler_params=pltpu.CompilerParams(vmem_limit_bytes=16 * mebibyte),
            cost_estimate=cost(0, 8 * frozen_rows * share),
            name="pack",
        )(own_down, far_down, own_up, far_up, before, after)

        def over_plane(value):
            over_both = [(at, plane_count - 1 - at) for at in range(plane_count)]
            return [
                shift(value, "batch", 1),
                shift(value, "groups", 1),
                lax.ppermute(value, ("groups", "batch"), over_both),
            ]

        plane_parts = over_plane(plane)
        forward = shift(forward, "seq", 1)
        middle = forward[:frozen_rows]
        middle_parts = over_plane(middle)
        payloads = [shift(part, "seq", steps + 2) for steps, part in enumerate(payloads)]
        arrays = [frozen_qkv_matrix, before, after, forward, payload] + payloads
        arrays += plane_parts + middle_parts

        def frozen_at(behind, batch_step, group_step):
            return frozen_place(seq_count, frozen_rows, share, behind, batch_step, group_step)

        def down_at(behind):
            return down_place(seq_count, features, down_width, behind)

        entries = [
            (0, 0, frozen_rows, frozen_place(seq_count, frozen_rows, None, 0, 0, 0)),
            (1, 0, frozen_rows, frozen_at(1, 0, 0)),
            (2, 0, frozen_rows, frozen_at(3, 0, 0)),
            (3, 0, frozen_rows, frozen_at(2, 0, 0)),
            (4, 0, 2 * joint_rank, down_at(0)),
            (3, frozen_rows, 2 * joint_rank, down_at(1)),
            (5, 0, 2 * joint_rank, down_at(2)),
            (6, 0, 2 * joint_rank, down_at(3)),
        ]
        up_entries = [(4, 2 * joint_rank, 0), (3, frozen_rows + 2 * joint_rank, 1)]
        up_entries += [(5, 2 * joint_rank, 2), (6, 2 * joint_rank, 3)]
        for number, (batch_step, group_step) in enumerate(((1, 0), (0, 1), (1, 1))):
            entries += [
                (7 + number, 0, frozen_rows, frozen_at(1, batch_step, group_step)),
                (7 + number, frozen_rows, frozen_rows, frozen_at(3, batch_step, group_step)),
                (10 + number, 0, frozen_rows, frozen_at(2, batch_step, group_step)),
            ]
        early = [forward, cosines, sines, bank_rows]
        column_blocks = pl.pallas_call(
            functools.partial(cut_kernel, len(early), seq_count),
            out_shape=[jax.ShapeDtypeStruct((rows, down_width), bf16)] * seq_count,
            in_specs=[in_vmem()] + [in_place()] * len(early),
            out_specs=[by_block((rows, down_width))] * seq_count,
            compiler_params=pltpu.CompilerParams(vmem_limit_bytes=16 * mebibyte),
            cost_estimate=cost(0, 4 * rows * width),
            name="cut",
        )(local_tokens, *early)
    else:
        bank_rows = sample_rows.reshape(-1)
        got_down = lax.all_to_all(
            down_bank[sample_rows], "batch", split_axis=0, concat_axis=0, tiled=True
        )
        got_up = lax.all_to_all(
            adapter_up_weight[sample_rows], "batch", split_axis=0, concat_axis=0, tiled=True
        )
        down_block = jnp.transpose(got_down, (1, 2, 0, 3)).reshape(SEGS * joint_rank, -1)
        up_block = jnp.transpose(got_up, (1, 2, 0, 3)).reshape(SEGS * low_width, -1)
        all_down = lax.all_gather(down_block, "seq", axis=0)
        all_up = lax.all_gather(up_block, "seq", axis=0)
        first = (seq_index >= half_count).astype(jnp.int32)
        merged = jnp.transpose(all_down, (1, 0, 2)).reshape(SEGS * joint_rank, -1)
        arrays = [
            lax.all_gather(frozen_qkv_matrix, "seq", axis=0, tiled=True),
            lax.dynamic_slice_in_dim(merged, first * joint_rank, 2 * joint_rank),
        ]
        entries = [
            (0, 0, features, whole_place(0)),
            (1, 0, 2 * joint_rank, whole_place(features)),
        ]
        up_rows = jnp.transpose(all_up, (1, 0, 2)).reshape(SEGS, low_width, -1)
        is_query = jnp.arange(up_rows.shape[2]) < query_columns
        up_blocks = jnp.concatenate(
            [
                jnp.where(is_query[None, None, :], up_rows, 0),
                jnp.where(is_query[None, None, :], 0, up_rows),
            ],
            axis=1,
        )
        column_blocks = [
            lax.dynamic_slice_in_dim(
                local_tokens,
                jnp.remainder(seq_index + steps, seq_count) * down_width,
                down_width,
                axis=1,
            )
            for steps in range(seq_count)
        ]

    column_parts = [
        shift(block, "seq", steps) if steps else block
        for steps, block in enumerate(column_blocks)
    ]
    early = [column_parts[2]] if direct and seq_count > 3 else []
    up_shape = (SEGS, joint_rank, query_columns + HEAD_WIDTH)
    matrix_rows = features + 2 * joint_rank
    arrived = [pltpu.VMEM((seq_count, low_width // 2, down_width), bf16)] if direct else []
    part, matrix, *built = pl.pallas_call(
        functools.partial(
            project_kernel, len(arrays), entries, up_entries, len(early), seq_count
        ),
        out_shape=[
            jax.ShapeDtypeStruct((rows, matrix_rows), f32),
            jax.ShapeDtypeStruct((matrix_rows, width), bf16),
        ]
        + ([jax.ShapeDtypeStruct(up_shape, bf16)] if direct else []),
        in_specs=[in_vmem()] + [in_place()] * (len(arrays) + len(early)),
        out_specs=[in_vmem(), in_place()] + ([by_block(up_shape)] if direct else []),
        scratch_shapes=arrived
        + [
            pltpu.VMEM((matrix_rows, width), bf16),
            pltpu.SemaphoreType.DMA((len(entries) + len(up_entries) + 1,)),
        ],
        compiler_params=pltpu.CompilerParams(vmem_limit_bytes=20 * mebibyte),
        cost_estimate=cost(2 * rows * width * matrix_rows, 2 * width * (matrix_rows + rows)),
        name="project",
    )(local_tokens, *arrays, *early)
    if direct:
        up_blocks = built[0]

    other_part = shift(part, "tp", 1)
    queries, pairs, low_rank = pl.pallas_call(
        functools.partial(qkv_kernel, seq_count, 0),
        out_shape=(
            jax.ShapeDtypeStruct((QHEADS * own_rows, HEAD_WIDTH), bf16),
            jax.ShapeDtypeStruct((rows, 2 * HEAD_WIDTH), bf16),
            jax.ShapeDtypeStruct((rows, joint_rank), bf16),
        ),
        in_specs=[in_smem()] + [in_vmem()] * 5,
        out_specs=(in_vmem(),) * 3,
        compiler_params=pltpu.CompilerParams(vmem_limit_bytes=8 * mebibyte),
        cost_estimate=cost(2 * rows * 3 * 64 * 640, 8 * rows * features),
        name="qkv",
    )(document_lengths, part, other_part, up_blocks, cosines, sines)

    blocks = [pairs] + [push(pairs, "seq", back) for back in range(1, half_count + 1)]
    block_count = len(blocks)
    column_parts[1] = shift(pass_after(column_blocks[1], *blocks[1:]), "seq", 1)
    incoming = output_gradient[0]
    early_columns = [down_zeros, up_zeros]
    attention, query_grad, kept, sent = pl.pallas_call(
        functools.partial(attention_kernel, block_count, len(early_columns)),
        out_shape=(
            jax.ShapeDtypeStruct((own_rows, query_columns), bf16),
            jax.ShapeDtypeStruct((own_rows, query_columns), bf16),
            jax.ShapeDtypeStruct((block_count, own_rows, 2 * HEAD_WIDTH), f32),
            jax.ShapeDtypeStruct((block_count, own_rows, 2 * HEAD_WIDTH), f32),
        ),
        in_specs=[in_smem()]
        + [in_vmem()] * (4 + block_count)
        + [in_place()] * len(early_columns),
        out_specs=(in_vmem(),) * 4,
        scratch_shapes=[pltpu.VMEM((block_count, QHEADS * own_rows, rows), bf16)],
        compiler_params=pltpu.CompilerParams(vmem_limit_bytes=(8 + 4 * block_count) * mebibyte),
        cost_estimate=cost(
            10 * block_count * QHEADS * own_rows * rows * HEAD_WIDTH,
            4 * rows * features,
            block_count * QHEADS * own_rows * rows,
        ),
        name="attention",
    )(document_lengths, queries, incoming, cosines, sines, *blocks, *early_columns)

    other_query = shift(query_grad, "tp", 1)
    due = [column_parts[1]]
    pair_sums = pl.pallas_call(
        functools.partial(sum_kernel, len(due)),
        out_shape=[jax.ShapeDtypeStruct((own_rows, 2 * HEAD_WIDTH), f32)] * block_count,
        in_specs=[in_vmem()] * 2 + [in_place()] * len(due),
        out_specs=[in_vmem()] * block_count,
        compiler_params=pltpu.CompilerParams(vmem_limit_bytes=8 * mebibyte),
        cost_estimate=cost(0, 12 * block_count * own_rows * 2 * HEAD_WIDTH),
        name="pair_sums",
    )(kept, shift(sent, "tp", 1), *due)
    pair_terms = [pair_sums[0]]
    pair_terms += [push(pair_sums[back], "seq", -back) for back in range(1, block_count)]
    pair_grad, late_block = pl.pallas_call(
        functools.partial(pair_kernel, block_count),
        out_shape=[
            jax.ShapeDtypeStruct((own_rows, 2 * HEAD_WIDTH), bf16),
            jax.ShapeDtypeStruct((rows, down_width), bf16),
        ],
        in_specs=[in_vmem()] * (2 + block_count) + [in_place()],
        out_specs=[in_vmem(), in_place()],
        input_output_aliases={2 + block_count: 1},
        compiler_params=pltpu.CompilerParams(vmem_limit_bytes=8 * mebibyte),
        cost_estimate=cost(0, 12 * block_count * own_rows * 2 * HEAD_WIDTH),
        name="pair_gradients",
    )(cosines, sines, *pair_terms, column_blocks[-1])
    column_parts[-1] = shift(late_block, "seq", seq_count - 1)
    other_pair = shift(pair_grad, "tp", 1)

    split_shapes = [(SEGS * low_width, up_width)] * seq_count
    if direct:
        sent_rows = SEGS * low_width * up_width // 128 + rows // 2
        split_shapes[1:] = [(sent_rows, 128)] * (seq_count - 1)
    gradients, rank_grad, *up_split = pl.pallas_call(
        functools.partial(rank_kernel, seq_count),
        out_shape=[
            jax.ShapeDtypeStruct((rows, matrix_rows), bf16),
            jax.ShapeDtypeStruct((rows, joint_rank), bf16),
        ]
        + [jax.ShapeDtypeStruct(shape, f32) for shape in split_shapes],
        in_specs=[in_smem()] + [in_vmem()] * 6,
        out_specs=[by_block((rows, matrix_rows)), in_vmem()]
        + [by_block(shape) for shape in split_shapes],
        scratch_shapes=[
            pltpu.VMEM((SEGS * low_width, features - HEAD_WIDTH), f32),
            pltpu.VMEM((seq_count, SEGS * low_width, held_up * batch_count), f32),
        ],
        compiler_params=pltpu.CompilerParams(vmem_limit_bytes=8 * mebibyte),
        cost_estimate=cost(4 * rows * 3 * 64 * 640, 4 * rows * features),
        name="rank_gradients",
    )(
        document_lengths, query_grad, other_query, pair_grad, other_pair, low_rank, up_blocks
    )

    rank_parts = [rank_grad]
    if not direct:
        rank_parts += [shift(rank_grad, "seq", steps) for steps in range(1, seq_count)]
    up_sums = [
        shift(block, "seq", steps) if steps else block for steps, block in enumerate(up_split)
    ]

    chunk = 512
    token_grad = pl.pallas_call(
        token_kernel,
        grid=(width // chunk,),
        out_shape=jax.ShapeDtypeStruct((rows, width), bf16),
        in_specs=[
            pl.BlockSpec((rows, matrix_rows), lambda step: (0, 0)),
            pl.BlockSpec((matrix_rows, chunk), lambda step: (0, step)),
        ],
        out_specs=pl.BlockSpec((rows, chunk), lambda step: (0, step)),
        compiler_params=pltpu.CompilerParams(vmem_limit_bytes=12 * mebibyte),
        cost_estimate=cost(2 * rows * width * matrix_rows, 2 * width * (matrix_rows + rows)),
        name="token_gradient",
    )(gradients, matrix)

    if direct:
        term_shapes = [(SEGS * joint_rank, held_down), (SEGS * joint_rank, padded_down)]
        term_shapes += [(SEGS * low_width, held_up)]
    else:
        term_shapes = [(SEGS * joint_rank, down_width), (SEGS * low_width, up_width)]
    terms = pl.pallas_call(
        functools.partial(down_kernel, seq_count),
        out_shape=[jax.ShapeDtypeStruct(shape, f32) for shape in term_shapes],
        in_specs=[in_smem()] + [in_vmem()] * (2 * seq_count + len(rank_parts)),
        out_specs=[in_vmem()] * len(term_shapes),
        scratch_shapes=[pltpu.VMEM((SEGS * low_width, up_width), f32)] if direct else [],
        compiler_params=pltpu.CompilerParams(vmem_limit_bytes=8 * mebibyte),
        cost_estimate=cost(
            2 * seq_count * rows * SEGS * joint_rank * down_width, 2 * seq_count * rows * down_width
        ),
        name="down_terms",
    )(document_lengths, *column_parts, *up_sums, *rank_parts)

    if direct:
        bank_terms = [terms[0], shift(terms[1], "batch", 1), terms[2]]
    else:
        down_send = jnp.transpose(
            terms[0].reshape(SEGS * joint_rank, batch_count, held_down), (1, 0, 2)
        )
        up_send = jnp.transpose(
            terms[1].reshape(SEGS * low_width, batch_count, held_up), (1, 0, 2)
        )
        back_down = lax.all_to_all(down_send, "batch", split_axis=0, concat_axis=0, tiled=True)
        back_up = lax.all_to_all(up_send, "batch", split_axis=0, concat_axis=0, tiled=True)
        bank_downs = [back_down[batch] for batch in range(batch_count)]
        bank_ups = [back_up[batch] for batch in range(batch_count)]
        bank_terms = bank_downs + bank_ups


    def whole(array):
        return pl.BlockSpec(array.shape, lambda step, bank: (0,) * array.ndim)

    term_count = len(bank_terms)
    down_grad, up_grad = pl.pallas_call(
        packed_bank_kernel if direct else functools.partial(bank_kernel, batch_count),
        out_shape=(
            jax.ShapeDtypeStruct(down_zeros.shape, f32),
            jax.ShapeDtypeStruct(up_zeros.shape, f32),
        ),
        grid_spec=pltpu.PrefetchScalarGridSpec(
            num_scalar_prefetch=1,
            grid=(batch_count * SEGS,),
            in_specs=[whole(array) for array in bank_terms] + [in_place()] * 2,
            out_specs=(
                pl.BlockSpec(
                    (1, joint_rank, 1, held_down),
                    lambda step, bank: (bank[step], 0, 0, 0),
                ),
                pl.BlockSpec(
                    (1, low_width, held_up),
                    lambda step, bank: (bank[step], 0, 0),
                ),
            ),
        ),
        input_output_aliases={1 + term_count: 0, 2 + term_count: 1},
        compiler_params=pltpu.CompilerParams(vmem_limit_bytes=16 * mebibyte),
        name="bank_rows",
    )(
        bank_rows,
        *bank_terms,
        down_zeros,
        up_zeros,
    )
    return (attention[None], token_grad[None], down_grad, up_grad)


def solution(mesh):
    in_specs = (
        P(("groups", "batch"), "seq", "tp"),
        P("seq", "tp"),
        P(None, None, "tp", ("seq", "batch")),
        P(None, None, ("seq", "batch")),
        P(),
        P("groups", None),
        P("groups", None),
        P(("groups", "batch"), ("seq", "tp"), None),
    )
    out_specs = (
        P(("groups", "batch"), ("seq", "tp"), None),
        P(("groups", "batch"), "seq", "tp"),
        P("groups", None, "tp", ("seq", "batch")),
        P("groups", None, ("seq", "batch")),
    )
    return jax.shard_map(shards, mesh=mesh, in_specs=in_specs, out_specs=out_specs, check_vma=False)
```
